32 devices in a mesh: blk: 8 (over z, y), sub: 4 (over x, core).
Axes of the slice: x: 2, y: 2, z: 4, core: 2. Of those that a mesh axis runs over, the one named last changes fastest.
Arguments:
- tracers: float32 [320, 4, 5400], P(('blk', 'sub')), may hold values from -6 to 6
- velocity: float32 [320, 4, 5400], P(('blk', 'sub')), may hold values from -3 to 3
- kappa: float32 [320, 5400], P(('blk', 'sub')), may hold values from 0.1 to 4
- kmt: float32 [320, 5400], P(('blk', 'sub')), may hold values from -1 to 2.5
- block_owner: int32 [160], replicated, may hold values from 0 to 319, as said below
- neighbours: int32 [160, 4], replicated, may hold values from -1 to 159, as said below
- fold_partner: int32 [160], replicated, may hold values from -1 to 159, as said below
Outputs:
- tracers_out: float32 [320, 4, 5400], P(('blk', 'sub'))
The draws below stay inside these ranges and needn't reach their ends.
Inputs may be any that keep to these rules, and one draw needn't show every extreme that they name: `block_owner`: the values are distinct. Every device holds between 3 and 10 blocks, in its first slots; devices in index order hold consecutive runs of the blocks taken along a serpentine curve over the block grid. `neighbours`: row b lists the blocks west, east, south and north of block b on a grid of 40 by 5 blocks that is periodic from west to east, or -1 where that place is land or off the grid; the north entry of the northernmost row is -1. The owner of every listed block lies at most 27 devices from the owner of block b. `fold_partner`: for a block of the northernmost row, the block of that row at the mirrored column (39 - column); -1 for all other blocks. Its owner lies at most 27 devices from block b's owner.
All inputs are finite; a program needn't handle non-finite values.
Results may differ from the reference program's by a relative error of at most 0.0003.
Values sent between devices are 32-bit elements; how exact they have to be, the bound alone decides.
No kernel may reach another device: no remote copies, remote signals or barrier semaphores. Data moves between devices by JAX's collectives and lax.ppermute only.
A program may use at most 192 MiB of HBM per device.

```python
import math
import jax
import jax.numpy as jnp
from jax import lax

IB = 90
JB = 60
VERTICAL_LEVELS = 2
TRACER_COUNT = 2
STEPS = 1
NBX = 40
DEVICE_SLOTS = 10
REACH = 27
NBY = 5
NBLK = 160
TOTAL_SLOTS = 320
BLOCK_COLUMNS = 5400


def device_loads(load_key):
    device_number = TOTAL_SLOTS // DEVICE_SLOTS
    light_count = min(REACH, 5 * device_number // 8)
    deficit = 2 * light_count
    heavy_count = deficit // 5
    extra_load = deficit % 5
    rest_count = device_number - light_count - heavy_count - 1
    pair_count = rest_count // 2
    lone_count = rest_count - 2 * pair_count
    prefix = jnp.array([3] * light_count + [10] * heavy_count + [5 + extra_load], jnp.int32)
    swing = jax.random.randint(load_key, (pair_count,), -2, 3).astype(jnp.int32)
    paired = jnp.stack([5 + swing, 5 - swing], axis=1).reshape(-1)
    trailing = jnp.full((lone_count,), 5, jnp.int32)
    return jnp.concatenate([prefix, paired, trailing])


def build_grid(key):
    key = jax.random.fold_in(key, 17)
    land_key, label_key, load_key = jax.random.split(key, 3)
    places = NBX * NBY
    block_count = NBLK
    land_count = places - block_count
    place_ids = jnp.arange(places, dtype=jnp.int32)
    row_ids = place_ids // NBX
    col_ids = place_ids % NBX
    eligible = (row_ids >= 1) & (row_ids <= NBY - 2)
    shuffled = jax.random.permutation(land_key, places).astype(jnp.int32)
    land_score = jnp.where(eligible, shuffled, places + place_ids)
    land_order = jnp.argsort(land_score)
    is_land = jnp.zeros((places,), jnp.int32).at[land_order[:land_count]].set(1)
    curve_key = row_ids * NBX + jnp.where(row_ids % 2 == 0, col_ids, NBX - 1 - col_ids)
    curve_order = jnp.argsort(jnp.where(is_land == 1, places + curve_key, curve_key)).astype(jnp.int32)
    curve_rank = jnp.zeros((places,), jnp.int32).at[curve_order].set(place_ids)
    labels = jax.random.permutation(label_key, block_count).astype(jnp.int32)
    place_label = jnp.where(is_land == 1, -1, labels[jnp.minimum(curve_rank, block_count - 1)])
    loads = device_loads(load_key)
    ends = jnp.cumsum(loads).astype(jnp.int32)
    starts = ends - loads
    ranks = jnp.arange(block_count, dtype=jnp.int32)
    owner_dev = jnp.sum((ends[None, :] <= ranks[:, None]).astype(jnp.int32), axis=1)
    owner_code = owner_dev * DEVICE_SLOTS + ranks - starts[owner_dev]
    block_owner = jnp.zeros((block_count,), jnp.int32).at[labels].set(owner_code)
    west_place = row_ids * NBX + (col_ids + NBX - 1) % NBX
    east_place = row_ids * NBX + (col_ids + 1) % NBX
    south_place = jnp.where(row_ids > 0, place_ids - NBX, -1)
    north_place = jnp.where(row_ids < NBY - 1, place_ids + NBX, -1)
    mirror_place = jnp.where(row_ids == NBY - 1, row_ids * NBX + NBX - 1 - col_ids, -1)

    def label_of(target):
        return jnp.where(target >= 0, place_label[jnp.maximum(target, 0)], -1)
    table = jnp.stack([label_of(west_place), label_of(east_place), label_of(south_place), label_of(north_place)], axis=1)
    ocean_places = curve_order[:block_count]
    neighbours = jnp.zeros((block_count, 4), jnp.int32).at[labels].set(table[ocean_places])
    fold_partner = jnp.zeros((block_count,), jnp.int32).at[labels].set(label_of(mirror_place)[ocean_places])
    return (block_owner, neighbours, fold_partner)


def draw_block_owner(key, part):
    return build_grid(key)[0]


def draw_neighbours(key, part):
    return build_grid(key)[1]


def draw_fold_partner(key, part):
    return build_grid(key)[2]


def level_of(key, extent, cuts, smallest, largest):
    def one(axis_at, parts):
        steps = jax.random.uniform(jax.random.fold_in(jax.random.fold_in(key, 6), axis_at), (parts,), jnp.float32, smallest / len(cuts), largest / len(cuts))
        return jnp.repeat(jnp.exp(steps), extent[axis_at] // parts).reshape((-1,) + (1,) * (len(extent) - axis_at - 1))

    gain = one(*cuts[0])
    for cut in cuts[1:]:
        gain = gain * one(*cut)
    return gain


def noise(own_key, shape, scale, most, cuts=(), kind=jnp.bfloat16):
    entries = jax.random.normal(own_key, shape, jnp.float32) * scale
    if len(cuts) > 0:
        entries = level_of(own_key, shape, cuts, -0.22, 0.18) * entries
    return jnp.clip(entries, min=-most, max=most).astype(kind)


def setup_inputs(seed: int = 0) -> dict:
    keys = jax.random.split(jax.random.key(seed), 8)
    return {
        "tracers": noise(keys[0], (TOTAL_SLOTS, TRACER_COUNT * VERTICAL_LEVELS, BLOCK_COLUMNS), 1.0, 6.0, ((0, 32),), jnp.float32),
        "velocity": noise(keys[1], (TOTAL_SLOTS, 2 * VERTICAL_LEVELS, BLOCK_COLUMNS), 0.5, 3.0, ((0, 32),), jnp.float32),
        "kappa": jnp.clip(jnp.exp(math.log(4.0) - 3.6888794 * jax.random.uniform(keys[2], (TOTAL_SLOTS, BLOCK_COLUMNS), jnp.float32) ** level_of(keys[2], (TOTAL_SLOTS, BLOCK_COLUMNS), ((0, 32),), -0.2, 0.2)), 0.1, 4.0),
        "kmt": jnp.clip(-1.0 + 3.5 * jax.random.uniform(keys[3], (TOTAL_SLOTS, BLOCK_COLUMNS), jnp.float32) ** level_of(keys[3], (TOTAL_SLOTS, BLOCK_COLUMNS), ((0, 32),), -0.2, 0.2), -1.0, 2.5),
        "block_owner": draw_block_owner(jax.random.fold_in(keys[7], 71), 0),
        "neighbours": draw_neighbours(jax.random.fold_in(keys[7], 71), 0),
        "fold_partner": draw_fold_partner(jax.random.fold_in(keys[7], 71), 0),
    }


COURANT = 0.2


def edge_pack(block_field):
    count, chans, rows, cols = block_field.shape
    west_edge = block_field[:, :, :, 0:2].reshape(count, chans, rows * 2)
    east_edge = block_field[:, :, :, cols - 2:].reshape(count, chans, rows * 2)
    south_edge = block_field[:, :, 0:2, :].reshape(count, chans, 2 * cols)
    north_edge = block_field[:, :, rows - 2:, :].reshape(count, chans, 2 * cols)
    return jnp.concatenate([west_edge, east_edge, south_edge, north_edge], axis=2)


def fetch(source, link_codes):
    safe_codes = jnp.maximum(link_codes, 0)
    picked = jnp.take(source, safe_codes.reshape(-1), axis=0)
    picked = picked.reshape(link_codes.shape + source.shape[1:])
    return jnp.where((link_codes >= 0)[..., None, None], picked, 0.0)


def extend(block_field, sources, fold_sign):
    count, chans, rows, cols = block_field.shape
    strip = 2 * rows
    west_halo = sources[:, 0, :, strip:2 * strip].reshape(count, chans, rows, 2)
    east_halo = sources[:, 1, :, 0:strip].reshape(count, chans, rows, 2)
    south_halo = sources[:, 2, :, 2 * strip + 2 * cols:].reshape(count, chans, 2, cols)
    north_halo = sources[:, 3, :, 2 * strip:2 * strip + 2 * cols].reshape(count, chans, 2, cols)
    mirrored = sources[:, 4, :, 2 * strip + 2 * cols:].reshape(count, chans, 2, cols)[:, :, ::-1, ::-1]
    north_halo = north_halo + fold_sign * mirrored
    middle = jnp.concatenate([west_halo, block_field, east_halo], axis=3)
    corner = jnp.zeros((count, chans, 2, 2), block_field.dtype)
    bottom = jnp.concatenate([corner, south_halo, corner], axis=3)
    top_rows = jnp.concatenate([corner, north_halo, corner], axis=3)
    return jnp.concatenate([bottom, middle, top_rows], axis=2)


def prepare(static_ext, diffusivity):
    levels = (static_ext.shape[1] - 1) // 2
    rows = static_ext.shape[2] - 4
    cols = static_ext.shape[3] - 4
    east_vel = static_ext[:, :levels]
    north_vel = static_ext[:, levels:2 * levels]
    depth = static_ext[:, 2 * levels:]
    level_ids = jnp.arange(levels).astype(static_ext.dtype).reshape(1, levels, 1, 1)
    wet = jnp.clip(depth - level_ids, 0.0, 1.0).astype(static_ext.dtype)
    face_x = 0.5 * (east_vel[:, :, 2:rows + 2, 1:cols + 2] + east_vel[:, :, 2:rows + 2, 2:cols + 3])
    face_x = face_x * wet[:, :, 2:rows + 2, 1:cols + 2] * wet[:, :, 2:rows + 2, 2:cols + 3]
    face_y = 0.5 * (north_vel[:, :, 1:rows + 2, 2:cols + 2] + north_vel[:, :, 2:rows + 3, 2:cols + 2])
    face_y = face_y * wet[:, :, 1:rows + 2, 2:cols + 2] * wet[:, :, 2:rows + 3, 2:cols + 2]
    inner = wet[:, :, 2:rows + 2, 2:cols + 2]
    coupling = diffusivity[:, None] * inner[:, :-1] * inner[:, 1:]
    return face_x, face_y, inner, coupling


def face_flux(velocity_face, left_far, left_near, right_near, right_far):
    centered = (7.0 * (left_near + right_near) - (left_far + right_far)) / 12.0
    upwind = (right_far - 3.0 * right_near + 3.0 * left_near - left_far) / 12.0
    return velocity_face * centered + jnp.abs(velocity_face) * upwind


def vertical_solve(rhs_cols, coupling):
    levels = rhs_cols.shape[2]
    partials = []
    ratios = []
    for level in range(levels):
        coef_below = coupling[:, :, level] if level < levels - 1 else 0.0
        coef_above = coupling[:, :, level - 1] if level > 0 else 0.0
        diagonal = 1.0 + coef_above + coef_below
        if level == 0:
            divider_value = diagonal
            partial_value = rhs_cols[:, :, 0] / divider_value
        else:
            divider_value = diagonal - coef_above * ratios[-1]
            partial_value = (rhs_cols[:, :, level] + coef_above * partials[-1]) / divider_value
        partials.append(partial_value)
        ratios.append(coef_below / divider_value)
    result = [None] * levels
    result[levels - 1] = partials[levels - 1]
    for level in range(levels - 2, -1, -1):
        result[level] = partials[level] + ratios[level] * result[level + 1]
    return jnp.stack(result, axis=2)


def advance(tracer_ext, face_x, face_y, inner, coupling):
    count, chans = tracer_ext.shape[0], tracer_ext.shape[1]
    levels, rows, cols = inner.shape[1], inner.shape[2], inner.shape[3]
    ext_cols = tracer_ext.reshape(count, chans // levels, levels, rows + 4, cols + 4)
    middle = ext_cols[:, :, :, 2:rows + 2]
    flux_x = face_flux(face_x[:, None], middle[..., 0:cols + 1], middle[..., 1:cols + 2], middle[..., 2:cols + 3], middle[..., 3:cols + 4])
    column = ext_cols[..., 2:cols + 2]
    flux_y = face_flux(face_y[:, None], column[:, :, :, 0:rows + 1], column[:, :, :, 1:rows + 2], column[:, :, :, 2:rows + 3], column[:, :, :, 3:rows + 4])
    center = middle[..., 2:cols + 2]
    divergence = (flux_x[..., 1:] - flux_x[..., :-1]) + (flux_y[:, :, :, 1:] - flux_y[:, :, :, :-1])
    explicit = center - COURANT * inner[:, None] * divergence
    solved = vertical_solve(explicit, coupling[:, None])
    return solved.reshape(count, chans, rows, cols)


def reference(tracers, velocity, kappa, kmt, block_owner, neighbours, fold_partner):
    slot_total = tracers.shape[0]
    block_count = block_owner.shape[0]
    slot_block = jnp.full((slot_total,), -1, jnp.int32).at[block_owner].set(jnp.arange(block_count, dtype=jnp.int32))
    live_slot = slot_block >= 0
    safe_ids = jnp.maximum(slot_block, 0)
    links = jnp.concatenate([neighbours[safe_ids], fold_partner[safe_ids][:, None]], axis=1)
    links = jnp.where(live_slot[:, None], links, -1)
    link_codes = jnp.where(links >= 0, block_owner[jnp.maximum(links, 0)], -1).astype(jnp.int32)
    levels = velocity.shape[1] // 2
    statics = jnp.concatenate([velocity, kmt[:, None, :]], axis=1)
    statics = statics.reshape(slot_total, 2 * levels + 1, JB, IB)
    static_pack = edge_pack(statics)
    fold_sign = jnp.concatenate([-jnp.ones((2 * levels,), jnp.float32), jnp.ones((1,), jnp.float32)]).reshape(1, -1, 1, 1)
    groups = slot_total // DEVICE_SLOTS
    chans = tracers.shape[1]
    state = tracers.reshape(slot_total, chans, JB, IB)
    grouped_statics = statics.reshape(groups, DEVICE_SLOTS, 2 * levels + 1, JB, IB)
    grouped_kappa = kappa.reshape(groups, DEVICE_SLOTS, JB, IB)
    grouped_codes = link_codes.reshape(groups, DEVICE_SLOTS, 5)
    for step in range(STEPS):
        tracer_pack = edge_pack(state)

        def one_group(input_arrays):
            block_state, block_static, diffusivity, codes = input_arrays
            static_ext = extend(block_static, fetch(static_pack, codes), fold_sign)
            face_x, face_y, inner, coupling = prepare(static_ext, diffusivity)
            tracer_ext = extend(block_state, fetch(tracer_pack, codes), 1.0)
            return advance(tracer_ext, face_x, face_y, inner, coupling)

        state = lax.map(one_group, (state.reshape(groups, DEVICE_SLOTS, chans, JB, IB), grouped_statics, grouped_kappa, grouped_codes))
        state = state.reshape(slot_total, chans, JB, IB)
    result = state.reshape(slot_total, chans, JB * IB)
    return jnp.where(live_slot[:, None, None], result, 0.0)
```

```python
import jax
import jax.numpy as jnp
from jax import lax
from jax.sharding import PartitionSpec as P

IB = 90
JB = 60
COURANT = 0.2
LANES = 128


def edge_pack(state, statics):
    count, chans = state.shape[:2]
    levels = (statics.shape[1] - 1) // 2
    east_vel, north_vel, depth = statics[:, :levels], statics[:, levels : 2 * levels], statics[:, 2 * levels :]
    x_part = jnp.concatenate([east_vel, depth], axis=1)
    y_part = jnp.concatenate([north_vel, depth], axis=1)
    pieces = [
        state[:, :, :, 0:2], x_part[:, :, :, 0],
        state[:, :, :, IB - 2 :], x_part[:, :, :, IB - 1],
        state[:, :, 0:2], y_part[:, :, 0],
        state[:, :, JB - 2 :], y_part[:, :, JB - 1],
    ]
    return jnp.concatenate([piece.reshape(count, -1) for piece in pieces], axis=1)


def face_flux(velocity_face, left_far, left_near, right_near, right_far):
    centered = (7.0 * (left_near + right_near) - (left_far + right_far)) / 12.0
    upwind = (right_far - 3.0 * right_near + 3.0 * left_near - left_far) / 12.0
    return velocity_face * centered + jnp.abs(velocity_face) * upwind


def per_device(tracers, velocity, kappa, kmt, block_owner, neighbours, fold_partner):
    slot_count, chans = tracers.shape[:2]
    levels = velocity.shape[1] // 2
    sub_count = lax.axis_size("sub")
    device_count = lax.axis_size("blk") * sub_count
    my_index = lax.axis_index("blk") * sub_count + lax.axis_index("sub")
    block_count = block_owner.shape[0]
    my_slots = my_index * slot_count + jnp.arange(slot_count, dtype=jnp.int32)
    hits = block_owner[None, :] == my_slots[:, None]
    live_slot = jnp.any(hits, axis=1)
    mine = jnp.sum(jnp.where(hits, jnp.arange(block_count, dtype=jnp.int32)[None, :], 0), axis=1)
    links = jnp.concatenate([neighbours[mine], fold_partner[mine][:, None]], axis=1)
    links = jnp.where(live_slot[:, None], links, -1)
    codes = jnp.where(links >= 0, block_owner[jnp.maximum(links, 0)], -1)

    state = tracers.reshape(slot_count, chans, JB, IB)
    statics = jnp.concatenate([velocity, kmt[:, None, :]], axis=1).reshape(slot_count, 2 * levels + 1, JB, IB)
    pack = edge_pack(state, statics)
    width = pack.shape[1]
    padded = -(-width // LANES) * LANES
    pack = jnp.pad(pack, ((0, 0), (0, padded - width))).reshape(-1, LANES)
    window = lax.all_gather(pack, ("blk", "sub"), axis=0, tiled=True)
    window = window.reshape(device_count * slot_count, padded)

    x_far, x_near = chans * JB * 2, (levels + 1) * JB
    y_far, y_near = chans * 2 * IB, (levels + 1) * IB
    x_wide, y_wide = x_far + x_near, y_far + y_near

    def strip(direction, start, wide):
        code = codes[:, direction]
        picked = jnp.take(window, jnp.maximum(code, 0), axis=0)[:, start : start + wide]
        return jnp.where((code >= 0)[:, None], picked, 0.0)

    west = strip(0, x_wide, x_wide)
    east = strip(1, 0, x_wide)
    south = strip(2, 2 * x_wide + y_wide, y_wide)
    north = strip(3, 2 * x_wide, y_wide)
    mirror = strip(4, 2 * x_wide + y_wide, y_wide)

    def halo_x(part):
        return part[:, :x_far].reshape(slot_count, chans, JB, 2), part[:, x_far:].reshape(slot_count, levels + 1, JB, 1)

    def halo_y(part):
        return part[:, :y_far].reshape(slot_count, chans, 2, IB), part[:, y_far:].reshape(slot_count, levels + 1, 1, IB)

    west_x, west_s = halo_x(west)
    east_x, east_s = halo_x(east)
    south_x, south_s = halo_y(south)
    north_x, north_s = halo_y(north)
    mirror_x, mirror_s = halo_y(mirror)
    sign = jnp.concatenate([-jnp.ones((levels,), jnp.float32), jnp.ones((1,), jnp.float32)]).reshape(1, -1, 1, 1)
    north_x = north_x + mirror_x[:, :, ::-1, ::-1]
    north_s = north_s + sign * mirror_s[:, :, :, ::-1]

    x_vel = jnp.concatenate([west_s[:, :levels], statics[:, :levels], east_s[:, :levels]], axis=3)
    y_vel = jnp.concatenate([south_s[:, :levels], statics[:, levels : 2 * levels], north_s[:, :levels]], axis=2)
    depth = statics[:, 2 * levels :]
    x_depth = jnp.concatenate([west_s[:, levels:], depth, east_s[:, levels:]], axis=3)
    y_depth = jnp.concatenate([south_s[:, levels:], depth, north_s[:, levels:]], axis=2)
    level_ids = jnp.arange(levels).astype(jnp.float32).reshape(1, levels, 1, 1)
    x_wet = jnp.clip(x_depth - level_ids, 0.0, 1.0)
    y_wet = jnp.clip(y_depth - level_ids, 0.0, 1.0)
    inner = jnp.clip(depth - level_ids, 0.0, 1.0)
    face_x = 0.5 * (x_vel[..., :-1] + x_vel[..., 1:]) * x_wet[..., :-1] * x_wet[..., 1:]
    face_y = 0.5 * (y_vel[:, :, :-1] + y_vel[:, :, 1:]) * y_wet[:, :, :-1] * y_wet[:, :, 1:]
    x_ext = jnp.concatenate([west_x, state, east_x], axis=3).reshape(slot_count, chans // levels, levels, JB, IB + 4)
    y_ext = jnp.concatenate([south_x, state, north_x], axis=2).reshape(slot_count, chans // levels, levels, JB + 4, IB)
    flux_x = face_flux(face_x[:, None], x_ext[..., 0 : IB + 1], x_ext[..., 1 : IB + 2], x_ext[..., 2 : IB + 3], x_ext[..., 3 : IB + 4])
    flux_y = face_flux(face_y[:, None], y_ext[..., 0 : JB + 1, :], y_ext[..., 1 : JB + 2, :], y_ext[..., 2 : JB + 3, :], y_ext[..., 3 : JB + 4, :])
    divergence = flux_x[..., 1:] - flux_x[..., :-1] + (flux_y[..., 1:, :] - flux_y[..., :-1, :])
    explicit = state.reshape(slot_count, chans // levels, levels, JB, IB) - COURANT * inner[:, None] * divergence

    below = kappa.reshape(slot_count, 1, JB, IB) * inner[:, 0][:, None] * inner[:, 1][:, None]
    divider = 1.0 + below
    ratio = below / divider
    first = explicit[:, :, 0] / divider
    second = (explicit[:, :, 1] + below * first) / (divider - below * ratio)
    solved = jnp.stack([first + ratio * second, second], axis=2)
    result = solved.reshape(slot_count, chans, JB * IB)
    return jnp.where(live_slot[:, None, None], result, 0.0)


def solution(mesh):
    placed = (
        P(("blk", "sub"), None, None),
        P(("blk", "sub"), None, None),
        P(("blk", "sub"), None),
        P(("blk", "sub"), None),
        P(),
        P(),
        P(),
    )
    return jax.shard_map(
        per_device,
        mesh=mesh,
        in_specs=placed,
        out_specs=P(("blk", "sub"), None, None),
        check_vma=False,
    )
```

```python
import jax
import jax.numpy as jnp
from jax import lax
from jax.sharding import PartitionSpec as P

IB = 90
JB = 60
COURANT = 0.2


def edge_pack(state, statics, parts):
    count, chans = state.shape[:2]
    levels = (statics.shape[1] - 1) // 2
    east_vel, north_vel, depth = statics[:, :levels], statics[:, levels : 2 * levels], statics[:, 2 * levels :]
    x_part = jnp.concatenate([east_vel, depth], axis=1)
    y_part = jnp.concatenate([north_vel, depth], axis=1)
    sides = [
        (state[:, :, :, 0:2], x_part[:, :, :, 0]),
        (state[:, :, :, IB - 2 :], x_part[:, :, :, IB - 1]),
        (state[:, :, 0:2], y_part[:, :, 0]),
        (state[:, :, JB - 2 :], y_part[:, :, JB - 1]),
    ]
    pieces = []
    for near, far in sides:
        flat = jnp.concatenate([near.reshape(count, -1), far.reshape(count, -1)], axis=1)
        wide = -(-flat.shape[1] // parts)
        flat = jnp.pad(flat, ((0, 0), (0, parts * wide - flat.shape[1])))
        pieces.append(flat.reshape(count, parts, wide))
    return jnp.concatenate(pieces, axis=2).transpose(1, 0, 2)


def chosen(codes, table):
    one_hot = (codes[:, None] == jnp.arange(table.shape[0], dtype=jnp.int32)[None, :]).astype(jnp.float32)
    return jnp.dot(one_hot, table, precision=lax.Precision.HIGHEST)


def face_flux(velocity_face, left_far, left_near, right_near, right_far):
    centered = (7.0 * (left_near + right_near) - (left_far + right_far)) / 12.0
    upwind = (right_far - 3.0 * right_near + 3.0 * left_near - left_far) / 12.0
    return velocity_face * centered + jnp.abs(velocity_face) * upwind


def per_device(tracers, velocity, kappa, kmt, block_owner, neighbours, fold_partner):
    slot_count, chans = tracers.shape[:2]
    levels = velocity.shape[1] // 2
    sub_count = lax.axis_size("sub")
    device_count = lax.axis_size("blk") * sub_count
    my_index = lax.axis_index("blk") * sub_count + lax.axis_index("sub")
    block_count = block_owner.shape[0]
    slot_total = device_count * slot_count
    axes = ("blk", "sub")

    state = tracers.reshape(slot_count, chans, JB, IB)
    statics = jnp.concatenate([velocity, kmt[:, None, :]], axis=1).reshape(slot_count, 2 * levels + 1, JB, IB)
    pack = edge_pack(state, statics, device_count)

    hits = block_owner[None, :] == jnp.arange(slot_total, dtype=jnp.int32)[:, None]
    live = jnp.any(hits, axis=1)
    links = jnp.concatenate([neighbours, fold_partner[:, None]], axis=1)
    link_blocks = jnp.max(jnp.where(hits[:, :, None], links[None], -1), axis=1)
    link_hits = link_blocks[:, :, None] == jnp.arange(block_count, dtype=jnp.int32)[None, None, :]
    codes = jnp.max(jnp.where(link_hits, block_owner[None, None, :], -1), axis=2)
    live_slot = lax.dynamic_slice_in_dim(live, my_index * slot_count, slot_count, 0)
    folded = lax.dynamic_slice_in_dim(codes[:, 4] >= 0, my_index * slot_count, slot_count, 0)

    x_far, x_near = chans * JB * 2, (levels + 1) * JB
    y_far, y_near = chans * 2 * IB, (levels + 1) * IB
    x_wide, y_wide = x_far + x_near, y_far + y_near

    x_piece, y_piece = -(-x_wide // device_count), -(-y_wide // device_count)
    cuts = [0, x_piece, 2 * x_piece, 2 * x_piece + y_piece, 2 * x_piece + 2 * y_piece]

    held = lax.all_to_all(pack, axes, 0, 0, tiled=True).reshape(slot_total, cuts[4])
    sides = [held[:, cuts[i] : cuts[i + 1]] for i in range(4)]
    picked = [
        chosen(codes[:, 0], sides[1]),
        chosen(codes[:, 1], sides[0]),
        chosen(codes[:, 2], sides[3]),
        chosen(codes[:, 3], sides[2]) + chosen(codes[:, 4], sides[3]),
    ]
    picked = jnp.concatenate(picked, axis=1).reshape(device_count, slot_count, cuts[4])
    window = lax.all_to_all(picked, axes, 0, 0, tiled=True).transpose(1, 0, 2)
    west = window[:, :, : cuts[1]].reshape(slot_count, -1)[:, :x_wide]
    east = window[:, :, cuts[1] : cuts[2]].reshape(slot_count, -1)[:, :x_wide]
    south = window[:, :, cuts[2] : cuts[3]].reshape(slot_count, -1)[:, :y_wide]
    north = window[:, :, cuts[3] :].reshape(slot_count, -1)[:, :y_wide]

    def halo_x(part):
        return part[:, :x_far].reshape(slot_count, chans, JB, 2), part[:, x_far:].reshape(slot_count, levels + 1, JB, 1)

    def halo_y(part):
        return part[:, :y_far].reshape(slot_count, chans, 2, IB), part[:, y_far:].reshape(slot_count, levels + 1, 1, IB)

    west_x, west_s = halo_x(west)
    east_x, east_s = halo_x(east)
    south_x, south_s = halo_y(south)
    north_x, north_s = halo_y(north)
    sign = jnp.concatenate([-jnp.ones((levels,), jnp.float32), jnp.ones((1,), jnp.float32)]).reshape(1, -1, 1, 1)
    flipped = folded[:, None, None, None]
    north_x = jnp.where(flipped, north_x[:, :, ::-1, ::-1], north_x)
    north_s = jnp.where(flipped, sign * north_s[:, :, :, ::-1], north_s)

    x_vel = jnp.concatenate([west_s[:, :levels], statics[:, :levels], east_s[:, :levels]], axis=3)
    y_vel = jnp.concatenate([south_s[:, :levels], statics[:, levels : 2 * levels], north_s[:, :levels]], axis=2)
    depth = statics[:, 2 * levels :]
    x_depth = jnp.concatenate([west_s[:, levels:], depth, east_s[:, levels:]], axis=3)
    y_depth = jnp.concatenate([south_s[:, levels:], depth, north_s[:, levels:]], axis=2)
    level_ids = jnp.arange(levels).astype(jnp.float32).reshape(1, levels, 1, 1)
    x_wet = jnp.clip(x_depth - level_ids, 0.0, 1.0)
    y_wet = jnp.clip(y_depth - level_ids, 0.0, 1.0)
    inner = jnp.clip(depth - level_ids, 0.0, 1.0)
    face_x = 0.5 * (x_vel[..., :-1] + x_vel[..., 1:]) * x_wet[..., :-1] * x_wet[..., 1:]
    face_y = 0.5 * (y_vel[:, :, :-1] + y_vel[:, :, 1:]) * y_wet[:, :, :-1] * y_wet[:, :, 1:]
    x_ext = jnp.concatenate([west_x, state, east_x], axis=3).reshape(slot_count, chans // levels, levels, JB, IB + 4)
    y_ext = jnp.concatenate([south_x, state, north_x], axis=2).reshape(slot_count, chans // levels, levels, JB + 4, IB)
    flux_x = face_flux(face_x[:, None], x_ext[..., 0 : IB + 1], x_ext[..., 1 : IB + 2], x_ext[..., 2 : IB + 3], x_ext[..., 3 : IB + 4])
    flux_y = face_flux(face_y[:, None], y_ext[..., 0 : JB + 1, :], y_ext[..., 1 : JB + 2, :], y_ext[..., 2 : JB + 3, :], y_ext[..., 3 : JB + 4, :])
    divergence = flux_x[..., 1:] - flux_x[..., :-1] + (flux_y[..., 1:, :] - flux_y[..., :-1, :])
    explicit = state.reshape(slot_count, chans // levels, levels, JB, IB) - COURANT * inner[:, None] * divergence

    below = kappa.reshape(slot_count, 1, JB, IB) * inner[:, 0][:, None] * inner[:, 1][:, None]
    divider = 1.0 + below
    ratio = below / divider
    first = explicit[:, :, 0] / divider
    second = (explicit[:, :, 1] + below * first) / (divider - below * ratio)
    solved = jnp.stack([first + ratio * second, second], axis=2)
    result = solved.reshape(slot_count, chans, JB * IB)
    return jnp.where(live_slot[:, None, None], result, 0.0)


def solution(mesh):
    placed = (
        P(("blk", "sub"), None, None),
        P(("blk", "sub"), None, None),
        P(("blk", "sub"), None),
        P(("blk", "sub"), None),
        P(),
        P(),
        P(),
    )
    return jax.shard_map(
        per_device,
        mesh=mesh,
        in_specs=placed,
        out_specs=P(("blk", "sub"), None, None),
        check_vma=False,
    )
```

```python
import functools

import jax
import jax.numpy as jnp
import numpy as np
from jax import lax
from jax.experimental import pallas as pl
from jax.experimental.pallas import tpu as pltpu
from jax.sharding import PartitionSpec as P

IB = 90
JB = 60
CELLS = IB * JB
COURANT = 0.2
LANES = 128
TILES = -(-CELLS // LANES)
WIDE = TILES * LANES
GAPS = JB + 1
HALF = IB // 2
ROWS = 16
PARTS = 32
X_PART = 22
SPARE = 48
PIECE = 16
SCALE = COURANT / 12.0
SIDES = 3


def lane_of(rows):
    return lax.broadcasted_iota(jnp.int32, (rows, LANES), 1)


def rot(value, shift):
    shift = shift % LANES
    return value if shift == 0 else pltpu.roll(value, shift, 1)


def window(get, start, rows):
    tile, offset = start // LANES, start % LANES
    head = rot(get(tile), -offset)
    if offset == 0 or tile + 1 >= TILES:
        return head
    return jnp.where(lane_of(rows) < LANES - offset, head, rot(get(tile + 1), -offset))


def gap_groups(get, first, wide, rows):
    lane = lane_of(rows)
    held = LANES // wide
    result = []
    for at in range(0, GAPS, held):
        value = jnp.zeros((rows, LANES), jnp.float32)
        for gap in range(at, min(at + held, GAPS)):
            start = IB * gap + first
            place = (gap - at) * wide
            for tile in range(max(start, 0) // LANES, min(start + wide - 1, CELLS - 1) // LANES + 1):
                low = max(start, tile * LANES, 0)
                value = jnp.where(lane >= place + low - start, rot(get(tile), place - start + tile * LANES), value)
        result.append(value)
    return result


def lane_pick(pair, index, rows):
    low = jnp.take_along_axis(pair[0], index % LANES, axis=1, mode="promise_in_bounds")
    high = jnp.take_along_axis(pair[1], index % LANES, axis=1, mode="promise_in_bounds")
    return jnp.where(index < LANES, low, high)


def both_slots(target, source):
    target[0:4, 0:CELLS] = source[0]
    target[4:8, 0:CELLS] = source[1]
    target[:, CELLS:] = jnp.zeros((8, WIDE - CELLS), jnp.float32)


def tile_getter(ref):
    return lambda tile: ref[:, tile * LANES : (tile + 1) * LANES]


def depth_getter(ref):
    rows = ref.shape[0]

    def get(tile):
        if tile + 1 < TILES:
            return ref[:, tile * LANES : (tile + 1) * LANES]
        rest = jnp.zeros((rows, WIDE - CELLS), jnp.float32)
        return jnp.concatenate([ref[:, tile * LANES : CELLS], rest], axis=1)

    return get


def joined(south, north, half, rows):
    if half == 0:
        return jnp.where(lane_of(rows) < 64, south, rot(north, 64))
    return jnp.where(lane_of(rows) < 64, rot(south, -HALF), rot(north, 64 - HALF))


def pack_kernel(tracer_ref, velocity_ref, depth_ref, out_ref, x_ref, v_ref, strip_ref):
    step = pl.program_id(0)
    count = depth_ref.shape[0]
    both_slots(x_ref, tracer_ref)
    both_slots(v_ref, velocity_ref)
    get_x, get_v = tile_getter(x_ref), tile_getter(v_ref)
    lane = lane_of(8)
    groups = gap_groups(get_x, -2, 4, 8)
    near = lane_pick(groups, 4 * (lane // 2) + 1 + lane % 2, 8)
    far = lane_pick(groups, 4 * (lane // 2) + 3 * (lane % 2), 8)
    south = [window(get_x, 0, 8), window(get_x, IB, 8)]
    north = [window(get_x, CELLS - IB, 8), window(get_x, CELLS - 2 * IB, 8)]
    v_south, v_north = window(get_v, 0, 8), window(get_v, CELLS - IB, 8)
    strips = [joined(south[0], north[0], half, 8) for half in range(2)]
    strips += [joined(south[1], north[1], half, 8) for half in range(2)]
    strips += [joined(v_south, v_north, half, 8) for half in range(2)]
    strips += [near, far, gap_groups(get_v, -1, 2, 8)[0]]
    own = pl.ds(pl.multiple_of(8 * step, 8), 8)
    for index, strip in enumerate(strips):
        strip_ref[index, own, :] = strip

    @pl.when(step == pl.num_programs(0) - 1)
    def _():
        out_ref[...] = jnp.zeros(out_ref.shape, jnp.float32)
        slots = pl.ds(0, count)
        slot_lane = lane_of(count)
        get_d = depth_getter(depth_ref)
        d_south, d_north = window(get_d, 0, count), window(get_d, CELLS - IB, count)
        d_gaps = gap_groups(get_d, -1, 2, count)[0]
        spare = (slot_lane >= SPARE) & (slot_lane < SPARE + PIECE)
        for chan in range(4):
            rows = pl.ds(chan, count, stride=4)
            for half in range(2):
                for deep in range(2):
                    part = 2 * (4 * deep + chan) + half
                    value = strip_ref[2 * deep + half, rows, :]
                    if part < 8:
                        value = jnp.where(spare, rot(d_gaps, SPARE - PIECE * part), value)
                    out_ref[part, slots, :] = value
                if chan >= 2:
                    out_ref[2 * (8 + chan - 2) + half, slots, :] = strip_ref[4 + half, rows, :]
            out_ref[X_PART + chan, slots, :] = strip_ref[6, rows, :]
            out_ref[X_PART + 4 + chan, slots, :] = strip_ref[7, rows, :]
            if chan < 2:
                out_ref[X_PART + 8 + chan, slots, :] = strip_ref[8, rows, :]
        for half in range(2):
            out_ref[20 + half, slots, :] = joined(d_south, d_north, half, count)


def route_kernel(part_ref, code_ref, held_ref, out_ref):
    total = held_ref.shape[0]
    rows = out_ref.shape[0]
    part = part_ref[0]
    picked = [jnp.zeros((rows, 2 * LANES), jnp.float32) for _ in range(5)]
    for start in range(0, total, rows):
        held = held_ref[start : start + rows, :]
        high = held.astype(jnp.bfloat16)
        low = (held - high.astype(jnp.float32)).astype(jnp.bfloat16)
        halves = jnp.concatenate([high, low], axis=1)
        source = lax.broadcasted_iota(jnp.int32, (rows, rows), 1) + start
        for side in range(5):
            one_hot = jnp.where(code_ref[:, side : side + 1] == source, 1.0, 0.0).astype(jnp.bfloat16)
            picked[side] += jnp.dot(one_hot, halves, preferred_element_type=jnp.float32)
    west, east, south, north, fold = [value[:, :LANES] + value[:, LANES:] for value in picked]
    lane = lane_of(rows)
    along_x = (part >= X_PART) | ((part < 8) & (lane >= SPARE) & (lane < SPARE + PIECE))
    x_side = jnp.where(lane % 2 == 0, west, east)
    y_side = jnp.where(lane < 64, north + rot(fold, 64), south)
    out_ref[...] = jnp.where(along_x, x_side, y_side)


def bulk_kernel(tracer_ref, velocity_ref, depth_ref, kappa_ref, column_ref, base_ref, edge_ref,
                x_ref, v_ref, d_ref, k_ref, w_ref, z_ref, strip_ref):
    step = pl.program_id(0)
    count = depth_ref.shape[0]
    both_slots(x_ref, tracer_ref)
    both_slots(v_ref, velocity_ref)
    for target, source in ((d_ref, depth_ref), (k_ref, kappa_ref)):
        for slot in range(2):
            row = source[pl.ds(2 * step + slot, 1), :]
            target[4 * slot : 4 * slot + 4, 0:CELLS] = jnp.broadcast_to(row, (4, CELLS))
        target[:, CELLS:] = jnp.zeros((8, WIDE - CELLS), jnp.float32)
    row = lax.broadcasted_iota(jnp.int32, (8, WIDE), 0)
    x_row, level = row % 4 < 2, row % 2
    column = column_ref[...]
    first, last = column == 0.0, column == IB - 1.0

    def lanes(value, shift):
        return pltpu.roll(value, shift % WIDE, 1)

    def sublanes(value, shift):
        return pltpu.roll(value, shift % 8, 0)

    depth = d_ref[...]
    top = jnp.clip(depth, 0.0, 1.0)
    low = jnp.clip(depth - 1.0, 0.0, 1.0)
    wet = jnp.where(level == 0, top, low)
    coupling = k_ref[...] * top * low
    ratio = coupling / (1.0 + 2.0 * coupling)
    velocity = v_ref[...]
    next_vel = jnp.where(x_row, lanes(velocity, -1), lanes(velocity, -IB))
    next_wet = jnp.where(x_row, jnp.where(last, 0.0, lanes(wet, -1)), lanes(wet, -IB))
    face = SCALE * (velocity + next_vel) * (wet * next_wet)
    w_ref[...] = face
    z_ref[...] = jnp.where(x_row, face, jnp.where(level == 0, ratio, depth))
    face_x = jnp.where(x_row, face, sublanes(face, 2))
    face_y = jnp.where(x_row, sublanes(face, -2), face)

    state = x_ref[...]

    def divergence(speed, distance, before, after):
        mine = 5.0 * state
        upper = lanes(mine - after, -distance)
        flux = jnp.maximum(speed, 0.0) * (mine - before + 2.0 * after)
        flux += jnp.minimum(speed, 0.0) * (2.0 * state + upper)
        return flux - lanes(flux, distance)

    change = divergence(face_x, 1, jnp.where(first, 0.0, lanes(state, 1)), jnp.where(last, 0.0, lanes(state, -1)))
    change += divergence(face_y, IB, lanes(state, IB), lanes(state, -IB))
    explicit = state - wet * change
    other = jnp.where(level == 0, sublanes(explicit, -1), sublanes(explicit, 1))
    base_ref[...] = explicit + ratio * (other - explicit)

    get_w, get_z = tile_getter(w_ref), tile_getter(z_ref)
    lane = lane_of(8)
    groups = gap_groups(get_z, -2, 4, 8)
    strips = [
        lane_pick(groups, 4 * (lane // 2) + 2 * (lane % 2), 8),
        lane_pick(groups, 4 * (lane // 2) + 1 + lane % 2, 8),
        lane_pick(groups, 4 * (lane // 2) + 3 * (lane % 2), 8),
        window(get_w, 0, 8),
        window(get_z, 0, 8),
        window(get_z, IB, 8),
        window(get_w, CELLS - 2 * IB, 8),
        window(get_z, CELLS - IB, 8),
        window(get_z, CELLS - 2 * IB, 8),
    ]
    own = pl.ds(pl.multiple_of(8 * step, 8), 8)
    for index, strip in enumerate(strips):
        strip_ref[index, own, :] = strip

    @pl.when(step == pl.num_programs(0) - 1)
    def _():
        edge_ref[...] = jnp.zeros(edge_ref.shape, jnp.float32)
        east_lane = lane_of(count) % 2 == 0
        slots = pl.ds(0, count)
        for side in range(SIDES):
            for k in range(2):
                speed = strip_ref[3 * side, pl.ds(k if side == 0 else 2 + k, count, stride=4), :]
                if side == 0:
                    speed = jnp.where(east_lane, -speed, speed)
                elif side == 2:
                    speed = -speed
                edge_ref[5 * side + k, slots, :] = jnp.maximum(speed, 0.0)
            edge_ref[5 * side + 2, slots, :] = strip_ref[3 * side + 1, pl.ds(2, count, stride=4), :]
            edge_ref[5 * side + 3, slots, :] = strip_ref[3 * side + 2, pl.ds(2, count, stride=4), :]
            edge_ref[5 * side + 4, slots, :] = strip_ref[3 * side + 2, pl.ds(3, count, stride=4), :]


def finish_kernel(live_ref, own_ref, halo_ref, fold_ref, edge_ref, base_ref, out_ref, delta_ref):
    step = pl.program_id(0)

    @pl.when(step == 0)
    def _():
        lane = lane_of(ROWS)
        folded = fold_ref[...] > 0.0
        mirror = jnp.where(lane < IB, IB - 1 - lane, lane)

        def lower(ref, value):
            return jnp.where(lane < HALF, ref[2 * value], rot(ref[2 * value + 1], HALF))

        def upper(ref, value):
            return jnp.where(lane < HALF, rot(ref[2 * value], 64), rot(ref[2 * value + 1], 64 + HALF))

        def across(ref, value):
            if value < 10:
                return ref[X_PART + value]
            whole = rot(ref[0], -SPARE)
            for part in range(1, 8):
                whole = jnp.where(lane >= PIECE * part, rot(ref[part], PIECE * part - SPARE), whole)
            return whole

        def x_halo(value):
            raw = across(halo_ref, value)
            return jnp.where(lane % 2 == 0, rot(raw, 1), rot(raw, -1))

        def north_halo(value):
            raw = lower(halo_ref, value)
            turned = jnp.take_along_axis(raw, mirror, axis=1, mode="promise_in_bounds")
            return jnp.where(folded, -turned if value in (8, 9) else turned, raw)

        readers = [
            (functools.partial(across, own_ref), x_halo),
            (functools.partial(lower, own_ref), functools.partial(upper, halo_ref)),
            (functools.partial(upper, own_ref), north_halo),
        ]
        for side, (mine, theirs) in enumerate(readers):
            near_depth, out_depth = mine(10), theirs(10)
            next_depth = edge_ref[5 * side + 4]
            ratio = [edge_ref[5 * side + 2], edge_ref[5 * side + 3]]
            change = {}
            for k in range(2):
                wet = [jnp.clip(depth - k, 0.0, 1.0) for depth in (out_depth, near_depth, next_depth)]
                speed = SCALE * (mine(8 + k) + theirs(8 + k)) * wet[0] * wet[1]
                if side == 0:
                    speed = jnp.where(lane % 2 == 0, -speed, speed)
                elif side == 2:
                    speed = -speed
                inward, outward = jnp.maximum(speed, 0.0), jnp.minimum(speed, 0.0)
                inner_speed = edge_ref[5 * side + k]
                for tracer in range(2):
                    chan = 2 * tracer + k
                    near, deep = mine(chan), mine(4 + chan)
                    out_near, out_far = theirs(chan), theirs(4 + chan)
                    flux = inward * (5.0 * out_near + 2.0 * near - out_far)
                    flux += outward * (2.0 * out_near + 5.0 * near - deep)
                    inner_flux = inner_speed * out_near
                    change[0, tracer, k] = wet[1] * (flux + inner_flux)
                    change[1, tracer, k] = -wet[2] * inner_flux
            for place in range(2):
                for tracer in range(2):
                    for k in range(2):
                        self, other = change[place, tracer, k], change[place, tracer, 1 - k]
                        rows = pl.ds(ROWS * (2 * tracer + k), ROWS)
                        delta_ref[2 * side + place, rows, :] = self + ratio[place] * (other - self)

    lane = lane_of(8)

    def slots_of(index):
        pair = [delta_ref[index, pl.ds(2 * step + slot, 4, stride=ROWS), :] for slot in range(2)]
        return jnp.concatenate(pair, axis=0)

    near, deep = slots_of(0), slots_of(1)
    groups = []
    for at in range(2):
        index = 2 * (lane // 4) + (lane % 4) // 2 + 64 * at
        outer = jnp.take_along_axis(near, index, axis=1, mode="promise_in_bounds")
        inner = jnp.take_along_axis(deep, index, axis=1, mode="promise_in_bounds")
        groups.append(jnp.where((lane % 4 == 1) | (lane % 4 == 2), outer, inner))
    placed = [(groups[gap // 32], 4 * (gap % 32), IB * gap - 2, 4) for gap in range(GAPS)]
    placed += [(slots_of(2), 0, 0, IB), (slots_of(3), 0, IB, IB)]
    placed += [(slots_of(4), 0, CELLS - IB, IB), (slots_of(5), 0, CELLS - 2 * IB, IB)]
    live = [live_ref[2 * step + slot] > 0 for slot in range(2)]
    for tile in range(TILES):
        at = tile * LANES
        value = base_ref[:, at : at + LANES]
        for source, origin, start, wide in placed:
            low, high = max(start, at, 0), min(start + wide, at + LANES, CELLS)
            if low < high:
                inside = (lane >= low - at) & (lane < high - at)
                value += jnp.where(inside, rot(source, start - at - origin), 0.0)
        stop = min(at + LANES, CELLS)
        for slot in range(2):
            out_ref[slot, :, at:stop] = jnp.where(live[slot], value[4 * slot : 4 * slot + 4, : stop - at], 0.0)


def route_codes(block_owner, neighbours, fold_partner, slot_count, device_count):
    total = device_count * ROWS
    block_count = block_owner.shape[0]
    row = block_owner // slot_count * ROWS + block_owner % slot_count
    hits = row[None, :] == jnp.arange(total, dtype=jnp.int32)[:, None]
    live = jnp.any(hits, axis=1)
    links = jnp.concatenate([neighbours, fold_partner[:, None]], axis=1)
    linked = links[:, :, None] == jnp.arange(block_count, dtype=jnp.int32)[None, None, :]
    link_rows = jnp.max(jnp.where(linked, row[None, None, :], -1), axis=2)
    codes = jnp.max(jnp.where(hits[:, :, None], link_rows[None], -1), axis=1)
    return codes, live


def per_device(tracers, velocity, kappa, kmt, block_owner, neighbours, fold_partner):
    slot_count, chans = tracers.shape[:2]
    sub_count = lax.axis_size("sub")
    device_count = lax.axis_size("blk") * sub_count
    if device_count < PARTS or chans != 4 or slot_count % 2 or slot_count > ROWS:
        raise ValueError("unsupported sizes")
    my_index = lax.axis_index("blk") * sub_count + lax.axis_index("sub")
    axes = ("blk", "sub")
    pairs = slot_count // 2
    f32 = jnp.float32
    limit = pltpu.CompilerParams(vmem_limit_bytes=40 * 1024 * 1024)

    def whole(shape):
        return pl.BlockSpec(shape, lambda *_: (0,) * len(shape))

    two_slots = pl.BlockSpec((2, 4, CELLS), lambda step: (step, 0, 0))
    by_slot = whole((slot_count, CELLS))
    wide = pltpu.VMEM((8, WIDE), f32)
    strips = pltpu.VMEM((9, 8 * pairs, LANES), f32)

    pack = pl.pallas_call(
        pack_kernel,
        grid=(pairs,),
        out_shape=jax.ShapeDtypeStruct((device_count, ROWS, LANES), f32),
        in_specs=[two_slots, two_slots, by_slot],
        out_specs=whole((device_count, ROWS, LANES)),
        scratch_shapes=[wide, wide, strips],
        compiler_params=limit,
        cost_estimate=pl.CostEstimate(flops=4_000_000, bytes_accessed=2_400_000, transcendentals=0),
    )(tracers, velocity, kmt)

    held = lax.all_to_all(pack, axes, 0, 0, tiled=True).reshape(device_count * ROWS, LANES)

    codes, live = route_codes(block_owner, neighbours, fold_partner, slot_count, device_count)
    my_rows = my_index * ROWS
    my_live = lax.dynamic_slice_in_dim(live, my_rows, ROWS, 0).astype(jnp.int32)
    my_fold = lax.dynamic_slice_in_dim(codes[:, 4:5], my_rows, ROWS, 0) >= 0
    my_fold = jnp.broadcast_to(my_fold.astype(f32), (ROWS, LANES))

    routed_rows = PARTS * ROWS
    routed = pl.pallas_call(
        route_kernel,
        grid=(device_count // PARTS,),
        out_shape=jax.ShapeDtypeStruct((device_count * ROWS, LANES), f32),
        in_specs=[
            pl.BlockSpec(memory_space=pltpu.SMEM),
            pl.BlockSpec((routed_rows, 5), lambda step: (step, 0)),
            whole((device_count * ROWS, LANES)),
        ],
        out_specs=pl.BlockSpec((routed_rows, LANES), lambda step: (step, 0)),
        compiler_params=limit,
    )(my_index.astype(jnp.int32).reshape(1), codes, held)

    halo = lax.all_to_all(routed.reshape(device_count, ROWS, LANES), axes, 0, 0, tiled=True)

    column = np.full((8, WIDE), IB - 1, np.float32)
    column[:, :CELLS] = np.arange(CELLS) % IB
    base, edges = pl.pallas_call(
        bulk_kernel,
        grid=(pairs,),
        out_shape=[
            jax.ShapeDtypeStruct((8 * pairs, WIDE), f32),
            jax.ShapeDtypeStruct((5 * SIDES, ROWS, LANES), f32),
        ],
        in_specs=[two_slots, two_slots, by_slot, by_slot, whole((8, WIDE))],
        out_specs=[pl.BlockSpec((8, WIDE), lambda step: (step, 0)), whole((5 * SIDES, ROWS, LANES))],
        scratch_shapes=[wide] * 6 + [strips],
        compiler_params=limit,
        cost_estimate=pl.CostEstimate(flops=22_000_000, bytes_accessed=4_000_000, transcendentals=0),
    )(tracers, velocity, kmt, kappa, jnp.asarray(column))

    return pl.pallas_call(
        finish_kernel,
        grid=(pairs,),
        out_shape=jax.ShapeDtypeStruct(tracers.shape, f32),
        in_specs=[
            pl.BlockSpec(memory_space=pltpu.SMEM),
            whole((PARTS, ROWS, LANES)),
            whole((PARTS, ROWS, LANES)),
            whole((ROWS, LANES)),
            whole((5 * SIDES, ROWS, LANES)),
            pl.BlockSpec((8, WIDE), lambda step: (step, 0)),
        ],
        out_specs=two_slots,
        scratch_shapes=[pltpu.VMEM((2 * SIDES, 4 * ROWS, LANES), f32)],
        compiler_params=limit,
    )(my_live, pack, halo, my_fold, edges, base)


def solution(mesh):
    placed = (
        P(("blk", "sub"), None, None),
        P(("blk", "sub"), None, None),
        P(("blk", "sub"), None),
        P(("blk", "sub"), None),
        P(),
        P(),
        P(),
    )
    return jax.shard_map(
        per_device,
        mesh=mesh,
        in_specs=placed,
        out_specs=P(("blk", "sub"), None, None),
        check_vma=False,
    )
```

```python
import functools

import jax
import jax.numpy as jnp
from jax import lax
from jax.experimental import pallas as pl
from jax.experimental.pallas import tpu as pltpu
from jax.sharding import PartitionSpec as P

IB = 90
JB = 60
CELLS = IB * JB
COURANT = 0.2
LANES = 128
TILES = -(-CELLS // LANES)
WIDE = TILES * LANES
GAPS = JB + 1
HALF = IB // 2
PARTS = 32
X_PART = 22
SPARE = 48
PIECE = 16
SCALE = COURANT / 12.0
SIDES = 3
OWN = 8
FIRST_PAIRS = 3


def lane_of(rows):
    return lax.broadcasted_iota(jnp.int32, (rows, LANES), 1)


def rot(value, shift):
    shift = shift % LANES
    return value if shift == 0 else pltpu.roll(value, shift, 1)


def sublanes(value, shift):
    return pltpu.roll(value, shift % 8, 0)


def once(make):
    held = {}

    def get(tile):
        if tile not in held:
            held[tile] = make(tile)
        return held[tile]

    return get


def shifted(get, distance):
    offset = distance % LANES
    turned = once(lambda tile: rot(get(tile), -offset))

    def make(tile):
        low = tile + distance // LANES
        first = turned(low) if 0 <= low < TILES else jnp.zeros((8, LANES), jnp.float32)
        second = turned(low + 1) if 0 <= low + 1 < TILES else jnp.zeros((8, LANES), jnp.float32)
        return jnp.where(lane_of(8) < LANES - offset, first, second)

    return once(make)


def window(get, start, rows):
    tile, offset = start // LANES, start % LANES
    head = rot(get(tile), -offset)
    if offset == 0 or tile + 1 >= TILES:
        return head
    return jnp.where(lane_of(rows) < LANES - offset, head, rot(get(tile + 1), -offset))


def gap_groups(get, first, wide, rows):
    lane = lane_of(rows)
    held = LANES // wide
    result = []
    for at in range(0, GAPS, held):
        value = jnp.zeros((rows, LANES), jnp.float32)
        for gap in range(at, min(at + held, GAPS)):
            start = IB * gap + first
            place = (gap - at) * wide
            for tile in range(max(start, 0) // LANES, min(start + wide - 1, CELLS - 1) // LANES + 1):
                low = max(start, tile * LANES, 0)
                value = jnp.where(lane >= place + low - start, rot(get(tile), place - start + tile * LANES), value)
        result.append(value)
    return result


def lane_take(value, index):
    return jnp.take_along_axis(value, index, axis=1, mode="promise_in_bounds")


def lane_pick(pair, index):
    return jnp.where(index < LANES, lane_take(pair[0], index % LANES), lane_take(pair[1], index % LANES))


def tile_getter(ref, rows, count):
    def get(tile):
        if tile + 1 < TILES:
            return ref[rows, tile * LANES : (tile + 1) * LANES]
        rest = jnp.zeros((count, WIDE - CELLS), jnp.float32)
        return jnp.concatenate([ref[rows, tile * LANES : CELLS], rest], axis=1)

    return get


def joined(south, north, half, rows):
    if half == 0:
        return jnp.where(lane_of(rows) < 64, south, rot(north, 64))
    return jnp.where(lane_of(rows) < 64, rot(south, -HALF), rot(north, 64 - HALF))


def pair_copies(source, target, sems, first, pairs):
    copies = []
    for pair in range(pairs):
        into = target.at[pl.ds(8 * pair, 8)].reshape(2, 4, CELLS)
        copies.append(pltpu.make_async_copy(source.at[pl.ds(2 * (first + pair), 2)], into, sems.at[pair]))
    return copies


def pack_kernel(tracer_ref, velocity_ref, depth_ref, out_ref, own_ref,
                x_ref, v_ref, d_ref, strip_ref, x_sems, v_sems, d_sem):
    count = depth_ref.shape[0]
    pairs = count // 2
    x_copies = pair_copies(tracer_ref, x_ref, x_sems, 0, pairs)
    v_copies = pair_copies(velocity_ref, v_ref, v_sems, 0, pairs)
    d_copy = pltpu.make_async_copy(depth_ref, d_ref, d_sem)
    for pair in range(pairs):
        x_copies[pair].start()
        v_copies[pair].start()
    d_copy.start()
    lane = lane_of(8)
    for pair in range(pairs):
        rows = pl.ds(8 * pair, 8)
        x_copies[pair].wait()
        get_x = tile_getter(x_ref, rows, 8)
        groups = gap_groups(get_x, -2, 4, 8)
        near = lane_pick(groups, 4 * (lane // 2) + 1 + lane % 2)
        far = lane_pick(groups, 4 * (lane // 2) + 3 * (lane % 2))
        south = [window(get_x, 0, 8), window(get_x, IB, 8)]
        north = [window(get_x, CELLS - IB, 8), window(get_x, CELLS - 2 * IB, 8)]
        v_copies[pair].wait()
        get_v = tile_getter(v_ref, rows, 8)
        v_south, v_north = window(get_v, 0, 8), window(get_v, CELLS - IB, 8)
        strips = [joined(south[0], north[0], half, 8) for half in range(2)]
        strips += [joined(south[1], north[1], half, 8) for half in range(2)]
        strips += [joined(v_south, v_north, half, 8) for half in range(2)]
        for index, strip in enumerate(strips):
            strip_ref[index, rows, :] = strip
        own_ref[0, rows, :] = near
        own_ref[1, rows, :] = far
        own_ref[2, rows, :] = gap_groups(get_v, -1, 2, 8)[0]

    d_copy.wait()
    if out_ref.shape[0] > PARTS * count:
        rest = out_ref.shape[0] - PARTS * count
        out_ref[PARTS * count :, :] = jnp.zeros((rest, LANES), jnp.float32)
    slot_lane = lane_of(count)
    get_d = tile_getter(d_ref, slice(None), count)
    d_south, d_north = window(get_d, 0, count), window(get_d, CELLS - IB, count)
    d_gaps = gap_groups(get_d, -1, 2, count)[0]
    spare = (slot_lane >= SPARE) & (slot_lane < SPARE + PIECE)

    def put(part, value):
        out_ref[part * count : (part + 1) * count, :] = value

    for chan in range(4):
        rows = pl.ds(chan, count, stride=4)
        for half in range(2):
            for deep in range(2):
                part = 2 * (4 * deep + chan) + half
                value = strip_ref[2 * deep + half, rows, :]
                if part < 8:
                    value = jnp.where(spare, rot(d_gaps, SPARE - PIECE * part), value)
                put(part, value)
            if chan >= 2:
                put(2 * (8 + chan - 2) + half, strip_ref[4 + half, rows, :])
        put(X_PART + chan, own_ref[0, rows, :])
        put(X_PART + 4 + chan, own_ref[1, rows, :])
        if chan < 2:
            put(X_PART + 8 + chan, own_ref[2, rows, :])
    for half in range(2):
        put(20 + half, joined(d_south, d_north, half, count))


def route_kernel(part_ref, code_ref, held_ref, after_ref, out_ref):
    del after_ref
    total = held_ref.shape[0]
    rows = out_ref.shape[0]
    part = part_ref[0]
    picked = [jnp.zeros((rows, 2 * LANES), jnp.float32) for _ in range(5)]
    for start in range(0, total, rows):
        held = held_ref[start : start + rows, :]
        high = held.astype(jnp.bfloat16)
        low = (held - high.astype(jnp.float32)).astype(jnp.bfloat16)
        halves = jnp.concatenate([high, low], axis=1)
        source = lax.broadcasted_iota(jnp.int32, (rows, rows), 1) + start
        for side in range(5):
            one_hot = jnp.where(code_ref[:, side : side + 1] == source, 1.0, 0.0).astype(jnp.bfloat16)
            picked[side] += jnp.dot(one_hot, halves, preferred_element_type=jnp.float32)
    west, east, south, north, fold = [value[:, :LANES] + value[:, LANES:] for value in picked]
    lane = lane_of(rows)
    along_x = (part >= X_PART) | ((part < 8) & (lane >= SPARE) & (lane < SPARE + PIECE))
    x_side = jnp.where(lane % 2 == 0, west, east)
    y_side = jnp.where(lane < 64, north + rot(fold, 64), south)
    out_ref[...] = jnp.where(along_x, x_side, y_side)


def bulk_kernel(first, my_ref, tracer_ref, velocity_ref, depth_ref, kappa_ref, code_ref, own_ref, after_ref,
                base_ref, edge_ref, x_ref, v_ref, d_ref, k_ref, w_ref, z_ref, x_sems, v_sems, d_sems):
    del after_ref
    count = depth_ref.shape[0]
    pairs = base_ref.shape[0] // 8
    x_copies = pair_copies(tracer_ref, x_ref, x_sems, first, pairs)
    v_copies = pair_copies(velocity_ref, v_ref, v_sems, first, pairs)
    d_copy = pltpu.make_async_copy(depth_ref, d_ref, d_sems.at[0])
    k_copy = pltpu.make_async_copy(kappa_ref, k_ref, d_sems.at[1])
    d_copy.start()
    k_copy.start()
    for pair in range(pairs):
        v_copies[pair].start()
        x_copies[pair].start()
    d_copy.wait()
    k_copy.wait()
    lane = lane_of(8)
    row = lax.broadcasted_iota(jnp.int32, (8, LANES), 0)
    x_row, even, place = row % 4 < 2, row % 2 == 0, row % 4
    level = (row % 2).astype(jnp.float32)
    zero = jnp.zeros((8, LANES), jnp.float32)

    def all_rows(value, chosen):
        result = value
        for at in range(4):
            if at != chosen:
                result = jnp.where(place == at, sublanes(value, at - chosen), result)
        return result

    def wet_of(depth):
        return jnp.clip(depth - level, 0.0, 1.0)

    def one_pair(pair):
        slot = 2 * (first + pair)
        rows = pl.ds(8 * pair, 8)

        def two_rows(ref, columns, width):
            top, low = ref[pl.ds(slot, 1), columns], ref[pl.ds(slot + 1, 1), columns]
            return jnp.where(row[:, :width] < 4, jnp.broadcast_to(top, (8, width)), jnp.broadcast_to(low, (8, width)))

        def slot_getter(ref):
            def get(tile):
                if tile + 1 < TILES:
                    return two_rows(ref, slice(tile * LANES, (tile + 1) * LANES), LANES)
                last = two_rows(ref, slice(tile * LANES, CELLS), CELLS - tile * LANES)
                return jnp.concatenate([last, jnp.zeros((8, WIDE - CELLS), jnp.float32)], axis=1)

            return once(get)

        codes = [code_ref[pl.ds(my_ref[0] * count + slot + at, 1), :] for at in range(2)]

        def flag(column):
            pieces = [jnp.broadcast_to(code[:, column : column + 1], (8, LANES)) for code in codes]
            return jnp.where(row < 4, pieces[0], pieces[1]) >= 0

        live, folded = flag(5), flag(4)
        state, velocity = once(tile_getter(x_ref, rows, 8)), once(tile_getter(v_ref, rows, 8))
        depth, kappa = slot_getter(d_ref), slot_getter(k_ref)
        wet = once(lambda tile: wet_of(depth(tile)))

        @once
        def ratio(tile):
            other = jnp.clip(depth(tile) - (1.0 - level), 0.0, 1.0)
            coupling = kappa(tile) * (wet(tile) * other)
            return coupling / (1.0 + 2.0 * coupling)

        next_vel = [shifted(velocity, 1), shifted(velocity, IB)]
        next_wet = [shifted(wet, 1), shifted(wet, IB)]

        @once
        def face(tile):
            rims = [at - tile * LANES for at in range(IB - 1, CELLS, IB) if at // LANES == tile]
            rim = functools.reduce(jnp.logical_or, [lane == at for at in rims]) if rims else None
            across = next_wet[0](tile) if rim is None else jnp.where(rim, 0.0, next_wet[0](tile))
            speed = velocity(tile) + jnp.where(x_row, next_vel[0](tile), next_vel[1](tile))
            value = SCALE * speed * (wet(tile) * jnp.where(x_row, across, next_wet[1](tile)))
            w_ref[:, tile * LANES : (tile + 1) * LANES] = value
            return value

        face_x = once(lambda tile: jnp.where(x_row, face(tile), sublanes(face(tile), 2)))
        face_y = once(lambda tile: jnp.where(x_row, sublanes(face(tile), -2), face(tile)))
        five = once(lambda tile: 5.0 * state(tile))
        two = once(lambda tile: 2.0 * state(tile))

        def divergence(speed, distance):
            before, after = shifted(state, -distance), shifted(state, distance)
            upper = shifted(once(lambda tile: five(tile) - after(tile)), distance)

            @once
            def flux(tile):
                value = jnp.maximum(speed(tile), 0.0) * (five(tile) - before(tile) + 2.0 * after(tile))
                return value + jnp.minimum(speed(tile), 0.0) * (two(tile) + upper(tile))

            back = shifted(flux, -distance)
            return lambda tile: flux(tile) - back(tile)

        change_x, change_y = divergence(face_x, 1), divergence(face_y, IB)
        for tile in range(TILES):
            explicit = state(tile) - wet(tile) * (change_x(tile) + change_y(tile))
            other = jnp.where(even, sublanes(explicit, -1), sublanes(explicit, 1))
            value = jnp.where(live, explicit + ratio(tile) * (other - explicit), zero)
            stop = min((tile + 1) * LANES, CELLS)
            base_ref[rows, tile * LANES : stop] = value[:, : stop - tile * LANES]
            mixed = jnp.where(x_row, face(tile), jnp.where(even, ratio(tile), depth(tile)))
            z_ref[:, tile * LANES : (tile + 1) * LANES] = mixed

        whole = slice(None)
        get_w, get_z = [lambda tile, ref=ref: ref[:, tile * LANES : (tile + 1) * LANES] for ref in (w_ref, z_ref)]
        groups = gap_groups(get_z, -2, 4, 8)
        east = lane % 2 == 0
        own_rows = pl.ds(8 * (first + pair), 8)
        near, far, normal = [own_ref[index, own_rows, :] for index in range(3)]
        normal = jnp.where(x_row, normal, sublanes(normal, 2))
        rim_speed = lane_pick(groups, 4 * (lane // 2) + 2 * (lane % 2))
        rim_speed = jnp.where(x_row, rim_speed, sublanes(rim_speed, 2))
        sides = [(
            near, far, jnp.where(east, -normal, normal), jnp.where(east, -rim_speed, rim_speed),
            lane_pick(groups, 4 * (lane // 2) + 1 + lane % 2), lane_pick(groups, 4 * (lane // 2) + 3 * (lane % 2)),
        )]
        for outer, inner, edge, sign in ((0, IB, 0, 1.0), (CELLS - IB, CELLS - 2 * IB, CELLS - 2 * IB, -1.0)):
            normal, rim_speed = window(velocity, outer, 8), window(get_w, edge, 8)
            normal = sign * jnp.where(x_row, sublanes(normal, -2), normal)
            rim_speed = sign * jnp.where(x_row, sublanes(rim_speed, -2), rim_speed)
            sides.append((window(state, outer, 8), window(state, inner, 8), normal, rim_speed,
                          window(get_z, outer, 8), window(get_z, inner, 8)))
        for side, (near, far, normal, rim_speed, outer, inner) in enumerate(sides):
            values = (near, far, normal, jnp.where(live, jnp.maximum(rim_speed, 0.0), zero), wet_of(all_rows(outer, 3)),
                      wet_of(all_rows(inner, 3)), all_rows(outer, 2), all_rows(inner, 2))
            for index, value in enumerate(values):
                edge_ref[OWN * side + index, rows, :] = value
        edge_ref[OWN * SIDES, rows, :] = jnp.where(folded, 1.0, zero)

    for pair in range(pairs):
        v_copies[pair].wait()
        x_copies[pair].wait()
        one_pair(pair)


def finish_kernel(halo_ref, edge_a_ref, edge_b_ref, base_a_ref, base_b_ref, out_ref,
                  y_ref, raw_ref, delta_ref, in_sems, out_sems):
    count = out_ref.shape[0]
    pairs = count // 2
    rows = 4 * count
    split = base_a_ref.shape[0]
    a_copy = pltpu.make_async_copy(base_a_ref, y_ref.at[pl.ds(0, split)], in_sems.at[0])
    b_copy = pltpu.make_async_copy(base_b_ref, y_ref.at[pl.ds(split, rows - split)], in_sems.at[1])
    a_copy.start()
    b_copy.start()
    lane = lane_of(rows)
    level = (lax.broadcasted_iota(jnp.int32, (rows, LANES), 0) % 2).astype(jnp.float32)

    def own(index):
        return jnp.concatenate([edge_a_ref[index], edge_b_ref[index]], axis=0)

    def part(index):
        return halo_ref[index * count : (index + 1) * count, :]

    def assembled(index, parts):
        for chan, value in enumerate(parts):
            raw_ref[index, pl.ds(chan, count, stride=4), :] = value
        return raw_ref[index]

    folded = own(OWN * SIDES) > 0.0
    mirror = jnp.where(lane < IB, IB - 1 - lane, lane)
    slot_lane = lane_of(count)
    depth_x = rot(part(0), -SPARE)
    for index in range(1, 8):
        depth_x = jnp.where(slot_lane >= PIECE * index, rot(part(index), PIECE * index - SPARE), depth_x)
    x_raw = [[part(X_PART + chan) for chan in range(4)], [part(X_PART + 4 + chan) for chan in range(4)],
             [part(X_PART + 8 + chan % 2) for chan in range(4)], [depth_x] * 4]
    y_values = [list(range(4)), list(range(4, 8)), [8, 9, 8, 9], [10] * 4]
    x_halo, south_halo, north_halo = [], [], []
    for kind in range(4):
        raw = assembled(3 * kind, x_raw[kind])
        x_halo.append(jnp.where(lane % 2 == 0, rot(raw, 1), rot(raw, -1)))
        first, second = [assembled(3 * kind + 1 + half, [part(2 * value + half) for value in y_values[kind]])
                         for half in range(2)]
        south_halo.append(jnp.where(lane < HALF, rot(first, 64), rot(second, 64 + HALF)))
        raw = jnp.where(lane < HALF, first, rot(second, HALF))
        turned = lane_take(raw, mirror)
        north_halo.append(jnp.where(folded, -turned if kind == 2 else turned, raw))

    for side, (out_near, out_far, out_normal, out_depth) in enumerate((x_halo, south_halo, north_halo)):
        near, far, normal, rim_speed, wet, inner_wet, ratio, inner_ratio = [
            own(OWN * side + index) for index in range(OWN)]
        if side == 0:
            out_normal = jnp.where(lane % 2 == 0, -out_normal, out_normal)
            beyond = out_near - jnp.where(lane % 2 == 0, rot(near, -1), rot(near, 1))
        else:
            out_normal = -out_normal if side == 2 else out_normal
            beyond = out_near
        speed = SCALE * (normal + out_normal) * (wet * jnp.clip(out_depth - level, 0.0, 1.0))
        flux = jnp.maximum(speed, 0.0) * (5.0 * out_near + 2.0 * near - out_far)
        flux += jnp.minimum(speed, 0.0) * (2.0 * out_near + 5.0 * near - far)
        inner_flux = rim_speed * beyond
        for place, (change, share) in enumerate(((wet * (flux + inner_flux), ratio),
                                                 (-inner_wet * inner_flux, inner_ratio))):
            other = jnp.where(level == 0.0, pltpu.roll(change, rows - 1, 0), pltpu.roll(change, 1, 0))
            delta_ref[2 * side + place] = change + share * (other - change)

    lane = lane_of(8)
    a_copy.wait()
    b_copy.wait()
    out_copies = []
    for pair in range(pairs):
        mine = pl.ds(8 * pair, 8)
        near, deep, south, south_in, north, north_in = [delta_ref[index, mine, :] for index in range(2 * SIDES)]
        groups = []
        for at in range(2):
            index = 2 * (lane // 4) + (lane % 4) // 2 + 64 * at
            outer, inner = lane_take(near, index), lane_take(deep, index)
            groups.append(jnp.where((lane % 4 == 1) | (lane % 4 == 2), outer, inner))
        placed = [(groups[gap // 32], 4 * (gap % 32), IB * gap - 2, 4) for gap in range(GAPS)]
        placed += [(south, 0, 0, IB), (south_in, 0, IB, IB)]
        placed += [(north, 0, CELLS - IB, IB), (north_in, 0, CELLS - 2 * IB, IB)]
        for tile in range(TILES):
            at, stop = tile * LANES, min((tile + 1) * LANES, CELLS)
            change = jnp.zeros((8, LANES), jnp.float32)
            for source, origin, start, wide in placed:
                low, high = max(start, at, 0), min(start + wide, stop)
                if low < high:
                    inside = (lane >= low - at) & (lane < high - at)
                    change += jnp.where(inside, rot(source, start - at - origin), 0.0)
            y_ref[mine, at:stop] = y_ref[mine, at:stop] + change[:, : stop - at]
        copy = pltpu.make_async_copy(
            y_ref.at[mine].reshape(2, 4, CELLS), out_ref.at[pl.ds(2 * pair, 2)], out_sems.at[pair])
        copy.start()
        out_copies.append(copy)
    for copy in out_copies:
        copy.wait()


def route_codes(block_owner, neighbours, fold_partner, slot_total):
    block_count = block_owner.shape[0]
    hits = block_owner[None, :] == jnp.arange(slot_total, dtype=jnp.int32)[:, None]
    links = jnp.concatenate([neighbours, fold_partner[:, None]], axis=1)
    linked = links[:, :, None] == jnp.arange(block_count, dtype=jnp.int32)[None, None, :]
    link_slots = jnp.max(jnp.where(linked, block_owner[None, None, :], -1), axis=2)
    link_slots = jnp.concatenate([link_slots, block_owner[:, None]], axis=1)
    return jnp.max(jnp.where(hits[:, :, None], link_slots[None], -1), axis=1)


def per_device(tracers, velocity, kappa, kmt, block_owner, neighbours, fold_partner):
    slot_count, chans = tracers.shape[:2]
    sub_count = lax.axis_size("sub")
    device_count = lax.axis_size("blk") * sub_count
    if device_count % PARTS or chans != 4 or slot_count % 2 or slot_count < 2 * FIRST_PAIRS + 2:
        raise ValueError("unsupported sizes")
    my_index = (lax.axis_index("blk") * sub_count + lax.axis_index("sub")).astype(jnp.int32).reshape(1)
    axes = ("blk", "sub")
    pairs = slot_count // 2
    slot_total = device_count * slot_count
    state_rows = 4 * slot_count
    f32 = jnp.float32
    in_hbm = pl.BlockSpec(memory_space=pltpu.HBM)
    anywhere = pl.BlockSpec(memory_space=pl.ANY)
    in_vmem = pl.BlockSpec(memory_space=pltpu.VMEM)
    in_smem = pl.BlockSpec(memory_space=pltpu.SMEM)
    dma = pltpu.SemaphoreType.DMA

    def exchanged(pieces):
        pieces = pieces.reshape(device_count, slot_count, 1, LANES)
        return lax.all_to_all(pieces, axes, 0, 0, tiled=True).reshape(slot_total, LANES)

    pack, own = pl.pallas_call(
        pack_kernel,
        out_shape=[jax.ShapeDtypeStruct((slot_total, LANES), f32), jax.ShapeDtypeStruct((3, state_rows, LANES), f32)],
        in_specs=[in_hbm, in_hbm, in_hbm],
        out_specs=[in_vmem, in_vmem],
        scratch_shapes=[
            pltpu.VMEM((state_rows, CELLS), f32),
            pltpu.VMEM((state_rows, CELLS), f32),
            pltpu.VMEM((slot_count, CELLS), f32),
            pltpu.VMEM((6, state_rows, LANES), f32),
            dma((pairs,)),
            dma((pairs,)),
            dma,
        ],
        cost_estimate=pl.CostEstimate(flops=4_000_000, bytes_accessed=2_400_000, transcendentals=0),
    )(tracers, velocity, kmt)
    held = exchanged(pack)
    codes = route_codes(block_owner, neighbours, fold_partner, slot_total)

    def bulk(first, some, after):
        return pl.pallas_call(
            functools.partial(bulk_kernel, first),
            out_shape=[
                jax.ShapeDtypeStruct((8 * some, CELLS), f32),
                jax.ShapeDtypeStruct((OWN * SIDES + 1, 8 * some, LANES), f32),
            ],
            in_specs=[in_smem, in_hbm, in_hbm, in_hbm, in_hbm, in_vmem, in_vmem, anywhere],
            out_specs=[in_vmem, in_vmem],
            scratch_shapes=[
                pltpu.VMEM((8 * some, CELLS), f32),
                pltpu.VMEM((8 * some, CELLS), f32),
                pltpu.VMEM((slot_count, CELLS), f32),
                pltpu.VMEM((slot_count, CELLS), f32),
                pltpu.VMEM((8, WIDE), f32),
                pltpu.VMEM((8, WIDE), f32),
                dma((some,)),
                dma((some,)),
                dma((2,)),
            ],
            cost_estimate=pl.CostEstimate(flops=4_000_000 * some, bytes_accessed=800_000 * some, transcendentals=0),
        )(my_index, tracers, velocity, kmt, kappa, codes, own, after)

    base_a, edge_a = bulk(0, FIRST_PAIRS, own)

    routed_rows = PARTS * slot_count
    routed = pl.pallas_call(
        route_kernel,
        grid=(device_count // PARTS,),
        out_shape=jax.ShapeDtypeStruct((slot_total, LANES), f32),
        in_specs=[
            in_smem,
            pl.BlockSpec((routed_rows, 6), lambda step: (step, 0)),
            pl.BlockSpec((slot_total, LANES), lambda step: (0, 0)),
            anywhere,
        ],
        out_specs=pl.BlockSpec((routed_rows, LANES), lambda step: (step, 0)),
    )(my_index, codes, held, edge_a)

    base_b, edge_b = bulk(FIRST_PAIRS, pairs - FIRST_PAIRS, routed)
    halo = exchanged(routed)[: PARTS * slot_count]

    return pl.pallas_call(
        finish_kernel,
        out_shape=jax.ShapeDtypeStruct(tracers.shape, f32),
        in_specs=[in_vmem, in_vmem, in_vmem, anywhere, anywhere],
        out_specs=in_hbm,
        scratch_shapes=[
            pltpu.VMEM((state_rows, CELLS), f32),
            pltpu.VMEM((12, state_rows, LANES), f32),
            pltpu.VMEM((2 * SIDES, state_rows, LANES), f32),
            dma((2,)),
            dma((pairs,)),
        ],
    )(halo, edge_a, edge_b, base_a, base_b)


def solution(mesh):
    placed = (
        P(("blk", "sub"), None, None),
        P(("blk", "sub"), None, None),
        P(("blk", "sub"), None),
        P(("blk", "sub"), None),
        P(),
        P(),
        P(),
    )
    return jax.shard_map(
        per_device,
        mesh=mesh,
        in_specs=placed,
        out_specs=P(("blk", "sub"), None, None),
        check_vma=False,
    )
```

```python
import functools

import jax
import jax.numpy as jnp
from jax import lax
from jax.experimental import pallas as pl
from jax.experimental.pallas import tpu as pltpu
from jax.sharding import PartitionSpec as P

IB = 90
JB = 60
CELLS = IB * JB
COURANT = 0.2
LANES = 128
TILES = -(-CELLS // LANES)
WIDE = TILES * LANES
GAPS = JB + 1
HALF = IB // 2
PARTS = 32
X_PART = 22
SPARE = 48
PIECE = 16
SCALE = COURANT / 12.0
SIDES = 3
OWN = 8
FIRST_PAIRS = 3


def lane_of(rows):
    return lax.broadcasted_iota(jnp.int32, (rows, LANES), 1)


def rot(value, shift):
    shift = shift % LANES
    return value if shift == 0 else pltpu.roll(value, shift, 1)


def sublanes(value, shift):
    return pltpu.roll(value, shift % 8, 0)


def once(make):
    held = {}

    def get(tile):
        if tile not in held:
            held[tile] = make(tile)
        return held[tile]

    return get


def shifted(get, distance):
    offset = distance % LANES
    turned = once(lambda tile: rot(get(tile), -offset))

    def make(tile):
        low = tile + distance // LANES
        first = turned(low) if 0 <= low < TILES else jnp.zeros((8, LANES), jnp.float32)
        second = turned(low + 1) if 0 <= low + 1 < TILES else jnp.zeros((8, LANES), jnp.float32)
        return jnp.where(lane_of(8) < LANES - offset, first, second)

    return once(make)


def window(get, start, rows):
    tile, offset = start // LANES, start % LANES
    head = rot(get(tile), -offset)
    if offset == 0 or tile + 1 >= TILES:
        return head
    return jnp.where(lane_of(rows) < LANES - offset, head, rot(get(tile + 1), -offset))


def gap_groups(get, first, wide, rows):
    lane = lane_of(rows)
    held = LANES // wide
    result = []
    for at in range(0, GAPS, held):
        value = jnp.zeros((rows, LANES), jnp.float32)
        for gap in range(at, min(at + held, GAPS)):
            start = IB * gap + first
            place = (gap - at) * wide
            for tile in range(max(start, 0) // LANES, min(start + wide - 1, CELLS - 1) // LANES + 1):
                low = max(start, tile * LANES, 0)
                value = jnp.where(lane >= place + low - start, rot(get(tile), place - start + tile * LANES), value)
        result.append(value)
    return result


def lane_take(value, index):
    return jnp.take_along_axis(value, index, axis=1, mode="promise_in_bounds")


def lane_pick(pair, index):
    return jnp.where(index < LANES, lane_take(pair[0], index % LANES), lane_take(pair[1], index % LANES))


def tile_getter(ref, rows, count):
    def get(tile):
        if tile + 1 < TILES:
            return ref[rows, tile * LANES : (tile + 1) * LANES]
        rest = jnp.zeros((count, WIDE - CELLS), jnp.float32)
        return jnp.concatenate([ref[rows, tile * LANES : CELLS], rest], axis=1)

    return get


def joined(south, north, half, rows):
    if half == 0:
        return jnp.where(lane_of(rows) < 64, south, rot(north, 64))
    return jnp.where(lane_of(rows) < 64, rot(south, -HALF), rot(north, 64 - HALF))


def pair_copies(source, target, sems, first, pairs):
    copies = []
    for pair in range(pairs):
        into = target.at[pl.ds(8 * pair, 8)].reshape(2, 4, CELLS)
        copies.append(pltpu.make_async_copy(source.at[pl.ds(2 * (first + pair), 2)], into, sems.at[pair]))
    return copies


def pack_kernel(tracer_ref, velocity_ref, depth_ref, out_ref, own_ref,
                x_ref, v_ref, d_ref, strip_ref, x_sems, v_sems, d_sem):
    count = depth_ref.shape[0]
    pairs = count // 2
    x_copies = pair_copies(tracer_ref, x_ref, x_sems, 0, pairs)
    v_copies = pair_copies(velocity_ref, v_ref, v_sems, 0, pairs)
    d_copy = pltpu.make_async_copy(depth_ref, d_ref, d_sem)
    for pair in range(pairs):
        x_copies[pair].start()
        v_copies[pair].start()
    d_copy.start()
    lane = lane_of(8)
    for pair in range(pairs):
        rows = pl.ds(8 * pair, 8)
        x_copies[pair].wait()
        get_x = tile_getter(x_ref, rows, 8)
        groups = gap_groups(get_x, -2, 4, 8)
        near = lane_pick(groups, 4 * (lane // 2) + 1 + lane % 2)
        far = lane_pick(groups, 4 * (lane // 2) + 3 * (lane % 2))
        south = [window(get_x, 0, 8), window(get_x, IB, 8)]
        north = [window(get_x, CELLS - IB, 8), window(get_x, CELLS - 2 * IB, 8)]
        v_copies[pair].wait()
        get_v = tile_getter(v_ref, rows, 8)
        v_south, v_north = window(get_v, 0, 8), window(get_v, CELLS - IB, 8)
        strips = [joined(south[0], north[0], half, 8) for half in range(2)]
        strips += [joined(south[1], north[1], half, 8) for half in range(2)]
        strips += [joined(v_south, v_north, half, 8) for half in range(2)]
        for index, strip in enumerate(strips):
            strip_ref[index, rows, :] = strip
        own_ref[0, rows, :] = near
        own_ref[1, rows, :] = far
        own_ref[2, rows, :] = gap_groups(get_v, -1, 2, 8)[0]

    d_copy.wait()
    if out_ref.shape[0] > PARTS * count:
        rest = out_ref.shape[0] - PARTS * count
        out_ref[PARTS * count :, :] = jnp.zeros((rest, LANES), jnp.float32)
    slot_lane = lane_of(count)
    get_d = tile_getter(d_ref, slice(None), count)
    d_south, d_north = window(get_d, 0, count), window(get_d, CELLS - IB, count)
    d_gaps = gap_groups(get_d, -1, 2, count)[0]
    spare = (slot_lane >= SPARE) & (slot_lane < SPARE + PIECE)

    def put(part, value):
        out_ref[part * count : (part + 1) * count, :] = value

    for chan in range(4):
        rows = pl.ds(chan, count, stride=4)
        for half in range(2):
            for deep in range(2):
                part = 2 * (4 * deep + chan) + half
                value = strip_ref[2 * deep + half, rows, :]
                if part < 8:
                    value = jnp.where(spare, rot(d_gaps, SPARE - PIECE * part), value)
                put(part, value)
            if chan >= 2:
                put(2 * (8 + chan - 2) + half, strip_ref[4 + half, rows, :])
        put(X_PART + chan, own_ref[0, rows, :])
        put(X_PART + 4 + chan, own_ref[1, rows, :])
        if chan < 2:
            put(X_PART + 8 + chan, own_ref[2, rows, :])
    for half in range(2):
        put(20 + half, joined(d_south, d_north, half, count))


def route_kernel(part_ref, code_ref, held_ref, after_ref, out_ref):
    del after_ref
    total = held_ref.shape[0]
    rows = out_ref.shape[0]
    part = part_ref[0]
    picked = [jnp.zeros((rows, 2 * LANES), jnp.float32) for _ in range(5)]
    for start in range(0, total, rows):
        held = held_ref[start : start + rows, :]
        high = held.astype(jnp.bfloat16)
        low = (held - high.astype(jnp.float32)).astype(jnp.bfloat16)
        halves = jnp.concatenate([high, low], axis=1)
        source = lax.broadcasted_iota(jnp.int32, (rows, rows), 1) + start
        for side in range(5):
            one_hot = jnp.where(code_ref[:, side : side + 1] == source, 1.0, 0.0).astype(jnp.bfloat16)
            picked[side] += jnp.dot(one_hot, halves, preferred_element_type=jnp.float32)
    west, east, south, north, fold = [value[:, :LANES] + value[:, LANES:] for value in picked]
    lane = lane_of(rows)
    along_x = (part >= X_PART) | ((part < 8) & (lane >= SPARE) & (lane < SPARE + PIECE))
    x_side = jnp.where(lane % 2 == 0, west, east)
    y_side = jnp.where(lane < 64, north + rot(fold, 64), south)
    out_ref[...] = jnp.where(along_x, x_side, y_side)


def bulk_kernel(first, my_ref, tracer_ref, velocity_ref, depth_ref, kappa_ref, code_ref, own_ref, after_ref,
                base_ref, edge_ref, x_ref, v_ref, d_ref, k_ref, d8_ref, k8_ref, w_ref, z_ref, x_sems, v_sems, d_sems):
    del after_ref
    count = depth_ref.shape[0]
    pairs = base_ref.shape[0] // 8
    x_copies = pair_copies(tracer_ref, x_ref, x_sems, first, pairs)
    v_copies = pair_copies(velocity_ref, v_ref, v_sems, first, pairs)
    d_copy = pltpu.make_async_copy(depth_ref, d_ref, d_sems.at[0])
    k_copy = pltpu.make_async_copy(kappa_ref, k_ref, d_sems.at[1])
    d_copy.start()
    k_copy.start()
    for pair in range(pairs):
        v_copies[pair].start()
        x_copies[pair].start()
    lane = lane_of(8)
    row = lax.broadcasted_iota(jnp.int32, (8, LANES), 0)
    x_row, even, place = row % 4 < 2, row % 2 == 0, row % 4
    level = (row % 2).astype(jnp.float32)
    zero = jnp.zeros((8, LANES), jnp.float32)

    def all_rows(value, chosen):
        result = value
        for at in range(4):
            if at != chosen:
                result = jnp.where(place == at, sublanes(value, at - chosen), result)
        return result

    def wet_of(depth):
        return jnp.clip(depth - level, 0.0, 1.0)

    for copy, source, target in ((d_copy, d_ref, d8_ref), (k_copy, k_ref, k8_ref)):
        copy.wait()
        for pair in range(pairs):
            slot = 2 * (first + pair)
            for start in range(0, CELLS, LANES):
                columns = slice(start, min(start + LANES, CELLS))
                shape = (8, columns.stop - start)
                top, low = [jnp.broadcast_to(source[slot + at : slot + at + 1, columns], shape) for at in range(2)]
                target[8 * pair : 8 * pair + 8, columns] = jnp.where(row[:, : shape[1]] < 4, top, low)

    def one_pair(pair):
        slot = 2 * (first + pair)
        rows = pl.ds(pl.multiple_of(8 * pair, 8), 8)
        for source, target, sems in ((velocity_ref, v_ref, v_sems), (tracer_ref, x_ref, x_sems)):
            pltpu.make_async_copy(
                source.at[pl.ds(0, 2)], target.at[rows].reshape(2, 4, CELLS), sems.at[pair]).wait()

        codes = [code_ref[pl.ds(my_ref[0] * count + slot + at, 1), :] for at in range(2)]

        def flag(column):
            pieces = [jnp.broadcast_to(code[:, column : column + 1], (8, LANES)) for code in codes]
            return jnp.where(row < 4, pieces[0], pieces[1]) >= 0

        live, folded = flag(5), flag(4)
        state, velocity = once(tile_getter(x_ref, rows, 8)), once(tile_getter(v_ref, rows, 8))
        depth, kappa = once(tile_getter(d8_ref, rows, 8)), once(tile_getter(k8_ref, rows, 8))
        wet = once(lambda tile: wet_of(depth(tile)))

        @once
        def ratio(tile):
            other = jnp.clip(depth(tile) - (1.0 - level), 0.0, 1.0)
            coupling = kappa(tile) * (wet(tile) * other)
            return coupling / (1.0 + 2.0 * coupling)

        next_vel = [shifted(velocity, 1), shifted(velocity, IB)]
        next_wet = [shifted(wet, 1), shifted(wet, IB)]

        @once
        def face(tile):
            rims = [at - tile * LANES for at in range(IB - 1, CELLS, IB) if at // LANES == tile]
            rim = functools.reduce(jnp.logical_or, [lane == at for at in rims]) if rims else None
            across = next_wet[0](tile) if rim is None else jnp.where(rim, 0.0, next_wet[0](tile))
            speed = velocity(tile) + jnp.where(x_row, next_vel[0](tile), next_vel[1](tile))
            value = SCALE * speed * (wet(tile) * jnp.where(x_row, across, next_wet[1](tile)))
            w_ref[:, tile * LANES : (tile + 1) * LANES] = value
            return value

        face_x = once(lambda tile: jnp.where(x_row, face(tile), sublanes(face(tile), 2)))
        face_y = once(lambda tile: jnp.where(x_row, sublanes(face(tile), -2), face(tile)))
        five = once(lambda tile: 5.0 * state(tile))
        two = once(lambda tile: 2.0 * state(tile))

        def divergence(speed, distance):
            before, after = shifted(state, -distance), shifted(state, distance)
            lower = once(lambda tile: five(tile) - before(tile) + 2.0 * after(tile))
            upper = shifted(once(lambda tile: five(tile) - after(tile)), distance)

            @once
            def flux(tile):
                value = jnp.maximum(speed(tile), 0.0) * lower(tile)
                return value + jnp.minimum(speed(tile), 0.0) * (two(tile) + upper(tile))

            back = shifted(flux, -distance)
            for stage in (after, before, lower, upper, flux, back):
                for tile in range(TILES):
                    stage(tile)
            return once(lambda tile: flux(tile) - back(tile))

        for stage in (depth, wet, ratio, *next_vel, *next_wet, face):
            for tile in range(TILES):
                stage(tile)
        change_x, change_y = divergence(face_x, 1), divergence(face_y, IB)
        for tile in range(TILES):
            explicit = state(tile) - wet(tile) * (change_x(tile) + change_y(tile))
            other = jnp.where(even, sublanes(explicit, -1), sublanes(explicit, 1))
            value = jnp.where(live, explicit + ratio(tile) * (other - explicit), zero)
            stop = min((tile + 1) * LANES, CELLS)
            base_ref[rows, tile * LANES : stop] = value[:, : stop - tile * LANES]
            mixed = jnp.where(x_row, face(tile), jnp.where(even, ratio(tile), depth(tile)))
            z_ref[:, tile * LANES : (tile + 1) * LANES] = mixed

        get_w, get_z = [lambda tile, ref=ref: ref[:, tile * LANES : (tile + 1) * LANES] for ref in (w_ref, z_ref)]
        groups = gap_groups(get_z, -2, 4, 8)
        east = lane % 2 == 0
        own_rows = pl.ds(pl.multiple_of(8 * (first + pair), 8), 8)
        near, far, normal = [own_ref[index, own_rows, :] for index in range(3)]
        normal = jnp.where(x_row, normal, sublanes(normal, 2))
        rim_speed = lane_pick(groups, 4 * (lane // 2) + 2 * (lane % 2))
        rim_speed = jnp.where(x_row, rim_speed, sublanes(rim_speed, 2))
        sides = [(
            near, far, jnp.where(east, -normal, normal), jnp.where(east, -rim_speed, rim_speed),
            lane_pick(groups, 4 * (lane // 2) + 1 + lane % 2), lane_pick(groups, 4 * (lane // 2) + 3 * (lane % 2)),
        )]
        for outer, inner, edge, sign in ((0, IB, 0, 1.0), (CELLS - IB, CELLS - 2 * IB, CELLS - 2 * IB, -1.0)):
            normal, rim_speed = window(velocity, outer, 8), window(get_w, edge, 8)
            normal = sign * jnp.where(x_row, sublanes(normal, -2), normal)
            rim_speed = sign * jnp.where(x_row, sublanes(rim_speed, -2), rim_speed)
            sides.append((window(state, outer, 8), window(state, inner, 8), normal, rim_speed,
                          window(get_z, outer, 8), window(get_z, inner, 8)))
        for side, (near, far, normal, rim_speed, outer, inner) in enumerate(sides):
            values = (near, far, normal, jnp.where(live, jnp.maximum(rim_speed, 0.0), zero), wet_of(all_rows(outer, 3)),
                      wet_of(all_rows(inner, 3)), all_rows(outer, 2), all_rows(inner, 2))
            for index, value in enumerate(values):
                edge_ref[OWN * side + index, rows, :] = value
        edge_ref[OWN * SIDES, rows, :] = jnp.where(folded, 1.0, zero)

    pl.loop(0, pairs)(one_pair)


def finish_kernel(halo_ref, edge_a_ref, edge_b_ref, base_a_ref, base_b_ref, out_ref,
                  y_ref, raw_ref, delta_ref, in_sems, out_sems):
    count = out_ref.shape[0]
    pairs = count // 2
    rows = 4 * count
    split = base_a_ref.shape[0]
    a_copy = pltpu.make_async_copy(base_a_ref, y_ref.at[pl.ds(0, split)], in_sems.at[0])
    b_copy = pltpu.make_async_copy(base_b_ref, y_ref.at[pl.ds(split, rows - split)], in_sems.at[1])
    a_copy.start()
    b_copy.start()
    lane = lane_of(rows)
    level = (lax.broadcasted_iota(jnp.int32, (rows, LANES), 0) % 2).astype(jnp.float32)

    def own(index):
        return jnp.concatenate([edge_a_ref[index], edge_b_ref[index]], axis=0)

    def part(index):
        return halo_ref[index * count : (index + 1) * count, :]

    def assembled(index, parts):
        for chan, value in enumerate(parts):
            raw_ref[index, pl.ds(chan, count, stride=4), :] = value
        return raw_ref[index]

    folded = own(OWN * SIDES) > 0.0
    mirror = jnp.where(lane < IB, IB - 1 - lane, lane)
    slot_lane = lane_of(count)
    depth_x = rot(part(0), -SPARE)
    for index in range(1, 8):
        depth_x = jnp.where(slot_lane >= PIECE * index, rot(part(index), PIECE * index - SPARE), depth_x)
    x_raw = [[part(X_PART + chan) for chan in range(4)], [part(X_PART + 4 + chan) for chan in range(4)],
             [part(X_PART + 8 + chan % 2) for chan in range(4)], [depth_x] * 4]
    y_values = [list(range(4)), list(range(4, 8)), [8, 9, 8, 9], [10] * 4]
    x_halo, south_halo, north_halo = [], [], []
    for kind in range(4):
        raw = assembled(3 * kind, x_raw[kind])
        x_halo.append(jnp.where(lane % 2 == 0, rot(raw, 1), rot(raw, -1)))
        first, second = [assembled(3 * kind + 1 + half, [part(2 * value + half) for value in y_values[kind]])
                         for half in range(2)]
        south_halo.append(jnp.where(lane < HALF, rot(first, 64), rot(second, 64 + HALF)))
        raw = jnp.where(lane < HALF, first, rot(second, HALF))
        turned = lane_take(raw, mirror)
        north_halo.append(jnp.where(folded, -turned if kind == 2 else turned, raw))

    for side, (out_near, out_far, out_normal, out_depth) in enumerate((x_halo, south_halo, north_halo)):
        near, far, normal, rim_speed, wet, inner_wet, ratio, inner_ratio = [
            own(OWN * side + index) for index in range(OWN)]
        if side == 0:
            out_normal = jnp.where(lane % 2 == 0, -out_normal, out_normal)
            beyond = out_near - jnp.where(lane % 2 == 0, rot(near, -1), rot(near, 1))
        else:
            out_normal = -out_normal if side == 2 else out_normal
            beyond = out_near
        speed = SCALE * (normal + out_normal) * (wet * jnp.clip(out_depth - level, 0.0, 1.0))
        flux = jnp.maximum(speed, 0.0) * (5.0 * out_near + 2.0 * near - out_far)
        flux += jnp.minimum(speed, 0.0) * (2.0 * out_near + 5.0 * near - far)
        inner_flux = rim_speed * beyond
        for place, (change, share) in enumerate(((wet * (flux + inner_flux), ratio),
                                                 (-inner_wet * inner_flux, inner_ratio))):
            other = jnp.where(level == 0.0, pltpu.roll(change, rows - 1, 0), pltpu.roll(change, 1, 0))
            delta_ref[2 * side + place] = change + share * (other - change)

    lane = lane_of(8)
    a_copy.wait()
    b_copy.wait()
    out_copies = []
    for pair in range(pairs):
        mine = pl.ds(8 * pair, 8)
        near, deep, south, south_in, north, north_in = [delta_ref[index, mine, :] for index in range(2 * SIDES)]
        groups = []
        for at in range(2):
            index = 2 * (lane // 4) + (lane % 4) // 2 + 64 * at
            outer, inner = lane_take(near, index), lane_take(deep, index)
            groups.append(jnp.where((lane % 4 == 1) | (lane % 4 == 2), outer, inner))
        placed = [(groups[gap // 32], 4 * (gap % 32), IB * gap - 2, 4) for gap in range(GAPS)]
        placed += [(south, 0, 0, IB), (south_in, 0, IB, IB)]
        placed += [(north, 0, CELLS - IB, IB), (north_in, 0, CELLS - 2 * IB, IB)]
        for tile in range(TILES):
            at, stop = tile * LANES, min((tile + 1) * LANES, CELLS)
            change = jnp.zeros((8, LANES), jnp.float32)
            for source, origin, start, wide in placed:
                low, high = max(start, at, 0), min(start + wide, stop)
                if low < high:
                    inside = (lane >= low - at) & (lane < high - at)
                    change += jnp.where(inside, rot(source, start - at - origin), 0.0)
            y_ref[mine, at:stop] = y_ref[mine, at:stop] + change[:, : stop - at]
        copy = pltpu.make_async_copy(
            y_ref.at[mine].reshape(2, 4, CELLS), out_ref.at[pl.ds(2 * pair, 2)], out_sems.at[pair])
        copy.start()
        out_copies.append(copy)
    for copy in out_copies:
        copy.wait()


def route_codes(block_owner, neighbours, fold_partner, slot_total):
    block_count = block_owner.shape[0]
    hits = block_owner[None, :] == jnp.arange(slot_total, dtype=jnp.int32)[:, None]
    links = jnp.concatenate([neighbours, fold_partner[:, None]], axis=1)
    linked = links[:, :, None] == jnp.arange(block_count, dtype=jnp.int32)[None, None, :]
    link_slots = jnp.max(jnp.where(linked, block_owner[None, None, :], -1), axis=2)
    link_slots = jnp.concatenate([link_slots, block_owner[:, None]], axis=1)
    return jnp.max(jnp.where(hits[:, :, None], link_slots[None], -1), axis=1)


def per_device(tracers, velocity, kappa, kmt, block_owner, neighbours, fold_partner):
    slot_count, chans = tracers.shape[:2]
    sub_count = lax.axis_size("sub")
    device_count = lax.axis_size("blk") * sub_count
    if device_count % PARTS or chans != 4 or slot_count % 2 or slot_count < 2 * FIRST_PAIRS + 2:
        raise ValueError("unsupported sizes")
    my_index = (lax.axis_index("blk") * sub_count + lax.axis_index("sub")).astype(jnp.int32).reshape(1)
    axes = ("blk", "sub")
    pairs = slot_count // 2
    slot_total = device_count * slot_count
    state_rows = 4 * slot_count
    f32 = jnp.float32
    in_hbm = pl.BlockSpec(memory_space=pltpu.HBM)
    anywhere = pl.BlockSpec(memory_space=pl.ANY)
    in_vmem = pl.BlockSpec(memory_space=pltpu.VMEM)
    in_smem = pl.BlockSpec(memory_space=pltpu.SMEM)
    dma = pltpu.SemaphoreType.DMA
    limit = pltpu.CompilerParams(vmem_limit_bytes=32 * 1024 * 1024)

    def exchanged(pieces):
        pieces = pieces.reshape(device_count, slot_count, 1, LANES)
        return lax.all_to_all(pieces, axes, 0, 0, tiled=True).reshape(slot_total, LANES)

    pack, own = pl.pallas_call(
        pack_kernel,
        out_shape=[jax.ShapeDtypeStruct((slot_total, LANES), f32), jax.ShapeDtypeStruct((3, state_rows, LANES), f32)],
        in_specs=[in_hbm, in_hbm, in_hbm],
        out_specs=[in_vmem, in_vmem],
        scratch_shapes=[
            pltpu.VMEM((state_rows, CELLS), f32),
            pltpu.VMEM((state_rows, CELLS), f32),
            pltpu.VMEM((slot_count, CELLS), f32),
            pltpu.VMEM((6, state_rows, LANES), f32),
            dma((pairs,)),
            dma((pairs,)),
            dma,
        ],
        cost_estimate=pl.CostEstimate(flops=4_000_000, bytes_accessed=2_400_000, transcendentals=0),
    )(tracers, velocity, kmt)
    held = exchanged(pack)
    codes = route_codes(block_owner, neighbours, fold_partner, slot_total)

    def bulk(first, some, after):
        return pl.pallas_call(
            functools.partial(bulk_kernel, first),
            out_shape=[
                jax.ShapeDtypeStruct((8 * some, CELLS), f32),
                jax.ShapeDtypeStruct((OWN * SIDES + 1, 8 * some, LANES), f32),
            ],
            in_specs=[in_smem, in_hbm, in_hbm, in_hbm, in_hbm, in_vmem, in_vmem, anywhere],
            out_specs=[in_vmem, in_vmem],
            scratch_shapes=[
                pltpu.VMEM((8 * some, CELLS), f32),
                pltpu.VMEM((8 * some, CELLS), f32),
                pltpu.VMEM((slot_count, CELLS), f32),
                pltpu.VMEM((slot_count, CELLS), f32),
                pltpu.VMEM((8 * some, CELLS), f32),
                pltpu.VMEM((8 * some, CELLS), f32),
                pltpu.VMEM((8, WIDE), f32),
                pltpu.VMEM((8, WIDE), f32),
                dma((some,)),
                dma((some,)),
                dma((2,)),
            ],
            compiler_params=limit,
            cost_estimate=pl.CostEstimate(flops=4_000_000 * some, bytes_accessed=800_000 * some, transcendentals=0),
        )(my_index, tracers, velocity, kmt, kappa, codes, own, after)

    base_a, edge_a = bulk(0, FIRST_PAIRS, own)

    routed_rows = PARTS * slot_count
    routed = pl.pallas_call(
        route_kernel,
        grid=(device_count // PARTS,),
        out_shape=jax.ShapeDtypeStruct((slot_total, LANES), f32),
        in_specs=[
            in_smem,
            pl.BlockSpec((routed_rows, 6), lambda step: (step, 0)),
            pl.BlockSpec((slot_total, LANES), lambda step: (0, 0)),
            anywhere,
        ],
        out_specs=pl.BlockSpec((routed_rows, LANES), lambda step: (step, 0)),
        compiler_params=limit,
    )(my_index, codes, held, edge_a)

    base_b, edge_b = bulk(FIRST_PAIRS, pairs - FIRST_PAIRS, routed)
    halo = exchanged(routed)[: PARTS * slot_count]

    return pl.pallas_call(
        finish_kernel,
        out_shape=jax.ShapeDtypeStruct(tracers.shape, f32),
        in_specs=[in_vmem, in_vmem, in_vmem, anywhere, anywhere],
        out_specs=in_hbm,
        scratch_shapes=[
            pltpu.VMEM((state_rows, CELLS), f32),
            pltpu.VMEM((12, state_rows, LANES), f32),
            pltpu.VMEM((2 * SIDES, state_rows, LANES), f32),
            dma((2,)),
            dma((pairs,)),
        ],
        compiler_params=limit,
    )(halo, edge_a, edge_b, base_a, base_b)


def solution(mesh):
    placed = (
        P(("blk", "sub"), None, None),
        P(("blk", "sub"), None, None),
        P(("blk", "sub"), None),
        P(("blk", "sub"), None),
        P(),
        P(),
        P(),
    )
    return jax.shard_map(
        per_device,
        mesh=mesh,
        in_specs=placed,
        out_specs=P(("blk", "sub"), None, None),
        check_vma=False,
    )
```

```python
import functools

import jax
import jax.numpy as jnp
from jax import lax
from jax.experimental import pallas as pl
from jax.experimental.pallas import tpu as pltpu
from jax.sharding import PartitionSpec as P

IB = 90
JB = 60
CELLS = IB * JB
COURANT = 0.2
LANES = 128
TILES = -(-CELLS // LANES)
WIDE = TILES * LANES
GAPS = JB + 1
HALF = IB // 2
PARTS = 32
X_PART = 22
SPARE = 48
PIECE = 16
SCALE = COURANT / 12.0
SIDES = 3
OWN = 8
FIRST_PAIRS = 2


def lane_of(rows):
    return lax.broadcasted_iota(jnp.int32, (rows, LANES), 1)


def rot(value, shift):
    shift = shift % LANES
    return value if shift == 0 else pltpu.roll(value, shift, 1)


def sublanes(value, shift):
    return pltpu.roll(value, shift % 8, 0)


def once(make):
    held = {}

    def get(tile):
        if tile not in held:
            held[tile] = make(tile)
        return held[tile]

    return get


def shifted(get, distance):
    offset = distance % LANES
    turned = once(lambda tile: rot(get(tile), -offset))

    def make(tile):
        low = tile + distance // LANES
        first = turned(low) if 0 <= low < TILES else jnp.zeros((8, LANES), jnp.float32)
        second = turned(low + 1) if 0 <= low + 1 < TILES else jnp.zeros((8, LANES), jnp.float32)
        return jnp.where(lane_of(8) < LANES - offset, first, second)

    return once(make)


def window(get, start, rows):
    tile, offset = start // LANES, start % LANES
    head = rot(get(tile), -offset)
    if offset == 0 or tile + 1 >= TILES:
        return head
    return jnp.where(lane_of(rows) < LANES - offset, head, rot(get(tile + 1), -offset))


def gap_groups(get, first, wide, rows):
    lane = lane_of(rows)
    held = LANES // wide
    result = []
    for at in range(0, GAPS, held):
        value = jnp.zeros((rows, LANES), jnp.float32)
        for gap in range(at, min(at + held, GAPS)):
            start = IB * gap + first
            place = (gap - at) * wide
            for tile in range(max(start, 0) // LANES, min(start + wide - 1, CELLS - 1) // LANES + 1):
                low = max(start, tile * LANES, 0)
                value = jnp.where(lane >= place + low - start, rot(get(tile), place - start + tile * LANES), value)
        result.append(value)
    return result


def lane_take(value, index):
    return jnp.take_along_axis(value, index, axis=1, mode="promise_in_bounds")


def lane_pick(pair, index):
    return jnp.where(index < LANES, lane_take(pair[0], index % LANES), lane_take(pair[1], index % LANES))


def tile_getter(ref, rows, count):
    def get(tile):
        if tile + 1 < TILES:
            return ref[rows, tile * LANES : (tile + 1) * LANES]
        rest = jnp.zeros((count, WIDE - CELLS), jnp.float32)
        return jnp.concatenate([ref[rows, tile * LANES : CELLS], rest], axis=1)

    return get


def across_pair(get):
    lane = lane_of(8)
    groups = gap_groups(get, -2, 4, 8)
    return lane_pick(groups, 4 * (lane // 2) + 1 + lane % 2), lane_pick(groups, 4 * (lane // 2) + 3 * (lane % 2))


def joined(south, north, half, rows):
    if half == 0:
        return jnp.where(lane_of(rows) < 64, south, rot(north, 64))
    return jnp.where(lane_of(rows) < 64, rot(south, -HALF), rot(north, 64 - HALF))


def pair_copies(source, target, sems, first, pairs):
    copies = []
    for pair in range(pairs):
        into = target.at[pl.ds(8 * pair, 8)].reshape(2, 4, CELLS)
        copies.append(pltpu.make_async_copy(source.at[pl.ds(2 * (first + pair), 2)], into, sems.at[pair]))
    return copies


def pack_kernel(tracer_ref, velocity_ref, depth_ref, out_ref, x_ref, v_ref, d_ref, strip_ref, x_sems, v_sems, d_sem):
    count = depth_ref.shape[0]
    pairs = count // 2
    x_copies = pair_copies(tracer_ref, x_ref, x_sems, 0, pairs)
    v_copies = pair_copies(velocity_ref, v_ref, v_sems, 0, pairs)
    d_copy = pltpu.make_async_copy(depth_ref, d_ref, d_sem)
    for pair in range(pairs):
        x_copies[pair].start()
        v_copies[pair].start()
    d_copy.start()
    for pair in range(pairs):
        rows = pl.ds(8 * pair, 8)
        x_copies[pair].wait()
        get_x = tile_getter(x_ref, rows, 8)
        near, far = across_pair(get_x)
        south = [window(get_x, 0, 8), window(get_x, IB, 8)]
        north = [window(get_x, CELLS - IB, 8), window(get_x, CELLS - 2 * IB, 8)]
        v_copies[pair].wait()
        get_v = tile_getter(v_ref, rows, 8)
        v_south, v_north = window(get_v, 0, 8), window(get_v, CELLS - IB, 8)
        strips = [joined(south[0], north[0], half, 8) for half in range(2)]
        strips += [joined(south[1], north[1], half, 8) for half in range(2)]
        strips += [joined(v_south, v_north, half, 8) for half in range(2)]
        strips += [near, far, gap_groups(get_v, -1, 2, 8)[0]]
        for index, strip in enumerate(strips):
            strip_ref[index, rows, :] = strip

    d_copy.wait()
    if out_ref.shape[0] > PARTS * count:
        rest = out_ref.shape[0] - PARTS * count
        out_ref[PARTS * count :, :] = jnp.zeros((rest, LANES), jnp.float32)
    slot_lane = lane_of(count)
    get_d = tile_getter(d_ref, slice(None), count)
    d_south, d_north = window(get_d, 0, count), window(get_d, CELLS - IB, count)
    d_gaps = gap_groups(get_d, -1, 2, count)[0]
    spare = (slot_lane >= SPARE) & (slot_lane < SPARE + PIECE)

    def put(part, value):
        out_ref[part * count : (part + 1) * count, :] = value

    for chan in range(4):
        rows = pl.ds(chan, count, stride=4)
        for half in range(2):
            for deep in range(2):
                part = 2 * (4 * deep + chan) + half
                value = strip_ref[2 * deep + half, rows, :]
                if part < 8:
                    value = jnp.where(spare, rot(d_gaps, SPARE - PIECE * part), value)
                put(part, value)
            if chan >= 2:
                put(2 * (8 + chan - 2) + half, strip_ref[4 + half, rows, :])
        put(X_PART + chan, strip_ref[6, rows, :])
        put(X_PART + 4 + chan, strip_ref[7, rows, :])
        if chan < 2:
            put(X_PART + 8 + chan, strip_ref[8, rows, :])
    for half in range(2):
        put(20 + half, joined(d_south, d_north, half, count))


def route_kernel(part_ref, code_ref, held_ref, after_ref, out_ref):
    del after_ref
    total = held_ref.shape[0]
    rows = out_ref.shape[0]
    part = part_ref[0]
    picked = [jnp.zeros((rows, 2 * LANES), jnp.float32) for _ in range(5)]
    for start in range(0, total, rows):
        held = held_ref[start : start + rows, :]
        high = held.astype(jnp.bfloat16)
        low = (held - high.astype(jnp.float32)).astype(jnp.bfloat16)
        halves = jnp.concatenate([high, low], axis=1)
        source = lax.broadcasted_iota(jnp.int32, (rows, rows), 1) + start
        for side in range(5):
            one_hot = jnp.where(code_ref[:, side : side + 1] == source, 1.0, 0.0).astype(jnp.bfloat16)
            picked[side] += jnp.dot(one_hot, halves, preferred_element_type=jnp.float32)
    west, east, south, north, fold = [value[:, :LANES] + value[:, LANES:] for value in picked]
    lane = lane_of(rows)
    along_x = (part >= X_PART) | ((part < 8) & (lane >= SPARE) & (lane < SPARE + PIECE))
    x_side = jnp.where(lane % 2 == 0, west, east)
    y_side = jnp.where(lane < 64, north + rot(fold, 64), south)
    out_ref[...] = jnp.where(along_x, x_side, y_side)


def bulk_kernel(first, my_ref, tracer_ref, velocity_ref, depth_ref, kappa_ref, code_ref, after_ref,
                base_ref, edge_ref, y_ref, x_ref, v_ref, d_ref, k_ref, d8_ref, k8_ref, w_ref, z_ref, x_sems, v_sems, y_sems, d_sems):
    del after_ref
    count = depth_ref.shape[0]
    pairs = edge_ref.shape[1] // 8
    x_copies = pair_copies(tracer_ref, x_ref, x_sems, first, pairs)
    v_copies = pair_copies(velocity_ref, v_ref, v_sems, first, pairs)
    d_copy = pltpu.make_async_copy(depth_ref, d_ref, d_sems.at[0])
    k_copy = pltpu.make_async_copy(kappa_ref, k_ref, d_sems.at[1])
    d_copy.start()
    k_copy.start()
    for pair in range(pairs):
        v_copies[pair].start()
        x_copies[pair].start()
    lane = lane_of(8)
    row = lax.broadcasted_iota(jnp.int32, (8, LANES), 0)
    x_row, even, place = row % 4 < 2, row % 2 == 0, row % 4
    level = (row % 2).astype(jnp.float32)
    zero = jnp.zeros((8, LANES), jnp.float32)

    def all_rows(value, chosen):
        result = value
        for at in range(4):
            if at != chosen:
                result = jnp.where(place == at, sublanes(value, at - chosen), result)
        return result

    def wet_of(depth):
        return jnp.clip(depth - level, 0.0, 1.0)

    for copy, source, target in ((d_copy, d_ref, d8_ref), (k_copy, k_ref, k8_ref)):
        copy.wait()
        for pair in range(pairs):
            slot = 2 * (first + pair)
            for start in range(0, CELLS, LANES):
                columns = slice(start, min(start + LANES, CELLS))
                shape = (8, columns.stop - start)
                top, low = [jnp.broadcast_to(source[slot + at : slot + at + 1, columns], shape) for at in range(2)]
                target[8 * pair : 8 * pair + 8, columns] = jnp.where(row[:, : shape[1]] < 4, top, low)

    def one_pair(pair):
        slot = 2 * (first + pair)
        rows = pl.ds(pl.multiple_of(8 * pair, 8), 8)
        for source, target, sems in ((velocity_ref, v_ref, v_sems), (tracer_ref, x_ref, x_sems)):
            pltpu.make_async_copy(
                source.at[pl.ds(0, 2)], target.at[rows].reshape(2, 4, CELLS), sems.at[pair]).wait()

        codes = [code_ref[pl.ds(my_ref[0] * count + slot + at, 1), :] for at in range(2)]

        def flag(column):
            pieces = [jnp.broadcast_to(code[:, column : column + 1], (8, LANES)) for code in codes]
            return jnp.where(row < 4, pieces[0], pieces[1]) >= 0

        live, folded = flag(5), flag(4)
        state, velocity = once(tile_getter(x_ref, rows, 8)), once(tile_getter(v_ref, rows, 8))
        depth, kappa = once(tile_getter(d8_ref, rows, 8)), once(tile_getter(k8_ref, rows, 8))
        wet = once(lambda tile: wet_of(depth(tile)))

        @once
        def ratio(tile):
            other = jnp.clip(depth(tile) - (1.0 - level), 0.0, 1.0)
            coupling = kappa(tile) * (wet(tile) * other)
            return coupling / (1.0 + 2.0 * coupling)

        next_vel = [shifted(velocity, 1), shifted(velocity, IB)]
        next_wet = [shifted(wet, 1), shifted(wet, IB)]

        @once
        def face(tile):
            rims = [at - tile * LANES for at in range(IB - 1, CELLS, IB) if at // LANES == tile]
            rim = functools.reduce(jnp.logical_or, [lane == at for at in rims]) if rims else None
            across = next_wet[0](tile) if rim is None else jnp.where(rim, 0.0, next_wet[0](tile))
            speed = velocity(tile) + jnp.where(x_row, next_vel[0](tile), next_vel[1](tile))
            value = SCALE * speed * (wet(tile) * jnp.where(x_row, across, next_wet[1](tile)))
            w_ref[:, tile * LANES : (tile + 1) * LANES] = value
            return value

        face_x = once(lambda tile: jnp.where(x_row, face(tile), sublanes(face(tile), 2)))
        face_y = once(lambda tile: jnp.where(x_row, sublanes(face(tile), -2), face(tile)))
        five = once(lambda tile: 5.0 * state(tile))
        two = once(lambda tile: 2.0 * state(tile))

        def divergence(speed, distance):
            before, after = shifted(state, -distance), shifted(state, distance)
            lower = once(lambda tile: five(tile) - before(tile) + 2.0 * after(tile))
            upper = shifted(once(lambda tile: five(tile) - after(tile)), distance)

            @once
            def flux(tile):
                value = jnp.maximum(speed(tile), 0.0) * lower(tile)
                return value + jnp.minimum(speed(tile), 0.0) * (two(tile) + upper(tile))

            back = shifted(flux, -distance)
            for stage in (after, before, lower, upper, flux, back):
                for tile in range(TILES):
                    stage(tile)
            return once(lambda tile: flux(tile) - back(tile))

        for stage in (depth, wet, ratio, *next_vel, *next_wet, face):
            for tile in range(TILES):
                stage(tile)
        change_x, change_y = divergence(face_x, 1), divergence(face_y, IB)
        for tile in range(TILES):
            explicit = state(tile) - wet(tile) * (change_x(tile) + change_y(tile))
            other = jnp.where(even, sublanes(explicit, -1), sublanes(explicit, 1))
            value = jnp.where(live, explicit + ratio(tile) * (other - explicit), zero)
            stop = min((tile + 1) * LANES, CELLS)
            y_ref[rows, tile * LANES : stop] = value[:, : stop - tile * LANES]
            mixed = jnp.where(x_row, face(tile), jnp.where(even, ratio(tile), depth(tile)))
            z_ref[:, tile * LANES : (tile + 1) * LANES] = mixed

        pltpu.make_async_copy(
            y_ref.at[rows].reshape(2, 4, CELLS), base_ref.at[pl.ds(slot, 2)], y_sems.at[pair]).start()
        get_w, get_z = [lambda tile, ref=ref: ref[:, tile * LANES : (tile + 1) * LANES] for ref in (w_ref, z_ref)]
        groups = gap_groups(get_z, -2, 4, 8)
        east = lane % 2 == 0
        near, far = across_pair(state)
        normal = gap_groups(velocity, -1, 2, 8)[0]
        normal = jnp.where(x_row, normal, sublanes(normal, 2))
        rim_speed = lane_pick(groups, 4 * (lane // 2) + 2 * (lane % 2))
        rim_speed = jnp.where(x_row, rim_speed, sublanes(rim_speed, 2))
        sides = [(
            near, far, jnp.where(east, -normal, normal), jnp.where(east, -rim_speed, rim_speed),
            lane_pick(groups, 4 * (lane // 2) + 1 + lane % 2), lane_pick(groups, 4 * (lane // 2) + 3 * (lane % 2)),
        )]
        for outer, inner, edge, sign in ((0, IB, 0, 1.0), (CELLS - IB, CELLS - 2 * IB, CELLS - 2 * IB, -1.0)):
            normal, rim_speed = window(velocity, outer, 8), window(get_w, edge, 8)
            normal = sign * jnp.where(x_row, sublanes(normal, -2), normal)
            rim_speed = sign * jnp.where(x_row, sublanes(rim_speed, -2), rim_speed)
            sides.append((window(state, outer, 8), window(state, inner, 8), normal, rim_speed,
                          window(get_z, outer, 8), window(get_z, inner, 8)))
        for side, (near, far, normal, rim_speed, outer, inner) in enumerate(sides):
            values = (near, far, normal, jnp.where(live, jnp.maximum(rim_speed, 0.0), zero), wet_of(all_rows(outer, 3)),
                      wet_of(all_rows(inner, 3)), all_rows(outer, 2), all_rows(inner, 2))
            for index, value in enumerate(values):
                edge_ref[OWN * side + index, rows, :] = value
        edge_ref[OWN * SIDES, rows, :] = jnp.where(folded, 1.0, zero)

    pl.loop(0, pairs)(one_pair)
    for pair in range(pairs):
        slots = pl.ds(2 * (first + pair), 2)
        rows = y_ref.at[pl.ds(8 * pair, 8)].reshape(2, 4, CELLS)
        pltpu.make_async_copy(rows, base_ref.at[slots], y_sems.at[pair]).wait()


def finish_kernel(halo_ref, edge_a_ref, edge_b_ref, base_ref, out_ref,
                  y_ref, own_ref, raw_ref, delta_ref, own_sems, in_sems, out_sems):
    count = out_ref.shape[0]
    pairs = count // 2
    rows = 4 * count
    split = edge_a_ref.shape[1]
    own_copies = [
        pltpu.make_async_copy(edge_a_ref, own_ref.at[:, pl.ds(0, split)], own_sems.at[0]),
        pltpu.make_async_copy(edge_b_ref, own_ref.at[:, pl.ds(split, rows - split)], own_sems.at[1]),
    ]
    in_copies = pair_copies(base_ref, y_ref, in_sems, 0, pairs)
    for copy in own_copies + in_copies:
        copy.start()
    lane = lane_of(rows)
    level = (lax.broadcasted_iota(jnp.int32, (rows, LANES), 0) % 2).astype(jnp.float32)

    def part(index):
        return halo_ref[index * count : (index + 1) * count, :]

    def assembled(index, parts):
        for chan, value in enumerate(parts):
            raw_ref[index, pl.ds(chan, count, stride=4), :] = value
        return raw_ref[index]

    mirror = jnp.where(lane < IB, IB - 1 - lane, lane)
    slot_lane = lane_of(count)
    depth_x = rot(part(0), -SPARE)
    for index in range(1, 8):
        depth_x = jnp.where(slot_lane >= PIECE * index, rot(part(index), PIECE * index - SPARE), depth_x)
    x_raw = [[part(X_PART + chan) for chan in range(4)], [part(X_PART + 4 + chan) for chan in range(4)],
             [part(X_PART + 8 + chan % 2) for chan in range(4)], [depth_x] * 4]
    y_values = [list(range(4)), list(range(4, 8)), [8, 9, 8, 9], [10] * 4]
    x_halo, south_halo, north_raw = [], [], []
    for kind in range(4):
        raw = assembled(3 * kind, x_raw[kind])
        x_halo.append(jnp.where(lane % 2 == 0, rot(raw, 1), rot(raw, -1)))
        first, second = [assembled(3 * kind + 1 + half, [part(2 * value + half) for value in y_values[kind]])
                         for half in range(2)]
        south_halo.append(jnp.where(lane < HALF, rot(first, 64), rot(second, 64 + HALF)))
        north_raw.append(jnp.where(lane < HALF, first, rot(second, HALF)))
    for copy in own_copies:
        copy.wait()
    folded = own_ref[OWN * SIDES] > 0.0
    north_halo = []
    for kind, raw in enumerate(north_raw):
        turned = lane_take(raw, mirror)
        north_halo.append(jnp.where(folded, -turned if kind == 2 else turned, raw))

    for side, (out_near, out_far, out_normal, out_depth) in enumerate((x_halo, south_halo, north_halo)):
        near, far, normal, rim_speed, wet, inner_wet, ratio, inner_ratio = [
            own_ref[OWN * side + index] for index in range(OWN)]
        if side == 0:
            out_normal = jnp.where(lane % 2 == 0, -out_normal, out_normal)
            beyond = out_near - jnp.where(lane % 2 == 0, rot(near, -1), rot(near, 1))
        else:
            out_normal = -out_normal if side == 2 else out_normal
            beyond = out_near
        speed = SCALE * (normal + out_normal) * (wet * jnp.clip(out_depth - level, 0.0, 1.0))
        flux = jnp.maximum(speed, 0.0) * (5.0 * out_near + 2.0 * near - out_far)
        flux += jnp.minimum(speed, 0.0) * (2.0 * out_near + 5.0 * near - far)
        inner_flux = rim_speed * beyond
        for place, (change, share) in enumerate(((wet * (flux + inner_flux), ratio),
                                                 (-inner_wet * inner_flux, inner_ratio))):
            other = jnp.where(level == 0.0, pltpu.roll(change, rows - 1, 0), pltpu.roll(change, 1, 0))
            delta_ref[2 * side + place] = change + share * (other - change)

    lane = lane_of(8)
    out_copies = []
    for pair in range(pairs):
        mine = pl.ds(8 * pair, 8)
        in_copies[pair].wait()
        near, deep, south, south_in, north, north_in = [delta_ref[index, mine, :] for index in range(2 * SIDES)]
        groups = []
        for at in range(2):
            index = 2 * (lane // 4) + (lane % 4) // 2 + 64 * at
            outer, inner = lane_take(near, index), lane_take(deep, index)
            groups.append(jnp.where((lane % 4 == 1) | (lane % 4 == 2), outer, inner))
        placed = [(groups[gap // 32], 4 * (gap % 32), IB * gap - 2, 4) for gap in range(GAPS)]
        placed += [(south, 0, 0, IB), (south_in, 0, IB, IB)]
        placed += [(north, 0, CELLS - IB, IB), (north_in, 0, CELLS - 2 * IB, IB)]
        for tile in range(TILES):
            at, stop = tile * LANES, min((tile + 1) * LANES, CELLS)
            change = jnp.zeros((8, LANES), jnp.float32)
            for source, origin, start, wide in placed:
                low, high = max(start, at, 0), min(start + wide, stop)
                if low < high:
                    inside = (lane >= low - at) & (lane < high - at)
                    change += jnp.where(inside, rot(source, start - at - origin), 0.0)
            y_ref[mine, at:stop] = y_ref[mine, at:stop] + change[:, : stop - at]
        copy = pltpu.make_async_copy(
            y_ref.at[mine].reshape(2, 4, CELLS), out_ref.at[pl.ds(2 * pair, 2)], out_sems.at[pair])
        copy.start()
        out_copies.append(copy)
    for copy in out_copies:
        copy.wait()


def route_codes(block_owner, neighbours, fold_partner, slot_total):
    block_count = block_owner.shape[0]
    hits = block_owner[None, :] == jnp.arange(slot_total, dtype=jnp.int32)[:, None]
    links = jnp.concatenate([neighbours, fold_partner[:, None]], axis=1)
    linked = links[:, :, None] == jnp.arange(block_count, dtype=jnp.int32)[None, None, :]
    link_slots = jnp.max(jnp.where(linked, block_owner[None, None, :], -1), axis=2)
    link_slots = jnp.concatenate([link_slots, block_owner[:, None]], axis=1)
    return jnp.max(jnp.where(hits[:, :, None], link_slots[None], -1), axis=1)


def per_device(tracers, velocity, kappa, kmt, block_owner, neighbours, fold_partner):
    slot_count, chans = tracers.shape[:2]
    sub_count = lax.axis_size("sub")
    device_count = lax.axis_size("blk") * sub_count
    if device_count % PARTS or chans != 4 or slot_count % 2 or slot_count < 2 * FIRST_PAIRS + 2:
        raise ValueError("unsupported sizes")
    my_index = (lax.axis_index("blk") * sub_count + lax.axis_index("sub")).astype(jnp.int32).reshape(1)
    axes = ("blk", "sub")
    pairs = slot_count // 2
    slot_total = device_count * slot_count
    state_rows = 4 * slot_count
    f32 = jnp.float32
    in_hbm = pl.BlockSpec(memory_space=pltpu.HBM)
    anywhere = pl.BlockSpec(memory_space=pl.ANY)
    in_vmem = pl.BlockSpec(memory_space=pltpu.VMEM)
    in_smem = pl.BlockSpec(memory_space=pltpu.SMEM)
    dma = pltpu.SemaphoreType.DMA
    limit = pltpu.CompilerParams(vmem_limit_bytes=32 * 1024 * 1024)

    def exchanged(pieces):
        pieces = pieces.reshape(device_count, slot_count, 1, LANES)
        return lax.all_to_all(pieces, axes, 0, 0, tiled=True).reshape(slot_total, LANES)

    pack = pl.pallas_call(
        pack_kernel,
        out_shape=jax.ShapeDtypeStruct((slot_total, LANES), f32),
        in_specs=[in_hbm, in_hbm, in_hbm],
        out_specs=in_vmem,
        scratch_shapes=[
            pltpu.VMEM((state_rows, CELLS), f32),
            pltpu.VMEM((state_rows, CELLS), f32),
            pltpu.VMEM((slot_count, CELLS), f32),
            pltpu.VMEM((9, state_rows, LANES), f32),
            dma((pairs,)),
            dma((pairs,)),
            dma,
        ],
        cost_estimate=pl.CostEstimate(flops=4_000_000, bytes_accessed=2_400_000, transcendentals=0),
    )(tracers, velocity, kmt)
    held = exchanged(pack)
    codes = route_codes(block_owner, neighbours, fold_partner, slot_total)

    def bulk(first, some, after, base):
        kernel = functools.partial(bulk_kernel, first)
        extra = [] if base is None else [base]
        if extra:
            kernel = lambda *refs: bulk_kernel(first, *refs[:7], *refs[8:])
        return pl.pallas_call(
            kernel,
            out_shape=[
                jax.ShapeDtypeStruct(tracers.shape, f32),
                jax.ShapeDtypeStruct((OWN * SIDES + 1, 8 * some, LANES), f32),
            ],
            in_specs=[in_smem, in_hbm, in_hbm, in_hbm, in_hbm, in_vmem, anywhere] + [in_hbm] * len(extra),
            out_specs=[in_hbm, in_vmem],
            scratch_shapes=[
                pltpu.VMEM((8 * some, CELLS), f32),
                pltpu.VMEM((8 * some, CELLS), f32),
                pltpu.VMEM((8 * some, CELLS), f32),
                pltpu.VMEM((slot_count, CELLS), f32),
                pltpu.VMEM((slot_count, CELLS), f32),
                pltpu.VMEM((8 * some, CELLS), f32),
                pltpu.VMEM((8 * some, CELLS), f32),
                pltpu.VMEM((8, WIDE), f32),
                pltpu.VMEM((8, WIDE), f32),
                dma((some,)),
                dma((some,)),
                dma((some,)),
                dma((2,)),
            ],
            input_output_aliases={7: 0} if extra else {},
            cost_estimate=pl.CostEstimate(flops=4_000_000 * some, bytes_accessed=800_000 * some, transcendentals=0),
        )(my_index, tracers, velocity, kmt, kappa, codes, after, *extra)

    base, edge_a = bulk(0, FIRST_PAIRS, pack, None)

    routed_rows = PARTS * slot_count
    routed = pl.pallas_call(
        route_kernel,
        grid=(device_count // PARTS,),
        out_shape=jax.ShapeDtypeStruct((slot_total, LANES), f32),
        in_specs=[
            in_smem,
            pl.BlockSpec((routed_rows, 6), lambda step: (step, 0)),
            pl.BlockSpec((slot_total, LANES), lambda step: (0, 0)),
            anywhere,
        ],
        out_specs=pl.BlockSpec((routed_rows, LANES), lambda step: (step, 0)),
        compiler_params=limit,
    )(my_index, codes, held, edge_a)

    base, edge_b = bulk(FIRST_PAIRS, pairs - FIRST_PAIRS, routed, base)
    halo = exchanged(routed)[: PARTS * slot_count]

    return pl.pallas_call(
        finish_kernel,
        out_shape=jax.ShapeDtypeStruct(tracers.shape, f32),
        in_specs=[in_vmem, anywhere, anywhere, in_hbm],
        out_specs=in_hbm,
        scratch_shapes=[
            pltpu.VMEM((state_rows, CELLS), f32),
            pltpu.VMEM((OWN * SIDES + 1, state_rows, LANES), f32),
            pltpu.VMEM((12, state_rows, LANES), f32),
            pltpu.VMEM((2 * SIDES, state_rows, LANES), f32),
            dma((2,)),
            dma((pairs,)),
            dma((pairs,)),
        ],
        input_output_aliases={3: 0},
        compiler_params=limit,
    )(halo, edge_a, edge_b, base)


def solution(mesh):
    placed = (
        P(("blk", "sub"), None, None),
        P(("blk", "sub"), None, None),
        P(("blk", "sub"), None),
        P(("blk", "sub"), None),
        P(),
        P(),
        P(),
    )
    return jax.shard_map(
        per_device,
        mesh=mesh,
        in_specs=placed,
        out_specs=P(("blk", "sub"), None, None),
        check_vma=False,
    )
```

```python
import functools

import jax
import jax.numpy as jnp
from jax import lax
from jax.experimental import pallas as pl
from jax.experimental.pallas import tpu as pltpu
from jax.sharding import PartitionSpec as P

IB = 90
JB = 60
CELLS = IB * JB
COURANT = 0.2
LANES = 128
TILES = -(-CELLS // LANES)
WIDE = TILES * LANES
GAPS = JB + 1
HALF = IB // 2
PARTS = 32
X_PART = 22
SPARE = 48
PIECE = 16
SCALE = COURANT / 12.0
SIDES = 3
OWN = 8
FIRST_PAIRS = 2


def lane_of(rows):
    return lax.broadcasted_iota(jnp.int32, (rows, LANES), 1)


def rot(value, shift):
    shift = shift % LANES
    return value if shift == 0 else pltpu.roll(value, shift, 1)


def sublanes(value, shift):
    return pltpu.roll(value, shift % 8, 0)


def once(make):
    held = {}

    def get(tile):
        if tile not in held:
            held[tile] = make(tile)
        return held[tile]

    return get


def shifted(get, distance):
    offset = distance % LANES
    turned = once(lambda tile: rot(get(tile), -offset))

    def make(tile):
        low = tile + distance // LANES
        first = turned(low) if 0 <= low < TILES else jnp.zeros((8, LANES), jnp.float32)
        second = turned(low + 1) if 0 <= low + 1 < TILES else jnp.zeros((8, LANES), jnp.float32)
        return jnp.where(lane_of(8) < LANES - offset, first, second)

    return once(make)


def window(get, start, rows):
    tile, offset = start // LANES, start % LANES
    head = rot(get(tile), -offset)
    if offset == 0 or tile + 1 >= TILES:
        return head
    return jnp.where(lane_of(rows) < LANES - offset, head, rot(get(tile + 1), -offset))


def gap_groups(get, first, wide, rows):
    lane = lane_of(rows)
    held = LANES // wide
    result = []
    for at in range(0, GAPS, held):
        value = jnp.zeros((rows, LANES), jnp.float32)
        for gap in range(at, min(at + held, GAPS)):
            start = IB * gap + first
            place = (gap - at) * wide
            for tile in range(max(start, 0) // LANES, min(start + wide - 1, CELLS - 1) // LANES + 1):
                low = max(start, tile * LANES, 0)
                value = jnp.where(lane >= place + low - start, rot(get(tile), place - start + tile * LANES), value)
        result.append(value)
    return result


def lane_take(value, index):
    return jnp.take_along_axis(value, index, axis=1, mode="promise_in_bounds")


def lane_pick(pair, index):
    return jnp.where(index < LANES, lane_take(pair[0], index % LANES), lane_take(pair[1], index % LANES))


def tile_getter(ref, rows, count):
    def get(tile):
        if tile + 1 < TILES:
            return ref[rows, tile * LANES : (tile + 1) * LANES]
        rest = jnp.zeros((count, WIDE - CELLS), jnp.float32)
        return jnp.concatenate([ref[rows, tile * LANES : CELLS], rest], axis=1)

    return get


def across_pair(get):
    lane = lane_of(8)
    groups = gap_groups(get, -2, 4, 8)
    return lane_pick(groups, 4 * (lane // 2) + 1 + lane % 2), lane_pick(groups, 4 * (lane // 2) + 3 * (lane % 2))


def joined(south, north, half, rows):
    if half == 0:
        return jnp.where(lane_of(rows) < 64, south, rot(north, 64))
    return jnp.where(lane_of(rows) < 64, rot(south, -HALF), rot(north, 64 - HALF))


def pair_copies(source, target, sems, first, pairs):
    copies = []
    for pair in range(pairs):
        into = target.at[pl.ds(8 * pair, 8)].reshape(2, 4, CELLS)
        copies.append(pltpu.make_async_copy(source.at[pl.ds(2 * (first + pair), 2)], into, sems.at[pair]))
    return copies


def pack_kernel(tracer_ref, velocity_ref, depth_ref, out_ref, x_ref, v_ref, d_ref, strip_ref, x_sems, v_sems, d_sem):
    count = depth_ref.shape[0]
    pairs = count // 2
    x_copies = pair_copies(tracer_ref, x_ref, x_sems, 0, pairs)
    v_copies = pair_copies(velocity_ref, v_ref, v_sems, 0, pairs)
    d_copy = pltpu.make_async_copy(depth_ref, d_ref, d_sem)
    for pair in range(pairs):
        x_copies[pair].start()
        v_copies[pair].start()
    d_copy.start()
    for pair in range(pairs):
        rows = pl.ds(8 * pair, 8)
        x_copies[pair].wait()
        get_x = tile_getter(x_ref, rows, 8)
        near, far = across_pair(get_x)
        south = [window(get_x, 0, 8), window(get_x, IB, 8)]
        north = [window(get_x, CELLS - IB, 8), window(get_x, CELLS - 2 * IB, 8)]
        v_copies[pair].wait()
        get_v = tile_getter(v_ref, rows, 8)
        v_south, v_north = window(get_v, 0, 8), window(get_v, CELLS - IB, 8)
        strips = [joined(south[0], north[0], half, 8) for half in range(2)]
        strips += [joined(south[1], north[1], half, 8) for half in range(2)]
        strips += [joined(v_south, v_north, half, 8) for half in range(2)]
        strips += [near, far, gap_groups(get_v, -1, 2, 8)[0]]
        for index, strip in enumerate(strips):
            strip_ref[index, rows, :] = strip

    d_copy.wait()
    if out_ref.shape[0] > PARTS * count:
        rest = out_ref.shape[0] - PARTS * count
        out_ref[PARTS * count :, :] = jnp.zeros((rest, LANES), jnp.float32)
    slot_lane = lane_of(count)
    get_d = tile_getter(d_ref, slice(None), count)
    d_south, d_north = window(get_d, 0, count), window(get_d, CELLS - IB, count)
    d_gaps = gap_groups(get_d, -1, 2, count)[0]
    spare = (slot_lane >= SPARE) & (slot_lane < SPARE + PIECE)

    def put(part, value):
        out_ref[part * count : (part + 1) * count, :] = value

    for chan in range(4):
        rows = pl.ds(chan, count, stride=4)
        for half in range(2):
            for deep in range(2):
                part = 2 * (4 * deep + chan) + half
                value = strip_ref[2 * deep + half, rows, :]
                if part < 8:
                    value = jnp.where(spare, rot(d_gaps, SPARE - PIECE * part), value)
                put(part, value)
            if chan >= 2:
                put(2 * (8 + chan - 2) + half, strip_ref[4 + half, rows, :])
        put(X_PART + chan, strip_ref[6, rows, :])
        put(X_PART + 4 + chan, strip_ref[7, rows, :])
        if chan < 2:
            put(X_PART + 8 + chan, strip_ref[8, rows, :])
    for half in range(2):
        put(20 + half, joined(d_south, d_north, half, count))


def route_kernel(part_ref, code_ref, held_ref, out_ref):
    total = held_ref.shape[0]
    rows = out_ref.shape[0]
    part = part_ref[0]
    picked = [jnp.zeros((rows, 2 * LANES), jnp.float32) for _ in range(5)]
    for start in range(0, total, rows):
        held = held_ref[start : start + rows, :]
        high = held.astype(jnp.bfloat16)
        low = (held - high.astype(jnp.float32)).astype(jnp.bfloat16)
        halves = jnp.concatenate([high, low], axis=1)
        source = lax.broadcasted_iota(jnp.int32, (rows, rows), 1) + start
        for side in range(5):
            one_hot = jnp.where(code_ref[:, side : side + 1] == source, 1.0, 0.0).astype(jnp.bfloat16)
            picked[side] += jnp.dot(one_hot, halves, preferred_element_type=jnp.float32)
    west, east, south, north, fold = [value[:, :LANES] + value[:, LANES:] for value in picked]
    lane = lane_of(rows)
    along_x = (part >= X_PART) | ((part < 8) & (lane >= SPARE) & (lane < SPARE + PIECE))
    x_side = jnp.where(lane % 2 == 0, west, east)
    y_side = jnp.where(lane < 64, north + rot(fold, 64), south)
    out_ref[...] = jnp.where(along_x, x_side, y_side)


def bulk_kernel(first, my_ref, tracer_ref, velocity_ref, depth_ref, kappa_ref, code_ref, after_ref,
                base_ref, edge_ref, part_ref, y_ref, x_ref, v_ref, d_ref, k_ref, d8_ref, k8_ref, w_ref, z_ref, x_sems, v_sems, y_sems, d_sems):
    del after_ref
    part_ref[0] = my_ref[0]
    count = depth_ref.shape[0]
    pairs = edge_ref.shape[1] // 8
    x_copies = pair_copies(tracer_ref, x_ref, x_sems, first, pairs)
    v_copies = pair_copies(velocity_ref, v_ref, v_sems, first, pairs)
    d_copy = pltpu.make_async_copy(depth_ref, d_ref, d_sems.at[0])
    k_copy = pltpu.make_async_copy(kappa_ref, k_ref, d_sems.at[1])
    d_copy.start()
    k_copy.start()
    for pair in range(pairs):
        v_copies[pair].start()
        x_copies[pair].start()
    lane = lane_of(8)
    row = lax.broadcasted_iota(jnp.int32, (8, LANES), 0)
    x_row, even, place = row % 4 < 2, row % 2 == 0, row % 4
    level = (row % 2).astype(jnp.float32)
    zero = jnp.zeros((8, LANES), jnp.float32)

    def all_rows(value, chosen):
        result = value
        for at in range(4):
            if at != chosen:
                result = jnp.where(place == at, sublanes(value, at - chosen), result)
        return result

    def wet_of(depth):
        return jnp.clip(depth - level, 0.0, 1.0)

    for copy, source, target in ((d_copy, d_ref, d8_ref), (k_copy, k_ref, k8_ref)):
        copy.wait()
        for pair in range(pairs):
            slot = 2 * (first + pair)
            for start in range(0, CELLS, LANES):
                columns = slice(start, min(start + LANES, CELLS))
                shape = (8, columns.stop - start)
                top, low = [jnp.broadcast_to(source[slot + at : slot + at + 1, columns], shape) for at in range(2)]
                target[8 * pair : 8 * pair + 8, columns] = jnp.where(row[:, : shape[1]] < 4, top, low)

    def one_pair(pair):
        slot = 2 * (first + pair)
        rows = pl.ds(pl.multiple_of(8 * pair, 8), 8)
        for source, target, sems in ((velocity_ref, v_ref, v_sems), (tracer_ref, x_ref, x_sems)):
            pltpu.make_async_copy(
                source.at[pl.ds(0, 2)], target.at[rows].reshape(2, 4, CELLS), sems.at[pair]).wait()

        codes = [code_ref[pl.ds(my_ref[0] * count + slot + at, 1), :] for at in range(2)]

        def flag(column):
            pieces = [jnp.broadcast_to(code[:, column : column + 1], (8, LANES)) for code in codes]
            return jnp.where(row < 4, pieces[0], pieces[1]) >= 0

        live, folded = flag(5), flag(4)
        state, velocity = once(tile_getter(x_ref, rows, 8)), once(tile_getter(v_ref, rows, 8))
        depth, kappa = once(tile_getter(d8_ref, rows, 8)), once(tile_getter(k8_ref, rows, 8))
        wet = once(lambda tile: wet_of(depth(tile)))

        @once
        def ratio(tile):
            other = jnp.clip(depth(tile) - (1.0 - level), 0.0, 1.0)
            coupling = kappa(tile) * (wet(tile) * other)
            return coupling / (1.0 + 2.0 * coupling)

        next_vel = [shifted(velocity, 1), shifted(velocity, IB)]
        next_wet = [shifted(wet, 1), shifted(wet, IB)]

        @once
        def face(tile):
            rims = [at - tile * LANES for at in range(IB - 1, CELLS, IB) if at // LANES == tile]
            rim = functools.reduce(jnp.logical_or, [lane == at for at in rims]) if rims else None
            across = next_wet[0](tile) if rim is None else jnp.where(rim, 0.0, next_wet[0](tile))
            speed = velocity(tile) + jnp.where(x_row, next_vel[0](tile), next_vel[1](tile))
            value = SCALE * speed * (wet(tile) * jnp.where(x_row, across, next_wet[1](tile)))
            w_ref[:, tile * LANES : (tile + 1) * LANES] = value
            return value

        face_x = once(lambda tile: jnp.where(x_row, face(tile), sublanes(face(tile), 2)))
        face_y = once(lambda tile: jnp.where(x_row, sublanes(face(tile), -2), face(tile)))
        five = once(lambda tile: 5.0 * state(tile))
        two = once(lambda tile: 2.0 * state(tile))

        def divergence(speed, distance):
            before, after = shifted(state, -distance), shifted(state, distance)
            lower = once(lambda tile: five(tile) - before(tile) + 2.0 * after(tile))
            upper = shifted(once(lambda tile: five(tile) - after(tile)), distance)

            @once
            def flux(tile):
                value = jnp.maximum(speed(tile), 0.0) * lower(tile)
                return value + jnp.minimum(speed(tile), 0.0) * (two(tile) + upper(tile))

            back = shifted(flux, -distance)
            for stage in (after, before, lower, upper, flux, back):
                for tile in range(TILES):
                    stage(tile)
            return once(lambda tile: flux(tile) - back(tile))

        for stage in (depth, wet, ratio, *next_vel, *next_wet, face):
            for tile in range(TILES):
                stage(tile)
        change_x, change_y = divergence(face_x, 1), divergence(face_y, IB)
        for tile in range(TILES):
            explicit = state(tile) - wet(tile) * (change_x(tile) + change_y(tile))
            other = jnp.where(even, sublanes(explicit, -1), sublanes(explicit, 1))
            value = jnp.where(live, explicit + ratio(tile) * (other - explicit), zero)
            stop = min((tile + 1) * LANES, CELLS)
            y_ref[rows, tile * LANES : stop] = value[:, : stop - tile * LANES]
            mixed = jnp.where(x_row, face(tile), jnp.where(even, ratio(tile), depth(tile)))
            z_ref[:, tile * LANES : (tile + 1) * LANES] = mixed

        pltpu.make_async_copy(
            y_ref.at[rows].reshape(2, 4, CELLS), base_ref.at[pl.ds(slot, 2)], y_sems.at[pair]).start()
        get_w, get_z = [lambda tile, ref=ref: ref[:, tile * LANES : (tile + 1) * LANES] for ref in (w_ref, z_ref)]
        groups = gap_groups(get_z, -2, 4, 8)
        east = lane % 2 == 0
        near, far = across_pair(state)
        normal = gap_groups(velocity, -1, 2, 8)[0]
        normal = jnp.where(x_row, normal, sublanes(normal, 2))
        rim_speed = lane_pick(groups, 4 * (lane // 2) + 2 * (lane % 2))
        rim_speed = jnp.where(x_row, rim_speed, sublanes(rim_speed, 2))
        sides = [(
            near, far, jnp.where(east, -normal, normal), jnp.where(east, -rim_speed, rim_speed),
            lane_pick(groups, 4 * (lane // 2) + 1 + lane % 2), lane_pick(groups, 4 * (lane // 2) + 3 * (lane % 2)),
        )]
        for outer, inner, edge, sign in ((0, IB, 0, 1.0), (CELLS - IB, CELLS - 2 * IB, CELLS - 2 * IB, -1.0)):
            normal, rim_speed = window(velocity, outer, 8), window(get_w, edge, 8)
            normal = sign * jnp.where(x_row, sublanes(normal, -2), normal)
            rim_speed = sign * jnp.where(x_row, sublanes(rim_speed, -2), rim_speed)
            sides.append((window(state, outer, 8), window(state, inner, 8), normal, rim_speed,
                          window(get_z, outer, 8), window(get_z, inner, 8)))
        for side, (near, far, normal, rim_speed, outer, inner) in enumerate(sides):
            values = (near, far, normal, jnp.where(live, jnp.maximum(rim_speed, 0.0), zero), wet_of(all_rows(outer, 3)),
                      wet_of(all_rows(inner, 3)), all_rows(outer, 2), all_rows(inner, 2))
            for index, value in enumerate(values):
                edge_ref[OWN * side + index, rows, :] = value
        edge_ref[OWN * SIDES, rows, :] = jnp.where(folded, 1.0, zero)

    pl.loop(0, pairs)(one_pair)
    for pair in range(pairs):
        slots = pl.ds(2 * (first + pair), 2)
        rows = y_ref.at[pl.ds(8 * pair, 8)].reshape(2, 4, CELLS)
        pltpu.make_async_copy(rows, base_ref.at[slots], y_sems.at[pair]).wait()


def finish_kernel(halo_ref, edge_a_ref, edge_b_ref, base_ref, out_ref,
                  y_ref, own_ref, raw_ref, delta_ref, own_sems, in_sems, out_sems):
    count = out_ref.shape[0]
    pairs = count // 2
    rows = 4 * count
    split = edge_a_ref.shape[1]
    own_copies = [
        pltpu.make_async_copy(edge_a_ref, own_ref.at[:, pl.ds(0, split)], own_sems.at[0]),
        pltpu.make_async_copy(edge_b_ref, own_ref.at[:, pl.ds(split, rows - split)], own_sems.at[1]),
    ]
    in_copies = pair_copies(base_ref, y_ref, in_sems, 0, pairs)
    for copy in own_copies + in_copies:
        copy.start()
    lane = lane_of(rows)
    level = (lax.broadcasted_iota(jnp.int32, (rows, LANES), 0) % 2).astype(jnp.float32)

    def part(index):
        return halo_ref[index * count : (index + 1) * count, :]

    def assembled(index, parts):
        for chan, value in enumerate(parts):
            raw_ref[index, pl.ds(chan, count, stride=4), :] = value
        return raw_ref[index]

    mirror = jnp.where(lane < IB, IB - 1 - lane, lane)
    slot_lane = lane_of(count)
    depth_x = rot(part(0), -SPARE)
    for index in range(1, 8):
        depth_x = jnp.where(slot_lane >= PIECE * index, rot(part(index), PIECE * index - SPARE), depth_x)
    x_raw = [[part(X_PART + chan) for chan in range(4)], [part(X_PART + 4 + chan) for chan in range(4)],
             [part(X_PART + 8 + chan % 2) for chan in range(4)], [depth_x] * 4]
    y_values = [list(range(4)), list(range(4, 8)), [8, 9, 8, 9], [10] * 4]
    x_halo, south_halo, north_raw = [], [], []
    for kind in range(4):
        raw = assembled(3 * kind, x_raw[kind])
        x_halo.append(jnp.where(lane % 2 == 0, rot(raw, 1), rot(raw, -1)))
        first, second = [assembled(3 * kind + 1 + half, [part(2 * value + half) for value in y_values[kind]])
                         for half in range(2)]
        south_halo.append(jnp.where(lane < HALF, rot(first, 64), rot(second, 64 + HALF)))
        north_raw.append(jnp.where(lane < HALF, first, rot(second, HALF)))
    for copy in own_copies:
        copy.wait()
    folded = own_ref[OWN * SIDES] > 0.0
    north_halo = []
    for kind, raw in enumerate(north_raw):
        turned = lane_take(raw, mirror)
        north_halo.append(jnp.where(folded, -turned if kind == 2 else turned, raw))

    for side, (out_near, out_far, out_normal, out_depth) in enumerate((x_halo, south_halo, north_halo)):
        near, far, normal, rim_speed, wet, inner_wet, ratio, inner_ratio = [
            own_ref[OWN * side + index] for index in range(OWN)]
        if side == 0:
            out_normal = jnp.where(lane % 2 == 0, -out_normal, out_normal)
            beyond = out_near - jnp.where(lane % 2 == 0, rot(near, -1), rot(near, 1))
        else:
            out_normal = -out_normal if side == 2 else out_normal
            beyond = out_near
        speed = SCALE * (normal + out_normal) * (wet * jnp.clip(out_depth - level, 0.0, 1.0))
        flux = jnp.maximum(speed, 0.0) * (5.0 * out_near + 2.0 * near - out_far)
        flux += jnp.minimum(speed, 0.0) * (2.0 * out_near + 5.0 * near - far)
        inner_flux = rim_speed * beyond
        for place, (change, share) in enumerate(((wet * (flux + inner_flux), ratio),
                                                 (-inner_wet * inner_flux, inner_ratio))):
            other = jnp.where(level == 0.0, pltpu.roll(change, rows - 1, 0), pltpu.roll(change, 1, 0))
            delta_ref[2 * side + place] = change + share * (other - change)

    lane = lane_of(8)
    out_copies = []
    for pair in range(pairs):
        mine = pl.ds(8 * pair, 8)
        in_copies[pair].wait()
        near, deep, south, south_in, north, north_in = [delta_ref[index, mine, :] for index in range(2 * SIDES)]
        groups = []
        for at in range(2):
            index = 2 * (lane // 4) + (lane % 4) // 2 + 64 * at
            outer, inner = lane_take(near, index), lane_take(deep, index)
            groups.append(jnp.where((lane % 4 == 1) | (lane % 4 == 2), outer, inner))
        placed = [(groups[gap // 32], 4 * (gap % 32), IB * gap - 2, 4) for gap in range(GAPS)]
        placed += [(south, 0, 0, IB), (south_in, 0, IB, IB)]
        placed += [(north, 0, CELLS - IB, IB), (north_in, 0, CELLS - 2 * IB, IB)]
        for tile in range(TILES):
            at, stop = tile * LANES, min((tile + 1) * LANES, CELLS)
            change = jnp.zeros((8, LANES), jnp.float32)
            for source, origin, start, wide in placed:
                low, high = max(start, at, 0), min(start + wide, stop)
                if low < high:
                    inside = (lane >= low - at) & (lane < high - at)
                    change += jnp.where(inside, rot(source, start - at - origin), 0.0)
            y_ref[mine, at:stop] = y_ref[mine, at:stop] + change[:, : stop - at]
        copy = pltpu.make_async_copy(
            y_ref.at[mine].reshape(2, 4, CELLS), out_ref.at[pl.ds(2 * pair, 2)], out_sems.at[pair])
        copy.start()
        out_copies.append(copy)
    for copy in out_copies:
        copy.wait()


def route_codes(block_owner, neighbours, fold_partner, slot_total):
    block_count = block_owner.shape[0]
    hits = block_owner[None, :] == jnp.arange(slot_total, dtype=jnp.int32)[:, None]
    links = jnp.concatenate([neighbours, fold_partner[:, None]], axis=1)
    linked = links[:, :, None] == jnp.arange(block_count, dtype=jnp.int32)[None, None, :]
    link_slots = jnp.max(jnp.where(linked, block_owner[None, None, :], -1), axis=2)
    link_slots = jnp.concatenate([link_slots, block_owner[:, None]], axis=1)
    return jnp.max(jnp.where(hits[:, :, None], link_slots[None], -1), axis=1)


def per_device(tracers, velocity, kappa, kmt, block_owner, neighbours, fold_partner):
    slot_count, chans = tracers.shape[:2]
    sub_count = lax.axis_size("sub")
    device_count = lax.axis_size("blk") * sub_count
    if device_count % PARTS or chans != 4 or slot_count % 2 or slot_count < 2 * FIRST_PAIRS + 2:
        raise ValueError("unsupported sizes")
    my_index = (lax.axis_index("blk") * sub_count + lax.axis_index("sub")).astype(jnp.int32).reshape(1)
    axes = ("blk", "sub")
    pairs = slot_count // 2
    slot_total = device_count * slot_count
    state_rows = 4 * slot_count
    f32 = jnp.float32
    in_hbm = pl.BlockSpec(memory_space=pltpu.HBM)
    anywhere = pl.BlockSpec(memory_space=pl.ANY)
    in_vmem = pl.BlockSpec(memory_space=pltpu.VMEM)
    in_smem = pl.BlockSpec(memory_space=pltpu.SMEM)
    dma = pltpu.SemaphoreType.DMA
    limit = pltpu.CompilerParams(vmem_limit_bytes=32 * 1024 * 1024)

    def exchanged(pieces):
        pieces = pieces.reshape(device_count, slot_count, 1, LANES)
        return lax.all_to_all(pieces, axes, 0, 0, tiled=True).reshape(slot_total, LANES)

    pack = pl.pallas_call(
        pack_kernel,
        out_shape=jax.ShapeDtypeStruct((slot_total, LANES), f32),
        in_specs=[in_hbm, in_hbm, in_hbm],
        out_specs=in_vmem,
        scratch_shapes=[
            pltpu.VMEM((state_rows, CELLS), f32),
            pltpu.VMEM((state_rows, CELLS), f32),
            pltpu.VMEM((slot_count, CELLS), f32),
            pltpu.VMEM((9, state_rows, LANES), f32),
            dma((pairs,)),
            dma((pairs,)),
            dma,
        ],
        cost_estimate=pl.CostEstimate(flops=4_000_000, bytes_accessed=2_400_000, transcendentals=0),
    )(tracers, velocity, kmt)
    held = exchanged(pack)
    codes = route_codes(block_owner, neighbours, fold_partner, slot_total)

    def bulk(first, some, after, base):
        kernel = functools.partial(bulk_kernel, first)
        extra = [] if base is None else [base]
        if extra:
            kernel = lambda *refs: bulk_kernel(first, *refs[:7], *refs[8:])
        return pl.pallas_call(
            kernel,
            out_shape=[
                jax.ShapeDtypeStruct(tracers.shape, f32),
                jax.ShapeDtypeStruct((OWN * SIDES + 1, 8 * some, LANES), f32),
                jax.ShapeDtypeStruct((1,), jnp.int32),
            ],
            in_specs=[in_smem, in_hbm, in_hbm, in_hbm, in_hbm, in_vmem, anywhere] + [in_hbm] * len(extra),
            out_specs=[in_hbm, in_vmem, in_smem],
            scratch_shapes=[
                pltpu.VMEM((8 * some, CELLS), f32),
                pltpu.VMEM((8 * some, CELLS), f32),
                pltpu.VMEM((8 * some, CELLS), f32),
                pltpu.VMEM((slot_count, CELLS), f32),
                pltpu.VMEM((slot_count, CELLS), f32),
                pltpu.VMEM((8 * some, CELLS), f32),
                pltpu.VMEM((8 * some, CELLS), f32),
                pltpu.VMEM((8, WIDE), f32),
                pltpu.VMEM((8, WIDE), f32),
                dma((some,)),
                dma((some,)),
                dma((some,)),
                dma((2,)),
            ],
            input_output_aliases={7: 0} if extra else {},
            compiler_params=limit,
            cost_estimate=pl.CostEstimate(flops=4_000_000 * some, bytes_accessed=800_000 * some, transcendentals=0),
        )(my_index, tracers, velocity, kmt, kappa, codes, after, *extra)

    base, edge_a, part = bulk(0, FIRST_PAIRS, pack, None)

    routed_rows = PARTS * slot_count
    routed = pl.pallas_call(
        route_kernel,
        grid=(device_count // PARTS,),
        out_shape=jax.ShapeDtypeStruct((slot_total, LANES), f32),
        in_specs=[
            in_smem,
            pl.BlockSpec((routed_rows, 6), lambda step: (step, 0)),
            pl.BlockSpec((slot_total, LANES), lambda step: (0, 0)),
        ],
        out_specs=pl.BlockSpec((routed_rows, LANES), lambda step: (step, 0)),
        compiler_params=limit,
    )(part, codes, held)

    base, edge_b, _ = bulk(FIRST_PAIRS, pairs - FIRST_PAIRS, routed, base)
    halo = exchanged(routed)[: PARTS * slot_count]

    return pl.pallas_call(
        finish_kernel,
        out_shape=jax.ShapeDtypeStruct(tracers.shape, f32),
        in_specs=[in_vmem, anywhere, anywhere, in_hbm],
        out_specs=in_hbm,
        scratch_shapes=[
            pltpu.VMEM((state_rows, CELLS), f32),
            pltpu.VMEM((OWN * SIDES + 1, state_rows, LANES), f32),
            pltpu.VMEM((12, state_rows, LANES), f32),
            pltpu.VMEM((2 * SIDES, state_rows, LANES), f32),
            dma((2,)),
            dma((pairs,)),
            dma((pairs,)),
        ],
        input_output_aliases={3: 0},
        compiler_params=limit,
    )(halo, edge_a, edge_b, base)


def solution(mesh):
    placed = (
        P(("blk", "sub"), None, None),
        P(("blk", "sub"), None, None),
        P(("blk", "sub"), None),
        P(("blk", "sub"), None),
        P(),
        P(),
        P(),
    )
    return jax.shard_map(
        per_device,
        mesh=mesh,
        in_specs=placed,
        out_specs=P(("blk", "sub"), None, None),
        check_vma=False,
    )
```

```python
import functools

import jax
import jax.numpy as jnp
from jax import lax
from jax.experimental import pallas as pl
from jax.experimental.pallas import tpu as pltpu
from jax.sharding import PartitionSpec as P

IB = 90
JB = 60
CELLS = IB * JB
COURANT = 0.2
LANES = 128
TILES = -(-CELLS // LANES)
WIDE = TILES * LANES
GAPS = JB + 1
HALF = IB // 2
PARTS = 32
X_PART = 22
SPARE = 48
PIECE = 16
SCALE = COURANT / 12.0
SIDES = 3
OWN = 8
FIRST_PAIRS = 2


def lane_of(rows):
    return lax.broadcasted_iota(jnp.int32, (rows, LANES), 1)


def rot(value, shift):
    shift = shift % LANES
    return value if shift == 0 else pltpu.roll(value, shift, 1)


def sublanes(value, shift):
    return pltpu.roll(value, shift % 8, 0)


def once(make):
    held = {}

    def get(tile):
        if tile not in held:
            held[tile] = make(tile)
        return held[tile]

    return get


def shifted(get, distance):
    offset = distance % LANES
    turned = once(lambda tile: rot(get(tile), -offset))

    def make(tile):
        low = tile + distance // LANES
        first = turned(low) if 0 <= low < TILES else jnp.zeros((8, LANES), jnp.float32)
        second = turned(low + 1) if 0 <= low + 1 < TILES else jnp.zeros((8, LANES), jnp.float32)
        return jnp.where(lane_of(8) < LANES - offset, first, second)

    return once(make)


def window(get, start, rows):
    tile, offset = start // LANES, start % LANES
    head = rot(get(tile), -offset)
    if offset == 0 or tile + 1 >= TILES:
        return head
    return jnp.where(lane_of(rows) < LANES - offset, head, rot(get(tile + 1), -offset))


def gap_groups(get, first, wide, rows):
    lane = lane_of(rows)
    held = LANES // wide
    result = []
    for at in range(0, GAPS, held):
        value = jnp.zeros((rows, LANES), jnp.float32)
        for gap in range(at, min(at + held, GAPS)):
            start = IB * gap + first
            place = (gap - at) * wide
            for tile in range(max(start, 0) // LANES, min(start + wide - 1, CELLS - 1) // LANES + 1):
                low = max(start, tile * LANES, 0)
                value = jnp.where(lane >= place + low - start, rot(get(tile), place - start + tile * LANES), value)
        result.append(value)
    return result


def lane_take(value, index):
    return jnp.take_along_axis(value, index, axis=1, mode="promise_in_bounds")


def lane_pick(pair, index):
    return jnp.where(index < LANES, lane_take(pair[0], index % LANES), lane_take(pair[1], index % LANES))


def tile_getter(ref, rows, count):
    def get(tile):
        if tile + 1 < TILES:
            return ref[rows, tile * LANES : (tile + 1) * LANES]
        rest = jnp.zeros((count, WIDE - CELLS), jnp.float32)
        return jnp.concatenate([ref[rows, tile * LANES : CELLS], rest], axis=1)

    return get


def across_pair(get):
    lane = lane_of(8)
    groups = gap_groups(get, -2, 4, 8)
    return lane_pick(groups, 4 * (lane // 2) + 1 + lane % 2), lane_pick(groups, 4 * (lane // 2) + 3 * (lane % 2))


def joined(south, north, half, rows):
    if half == 0:
        return jnp.where(lane_of(rows) < 64, south, rot(north, 64))
    return jnp.where(lane_of(rows) < 64, rot(south, -HALF), rot(north, 64 - HALF))


def pair_copies(source, target, sems, first, pairs):
    copies = []
    for pair in range(pairs):
        into = target.at[pl.ds(8 * pair, 8)].reshape(2, 4, CELLS)
        copies.append(pltpu.make_async_copy(source.at[pl.ds(2 * (first + pair), 2)], into, sems.at[pair]))
    return copies


def pack_kernel(tracer_ref, velocity_ref, depth_ref, out_ref, x_ref, v_ref, d_ref, strip_ref, x_sems, v_sems, d_sem):
    count = depth_ref.shape[0]
    pairs = count // 2
    x_copies = pair_copies(tracer_ref, x_ref, x_sems, 0, pairs)
    v_copies = pair_copies(velocity_ref, v_ref, v_sems, 0, pairs)
    d_copy = pltpu.make_async_copy(depth_ref, d_ref, d_sem)
    for pair in range(pairs):
        x_copies[pair].start()
        v_copies[pair].start()
    d_copy.start()
    for pair in range(pairs):
        rows = pl.ds(8 * pair, 8)
        x_copies[pair].wait()
        get_x = tile_getter(x_ref, rows, 8)
        near, far = across_pair(get_x)
        south = [window(get_x, 0, 8), window(get_x, IB, 8)]
        north = [window(get_x, CELLS - IB, 8), window(get_x, CELLS - 2 * IB, 8)]
        v_copies[pair].wait()
        get_v = tile_getter(v_ref, rows, 8)
        v_south, v_north = window(get_v, 0, 8), window(get_v, CELLS - IB, 8)
        strips = [joined(south[0], north[0], half, 8) for half in range(2)]
        strips += [joined(south[1], north[1], half, 8) for half in range(2)]
        strips += [joined(v_south, v_north, half, 8) for half in range(2)]
        strips += [near, far, gap_groups(get_v, -1, 2, 8)[0]]
        for index, strip in enumerate(strips):
            strip_ref[index, rows, :] = strip

    d_copy.wait()
    if out_ref.shape[0] > PARTS * count:
        rest = out_ref.shape[0] - PARTS * count
        out_ref[PARTS * count :, :] = jnp.zeros((rest, LANES), jnp.float32)
    slot_lane = lane_of(count)
    get_d = tile_getter(d_ref, slice(None), count)
    d_south, d_north = window(get_d, 0, count), window(get_d, CELLS - IB, count)
    d_gaps = gap_groups(get_d, -1, 2, count)[0]
    spare = (slot_lane >= SPARE) & (slot_lane < SPARE + PIECE)

    def put(part, value):
        out_ref[part * count : (part + 1) * count, :] = value

    for chan in range(4):
        rows = pl.ds(chan, count, stride=4)
        for half in range(2):
            for deep in range(2):
                part = 2 * (4 * deep + chan) + half
                value = strip_ref[2 * deep + half, rows, :]
                if part < 8:
                    value = jnp.where(spare, rot(d_gaps, SPARE - PIECE * part), value)
                put(part, value)
            if chan >= 2:
                put(2 * (8 + chan - 2) + half, strip_ref[4 + half, rows, :])
        put(X_PART + chan, strip_ref[6, rows, :])
        put(X_PART + 4 + chan, strip_ref[7, rows, :])
        if chan < 2:
            put(X_PART + 8 + chan, strip_ref[8, rows, :])
    for half in range(2):
        put(20 + half, joined(d_south, d_north, half, count))


def route_kernel(part_ref, code_ref, held_ref, out_ref):
    total = held_ref.shape[0]
    rows = out_ref.shape[0]
    part = part_ref[0]
    picked = [jnp.zeros((rows, 2 * LANES), jnp.float32) for _ in range(5)]
    for start in range(0, total, rows):
        held = held_ref[start : start + rows, :]
        high = held.astype(jnp.bfloat16)
        low = (held - high.astype(jnp.float32)).astype(jnp.bfloat16)
        halves = jnp.concatenate([high, low], axis=1)
        source = lax.broadcasted_iota(jnp.int32, (rows, rows), 1) + start
        for side in range(5):
            one_hot = jnp.where(code_ref[:, side : side + 1] == source, 1.0, 0.0).astype(jnp.bfloat16)
            picked[side] += jnp.dot(one_hot, halves, preferred_element_type=jnp.float32)
    west, east, south, north, fold = [value[:, :LANES] + value[:, LANES:] for value in picked]
    lane = lane_of(rows)
    along_x = (part >= X_PART) | ((part < 8) & (lane >= SPARE) & (lane < SPARE + PIECE))
    x_side = jnp.where(lane % 2 == 0, west, east)
    y_side = jnp.where(lane < 64, north + rot(fold, 64), south)
    out_ref[...] = jnp.where(along_x, x_side, y_side)


def bulk_kernel(first, my_ref, tracer_ref, velocity_ref, depth_ref, kappa_ref, code_ref,
                base_ref, edge_ref, y_ref, x_ref, v_ref, d_ref, k_ref, d8_ref, k8_ref, w_ref, z_ref, x_sems, v_sems, y_sems, d_sems):
    count = depth_ref.shape[0]
    pairs = edge_ref.shape[1] // 8
    x_copies = pair_copies(tracer_ref, x_ref, x_sems, first, pairs)
    v_copies = pair_copies(velocity_ref, v_ref, v_sems, first, pairs)
    d_copy = pltpu.make_async_copy(depth_ref, d_ref, d_sems.at[0])
    k_copy = pltpu.make_async_copy(kappa_ref, k_ref, d_sems.at[1])
    d_copy.start()
    k_copy.start()
    for pair in range(pairs):
        v_copies[pair].start()
        x_copies[pair].start()
    lane = lane_of(8)
    row = lax.broadcasted_iota(jnp.int32, (8, LANES), 0)
    x_row, even, place = row % 4 < 2, row % 2 == 0, row % 4
    level = (row % 2).astype(jnp.float32)
    zero = jnp.zeros((8, LANES), jnp.float32)

    def all_rows(value, chosen):
        result = value
        for at in range(4):
            if at != chosen:
                result = jnp.where(place == at, sublanes(value, at - chosen), result)
        return result

    def wet_of(depth):
        return jnp.clip(depth - level, 0.0, 1.0)

    for copy, source, target in ((d_copy, d_ref, d8_ref), (k_copy, k_ref, k8_ref)):
        copy.wait()
        for pair in range(pairs):
            slot = 2 * (first + pair)
            for start in range(0, CELLS, LANES):
                columns = slice(start, min(start + LANES, CELLS))
                shape = (8, columns.stop - start)
                top, low = [jnp.broadcast_to(source[slot + at : slot + at + 1, columns], shape) for at in range(2)]
                target[8 * pair : 8 * pair + 8, columns] = jnp.where(row[:, : shape[1]] < 4, top, low)

    def one_pair(pair):
        slot = 2 * (first + pair)
        rows = pl.ds(pl.multiple_of(8 * pair, 8), 8)
        for source, target, sems in ((velocity_ref, v_ref, v_sems), (tracer_ref, x_ref, x_sems)):
            pltpu.make_async_copy(
                source.at[pl.ds(0, 2)], target.at[rows].reshape(2, 4, CELLS), sems.at[pair]).wait()

        codes = [code_ref[pl.ds(my_ref[0] * count + slot + at, 1), :] for at in range(2)]

        def flag(column):
            pieces = [jnp.broadcast_to(code[:, column : column + 1], (8, LANES)) for code in codes]
            return jnp.where(row < 4, pieces[0], pieces[1]) >= 0

        live, folded = flag(5), flag(4)
        state, velocity = once(tile_getter(x_ref, rows, 8)), once(tile_getter(v_ref, rows, 8))
        depth, kappa = once(tile_getter(d8_ref, rows, 8)), once(tile_getter(k8_ref, rows, 8))
        wet = once(lambda tile: wet_of(depth(tile)))

        @once
        def ratio(tile):
            other = jnp.clip(depth(tile) - (1.0 - level), 0.0, 1.0)
            coupling = kappa(tile) * (wet(tile) * other)
            return coupling / (1.0 + 2.0 * coupling)

        next_vel = [shifted(velocity, 1), shifted(velocity, IB)]
        next_wet = [shifted(wet, 1), shifted(wet, IB)]

        @once
        def face(tile):
            rims = [at - tile * LANES for at in range(IB - 1, CELLS, IB) if at // LANES == tile]
            rim = functools.reduce(jnp.logical_or, [lane == at for at in rims]) if rims else None
            across = next_wet[0](tile) if rim is None else jnp.where(rim, 0.0, next_wet[0](tile))
            speed = velocity(tile) + jnp.where(x_row, next_vel[0](tile), next_vel[1](tile))
            value = SCALE * speed * (wet(tile) * jnp.where(x_row, across, next_wet[1](tile)))
            w_ref[:, tile * LANES : (tile + 1) * LANES] = value
            return value

        face_x = once(lambda tile: jnp.where(x_row, face(tile), sublanes(face(tile), 2)))
        face_y = once(lambda tile: jnp.where(x_row, sublanes(face(tile), -2), face(tile)))
        five = once(lambda tile: 5.0 * state(tile))
        two = once(lambda tile: 2.0 * state(tile))

        def divergence(speed, distance):
            before, after = shifted(state, -distance), shifted(state, distance)
            lower = once(lambda tile: five(tile) - before(tile) + 2.0 * after(tile))
            upper = shifted(once(lambda tile: five(tile) - after(tile)), distance)

            @once
            def flux(tile):
                value = jnp.maximum(speed(tile), 0.0) * lower(tile)
                return value + jnp.minimum(speed(tile), 0.0) * (two(tile) + upper(tile))

            back = shifted(flux, -distance)
            for stage in (after, before, lower, upper, flux, back):
                for tile in range(TILES):
                    stage(tile)
            return once(lambda tile: flux(tile) - back(tile))

        for stage in (depth, wet, ratio, *next_vel, *next_wet, face):
            for tile in range(TILES):
                stage(tile)
        change_x, change_y = divergence(face_x, 1), divergence(face_y, IB)
        for tile in range(TILES):
            explicit = state(tile) - wet(tile) * (change_x(tile) + change_y(tile))
            other = jnp.where(even, sublanes(explicit, -1), sublanes(explicit, 1))
            value = jnp.where(live, explicit + ratio(tile) * (other - explicit), zero)
            stop = min((tile + 1) * LANES, CELLS)
            y_ref[rows, tile * LANES : stop] = value[:, : stop - tile * LANES]
            mixed = jnp.where(x_row, face(tile), jnp.where(even, ratio(tile), depth(tile)))
            z_ref[:, tile * LANES : (tile + 1) * LANES] = mixed

        pltpu.make_async_copy(
            y_ref.at[rows].reshape(2, 4, CELLS), base_ref.at[pl.ds(slot, 2)], y_sems.at[pair]).start()
        get_w, get_z = [lambda tile, ref=ref: ref[:, tile * LANES : (tile + 1) * LANES] for ref in (w_ref, z_ref)]
        groups = gap_groups(get_z, -2, 4, 8)
        east = lane % 2 == 0
        near, far = across_pair(state)
        normal = gap_groups(velocity, -1, 2, 8)[0]
        normal = jnp.where(x_row, normal, sublanes(normal, 2))
        rim_speed = lane_pick(groups, 4 * (lane // 2) + 2 * (lane % 2))
        rim_speed = jnp.where(x_row, rim_speed, sublanes(rim_speed, 2))
        sides = [(
            near, far, jnp.where(east, -normal, normal), jnp.where(east, -rim_speed, rim_speed),
            lane_pick(groups, 4 * (lane // 2) + 1 + lane % 2), lane_pick(groups, 4 * (lane // 2) + 3 * (lane % 2)),
        )]
        for outer, inner, edge, sign in ((0, IB, 0, 1.0), (CELLS - IB, CELLS - 2 * IB, CELLS - 2 * IB, -1.0)):
            normal, rim_speed = window(velocity, outer, 8), window(get_w, edge, 8)
            normal = sign * jnp.where(x_row, sublanes(normal, -2), normal)
            rim_speed = sign * jnp.where(x_row, sublanes(rim_speed, -2), rim_speed)
            sides.append((window(state, outer, 8), window(state, inner, 8), normal, rim_speed,
                          window(get_z, outer, 8), window(get_z, inner, 8)))
        for side, (near, far, normal, rim_speed, outer, inner) in enumerate(sides):
            values = (near, far, normal, jnp.where(live, jnp.maximum(rim_speed, 0.0), zero), wet_of(all_rows(outer, 3)),
                      wet_of(all_rows(inner, 3)), all_rows(outer, 2), all_rows(inner, 2))
            for index, value in enumerate(values):
                edge_ref[OWN * side + index, rows, :] = value
        edge_ref[OWN * SIDES, rows, :] = jnp.where(folded, 1.0, zero)

    pl.loop(0, pairs)(one_pair)
    for pair in range(pairs):
        slots = pl.ds(2 * (first + pair), 2)
        rows = y_ref.at[pl.ds(8 * pair, 8)].reshape(2, 4, CELLS)
        pltpu.make_async_copy(rows, base_ref.at[slots], y_sems.at[pair]).wait()


def finish_kernel(halo_ref, edge_a_ref, edge_b_ref, base_ref, out_ref,
                  y_ref, own_ref, raw_ref, delta_ref, own_sems, in_sems, out_sems):
    count = out_ref.shape[0]
    pairs = count // 2
    rows = 4 * count
    split = edge_a_ref.shape[1]
    own_copies = [
        pltpu.make_async_copy(edge_a_ref, own_ref.at[:, pl.ds(0, split)], own_sems.at[0]),
        pltpu.make_async_copy(edge_b_ref, own_ref.at[:, pl.ds(split, rows - split)], own_sems.at[1]),
    ]
    in_copies = pair_copies(base_ref, y_ref, in_sems, 0, pairs)
    for copy in own_copies + in_copies:
        copy.start()
    lane = lane_of(rows)
    level = (lax.broadcasted_iota(jnp.int32, (rows, LANES), 0) % 2).astype(jnp.float32)

    def part(index):
        return halo_ref[index * count : (index + 1) * count, :]

    def assembled(index, parts):
        for chan, value in enumerate(parts):
            raw_ref[index, pl.ds(chan, count, stride=4), :] = value
        return raw_ref[index]

    mirror = jnp.where(lane < IB, IB - 1 - lane, lane)
    slot_lane = lane_of(count)
    depth_x = rot(part(0), -SPARE)
    for index in range(1, 8):
        depth_x = jnp.where(slot_lane >= PIECE * index, rot(part(index), PIECE * index - SPARE), depth_x)
    x_raw = [[part(X_PART + chan) for chan in range(4)], [part(X_PART + 4 + chan) for chan in range(4)],
             [part(X_PART + 8 + chan % 2) for chan in range(4)], [depth_x] * 4]
    y_values = [list(range(4)), list(range(4, 8)), [8, 9, 8, 9], [10] * 4]
    x_halo, south_halo, north_raw = [], [], []
    for kind in range(4):
        raw = assembled(3 * kind, x_raw[kind])
        x_halo.append(jnp.where(lane % 2 == 0, rot(raw, 1), rot(raw, -1)))
        first, second = [assembled(3 * kind + 1 + half, [part(2 * value + half) for value in y_values[kind]])
                         for half in range(2)]
        south_halo.append(jnp.where(lane < HALF, rot(first, 64), rot(second, 64 + HALF)))
        north_raw.append(jnp.where(lane < HALF, first, rot(second, HALF)))
    for copy in own_copies:
        copy.wait()
    folded = own_ref[OWN * SIDES] > 0.0
    north_halo = []
    for kind, raw in enumerate(north_raw):
        turned = lane_take(raw, mirror)
        north_halo.append(jnp.where(folded, -turned if kind == 2 else turned, raw))

    for side, (out_near, out_far, out_normal, out_depth) in enumerate((x_halo, south_halo, north_halo)):
        near, far, normal, rim_speed, wet, inner_wet, ratio, inner_ratio = [
            own_ref[OWN * side + index] for index in range(OWN)]
        if side == 0:
            out_normal = jnp.where(lane % 2 == 0, -out_normal, out_normal)
            beyond = out_near - jnp.where(lane % 2 == 0, rot(near, -1), rot(near, 1))
        else:
            out_normal = -out_normal if side == 2 else out_normal
            beyond = out_near
        speed = SCALE * (normal + out_normal) * (wet * jnp.clip(out_depth - level, 0.0, 1.0))
        flux = jnp.maximum(speed, 0.0) * (5.0 * out_near + 2.0 * near - out_far)
        flux += jnp.minimum(speed, 0.0) * (2.0 * out_near + 5.0 * near - far)
        inner_flux = rim_speed * beyond
        for place, (change, share) in enumerate(((wet * (flux + inner_flux), ratio),
                                                 (-inner_wet * inner_flux, inner_ratio))):
            other = jnp.where(level == 0.0, pltpu.roll(change, rows - 1, 0), pltpu.roll(change, 1, 0))
            delta_ref[2 * side + place] = change + share * (other - change)

    lane = lane_of(8)
    out_copies = []
    for pair in range(pairs):
        mine = pl.ds(8 * pair, 8)
        in_copies[pair].wait()
        near, deep, south, south_in, north, north_in = [delta_ref[index, mine, :] for index in range(2 * SIDES)]
        groups = []
        for at in range(2):
            index = 2 * (lane // 4) + (lane % 4) // 2 + 64 * at
            outer, inner = lane_take(near, index), lane_take(deep, index)
            groups.append(jnp.where((lane % 4 == 1) | (lane % 4 == 2), outer, inner))
        placed = [(groups[gap // 32], 4 * (gap % 32), IB * gap - 2, 4) for gap in range(GAPS)]
        placed += [(south, 0, 0, IB), (south_in, 0, IB, IB)]
        placed += [(north, 0, CELLS - IB, IB), (north_in, 0, CELLS - 2 * IB, IB)]
        for tile in range(TILES):
            at, stop = tile * LANES, min((tile + 1) * LANES, CELLS)
            change = jnp.zeros((8, LANES), jnp.float32)
            for source, origin, start, wide in placed:
                low, high = max(start, at, 0), min(start + wide, stop)
                if low < high:
                    inside = (lane >= low - at) & (lane < high - at)
                    change += jnp.where(inside, rot(source, start - at - origin), 0.0)
            y_ref[mine, at:stop] = y_ref[mine, at:stop] + change[:, : stop - at]
        copy = pltpu.make_async_copy(
            y_ref.at[mine].reshape(2, 4, CELLS), out_ref.at[pl.ds(2 * pair, 2)], out_sems.at[pair])
        copy.start()
        out_copies.append(copy)
    for copy in out_copies:
        copy.wait()


def route_codes(block_owner, neighbours, fold_partner, slot_total):
    block_count = block_owner.shape[0]
    hits = block_owner[None, :] == jnp.arange(slot_total, dtype=jnp.int32)[:, None]
    links = jnp.concatenate([neighbours, fold_partner[:, None]], axis=1)
    linked = links[:, :, None] == jnp.arange(block_count, dtype=jnp.int32)[None, None, :]
    link_slots = jnp.max(jnp.where(linked, block_owner[None, None, :], -1), axis=2)
    link_slots = jnp.concatenate([link_slots, block_owner[:, None]], axis=1)
    return jnp.max(jnp.where(hits[:, :, None], link_slots[None], -1), axis=1)


def per_device(tracers, velocity, kappa, kmt, block_owner, neighbours, fold_partner):
    slot_count, chans = tracers.shape[:2]
    sub_count = lax.axis_size("sub")
    device_count = lax.axis_size("blk") * sub_count
    if device_count % PARTS or chans != 4 or slot_count % 2 or slot_count < 2 * FIRST_PAIRS + 2:
        raise ValueError("unsupported sizes")
    my_index = (lax.axis_index("blk") * sub_count + lax.axis_index("sub")).astype(jnp.int32).reshape(1)
    axes = ("blk", "sub")
    pairs = slot_count // 2
    slot_total = device_count * slot_count
    state_rows = 4 * slot_count
    f32 = jnp.float32
    in_hbm = pl.BlockSpec(memory_space=pltpu.HBM)
    anywhere = pl.BlockSpec(memory_space=pl.ANY)
    in_vmem = pl.BlockSpec(memory_space=pltpu.VMEM)
    in_smem = pl.BlockSpec(memory_space=pltpu.SMEM)
    dma = pltpu.SemaphoreType.DMA
    limit = pltpu.CompilerParams(vmem_limit_bytes=32 * 1024 * 1024)

    def exchanged(pieces):
        pieces = pieces.reshape(device_count, slot_count, 1, LANES)
        return lax.all_to_all(pieces, axes, 0, 0, tiled=True).reshape(slot_total, LANES)

    pack = pl.pallas_call(
        pack_kernel,
        out_shape=jax.ShapeDtypeStruct((slot_total, LANES), f32),
        in_specs=[in_hbm, in_hbm, in_hbm],
        out_specs=in_vmem,
        scratch_shapes=[
            pltpu.VMEM((state_rows, CELLS), f32),
            pltpu.VMEM((state_rows, CELLS), f32),
            pltpu.VMEM((slot_count, CELLS), f32),
            pltpu.VMEM((9, state_rows, LANES), f32),
            dma((pairs,)),
            dma((pairs,)),
            dma,
        ],
        cost_estimate=pl.CostEstimate(flops=4_000_000, bytes_accessed=2_400_000, transcendentals=0),
    )(tracers, velocity, kmt)
    held = exchanged(pack)
    codes = route_codes(block_owner, neighbours, fold_partner, slot_total)

    def bulk(first, some, codes, base):
        kernel = functools.partial(bulk_kernel, first)
        extra = [] if base is None else [base]
        if extra:
            kernel = lambda *refs: bulk_kernel(first, *refs[:6], *refs[7:])
        return pl.pallas_call(
            kernel,
            out_shape=[
                jax.ShapeDtypeStruct(tracers.shape, f32),
                jax.ShapeDtypeStruct((OWN * SIDES + 1, 8 * some, LANES), f32),
            ],
            in_specs=[in_smem, in_hbm, in_hbm, in_hbm, in_hbm, in_vmem] + [in_hbm] * len(extra),
            out_specs=[in_hbm, in_vmem],
            scratch_shapes=[
                pltpu.VMEM((8 * some, CELLS), f32),
                pltpu.VMEM((8 * some, CELLS), f32),
                pltpu.VMEM((8 * some, CELLS), f32),
                pltpu.VMEM((slot_count, CELLS), f32),
                pltpu.VMEM((slot_count, CELLS), f32),
                pltpu.VMEM((8 * some, CELLS), f32),
                pltpu.VMEM((8 * some, CELLS), f32),
                pltpu.VMEM((8, WIDE), f32),
                pltpu.VMEM((8, WIDE), f32),
                dma((some,)),
                dma((some,)),
                dma((some,)),
                dma((2,)),
            ],
            input_output_aliases={6: 0} if extra else {},
            compiler_params=limit,
            cost_estimate=pl.CostEstimate(flops=4_000_000 * some, bytes_accessed=800_000 * some, transcendentals=0),
        )(my_index, tracers, velocity, kmt, kappa, codes, *extra)

    base, edge_a = bulk(0, FIRST_PAIRS, codes, None)
    held, edge_a = lax.optimization_barrier((held, edge_a))

    routed_rows = PARTS * slot_count
    routed = pl.pallas_call(
        route_kernel,
        grid=(device_count // PARTS,),
        out_shape=jax.ShapeDtypeStruct((slot_total, LANES), f32),
        in_specs=[
            in_smem,
            pl.BlockSpec((routed_rows, 6), lambda step: (step, 0)),
            pl.BlockSpec((slot_total, LANES), lambda step: (0, 0)),
        ],
        out_specs=pl.BlockSpec((routed_rows, LANES), lambda step: (step, 0)),
        compiler_params=limit,
    )(my_index, codes, held)

    routed, base = lax.optimization_barrier((routed, base))
    base, edge_b = bulk(FIRST_PAIRS, pairs - FIRST_PAIRS, codes, base)
    halo = exchanged(routed)[: PARTS * slot_count]

    return pl.pallas_call(
        finish_kernel,
        out_shape=jax.ShapeDtypeStruct(tracers.shape, f32),
        in_specs=[in_vmem, anywhere, anywhere, in_hbm],
        out_specs=in_hbm,
        scratch_shapes=[
            pltpu.VMEM((state_rows, CELLS), f32),
            pltpu.VMEM((OWN * SIDES + 1, state_rows, LANES), f32),
            pltpu.VMEM((12, state_rows, LANES), f32),
            pltpu.VMEM((2 * SIDES, state_rows, LANES), f32),
            dma((2,)),
            dma((pairs,)),
            dma((pairs,)),
        ],
        input_output_aliases={3: 0},
        compiler_params=limit,
    )(halo, edge_a, edge_b, base)


def solution(mesh):
    placed = (
        P(("blk", "sub"), None, None),
        P(("blk", "sub"), None, None),
        P(("blk", "sub"), None),
        P(("blk", "sub"), None),
        P(),
        P(),
        P(),
    )
    return jax.shard_map(
        per_device,
        mesh=mesh,
        in_specs=placed,
        out_specs=P(("blk", "sub"), None, None),
        check_vma=False,
    )
```

```python
import functools

import jax
import jax.numpy as jnp
from jax import lax
from jax.experimental import pallas as pl
from jax.experimental.pallas import tpu as pltpu
from jax.sharding import PartitionSpec as P

IB = 90
JB = 60
CELLS = IB * JB
COURANT = 0.2
LANES = 128
TILES = -(-CELLS // LANES)
WIDE = TILES * LANES
GAPS = JB + 1
HALF = IB // 2
PARTS = 32
X_PART = 22
SPARE = 48
PIECE = 16
SCALE = COURANT / 12.0
SIDES = 3
OWN = 8
FIRST_PAIRS = 2


def lane_of(rows):
    return lax.broadcasted_iota(jnp.int32, (rows, LANES), 1)


def rot(value, shift):
    shift = shift % LANES
    return value if shift == 0 else pltpu.roll(value, shift, 1)


def sublanes(value, shift):
    return pltpu.roll(value, shift % 8, 0)


def once(make):
    held = {}

    def get(tile):
        if tile not in held:
            held[tile] = make(tile)
        return held[tile]

    return get


def shifted(get, distance):
    offset = distance % LANES
    turned = once(lambda tile: rot(get(tile), -offset))

    def make(tile):
        low = tile + distance // LANES
        first = turned(low) if 0 <= low < TILES else jnp.zeros((8, LANES), jnp.float32)
        second = turned(low + 1) if 0 <= low + 1 < TILES else jnp.zeros((8, LANES), jnp.float32)
        return jnp.where(lane_of(8) < LANES - offset, first, second)

    return once(make)


def window(get, start, rows):
    tile, offset = start // LANES, start % LANES
    head = rot(get(tile), -offset)
    if offset == 0 or tile + 1 >= TILES:
        return head
    return jnp.where(lane_of(rows) < LANES - offset, head, rot(get(tile + 1), -offset))


def gap_groups(get, first, wide, rows):
    lane = lane_of(rows)
    held = LANES // wide
    result = []
    for at in range(0, GAPS, held):
        value = jnp.zeros((rows, LANES), jnp.float32)
        for gap in range(at, min(at + held, GAPS)):
            start = IB * gap + first
            place = (gap - at) * wide
            for tile in range(max(start, 0) // LANES, min(start + wide - 1, CELLS - 1) // LANES + 1):
                low = max(start, tile * LANES, 0)
                value = jnp.where(lane >= place + low - start, rot(get(tile), place - start + tile * LANES), value)
        result.append(value)
    return result


def lane_take(value, index):
    return jnp.take_along_axis(value, index, axis=1, mode="promise_in_bounds")


def lane_pick(pair, index):
    return jnp.where(index < LANES, lane_take(pair[0], index % LANES), lane_take(pair[1], index % LANES))


def tile_getter(ref, rows, count):
    def get(tile):
        if tile + 1 < TILES:
            return ref[rows, tile * LANES : (tile + 1) * LANES]
        rest = jnp.zeros((count, WIDE - CELLS), jnp.float32)
        return jnp.concatenate([ref[rows, tile * LANES : CELLS], rest], axis=1)

    return get


def across_pair(get):
    lane = lane_of(8)
    groups = gap_groups(get, -2, 4, 8)
    return lane_pick(groups, 4 * (lane // 2) + 1 + lane % 2), lane_pick(groups, 4 * (lane // 2) + 3 * (lane % 2))


def joined(south, north, half, rows):
    if half == 0:
        return jnp.where(lane_of(rows) < 64, south, rot(north, 64))
    return jnp.where(lane_of(rows) < 64, rot(south, -HALF), rot(north, 64 - HALF))


def pair_copies(source, target, sems, first, pairs):
    copies = []
    for pair in range(pairs):
        into = target.at[pl.ds(8 * pair, 8)].reshape(2, 4, CELLS)
        copies.append(pltpu.make_async_copy(source.at[pl.ds(2 * (first + pair), 2)], into, sems.at[pair]))
    return copies


def pack_kernel(blk_count, sub_count, tracer_ref, velocity_ref, depth_ref, out_ref, x_ref, v_ref, d_ref, strip_ref, x_sems, v_sems, d_sem):
    count = depth_ref.shape[0]
    pairs = count // 2
    x_copies = pair_copies(tracer_ref, x_ref, x_sems, 0, pairs)
    v_copies = pair_copies(velocity_ref, v_ref, v_sems, 0, pairs)
    d_copy = pltpu.make_async_copy(depth_ref, d_ref, d_sem)
    for pair in range(pairs):
        x_copies[pair].start()
        v_copies[pair].start()
    d_copy.start()
    for pair in range(pairs):
        rows = pl.ds(8 * pair, 8)
        x_copies[pair].wait()
        get_x = tile_getter(x_ref, rows, 8)
        near, far = across_pair(get_x)
        south = [window(get_x, 0, 8), window(get_x, IB, 8)]
        north = [window(get_x, CELLS - IB, 8), window(get_x, CELLS - 2 * IB, 8)]
        v_copies[pair].wait()
        get_v = tile_getter(v_ref, rows, 8)
        v_south, v_north = window(get_v, 0, 8), window(get_v, CELLS - IB, 8)
        strips = [joined(south[0], north[0], half, 8) for half in range(2)]
        strips += [joined(south[1], north[1], half, 8) for half in range(2)]
        strips += [joined(v_south, v_north, half, 8) for half in range(2)]
        strips += [near, far, gap_groups(get_v, -1, 2, 8)[0]]
        for index, strip in enumerate(strips):
            strip_ref[index, rows, :] = strip

    d_copy.wait()
    if out_ref.shape[0] > PARTS * count:
        out_ref[...] = jnp.zeros(out_ref.shape, jnp.float32)
    slot_lane = lane_of(count)
    get_d = tile_getter(d_ref, slice(None), count)
    d_south, d_north = window(get_d, 0, count), window(get_d, CELLS - IB, count)
    d_gaps = gap_groups(get_d, -1, 2, count)[0]
    spare = (slot_lane >= SPARE) & (slot_lane < SPARE + PIECE)

    def put(part, value):
        at = (part % sub_count * blk_count + part // sub_count) * count
        out_ref[at : at + count, :] = value

    for chan in range(4):
        rows = pl.ds(chan, count, stride=4)
        for half in range(2):
            for deep in range(2):
                part = 2 * (4 * deep + chan) + half
                value = strip_ref[2 * deep + half, rows, :]
                if part < 8:
                    value = jnp.where(spare, rot(d_gaps, SPARE - PIECE * part), value)
                put(part, value)
            if chan >= 2:
                put(2 * (8 + chan - 2) + half, strip_ref[4 + half, rows, :])
        put(X_PART + chan, strip_ref[6, rows, :])
        put(X_PART + 4 + chan, strip_ref[7, rows, :])
        if chan < 2:
            put(X_PART + 8 + chan, strip_ref[8, rows, :])
    for half in range(2):
        put(20 + half, joined(d_south, d_north, half, count))


def regroup_kernel(outer, inner, in_ref, out_ref):
    size = in_ref.shape[0] // (outer * inner)
    for major in range(outer):
        for minor in range(inner):
            source, target = (major * inner + minor) * size, (minor * outer + major) * size
            out_ref[target : target + size, :] = in_ref[source : source + size, :]


def route_kernel(part_ref, code_ref, held_ref, out_ref):
    total = held_ref.shape[0]
    rows = out_ref.shape[0]
    part = part_ref[0]
    picked = [jnp.zeros((rows, 2 * LANES), jnp.float32) for _ in range(5)]
    for start in range(0, total, rows):
        held = held_ref[start : start + rows, :]
        high = held.astype(jnp.bfloat16)
        low = (held - high.astype(jnp.float32)).astype(jnp.bfloat16)
        halves = jnp.concatenate([high, low], axis=1)
        source = lax.broadcasted_iota(jnp.int32, (rows, rows), 1) + start
        for side in range(5):
            one_hot = jnp.where(code_ref[:, side : side + 1] == source, 1.0, 0.0).astype(jnp.bfloat16)
            picked[side] += jnp.dot(one_hot, halves, preferred_element_type=jnp.float32)
    west, east, south, north, fold = [value[:, :LANES] + value[:, LANES:] for value in picked]
    lane = lane_of(rows)
    along_x = (part >= X_PART) | ((part < 8) & (lane >= SPARE) & (lane < SPARE + PIECE))
    x_side = jnp.where(lane % 2 == 0, west, east)
    y_side = jnp.where(lane < 64, north + rot(fold, 64), south)
    out_ref[...] = jnp.where(along_x, x_side, y_side)


def bulk_kernel(first, my_ref, tracer_ref, velocity_ref, depth_ref, kappa_ref, code_ref,
                base_ref, edge_ref, y_ref, x_ref, v_ref, d_ref, k_ref, d8_ref, k8_ref, w_ref, z_ref, x_sems, v_sems, y_sems, d_sems):
    count = depth_ref.shape[0]
    pairs = edge_ref.shape[1] // 8
    x_copies = pair_copies(tracer_ref, x_ref, x_sems, first, pairs)
    v_copies = pair_copies(velocity_ref, v_ref, v_sems, first, pairs)
    d_copy = pltpu.make_async_copy(depth_ref, d_ref, d_sems.at[0])
    k_copy = pltpu.make_async_copy(kappa_ref, k_ref, d_sems.at[1])
    d_copy.start()
    k_copy.start()
    for pair in range(pairs):
        v_copies[pair].start()
        x_copies[pair].start()
    lane = lane_of(8)
    row = lax.broadcasted_iota(jnp.int32, (8, LANES), 0)
    x_row, even, place = row % 4 < 2, row % 2 == 0, row % 4
    level = (row % 2).astype(jnp.float32)
    zero = jnp.zeros((8, LANES), jnp.float32)

    def all_rows(value, chosen):
        result = value
        for at in range(4):
            if at != chosen:
                result = jnp.where(place == at, sublanes(value, at - chosen), result)
        return result

    def wet_of(depth):
        return jnp.clip(depth - level, 0.0, 1.0)

    for copy, source, target in ((d_copy, d_ref, d8_ref), (k_copy, k_ref, k8_ref)):
        copy.wait()
        for pair in range(pairs):
            slot = 2 * (first + pair)
            for start in range(0, CELLS, LANES):
                columns = slice(start, min(start + LANES, CELLS))
                shape = (8, columns.stop - start)
                top, low = [jnp.broadcast_to(source[slot + at : slot + at + 1, columns], shape) for at in range(2)]
                target[8 * pair : 8 * pair + 8, columns] = jnp.where(row[:, : shape[1]] < 4, top, low)

    def one_pair(pair):
        slot = 2 * (first + pair)
        rows = pl.ds(pl.multiple_of(8 * pair, 8), 8)
        for source, target, sems in ((velocity_ref, v_ref, v_sems), (tracer_ref, x_ref, x_sems)):
            pltpu.make_async_copy(
                source.at[pl.ds(0, 2)], target.at[rows].reshape(2, 4, CELLS), sems.at[pair]).wait()

        codes = [code_ref[pl.ds(my_ref[0] * count + slot + at, 1), :] for at in range(2)]

        def flag(column):
            pieces = [jnp.broadcast_to(code[:, column : column + 1], (8, LANES)) for code in codes]
            return jnp.where(row < 4, pieces[0], pieces[1]) >= 0

        live, folded = flag(5), flag(4)
        state, velocity = once(tile_getter(x_ref, rows, 8)), once(tile_getter(v_ref, rows, 8))
        depth, kappa = once(tile_getter(d8_ref, rows, 8)), once(tile_getter(k8_ref, rows, 8))
        wet = once(lambda tile: wet_of(depth(tile)))

        @once
        def ratio(tile):
            other = jnp.clip(depth(tile) - (1.0 - level), 0.0, 1.0)
            coupling = kappa(tile) * (wet(tile) * other)
            return coupling / (1.0 + 2.0 * coupling)

        next_vel = [shifted(velocity, 1), shifted(velocity, IB)]
        next_wet = [shifted(wet, 1), shifted(wet, IB)]

        @once
        def face(tile):
            rims = [at - tile * LANES for at in range(IB - 1, CELLS, IB) if at // LANES == tile]
            rim = functools.reduce(jnp.logical_or, [lane == at for at in rims]) if rims else None
            across = next_wet[0](tile) if rim is None else jnp.where(rim, 0.0, next_wet[0](tile))
            speed = velocity(tile) + jnp.where(x_row, next_vel[0](tile), next_vel[1](tile))
            value = SCALE * speed * (wet(tile) * jnp.where(x_row, across, next_wet[1](tile)))
            w_ref[:, tile * LANES : (tile + 1) * LANES] = value
            return value

        face_x = once(lambda tile: jnp.where(x_row, face(tile), sublanes(face(tile), 2)))
        face_y = once(lambda tile: jnp.where(x_row, sublanes(face(tile), -2), face(tile)))
        five = once(lambda tile: 5.0 * state(tile))
        two = once(lambda tile: 2.0 * state(tile))

        def divergence(speed, distance):
            before, after = shifted(state, -distance), shifted(state, distance)
            lower = once(lambda tile: five(tile) - before(tile) + 2.0 * after(tile))
            upper = shifted(once(lambda tile: five(tile) - after(tile)), distance)

            @once
            def flux(tile):
                value = jnp.maximum(speed(tile), 0.0) * lower(tile)
                return value + jnp.minimum(speed(tile), 0.0) * (two(tile) + upper(tile))

            back = shifted(flux, -distance)
            for stage in (after, before, lower, upper, flux, back):
                for tile in range(TILES):
                    stage(tile)
            return once(lambda tile: flux(tile) - back(tile))

        for stage in (depth, wet, ratio, *next_vel, *next_wet, face):
            for tile in range(TILES):
                stage(tile)
        change_x, change_y = divergence(face_x, 1), divergence(face_y, IB)
        for tile in range(TILES):
            explicit = state(tile) - wet(tile) * (change_x(tile) + change_y(tile))
            other = jnp.where(even, sublanes(explicit, -1), sublanes(explicit, 1))
            value = jnp.where(live, explicit + ratio(tile) * (other - explicit), zero)
            stop = min((tile + 1) * LANES, CELLS)
            y_ref[rows, tile * LANES : stop] = value[:, : stop - tile * LANES]
            mixed = jnp.where(x_row, face(tile), jnp.where(even, ratio(tile), depth(tile)))
            z_ref[:, tile * LANES : (tile + 1) * LANES] = mixed

        pltpu.make_async_copy(
            y_ref.at[rows].reshape(2, 4, CELLS), base_ref.at[pl.ds(slot, 2)], y_sems.at[pair]).start()
        get_w, get_z = [lambda tile, ref=ref: ref[:, tile * LANES : (tile + 1) * LANES] for ref in (w_ref, z_ref)]
        groups = gap_groups(get_z, -2, 4, 8)
        east = lane % 2 == 0
        near, far = across_pair(state)
        normal = gap_groups(velocity, -1, 2, 8)[0]
        normal = jnp.where(x_row, normal, sublanes(normal, 2))
        rim_speed = lane_pick(groups, 4 * (lane // 2) + 2 * (lane % 2))
        rim_speed = jnp.where(x_row, rim_speed, sublanes(rim_speed, 2))
        sides = [(
            near, far, jnp.where(east, -normal, normal), jnp.where(east, -rim_speed, rim_speed),
            lane_pick(groups, 4 * (lane // 2) + 1 + lane % 2), lane_pick(groups, 4 * (lane // 2) + 3 * (lane % 2)),
        )]
        for outer, inner, edge, sign in ((0, IB, 0, 1.0), (CELLS - IB, CELLS - 2 * IB, CELLS - 2 * IB, -1.0)):
            normal, rim_speed = window(velocity, outer, 8), window(get_w, edge, 8)
            normal = sign * jnp.where(x_row, sublanes(normal, -2), normal)
            rim_speed = sign * jnp.where(x_row, sublanes(rim_speed, -2), rim_speed)
            sides.append((window(state, outer, 8), window(state, inner, 8), normal, rim_speed,
                          window(get_z, outer, 8), window(get_z, inner, 8)))
        for side, (near, far, normal, rim_speed, outer, inner) in enumerate(sides):
            values = (near, far, normal, jnp.where(live, jnp.maximum(rim_speed, 0.0), zero), wet_of(all_rows(outer, 3)),
                      wet_of(all_rows(inner, 3)), all_rows(outer, 2), all_rows(inner, 2))
            for index, value in enumerate(values):
                edge_ref[OWN * side + index, rows, :] = value
        edge_ref[OWN * SIDES, rows, :] = jnp.where(folded, 1.0, zero)

    pl.loop(0, pairs)(one_pair)
    for pair in range(pairs):
        slots = pl.ds(2 * (first + pair), 2)
        rows = y_ref.at[pl.ds(8 * pair, 8)].reshape(2, 4, CELLS)
        pltpu.make_async_copy(rows, base_ref.at[slots], y_sems.at[pair]).wait()


def finish_kernel(halo_ref, edge_a_ref, edge_b_ref, base_ref, out_ref,
                  y_ref, own_ref, raw_ref, delta_ref, own_sems, in_sems, out_sems):
    count = out_ref.shape[0]
    pairs = count // 2
    rows = 4 * count
    split = edge_a_ref.shape[1]
    own_copies = [
        pltpu.make_async_copy(edge_a_ref, own_ref.at[:, pl.ds(0, split)], own_sems.at[0]),
        pltpu.make_async_copy(edge_b_ref, own_ref.at[:, pl.ds(split, rows - split)], own_sems.at[1]),
    ]
    in_copies = pair_copies(base_ref, y_ref, in_sems, 0, pairs)
    for copy in own_copies + in_copies:
        copy.start()
    lane = lane_of(rows)
    level = (lax.broadcasted_iota(jnp.int32, (rows, LANES), 0) % 2).astype(jnp.float32)

    def part(index):
        return halo_ref[index * count : (index + 1) * count, :]

    def assembled(index, parts):
        for chan, value in enumerate(parts):
            raw_ref[index, pl.ds(chan, count, stride=4), :] = value
        return raw_ref[index]

    mirror = jnp.where(lane < IB, IB - 1 - lane, lane)
    slot_lane = lane_of(count)
    depth_x = rot(part(0), -SPARE)
    for index in range(1, 8):
        depth_x = jnp.where(slot_lane >= PIECE * index, rot(part(index), PIECE * index - SPARE), depth_x)
    x_raw = [[part(X_PART + chan) for chan in range(4)], [part(X_PART + 4 + chan) for chan in range(4)],
             [part(X_PART + 8 + chan % 2) for chan in range(4)], [depth_x] * 4]
    y_values = [list(range(4)), list(range(4, 8)), [8, 9, 8, 9], [10] * 4]
    x_halo, south_halo, north_raw = [], [], []
    for kind in range(4):
        raw = assembled(3 * kind, x_raw[kind])
        x_halo.append(jnp.where(lane % 2 == 0, rot(raw, 1), rot(raw, -1)))
        first, second = [assembled(3 * kind + 1 + half, [part(2 * value + half) for value in y_values[kind]])
                         for half in range(2)]
        south_halo.append(jnp.where(lane < HALF, rot(first, 64), rot(second, 64 + HALF)))
        north_raw.append(jnp.where(lane < HALF, first, rot(second, HALF)))
    for copy in own_copies:
        copy.wait()
    folded = own_ref[OWN * SIDES] > 0.0
    north_halo = []
    for kind, raw in enumerate(north_raw):
        turned = lane_take(raw, mirror)
        north_halo.append(jnp.where(folded, -turned if kind == 2 else turned, raw))

    for side, (out_near, out_far, out_normal, out_depth) in enumerate((x_halo, south_halo, north_halo)):
        near, far, normal, rim_speed, wet, inner_wet, ratio, inner_ratio = [
            own_ref[OWN * side + index] for index in range(OWN)]
        if side == 0:
            out_normal = jnp.where(lane % 2 == 0, -out_normal, out_normal)
            beyond = out_near - jnp.where(lane % 2 == 0, rot(near, -1), rot(near, 1))
        else:
            out_normal = -out_normal if side == 2 else out_normal
            beyond = out_near
        speed = SCALE * (normal + out_normal) * (wet * jnp.clip(out_depth - level, 0.0, 1.0))
        flux = jnp.maximum(speed, 0.0) * (5.0 * out_near + 2.0 * near - out_far)
        flux += jnp.minimum(speed, 0.0) * (2.0 * out_near + 5.0 * near - far)
        inner_flux = rim_speed * beyond
        for place, (change, share) in enumerate(((wet * (flux + inner_flux), ratio),
                                                 (-inner_wet * inner_flux, inner_ratio))):
            other = jnp.where(level == 0.0, pltpu.roll(change, rows - 1, 0), pltpu.roll(change, 1, 0))
            delta_ref[2 * side + place] = change + share * (other - change)

    lane = lane_of(8)
    out_copies = []
    for pair in range(pairs):
        mine = pl.ds(8 * pair, 8)
        in_copies[pair].wait()
        near, deep, south, south_in, north, north_in = [delta_ref[index, mine, :] for index in range(2 * SIDES)]
        groups = []
        for at in range(2):
            index = 2 * (lane // 4) + (lane % 4) // 2 + 64 * at
            outer, inner = lane_take(near, index), lane_take(deep, index)
            groups.append(jnp.where((lane % 4 == 1) | (lane % 4 == 2), outer, inner))
        placed = [(groups[gap // 32], 4 * (gap % 32), IB * gap - 2, 4) for gap in range(GAPS)]
        placed += [(south, 0, 0, IB), (south_in, 0, IB, IB)]
        placed += [(north, 0, CELLS - IB, IB), (north_in, 0, CELLS - 2 * IB, IB)]
        for tile in range(TILES):
            at, stop = tile * LANES, min((tile + 1) * LANES, CELLS)
            change = jnp.zeros((8, LANES), jnp.float32)
            for source, origin, start, wide in placed:
                low, high = max(start, at, 0), min(start + wide, stop)
                if low < high:
                    inside = (lane >= low - at) & (lane < high - at)
                    change += jnp.where(inside, rot(source, start - at - origin), 0.0)
            y_ref[mine, at:stop] = y_ref[mine, at:stop] + change[:, : stop - at]
        copy = pltpu.make_async_copy(
            y_ref.at[mine].reshape(2, 4, CELLS), out_ref.at[pl.ds(2 * pair, 2)], out_sems.at[pair])
        copy.start()
        out_copies.append(copy)
    for copy in out_copies:
        copy.wait()


def route_codes(block_owner, neighbours, fold_partner, slots):
    block_count = block_owner.shape[0]
    hits = block_owner[None, :] == slots[:, None]
    links = jnp.concatenate([neighbours, fold_partner[:, None]], axis=1)
    linked = links[:, :, None] == jnp.arange(block_count, dtype=jnp.int32)[None, None, :]
    link_slots = jnp.max(jnp.where(linked, block_owner[None, None, :], -1), axis=2)
    link_slots = jnp.concatenate([link_slots, block_owner[:, None]], axis=1)
    return jnp.max(jnp.where(hits[:, :, None], link_slots[None], -1), axis=1)


def per_device(tracers, velocity, kappa, kmt, block_owner, neighbours, fold_partner):
    slot_count, chans = tracers.shape[:2]
    blk_count, sub_count = lax.axis_size("blk"), lax.axis_size("sub")
    device_count = blk_count * sub_count
    if device_count % PARTS or chans != 4 or slot_count % 2 or slot_count < 2 * FIRST_PAIRS + 2:
        raise ValueError("unsupported sizes")
    my_index = (lax.axis_index("blk") * sub_count + lax.axis_index("sub")).astype(jnp.int32).reshape(1)
    my_place = (lax.axis_index("sub") * blk_count + lax.axis_index("blk")).astype(jnp.int32).reshape(1)
    pairs = slot_count // 2
    slot_total = device_count * slot_count
    state_rows = 4 * slot_count
    f32 = jnp.float32
    in_hbm = pl.BlockSpec(memory_space=pltpu.HBM)
    anywhere = pl.BlockSpec(memory_space=pl.ANY)
    in_vmem = pl.BlockSpec(memory_space=pltpu.VMEM)
    in_smem = pl.BlockSpec(memory_space=pltpu.SMEM)
    dma = pltpu.SemaphoreType.DMA
    limit = pltpu.CompilerParams(vmem_limit_bytes=32 * 1024 * 1024)

    def exchanged(pieces):
        width = slot_count * LANES
        pieces = lax.all_to_all(pieces.reshape(sub_count, 1, blk_count * width), "sub", 0, 0, tiled=True)
        pieces = pl.pallas_call(
            functools.partial(regroup_kernel, sub_count, blk_count),
            out_shape=jax.ShapeDtypeStruct((slot_total, LANES), f32),
            compiler_params=limit,
        )(pieces.reshape(slot_total, LANES))
        pieces = lax.all_to_all(pieces.reshape(blk_count, 1, sub_count * width), "blk", 0, 0, tiled=True)
        return pieces.reshape(slot_total, LANES)

    pack = pl.pallas_call(
        functools.partial(pack_kernel, blk_count, sub_count),
        out_shape=jax.ShapeDtypeStruct((slot_total, LANES), f32),
        in_specs=[in_hbm, in_hbm, in_hbm],
        out_specs=in_vmem,
        scratch_shapes=[
            pltpu.VMEM((state_rows, CELLS), f32),
            pltpu.VMEM((state_rows, CELLS), f32),
            pltpu.VMEM((slot_count, CELLS), f32),
            pltpu.VMEM((9, state_rows, LANES), f32),
            dma((pairs,)),
            dma((pairs,)),
            dma,
        ],
        cost_estimate=pl.CostEstimate(flops=4_000_000, bytes_accessed=2_400_000, transcendentals=0),
    )(tracers, velocity, kmt)
    held = exchanged(pack)
    slots = jnp.arange(slot_total, dtype=jnp.int32).reshape(blk_count, sub_count, slot_count)
    codes = route_codes(block_owner, neighbours, fold_partner, slots.transpose(1, 0, 2).reshape(-1))

    def bulk(first, some, codes, base):
        kernel = functools.partial(bulk_kernel, first)
        extra = [] if base is None else [base]
        if extra:
            kernel = lambda *refs: bulk_kernel(first, *refs[:6], *refs[7:])
        return pl.pallas_call(
            kernel,
            out_shape=[
                jax.ShapeDtypeStruct(tracers.shape, f32),
                jax.ShapeDtypeStruct((OWN * SIDES + 1, 8 * some, LANES), f32),
            ],
            in_specs=[in_smem, in_hbm, in_hbm, in_hbm, in_hbm, in_vmem] + [in_hbm] * len(extra),
            out_specs=[in_hbm, in_vmem],
            scratch_shapes=[
                pltpu.VMEM((8 * some, CELLS), f32),
                pltpu.VMEM((8 * some, CELLS), f32),
                pltpu.VMEM((8 * some, CELLS), f32),
                pltpu.VMEM((slot_count, CELLS), f32),
                pltpu.VMEM((slot_count, CELLS), f32),
                pltpu.VMEM((8 * some, CELLS), f32),
                pltpu.VMEM((8 * some, CELLS), f32),
                pltpu.VMEM((8, WIDE), f32),
                pltpu.VMEM((8, WIDE), f32),
                dma((some,)),
                dma((some,)),
                dma((some,)),
                dma((2,)),
            ],
            input_output_aliases={6: 0} if extra else {},
            compiler_params=limit,
            cost_estimate=pl.CostEstimate(flops=4_000_000 * some, bytes_accessed=800_000 * some, transcendentals=0),
        )(my_place, tracers, velocity, kmt, kappa, codes, *extra)

    base, edge_a = bulk(0, FIRST_PAIRS, codes, None)
    held, edge_a = lax.optimization_barrier((held, edge_a))

    routed_rows = PARTS * slot_count
    routed = pl.pallas_call(
        route_kernel,
        grid=(device_count // PARTS,),
        out_shape=jax.ShapeDtypeStruct((slot_total, LANES), f32),
        in_specs=[
            in_smem,
            pl.BlockSpec((routed_rows, 6), lambda step: (step, 0)),
            pl.BlockSpec((slot_total, LANES), lambda step: (0, 0)),
        ],
        out_specs=pl.BlockSpec((routed_rows, LANES), lambda step: (step, 0)),
        compiler_params=limit,
    )(my_index, codes, held)

    routed, base = lax.optimization_barrier((routed, base))
    base, edge_b = bulk(FIRST_PAIRS, pairs - FIRST_PAIRS, codes, base)
    halo = exchanged(routed)[: PARTS * slot_count]

    return pl.pallas_call(
        finish_kernel,
        out_shape=jax.ShapeDtypeStruct(tracers.shape, f32),
        in_specs=[in_vmem, anywhere, anywhere, in_hbm],
        out_specs=in_hbm,
        scratch_shapes=[
            pltpu.VMEM((state_rows, CELLS), f32),
            pltpu.VMEM((OWN * SIDES + 1, state_rows, LANES), f32),
            pltpu.VMEM((12, state_rows, LANES), f32),
            pltpu.VMEM((2 * SIDES, state_rows, LANES), f32),
            dma((2,)),
            dma((pairs,)),
            dma((pairs,)),
        ],
        input_output_aliases={3: 0},
        compiler_params=limit,
    )(halo, edge_a, edge_b, base)


def solution(mesh):
    placed = (
        P(("blk", "sub"), None, None),
        P(("blk", "sub"), None, None),
        P(("blk", "sub"), None),
        P(("blk", "sub"), None),
        P(),
        P(),
        P(),
    )
    return jax.shard_map(
        per_device,
        mesh=mesh,
        in_specs=placed,
        out_specs=P(("blk", "sub"), None, None),
        check_vma=False,
    )
```

```python
import functools

import jax
import jax.numpy as jnp
from jax import lax
from jax.experimental import pallas as pl
from jax.experimental.pallas import tpu as pltpu
from jax.sharding import PartitionSpec as P

IB = 90
JB = 60
CELLS = IB * JB
COURANT = 0.2
LANES = 128
TILES = -(-CELLS // LANES)
WIDE = TILES * LANES
GAPS = JB + 1
HALF = IB // 2
PARTS = 32
X_PART = 22
SPARE = 48
PIECE = 16
SCALE = COURANT / 12.0
SIDES = 3
OWN = 8
FIRST_PAIRS = 2
CHAIN = 8


def lane_of(rows):
    return lax.broadcasted_iota(jnp.int32, (rows, LANES), 1)


def rot(value, shift):
    shift = shift % LANES
    return value if shift == 0 else pltpu.roll(value, shift, 1)


def sublanes(value, shift):
    return pltpu.roll(value, shift % 8, 0)


def once(make):
    held = {}

    def get(tile):
        if tile not in held:
            held[tile] = make(tile)
        return held[tile]

    return get


def shifted(get, distance):
    offset = distance % LANES
    turned = once(lambda tile: rot(get(tile), -offset))

    def make(tile):
        low = tile + distance // LANES
        first = turned(low) if 0 <= low < TILES else jnp.zeros((8, LANES), jnp.float32)
        second = turned(low + 1) if 0 <= low + 1 < TILES else jnp.zeros((8, LANES), jnp.float32)
        return jnp.where(lane_of(8) < LANES - offset, first, second)

    return once(make)


def window(get, start, rows):
    tile, offset = start // LANES, start % LANES
    head = rot(get(tile), -offset)
    if offset == 0 or tile + 1 >= TILES:
        return head
    return jnp.where(lane_of(rows) < LANES - offset, head, rot(get(tile + 1), -offset))


def gap_groups(get, first, wide, rows):
    lane = lane_of(rows)
    held = LANES // wide
    result = []
    for at in range(0, GAPS, held):
        value = jnp.zeros((rows, LANES), jnp.float32)
        for chain in range(at, min(at + held, GAPS), CHAIN):
            link = jnp.zeros((rows, LANES), jnp.float32)
            for gap in range(chain, min(chain + CHAIN, at + held, GAPS)):
                start = IB * gap + first
                place = (gap - at) * wide
                for tile in range(max(start, 0) // LANES, min(start + wide - 1, CELLS - 1) // LANES + 1):
                    low = max(start, tile * LANES, 0)
                    link = jnp.where(lane >= place + low - start, rot(get(tile), place - start + tile * LANES), link)
            value = jnp.where(lane >= (chain - at) * wide, link, value)
        result.append(value)
    return result


def lane_take(value, index):
    return jnp.take_along_axis(value, index, axis=1, mode="promise_in_bounds")


def lane_pick(pair, index):
    return jnp.where(index < LANES, lane_take(pair[0], index % LANES), lane_take(pair[1], index % LANES))


def tile_getter(ref, rows, count):
    def get(tile):
        if tile + 1 < TILES:
            return ref[rows, tile * LANES : (tile + 1) * LANES]
        rest = jnp.zeros((count, WIDE - CELLS), jnp.float32)
        return jnp.concatenate([ref[rows, tile * LANES : CELLS], rest], axis=1)

    return get


def across_pair(get):
    lane = lane_of(8)
    groups = gap_groups(get, -2, 4, 8)
    return lane_pick(groups, 4 * (lane // 2) + 1 + lane % 2), lane_pick(groups, 4 * (lane // 2) + 3 * (lane % 2))


def joined(south, north, half, rows):
    if half == 0:
        return jnp.where(lane_of(rows) < 64, south, rot(north, 64))
    return jnp.where(lane_of(rows) < 64, rot(south, -HALF), rot(north, 64 - HALF))


def pair_copies(source, target, sems, first, pairs):
    copies = []
    for pair in range(pairs):
        into = target.at[pl.ds(8 * pair, 8)].reshape(2, 4, CELLS)
        copies.append(pltpu.make_async_copy(source.at[pl.ds(2 * (first + pair), 2)], into, sems.at[pair]))
    return copies


def pack_kernel(tracer_ref, velocity_ref, depth_ref, out_ref, x_ref, v_ref, d_ref, strip_ref, x_sems, v_sems, d_sem):
    count = depth_ref.shape[0]
    pairs = count // 2
    x_copies = pair_copies(tracer_ref, x_ref, x_sems, 0, pairs)
    v_copies = pair_copies(velocity_ref, v_ref, v_sems, 0, pairs)
    d_copy = pltpu.make_async_copy(depth_ref, d_ref, d_sem)
    d_copy.start()
    for pair in range(pairs):
        x_copies[pair].start()
        v_copies[pair].start()
    d_copy.wait()
    slot_lane = lane_of(count)
    get_d = tile_getter(d_ref, slice(None), count)
    d_south, d_north = window(get_d, 0, count), window(get_d, CELLS - IB, count)
    d_gaps = gap_groups(get_d, -1, 2, count)[0]
    for pair in range(pairs):
        rows = pl.ds(8 * pair, 8)
        x_copies[pair].wait()
        get_x = tile_getter(x_ref, rows, 8)
        near, far = across_pair(get_x)
        south = [window(get_x, 0, 8), window(get_x, IB, 8)]
        north = [window(get_x, CELLS - IB, 8), window(get_x, CELLS - 2 * IB, 8)]
        v_copies[pair].wait()
        get_v = tile_getter(v_ref, rows, 8)
        v_south, v_north = window(get_v, 0, 8), window(get_v, CELLS - IB, 8)
        strips = [joined(south[0], north[0], half, 8) for half in range(2)]
        strips += [joined(south[1], north[1], half, 8) for half in range(2)]
        strips += [joined(v_south, v_north, half, 8) for half in range(2)]
        strips += [near, far, gap_groups(get_v, -1, 2, 8)[0]]
        for index, strip in enumerate(strips):
            strip_ref[index, rows, :] = strip

    if out_ref.shape[0] > PARTS * count:
        rest = out_ref.shape[0] - PARTS * count
        out_ref[PARTS * count :, :] = jnp.zeros((rest, LANES), jnp.float32)
    spare = (slot_lane >= SPARE) & (slot_lane < SPARE + PIECE)

    def put(part, value):
        out_ref[part * count : (part + 1) * count, :] = value

    for chan in range(4):
        rows = pl.ds(chan, count, stride=4)
        for half in range(2):
            for deep in range(2):
                part = 2 * (4 * deep + chan) + half
                value = strip_ref[2 * deep + half, rows, :]
                if part < 8:
                    value = jnp.where(spare, rot(d_gaps, SPARE - PIECE * part), value)
                put(part, value)
            if chan >= 2:
                put(2 * (8 + chan - 2) + half, strip_ref[4 + half, rows, :])
        put(X_PART + chan, strip_ref[6, rows, :])
        put(X_PART + 4 + chan, strip_ref[7, rows, :])
        if chan < 2:
            put(X_PART + 8 + chan, strip_ref[8, rows, :])
    for half in range(2):
        put(20 + half, joined(d_south, d_north, half, count))


def route_kernel(part_ref, code_ref, held_ref, out_ref):
    total = held_ref.shape[0]
    rows = out_ref.shape[0]
    part = part_ref[0]
    picked = [jnp.zeros((rows, 2 * LANES), jnp.float32) for _ in range(5)]
    for start in range(0, total, rows):
        held = held_ref[start : start + rows, :]
        high = held.astype(jnp.bfloat16)
        low = (held - high.astype(jnp.float32)).astype(jnp.bfloat16)
        halves = jnp.concatenate([high, low], axis=1)
        source = lax.broadcasted_iota(jnp.int32, (rows, rows), 1) + start
        for side in range(5):
            one_hot = jnp.where(code_ref[:, side : side + 1] == source, 1.0, 0.0).astype(jnp.bfloat16)
            picked[side] += jnp.dot(one_hot, halves, preferred_element_type=jnp.float32)
    west, east, south, north, fold = [value[:, :LANES] + value[:, LANES:] for value in picked]
    lane = lane_of(rows)
    along_x = (part >= X_PART) | ((part < 8) & (lane >= SPARE) & (lane < SPARE + PIECE))
    x_side = jnp.where(lane % 2 == 0, west, east)
    y_side = jnp.where(lane < 64, north + rot(fold, 64), south)
    out_ref[...] = jnp.where(along_x, x_side, y_side)


def bulk_kernel(first, my_ref, tracer_ref, velocity_ref, depth_ref, kappa_ref, code_ref,
                base_ref, edge_ref, y_ref, x_ref, v_ref, d_ref, k_ref, d8_ref, k8_ref, w_ref, z_ref, x_sems, v_sems, y_sems, d_sems):
    count = depth_ref.shape[0]
    pairs = edge_ref.shape[1] // 8
    x_copies = pair_copies(tracer_ref, x_ref, x_sems, first, pairs)
    v_copies = pair_copies(velocity_ref, v_ref, v_sems, first, pairs)
    d_copy = pltpu.make_async_copy(depth_ref, d_ref, d_sems.at[0])
    k_copy = pltpu.make_async_copy(kappa_ref, k_ref, d_sems.at[1])
    d_copy.start()
    k_copy.start()
    for pair in range(pairs):
        v_copies[pair].start()
        x_copies[pair].start()
    lane = lane_of(8)
    row = lax.broadcasted_iota(jnp.int32, (8, LANES), 0)
    x_row, even, place = row % 4 < 2, row % 2 == 0, row % 4
    level = (row % 2).astype(jnp.float32)
    zero = jnp.zeros((8, LANES), jnp.float32)

    def all_rows(value, chosen):
        result = value
        for at in range(4):
            if at != chosen:
                result = jnp.where(place == at, sublanes(value, at - chosen), result)
        return result

    def wet_of(depth):
        return jnp.clip(depth - level, 0.0, 1.0)

    for copy, source, target in ((d_copy, d_ref, d8_ref), (k_copy, k_ref, k8_ref)):
        copy.wait()
        for pair in range(pairs):
            slot = 2 * (first + pair)
            for start in range(0, CELLS, LANES):
                columns = slice(start, min(start + LANES, CELLS))
                shape = (8, columns.stop - start)
                top, low = [jnp.broadcast_to(source[slot + at : slot + at + 1, columns], shape) for at in range(2)]
                target[8 * pair : 8 * pair + 8, columns] = jnp.where(row[:, : shape[1]] < 4, top, low)

    def one_pair(pair):
        slot = 2 * (first + pair)
        rows = pl.ds(pl.multiple_of(8 * pair, 8), 8)
        for source, target, sems in ((velocity_ref, v_ref, v_sems), (tracer_ref, x_ref, x_sems)):
            pltpu.make_async_copy(
                source.at[pl.ds(0, 2)], target.at[rows].reshape(2, 4, CELLS), sems.at[pair]).wait()

        codes = [code_ref[pl.ds(my_ref[0] * count + slot + at, 1), :] for at in range(2)]

        def flag(column):
            pieces = [jnp.broadcast_to(code[:, column : column + 1], (8, LANES)) for code in codes]
            return jnp.where(row < 4, pieces[0], pieces[1]) >= 0

        live, folded = flag(5), flag(4)
        state, velocity = once(tile_getter(x_ref, rows, 8)), once(tile_getter(v_ref, rows, 8))
        depth, kappa = once(tile_getter(d8_ref, rows, 8)), once(tile_getter(k8_ref, rows, 8))
        wet = once(lambda tile: wet_of(depth(tile)))

        @once
        def ratio(tile):
            other = jnp.clip(depth(tile) - (1.0 - level), 0.0, 1.0)
            coupling = kappa(tile) * (wet(tile) * other)
            return coupling / (1.0 + 2.0 * coupling)

        next_vel = [shifted(velocity, 1), shifted(velocity, IB)]
        next_wet = [shifted(wet, 1), shifted(wet, IB)]

        @once
        def face(tile):
            rims = [at - tile * LANES for at in range(IB - 1, CELLS, IB) if at // LANES == tile]
            rim = functools.reduce(jnp.logical_or, [lane == at for at in rims]) if rims else None
            across = next_wet[0](tile) if rim is None else jnp.where(rim, 0.0, next_wet[0](tile))
            speed = velocity(tile) + jnp.where(x_row, next_vel[0](tile), next_vel[1](tile))
            value = SCALE * speed * (wet(tile) * jnp.where(x_row, across, next_wet[1](tile)))
            w_ref[:, tile * LANES : (tile + 1) * LANES] = value
            return value

        face_x = once(lambda tile: jnp.where(x_row, face(tile), sublanes(face(tile), 2)))
        face_y = once(lambda tile: jnp.where(x_row, sublanes(face(tile), -2), face(tile)))
        five = once(lambda tile: 5.0 * state(tile))
        two = once(lambda tile: 2.0 * state(tile))

        def divergence(speed, distance):
            before, after = shifted(state, -distance), shifted(state, distance)
            lower = once(lambda tile: five(tile) - before(tile) + 2.0 * after(tile))
            upper = shifted(once(lambda tile: five(tile) - after(tile)), distance)

            @once
            def flux(tile):
                value = jnp.maximum(speed(tile), 0.0) * lower(tile)
                return value + jnp.minimum(speed(tile), 0.0) * (two(tile) + upper(tile))

            back = shifted(flux, -distance)
            for stage in (after, before, lower, upper, flux, back):
                for tile in range(TILES):
                    stage(tile)
            return once(lambda tile: flux(tile) - back(tile))

        for stage in (depth, wet, ratio, *next_vel, *next_wet, face):
            for tile in range(TILES):
                stage(tile)
        change_x, change_y = divergence(face_x, 1), divergence(face_y, IB)
        for tile in range(TILES):
            explicit = state(tile) - wet(tile) * (change_x(tile) + change_y(tile))
            other = jnp.where(even, sublanes(explicit, -1), sublanes(explicit, 1))
            value = jnp.where(live, explicit + ratio(tile) * (other - explicit), zero)
            stop = min((tile + 1) * LANES, CELLS)
            y_ref[rows, tile * LANES : stop] = value[:, : stop - tile * LANES]
            mixed = jnp.where(x_row, face(tile), jnp.where(even, ratio(tile), depth(tile)))
            z_ref[:, tile * LANES : (tile + 1) * LANES] = mixed

        pltpu.make_async_copy(
            y_ref.at[rows].reshape(2, 4, CELLS), base_ref.at[pl.ds(slot, 2)], y_sems.at[pair]).start()
        get_w, get_z = [lambda tile, ref=ref: ref[:, tile * LANES : (tile + 1) * LANES] for ref in (w_ref, z_ref)]
        groups = gap_groups(get_z, -2, 4, 8)
        east = lane % 2 == 0
        near, far = across_pair(state)
        normal = gap_groups(velocity, -1, 2, 8)[0]
        normal = jnp.where(x_row, normal, sublanes(normal, 2))
        rim_speed = lane_pick(groups, 4 * (lane // 2) + 2 * (lane % 2))
        rim_speed = jnp.where(x_row, rim_speed, sublanes(rim_speed, 2))
        sides = [(
            near, far, jnp.where(east, -normal, normal), jnp.where(east, -rim_speed, rim_speed),
            lane_pick(groups, 4 * (lane // 2) + 1 + lane % 2), lane_pick(groups, 4 * (lane // 2) + 3 * (lane % 2)),
        )]
        for outer, inner, edge, sign in ((0, IB, 0, 1.0), (CELLS - IB, CELLS - 2 * IB, CELLS - 2 * IB, -1.0)):
            normal, rim_speed = window(velocity, outer, 8), window(get_w, edge, 8)
            normal = sign * jnp.where(x_row, sublanes(normal, -2), normal)
            rim_speed = sign * jnp.where(x_row, sublanes(rim_speed, -2), rim_speed)
            sides.append((window(state, outer, 8), window(state, inner, 8), normal, rim_speed,
                          window(get_z, outer, 8), window(get_z, inner, 8)))
        for side, (near, far, normal, rim_speed, outer, inner) in enumerate(sides):
            values = (near, far, normal, jnp.where(live, jnp.maximum(rim_speed, 0.0), zero), wet_of(all_rows(outer, 3)),
                      wet_of(all_rows(inner, 3)), all_rows(outer, 2), all_rows(inner, 2))
            for index, value in enumerate(values):
                edge_ref[OWN * side + index, rows, :] = value
        edge_ref[OWN * SIDES, rows, :] = jnp.where(folded, 1.0, zero)

    pl.loop(0, pairs)(one_pair)
    for pair in range(pairs):
        slots = pl.ds(2 * (first + pair), 2)
        rows = y_ref.at[pl.ds(8 * pair, 8)].reshape(2, 4, CELLS)
        pltpu.make_async_copy(rows, base_ref.at[slots], y_sems.at[pair]).wait()


def finish_kernel(arrived_ref, edge_a_ref, edge_b_ref, base_ref, out_ref,
                  halo_ref, y_ref, own_ref, raw_ref, delta_ref, own_sems, in_sems, out_sems):
    count = out_ref.shape[0]
    pairs = count // 2
    rows = 4 * count
    split = edge_a_ref.shape[1]
    halo_copy = pltpu.make_async_copy(arrived_ref, halo_ref, own_sems.at[2])
    own_copies = [
        pltpu.make_async_copy(edge_a_ref, own_ref.at[:, pl.ds(0, split)], own_sems.at[0]),
        pltpu.make_async_copy(edge_b_ref, own_ref.at[:, pl.ds(split, rows - split)], own_sems.at[1]),
    ]
    in_copies = pair_copies(base_ref, y_ref, in_sems, 0, pairs)
    for copy in [halo_copy] + in_copies + own_copies:
        copy.start()
    lane = lane_of(rows)
    level = (lax.broadcasted_iota(jnp.int32, (rows, LANES), 0) % 2).astype(jnp.float32)

    def part(index):
        return halo_ref[index * count : (index + 1) * count, :]

    def assembled(index, parts):
        for chan, value in enumerate(parts):
            raw_ref[index, pl.ds(chan, count, stride=4), :] = value
        return raw_ref[index]

    mirror = jnp.where(lane < IB, IB - 1 - lane, lane)
    slot_lane = lane_of(count)
    halo_copy.wait()
    depth_x = rot(part(0), -SPARE)
    for index in range(1, 8):
        depth_x = jnp.where(slot_lane >= PIECE * index, rot(part(index), PIECE * index - SPARE), depth_x)
    x_raw = [[part(X_PART + chan) for chan in range(4)], [part(X_PART + 4 + chan) for chan in range(4)],
             [part(X_PART + 8 + chan % 2) for chan in range(4)], [depth_x] * 4]
    y_values = [list(range(4)), list(range(4, 8)), [8, 9, 8, 9], [10] * 4]
    x_halo, south_halo, north_raw = [], [], []
    for kind in range(4):
        raw = assembled(3 * kind, x_raw[kind])
        x_halo.append(jnp.where(lane % 2 == 0, rot(raw, 1), rot(raw, -1)))
        first, second = [assembled(3 * kind + 1 + half, [part(2 * value + half) for value in y_values[kind]])
                         for half in range(2)]
        south_halo.append(jnp.where(lane < HALF, rot(first, 64), rot(second, 64 + HALF)))
        north_raw.append(jnp.where(lane < HALF, first, rot(second, HALF)))
    for copy in own_copies:
        copy.wait()
    folded = own_ref[OWN * SIDES] > 0.0
    north_halo = []
    for kind, raw in enumerate(north_raw):
        turned = lane_take(raw, mirror)
        north_halo.append(jnp.where(folded, -turned if kind == 2 else turned, raw))

    for side, (out_near, out_far, out_normal, out_depth) in enumerate((x_halo, south_halo, north_halo)):
        near, far, normal, rim_speed, wet, inner_wet, ratio, inner_ratio = [
            own_ref[OWN * side + index] for index in range(OWN)]
        if side == 0:
            out_normal = jnp.where(lane % 2 == 0, -out_normal, out_normal)
            beyond = out_near - jnp.where(lane % 2 == 0, rot(near, -1), rot(near, 1))
        else:
            out_normal = -out_normal if side == 2 else out_normal
            beyond = out_near
        speed = SCALE * (normal + out_normal) * (wet * jnp.clip(out_depth - level, 0.0, 1.0))
        flux = jnp.maximum(speed, 0.0) * (5.0 * out_near + 2.0 * near - out_far)
        flux += jnp.minimum(speed, 0.0) * (2.0 * out_near + 5.0 * near - far)
        inner_flux = rim_speed * beyond
        for place, (change, share) in enumerate(((wet * (flux + inner_flux), ratio),
                                                 (-inner_wet * inner_flux, inner_ratio))):
            other = jnp.where(level == 0.0, pltpu.roll(change, rows - 1, 0), pltpu.roll(change, 1, 0))
            delta_ref[2 * side + place] = change + share * (other - change)

    lane = lane_of(8)
    out_copies = []
    for pair in range(pairs):
        mine = pl.ds(8 * pair, 8)
        in_copies[pair].wait()
        near, deep, south, south_in, north, north_in = [delta_ref[index, mine, :] for index in range(2 * SIDES)]
        groups = []
        for at in range(2):
            index = 2 * (lane // 4) + (lane % 4) // 2 + 64 * at
            outer, inner = lane_take(near, index), lane_take(deep, index)
            groups.append(jnp.where((lane % 4 == 1) | (lane % 4 == 2), outer, inner))
        placed = [(groups[gap // 32], 4 * (gap % 32), IB * gap - 2, 4) for gap in range(GAPS)]
        placed += [(south, 0, 0, IB), (south_in, 0, IB, IB)]
        placed += [(north, 0, CELLS - IB, IB), (north_in, 0, CELLS - 2 * IB, IB)]
        for tile in range(TILES):
            at, stop = tile * LANES, min((tile + 1) * LANES, CELLS)
            change = jnp.zeros((8, LANES), jnp.float32)
            for source, origin, start, wide in placed:
                low, high = max(start, at, 0), min(start + wide, stop)
                if low < high:
                    inside = (lane >= low - at) & (lane < high - at)
                    change += jnp.where(inside, rot(source, start - at - origin), 0.0)
            y_ref[mine, at:stop] = y_ref[mine, at:stop] + change[:, : stop - at]
        copy = pltpu.make_async_copy(
            y_ref.at[mine].reshape(2, 4, CELLS), out_ref.at[pl.ds(2 * pair, 2)], out_sems.at[pair])
        copy.start()
        out_copies.append(copy)
    for copy in out_copies:
        copy.wait()


def route_codes(block_owner, neighbours, fold_partner, slot_total):
    block_count = block_owner.shape[0]
    hits = block_owner[None, :] == jnp.arange(slot_total, dtype=jnp.int32)[:, None]
    links = jnp.concatenate([neighbours, fold_partner[:, None]], axis=1)
    linked = links[:, :, None] == jnp.arange(block_count, dtype=jnp.int32)[None, None, :]
    link_slots = jnp.max(jnp.where(linked, block_owner[None, None, :], -1), axis=2)
    link_slots = jnp.concatenate([link_slots, block_owner[:, None]], axis=1)
    return jnp.max(jnp.where(hits[:, :, None], link_slots[None], -1), axis=1)


def per_device(tracers, velocity, kappa, kmt, block_owner, neighbours, fold_partner):
    slot_count, chans = tracers.shape[:2]
    sub_count = lax.axis_size("sub")
    device_count = lax.axis_size("blk") * sub_count
    if device_count % PARTS or chans != 4 or slot_count % 2 or slot_count < 2 * FIRST_PAIRS + 2:
        raise ValueError("unsupported sizes")
    my_index = (lax.axis_index("blk") * sub_count + lax.axis_index("sub")).astype(jnp.int32).reshape(1)
    axes = ("blk", "sub")
    pairs = slot_count // 2
    slot_total = device_count * slot_count
    state_rows = 4 * slot_count
    f32 = jnp.float32
    in_hbm = pl.BlockSpec(memory_space=pltpu.HBM)
    anywhere = pl.BlockSpec(memory_space=pl.ANY)
    in_vmem = pl.BlockSpec(memory_space=pltpu.VMEM)
    in_smem = pl.BlockSpec(memory_space=pltpu.SMEM)
    dma = pltpu.SemaphoreType.DMA
    limit = pltpu.CompilerParams(vmem_limit_bytes=32 * 1024 * 1024)

    def exchanged(pieces):
        pieces = pieces.reshape(device_count, slot_count, 1, LANES)
        return lax.all_to_all(pieces, axes, 0, 0, tiled=True).reshape(slot_total, LANES)

    pack = pl.pallas_call(
        pack_kernel,
        out_shape=jax.ShapeDtypeStruct((slot_total, LANES), f32),
        in_specs=[in_hbm, in_hbm, in_hbm],
        out_specs=in_vmem,
        scratch_shapes=[
            pltpu.VMEM((state_rows, CELLS), f32),
            pltpu.VMEM((state_rows, CELLS), f32),
            pltpu.VMEM((slot_count, CELLS), f32),
            pltpu.VMEM((9, state_rows, LANES), f32),
            dma((pairs,)),
            dma((pairs,)),
            dma,
        ],
        cost_estimate=pl.CostEstimate(flops=4_000_000, bytes_accessed=2_400_000, transcendentals=0),
    )(tracers, velocity, kmt)
    held = exchanged(pack)
    codes = route_codes(block_owner, neighbours, fold_partner, slot_total)

    def bulk(first, some, codes, base):
        kernel = functools.partial(bulk_kernel, first)
        extra = [] if base is None else [base]
        if extra:
            kernel = lambda *refs: bulk_kernel(first, *refs[:6], *refs[7:])
        return pl.pallas_call(
            kernel,
            out_shape=[
                jax.ShapeDtypeStruct(tracers.shape, f32),
                jax.ShapeDtypeStruct((OWN * SIDES + 1, 8 * some, LANES), f32),
            ],
            in_specs=[in_smem, in_hbm, in_hbm, in_hbm, in_hbm, in_vmem] + [in_hbm] * len(extra),
            out_specs=[in_hbm, in_vmem],
            scratch_shapes=[
                pltpu.VMEM((8 * some, CELLS), f32),
                pltpu.VMEM((8 * some, CELLS), f32),
                pltpu.VMEM((8 * some, CELLS), f32),
                pltpu.VMEM((slot_count, CELLS), f32),
                pltpu.VMEM((slot_count, CELLS), f32),
                pltpu.VMEM((8 * some, CELLS), f32),
                pltpu.VMEM((8 * some, CELLS), f32),
                pltpu.VMEM((8, WIDE), f32),
                pltpu.VMEM((8, WIDE), f32),
                dma((some,)),
                dma((some,)),
                dma((some,)),
                dma((2,)),
            ],
            input_output_aliases={6: 0} if extra else {},
            compiler_params=limit,
            cost_estimate=pl.CostEstimate(flops=4_000_000 * some, bytes_accessed=800_000 * some, transcendentals=0),
        )(my_index, tracers, velocity, kmt, kappa, codes, *extra)

    base, edge_a = bulk(0, FIRST_PAIRS, codes, None)
    held, edge_a = lax.optimization_barrier((held, edge_a))

    routed_rows = PARTS * slot_count
    routed = pl.pallas_call(
        route_kernel,
        grid=(device_count // PARTS,),
        out_shape=jax.ShapeDtypeStruct((slot_total, LANES), f32),
        in_specs=[
            in_smem,
            pl.BlockSpec((routed_rows, 6), lambda step: (step, 0)),
            pl.BlockSpec((slot_total, LANES), lambda step: (0, 0)),
        ],
        out_specs=pl.BlockSpec((routed_rows, LANES), lambda step: (step, 0)),
        compiler_params=limit,
    )(my_index, codes, held)

    routed, base = lax.optimization_barrier((routed, base))
    base, edge_b = bulk(FIRST_PAIRS, pairs - FIRST_PAIRS, codes, base)
    halo = exchanged(routed)[: PARTS * slot_count]

    return pl.pallas_call(
        finish_kernel,
        out_shape=jax.ShapeDtypeStruct(tracers.shape, f32),
        in_specs=[anywhere, anywhere, anywhere, in_hbm],
        out_specs=in_hbm,
        scratch_shapes=[
            pltpu.VMEM((PARTS * slot_count, LANES), f32),
            pltpu.VMEM((state_rows, CELLS), f32),
            pltpu.VMEM((OWN * SIDES + 1, state_rows, LANES), f32),
            pltpu.VMEM((12, state_rows, LANES), f32),
            pltpu.VMEM((2 * SIDES, state_rows, LANES), f32),
            dma((3,)),
            dma((pairs,)),
            dma((pairs,)),
        ],
        input_output_aliases={3: 0},
        compiler_params=limit,
    )(halo, edge_a, edge_b, base)


def solution(mesh):
    placed = (
        P(("blk", "sub"), None, None),
        P(("blk", "sub"), None, None),
        P(("blk", "sub"), None),
        P(("blk", "sub"), None),
        P(),
        P(),
        P(),
    )
    return jax.shard_map(
        per_device,
        mesh=mesh,
        in_specs=placed,
        out_specs=P(("blk", "sub"), None, None),
        check_vma=False,
    )
```

```python
import functools

import jax
import jax.numpy as jnp
from jax import lax
from jax.experimental import pallas as pl
from jax.experimental.pallas import tpu as pltpu
from jax.sharding import PartitionSpec as P

IB = 90
JB = 60
CELLS = IB * JB
COURANT = 0.2
LANES = 128
TILES = -(-CELLS // LANES)
WIDE = TILES * LANES
GAPS = JB + 1
HALF = IB // 2
PARTS = 32
X_PART = 22
SPARE = 48
PIECE = 16
SCALE = COURANT / 12.0
SIDES = 3
OWN = 8
FIRST_PAIRS = 2


def lane_of(rows):
    return lax.broadcasted_iota(jnp.int32, (rows, LANES), 1)


def rot(value, shift):
    shift = shift % LANES
    return value if shift == 0 else pltpu.roll(value, shift, 1)


def sublanes(value, shift):
    return pltpu.roll(value, shift % 8, 0)


def once(make):
    held = {}

    def get(tile):
        if tile not in held:
            held[tile] = make(tile)
        return held[tile]

    return get


def shifted(get, distance):
    offset = distance % LANES
    turned = once(lambda tile: rot(get(tile), -offset))

    def make(tile):
        low = tile + distance // LANES
        first = turned(low) if 0 <= low < TILES else jnp.zeros((8, LANES), jnp.float32)
        second = turned(low + 1) if 0 <= low + 1 < TILES else jnp.zeros((8, LANES), jnp.float32)
        return jnp.where(lane_of(8) < LANES - offset, first, second)

    return once(make)


def window(get, start, rows):
    tile, offset = start // LANES, start % LANES
    head = rot(get(tile), -offset)
    if offset == 0 or tile + 1 >= TILES:
        return head
    return jnp.where(lane_of(rows) < LANES - offset, head, rot(get(tile + 1), -offset))


def gap_groups(get, first, wide, rows):
    lane = lane_of(rows)
    held = LANES // wide
    result = []
    for at in range(0, GAPS, held):
        value = jnp.zeros((rows, LANES), jnp.float32)
        for gap in range(at, min(at + held, GAPS)):
            start = IB * gap + first
            place = (gap - at) * wide
            for tile in range(max(start, 0) // LANES, min(start + wide - 1, CELLS - 1) // LANES + 1):
                low = max(start, tile * LANES, 0)
                value = jnp.where(lane >= place + low - start, rot(get(tile), place - start + tile * LANES), value)
        result.append(value)
    return result


def lane_take(value, index):
    return jnp.take_along_axis(value, index, axis=1, mode="promise_in_bounds")


def lane_pick(pair, index):
    return jnp.where(index < LANES, lane_take(pair[0], index % LANES), lane_take(pair[1], index % LANES))


def tile_getter(ref, rows, count):
    def get(tile):
        if tile + 1 < TILES:
            return ref[rows, tile * LANES : (tile + 1) * LANES]
        rest = jnp.zeros((count, WIDE - CELLS), jnp.float32)
        return jnp.concatenate([ref[rows, tile * LANES : CELLS], rest], axis=1)

    return get


def across_pair(get):
    lane = lane_of(8)
    groups = gap_groups(get, -2, 4, 8)
    return lane_pick(groups, 4 * (lane // 2) + 1 + lane % 2), lane_pick(groups, 4 * (lane // 2) + 3 * (lane % 2))


def slots_getter(ref, pair):
    def get(tile):
        columns = slice(tile * LANES, min((tile + 1) * LANES, CELLS))
        both = jnp.concatenate([ref[2 * pair, :, columns], ref[2 * pair + 1, :, columns]], axis=0)
        if tile + 1 < TILES:
            return both
        return jnp.concatenate([both, jnp.zeros((8, WIDE - CELLS), jnp.float32)], axis=1)

    return once(get)


def slot_copies(source, target, sems):
    count = source.shape[0]
    return [pltpu.make_async_copy(source.at[pl.ds(at, 2)], target.at[pl.ds(at, 2)], sems.at[at // 2])
            for at in range(0, count, 2)]


def joined(south, north, half, rows):
    if half == 0:
        return jnp.where(lane_of(rows) < 64, south, rot(north, 64))
    return jnp.where(lane_of(rows) < 64, rot(south, -HALF), rot(north, 64 - HALF))


def pair_copies(source, target, sems, first, pairs):
    copies = []
    for pair in range(pairs):
        into = target.at[pl.ds(8 * pair, 8)].reshape(2, 4, CELLS)
        copies.append(pltpu.make_async_copy(source.at[pl.ds(2 * (first + pair), 2)], into, sems.at[pair]))
    return copies


def pack_kernel(tracer_ref, velocity_ref, depth_ref, out_ref, x_ref, v_ref, d_ref, strip_ref, x_sems, v_sems, d_sem):
    count = depth_ref.shape[0]
    pairs = count // 2
    x_copies = slot_copies(tracer_ref, x_ref, x_sems)
    v_copies = slot_copies(velocity_ref, v_ref, v_sems)
    d_copy = pltpu.make_async_copy(depth_ref, d_ref, d_sem)
    for pair in range(pairs):
        x_copies[pair].start()
        v_copies[pair].start()
    d_copy.start()
    for pair in range(pairs):
        rows = pl.ds(8 * pair, 8)
        x_copies[pair].wait()
        get_x = slots_getter(x_ref, pair)
        near, far = across_pair(get_x)
        south = [window(get_x, 0, 8), window(get_x, IB, 8)]
        north = [window(get_x, CELLS - IB, 8), window(get_x, CELLS - 2 * IB, 8)]
        v_copies[pair].wait()
        get_v = slots_getter(v_ref, pair)
        v_south, v_north = window(get_v, 0, 8), window(get_v, CELLS - IB, 8)
        strips = [joined(south[0], north[0], half, 8) for half in range(2)]
        strips += [joined(south[1], north[1], half, 8) for half in range(2)]
        strips += [joined(v_south, v_north, half, 8) for half in range(2)]
        strips += [near, far, gap_groups(get_v, -1, 2, 8)[0]]
        for index, strip in enumerate(strips):
            strip_ref[index, rows, :] = strip

    d_copy.wait()
    if out_ref.shape[0] > PARTS * count:
        rest = out_ref.shape[0] - PARTS * count
        out_ref[PARTS * count :, :] = jnp.zeros((rest, LANES), jnp.float32)
    slot_lane = lane_of(count)
    get_d = tile_getter(d_ref, slice(None), count)
    d_south, d_north = window(get_d, 0, count), window(get_d, CELLS - IB, count)
    d_gaps = gap_groups(get_d, -1, 2, count)[0]
    spare = (slot_lane >= SPARE) & (slot_lane < SPARE + PIECE)

    def put(part, value):
        out_ref[part * count : (part + 1) * count, :] = value

    for chan in range(4):
        rows = pl.ds(chan, count, stride=4)
        for half in range(2):
            for deep in range(2):
                part = 2 * (4 * deep + chan) + half
                value = strip_ref[2 * deep + half, rows, :]
                if part < 8:
                    value = jnp.where(spare, rot(d_gaps, SPARE - PIECE * part), value)
                put(part, value)
            if chan >= 2:
                put(2 * (8 + chan - 2) + half, strip_ref[4 + half, rows, :])
        put(X_PART + chan, strip_ref[6, rows, :])
        put(X_PART + 4 + chan, strip_ref[7, rows, :])
        if chan < 2:
            put(X_PART + 8 + chan, strip_ref[8, rows, :])
    for half in range(2):
        put(20 + half, joined(d_south, d_north, half, count))


def route_kernel(part_ref, code_ref, held_ref, out_ref):
    total = held_ref.shape[0]
    rows = out_ref.shape[0]
    part = part_ref[0]
    picked = [jnp.zeros((rows, 2 * LANES), jnp.float32) for _ in range(5)]
    for start in range(0, total, rows):
        held = held_ref[start : start + rows, :]
        high = held.astype(jnp.bfloat16)
        low = (held - high.astype(jnp.float32)).astype(jnp.bfloat16)
        halves = jnp.concatenate([high, low], axis=1)
        source = lax.broadcasted_iota(jnp.int32, (rows, rows), 1) + start
        for side in range(5):
            one_hot = jnp.where(code_ref[:, side : side + 1] == source, 1.0, 0.0).astype(jnp.bfloat16)
            picked[side] += jnp.dot(one_hot, halves, preferred_element_type=jnp.float32)
    west, east, south, north, fold = [value[:, :LANES] + value[:, LANES:] for value in picked]
    lane = lane_of(rows)
    along_x = (part >= X_PART) | ((part < 8) & (lane >= SPARE) & (lane < SPARE + PIECE))
    x_side = jnp.where(lane % 2 == 0, west, east)
    y_side = jnp.where(lane < 64, north + rot(fold, 64), south)
    out_ref[...] = jnp.where(along_x, x_side, y_side)


def bulk_kernel(first, my_ref, tracer_ref, velocity_ref, depth_ref, kappa_ref, code_ref,
                base_ref, edge_ref, y_ref, x_ref, v_ref, d_ref, k_ref, d8_ref, k8_ref, w_ref, z_ref, x_sems, v_sems, y_sems, d_sems):
    count = depth_ref.shape[0]
    pairs = edge_ref.shape[1] // 8
    x_copies = pair_copies(tracer_ref, x_ref, x_sems, first, pairs)
    v_copies = pair_copies(velocity_ref, v_ref, v_sems, first, pairs)
    d_copy = pltpu.make_async_copy(depth_ref, d_ref, d_sems.at[0])
    k_copy = pltpu.make_async_copy(kappa_ref, k_ref, d_sems.at[1])
    d_copy.start()
    k_copy.start()
    for pair in range(pairs):
        v_copies[pair].start()
        x_copies[pair].start()
    lane = lane_of(8)
    row = lax.broadcasted_iota(jnp.int32, (8, LANES), 0)
    x_row, even, place = row % 4 < 2, row % 2 == 0, row % 4
    level = (row % 2).astype(jnp.float32)
    zero = jnp.zeros((8, LANES), jnp.float32)

    def all_rows(value, chosen):
        result = value
        for at in range(4):
            if at != chosen:
                result = jnp.where(place == at, sublanes(value, at - chosen), result)
        return result

    def wet_of(depth):
        return jnp.clip(depth - level, 0.0, 1.0)

    for copy, source, target in ((d_copy, d_ref, d8_ref), (k_copy, k_ref, k8_ref)):
        copy.wait()
        for pair in range(pairs):
            slot = 2 * (first + pair)
            for start in range(0, CELLS, LANES):
                columns = slice(start, min(start + LANES, CELLS))
                shape = (8, columns.stop - start)
                top, low = [jnp.broadcast_to(source[slot + at : slot + at + 1, columns], shape) for at in range(2)]
                target[8 * pair : 8 * pair + 8, columns] = jnp.where(row[:, : shape[1]] < 4, top, low)

    def one_pair(pair):
        slot = 2 * (first + pair)
        rows = pl.ds(pl.multiple_of(8 * pair, 8), 8)
        for source, target, sems in ((velocity_ref, v_ref, v_sems), (tracer_ref, x_ref, x_sems)):
            pltpu.make_async_copy(
                source.at[pl.ds(0, 2)], target.at[rows].reshape(2, 4, CELLS), sems.at[pair]).wait()

        codes = [code_ref[pl.ds(my_ref[0] * count + slot + at, 1), :] for at in range(2)]

        def flag(column):
            pieces = [jnp.broadcast_to(code[:, column : column + 1], (8, LANES)) for code in codes]
            return jnp.where(row < 4, pieces[0], pieces[1]) >= 0

        live, folded = flag(5), flag(4)
        state, velocity = once(tile_getter(x_ref, rows, 8)), once(tile_getter(v_ref, rows, 8))
        depth, kappa = once(tile_getter(d8_ref, rows, 8)), once(tile_getter(k8_ref, rows, 8))
        wet = once(lambda tile: wet_of(depth(tile)))

        @once
        def ratio(tile):
            other = jnp.clip(depth(tile) - (1.0 - level), 0.0, 1.0)
            coupling = kappa(tile) * (wet(tile) * other)
            return coupling / (1.0 + 2.0 * coupling)

        next_vel = [shifted(velocity, 1), shifted(velocity, IB)]
        next_wet = [shifted(wet, 1), shifted(wet, IB)]

        @once
        def face(tile):
            rims = [at - tile * LANES for at in range(IB - 1, CELLS, IB) if at // LANES == tile]
            rim = functools.reduce(jnp.logical_or, [lane == at for at in rims]) if rims else None
            across = next_wet[0](tile) if rim is None else jnp.where(rim, 0.0, next_wet[0](tile))
            speed = velocity(tile) + jnp.where(x_row, next_vel[0](tile), next_vel[1](tile))
            value = SCALE * speed * (wet(tile) * jnp.where(x_row, across, next_wet[1](tile)))
            w_ref[:, tile * LANES : (tile + 1) * LANES] = value
            return value

        face_x = once(lambda tile: jnp.where(x_row, face(tile), sublanes(face(tile), 2)))
        face_y = once(lambda tile: jnp.where(x_row, sublanes(face(tile), -2), face(tile)))
        five = once(lambda tile: 5.0 * state(tile))
        two = once(lambda tile: 2.0 * state(tile))

        def divergence(speed, distance):
            before, after = shifted(state, -distance), shifted(state, distance)
            lower = once(lambda tile: five(tile) - before(tile) + 2.0 * after(tile))
            upper = shifted(once(lambda tile: five(tile) - after(tile)), distance)

            @once
            def flux(tile):
                value = jnp.maximum(speed(tile), 0.0) * lower(tile)
                return value + jnp.minimum(speed(tile), 0.0) * (two(tile) + upper(tile))

            back = shifted(flux, -distance)
            for stage in (after, before, lower, upper, flux, back):
                for tile in range(TILES):
                    stage(tile)
            return once(lambda tile: flux(tile) - back(tile))

        for stage in (depth, wet, ratio, *next_vel, *next_wet, face):
            for tile in range(TILES):
                stage(tile)
        change_x, change_y = divergence(face_x, 1), divergence(face_y, IB)
        for tile in range(TILES):
            explicit = state(tile) - wet(tile) * (change_x(tile) + change_y(tile))
            other = jnp.where(even, sublanes(explicit, -1), sublanes(explicit, 1))
            value = jnp.where(live, explicit + ratio(tile) * (other - explicit), zero)
            stop = min((tile + 1) * LANES, CELLS)
            y_ref[rows, tile * LANES : stop] = value[:, : stop - tile * LANES]
            mixed = jnp.where(x_row, face(tile), jnp.where(even, ratio(tile), depth(tile)))
            z_ref[:, tile * LANES : (tile + 1) * LANES] = mixed

        pltpu.make_async_copy(
            y_ref.at[rows].reshape(2, 4, CELLS), base_ref.at[pl.ds(slot, 2)], y_sems.at[pair]).start()
        get_w, get_z = [lambda tile, ref=ref: ref[:, tile * LANES : (tile + 1) * LANES] for ref in (w_ref, z_ref)]
        groups = gap_groups(get_z, -2, 4, 8)
        east = lane % 2 == 0
        near, far = across_pair(state)
        normal = gap_groups(velocity, -1, 2, 8)[0]
        normal = jnp.where(x_row, normal, sublanes(normal, 2))
        rim_speed = lane_pick(groups, 4 * (lane // 2) + 2 * (lane % 2))
        rim_speed = jnp.where(x_row, rim_speed, sublanes(rim_speed, 2))
        sides = [(
            near, far, jnp.where(east, -normal, normal), jnp.where(east, -rim_speed, rim_speed),
            lane_pick(groups, 4 * (lane // 2) + 1 + lane % 2), lane_pick(groups, 4 * (lane // 2) + 3 * (lane % 2)),
        )]
        for outer, inner, edge, sign in ((0, IB, 0, 1.0), (CELLS - IB, CELLS - 2 * IB, CELLS - 2 * IB, -1.0)):
            normal, rim_speed = window(velocity, outer, 8), window(get_w, edge, 8)
            normal = sign * jnp.where(x_row, sublanes(normal, -2), normal)
            rim_speed = sign * jnp.where(x_row, sublanes(rim_speed, -2), rim_speed)
            sides.append((window(state, outer, 8), window(state, inner, 8), normal, rim_speed,
                          window(get_z, outer, 8), window(get_z, inner, 8)))
        for side, (near, far, normal, rim_speed, outer, inner) in enumerate(sides):
            values = (near, far, normal, jnp.where(live, jnp.maximum(rim_speed, 0.0), zero), wet_of(all_rows(outer, 3)),
                      wet_of(all_rows(inner, 3)), all_rows(outer, 2), all_rows(inner, 2))
            for index, value in enumerate(values):
                edge_ref[OWN * side + index, rows, :] = value
        edge_ref[OWN * SIDES, rows, :] = jnp.where(folded, 1.0, zero)

    pl.loop(0, pairs)(one_pair)
    for pair in range(pairs):
        slots = pl.ds(2 * (first + pair), 2)
        rows = y_ref.at[pl.ds(8 * pair, 8)].reshape(2, 4, CELLS)
        pltpu.make_async_copy(rows, base_ref.at[slots], y_sems.at[pair]).wait()


def finish_kernel(halo_ref, edge_a_ref, edge_b_ref, base_ref, out_ref,
                  y_ref, own_ref, raw_ref, delta_ref, own_sems, in_sems, out_sems):
    count = out_ref.shape[0]
    pairs = count // 2
    rows = 4 * count
    split = edge_a_ref.shape[1]
    own_copies = [
        pltpu.make_async_copy(edge_a_ref, own_ref.at[:, pl.ds(0, split)], own_sems.at[0]),
        pltpu.make_async_copy(edge_b_ref, own_ref.at[:, pl.ds(split, rows - split)], own_sems.at[1]),
    ]
    in_copies = slot_copies(base_ref, y_ref, in_sems)
    for copy in own_copies + in_copies:
        copy.start()
    lane = lane_of(rows)
    level = (lax.broadcasted_iota(jnp.int32, (rows, LANES), 0) % 2).astype(jnp.float32)

    def part(index):
        return halo_ref[index * count : (index + 1) * count, :]

    def assembled(index, parts):
        for chan, value in enumerate(parts):
            raw_ref[index, pl.ds(chan, count, stride=4), :] = value
        return raw_ref[index]

    mirror = jnp.where(lane < IB, IB - 1 - lane, lane)
    slot_lane = lane_of(count)
    depth_x = rot(part(0), -SPARE)
    for index in range(1, 8):
        depth_x = jnp.where(slot_lane >= PIECE * index, rot(part(index), PIECE * index - SPARE), depth_x)
    x_raw = [[part(X_PART + chan) for chan in range(4)], [part(X_PART + 4 + chan) for chan in range(4)],
             [part(X_PART + 8 + chan % 2) for chan in range(4)], [depth_x] * 4]
    y_values = [list(range(4)), list(range(4, 8)), [8, 9, 8, 9], [10] * 4]
    x_halo, south_halo, north_raw = [], [], []
    for kind in range(4):
        raw = assembled(3 * kind, x_raw[kind])
        x_halo.append(jnp.where(lane % 2 == 0, rot(raw, 1), rot(raw, -1)))
        first, second = [assembled(3 * kind + 1 + half, [part(2 * value + half) for value in y_values[kind]])
                         for half in range(2)]
        south_halo.append(jnp.where(lane < HALF, rot(first, 64), rot(second, 64 + HALF)))
        north_raw.append(jnp.where(lane < HALF, first, rot(second, HALF)))
    for copy in own_copies:
        copy.wait()
    folded = own_ref[OWN * SIDES] > 0.0
    north_halo = []
    for kind, raw in enumerate(north_raw):
        turned = lane_take(raw, mirror)
        north_halo.append(jnp.where(folded, -turned if kind == 2 else turned, raw))

    for side, (out_near, out_far, out_normal, out_depth) in enumerate((x_halo, south_halo, north_halo)):
        near, far, normal, rim_speed, wet, inner_wet, ratio, inner_ratio = [
            own_ref[OWN * side + index] for index in range(OWN)]
        if side == 0:
            out_normal = jnp.where(lane % 2 == 0, -out_normal, out_normal)
            beyond = out_near - jnp.where(lane % 2 == 0, rot(near, -1), rot(near, 1))
        else:
            out_normal = -out_normal if side == 2 else out_normal
            beyond = out_near
        speed = SCALE * (normal + out_normal) * (wet * jnp.clip(out_depth - level, 0.0, 1.0))
        flux = jnp.maximum(speed, 0.0) * (5.0 * out_near + 2.0 * near - out_far)
        flux += jnp.minimum(speed, 0.0) * (2.0 * out_near + 5.0 * near - far)
        inner_flux = rim_speed * beyond
        for place, (change, share) in enumerate(((wet * (flux + inner_flux), ratio),
                                                 (-inner_wet * inner_flux, inner_ratio))):
            other = jnp.where(level == 0.0, pltpu.roll(change, rows - 1, 0), pltpu.roll(change, 1, 0))
            delta_ref[2 * side + place] = change + share * (other - change)

    lane = lane_of(8)
    out_copies = slot_copies(y_ref, out_ref, out_sems)
    for pair in range(pairs):
        mine = pl.ds(8 * pair, 8)
        in_copies[pair].wait()
        near, deep, south, south_in, north, north_in = [delta_ref[index, mine, :] for index in range(2 * SIDES)]
        groups = []
        for at in range(2):
            index = 2 * (lane // 4) + (lane % 4) // 2 + 64 * at
            outer, inner = lane_take(near, index), lane_take(deep, index)
            groups.append(jnp.where((lane % 4 == 1) | (lane % 4 == 2), outer, inner))
        placed = [(groups[gap // 32], 4 * (gap % 32), IB * gap - 2, 4) for gap in range(GAPS)]
        placed += [(south, 0, 0, IB), (south_in, 0, IB, IB)]
        placed += [(north, 0, CELLS - IB, IB), (north_in, 0, CELLS - 2 * IB, IB)]
        for tile in range(TILES):
            at, stop = tile * LANES, min((tile + 1) * LANES, CELLS)
            change = jnp.zeros((8, LANES), jnp.float32)
            for source, origin, start, wide in placed:
                low, high = max(start, at, 0), min(start + wide, stop)
                if low < high:
                    inside = (lane >= low - at) & (lane < high - at)
                    change += jnp.where(inside, rot(source, start - at - origin), 0.0)
            for slot in range(2):
                index = 2 * pair + slot
                part_of = change[4 * slot : 4 * slot + 4, : stop - at]
                y_ref[index, :, at:stop] = y_ref[index, :, at:stop] + part_of
        out_copies[pair].start()
    for copy in out_copies:
        copy.wait()


def route_codes(block_owner, neighbours, fold_partner, slot_total):
    block_count = block_owner.shape[0]
    hits = block_owner[None, :] == jnp.arange(slot_total, dtype=jnp.int32)[:, None]
    links = jnp.concatenate([neighbours, fold_partner[:, None]], axis=1)
    linked = links[:, :, None] == jnp.arange(block_count, dtype=jnp.int32)[None, None, :]
    link_slots = jnp.max(jnp.where(linked, block_owner[None, None, :], -1), axis=2)
    link_slots = jnp.concatenate([link_slots, block_owner[:, None]], axis=1)
    return jnp.max(jnp.where(hits[:, :, None], link_slots[None], -1), axis=1)


def per_device(tracers, velocity, kappa, kmt, block_owner, neighbours, fold_partner):
    slot_count, chans = tracers.shape[:2]
    sub_count = lax.axis_size("sub")
    device_count = lax.axis_size("blk") * sub_count
    if device_count % PARTS or chans != 4 or slot_count % 2 or slot_count < 2 * FIRST_PAIRS + 2:
        raise ValueError("unsupported sizes")
    my_index = (lax.axis_index("blk") * sub_count + lax.axis_index("sub")).astype(jnp.int32).reshape(1)
    axes = ("blk", "sub")
    pairs = slot_count // 2
    slot_total = device_count * slot_count
    state_rows = 4 * slot_count
    f32 = jnp.float32
    in_hbm = pl.BlockSpec(memory_space=pltpu.HBM)
    anywhere = pl.BlockSpec(memory_space=pl.ANY)
    in_vmem = pl.BlockSpec(memory_space=pltpu.VMEM)
    in_smem = pl.BlockSpec(memory_space=pltpu.SMEM)
    dma = pltpu.SemaphoreType.DMA
    limit = pltpu.CompilerParams(vmem_limit_bytes=32 * 1024 * 1024)

    def exchanged(pieces):
        pieces = pieces.reshape(device_count, slot_count, 1, LANES)
        return lax.all_to_all(pieces, axes, 0, 0, tiled=True).reshape(slot_total, LANES)

    pack = pl.pallas_call(
        pack_kernel,
        out_shape=jax.ShapeDtypeStruct((slot_total, LANES), f32),
        in_specs=[in_hbm, in_hbm, in_hbm],
        out_specs=in_vmem,
        scratch_shapes=[
            pltpu.VMEM(tracers.shape, f32),
            pltpu.VMEM(tracers.shape, f32),
            pltpu.VMEM((slot_count, CELLS), f32),
            pltpu.VMEM((9, state_rows, LANES), f32),
            dma((pairs,)),
            dma((pairs,)),
            dma,
        ],
        cost_estimate=pl.CostEstimate(flops=4_000_000, bytes_accessed=2_400_000, transcendentals=0),
    )(tracers, velocity, kmt)
    held = exchanged(pack)
    codes = route_codes(block_owner, neighbours, fold_partner, slot_total)

    def bulk(first, some, codes, base):
        kernel = functools.partial(bulk_kernel, first)
        extra = [] if base is None else [base]
        if extra:
            kernel = lambda *refs: bulk_kernel(first, *refs[:6], *refs[7:])
        return pl.pallas_call(
            kernel,
            out_shape=[
                jax.ShapeDtypeStruct(tracers.shape, f32),
                jax.ShapeDtypeStruct((OWN * SIDES + 1, 8 * some, LANES), f32),
            ],
            in_specs=[in_smem, in_hbm, in_hbm, in_hbm, in_hbm, in_vmem] + [in_hbm] * len(extra),
            out_specs=[in_hbm, in_vmem],
            scratch_shapes=[
                pltpu.VMEM((8 * some, CELLS), f32),
                pltpu.VMEM((8 * some, CELLS), f32),
                pltpu.VMEM((8 * some, CELLS), f32),
                pltpu.VMEM((slot_count, CELLS), f32),
                pltpu.VMEM((slot_count, CELLS), f32),
                pltpu.VMEM((8 * some, CELLS), f32),
                pltpu.VMEM((8 * some, CELLS), f32),
                pltpu.VMEM((8, WIDE), f32),
                pltpu.VMEM((8, WIDE), f32),
                dma((some,)),
                dma((some,)),
                dma((some,)),
                dma((2,)),
            ],
            input_output_aliases={6: 0} if extra else {},
            compiler_params=limit,
            cost_estimate=pl.CostEstimate(flops=4_000_000 * some, bytes_accessed=800_000 * some, transcendentals=0),
        )(my_index, tracers, velocity, kmt, kappa, codes, *extra)

    base, edge_a = bulk(0, FIRST_PAIRS, codes, None)
    held, edge_a = lax.optimization_barrier((held, edge_a))

    routed_rows = PARTS * slot_count
    routed = pl.pallas_call(
        route_kernel,
        grid=(device_count // PARTS,),
        out_shape=jax.ShapeDtypeStruct((slot_total, LANES), f32),
        in_specs=[
            in_smem,
            pl.BlockSpec((routed_rows, 6), lambda step: (step, 0)),
            pl.BlockSpec((slot_total, LANES), lambda step: (0, 0)),
        ],
        out_specs=pl.BlockSpec((routed_rows, LANES), lambda step: (step, 0)),
        compiler_params=limit,
    )(my_index, codes, held)

    routed, base = lax.optimization_barrier((routed, base))
    base, edge_b = bulk(FIRST_PAIRS, pairs - FIRST_PAIRS, codes, base)
    halo = exchanged(routed)[: PARTS * slot_count]

    return pl.pallas_call(
        finish_kernel,
        out_shape=jax.ShapeDtypeStruct(tracers.shape, f32),
        in_specs=[in_vmem, anywhere, anywhere, in_hbm],
        out_specs=in_hbm,
        scratch_shapes=[
            pltpu.VMEM(tracers.shape, f32),
            pltpu.VMEM((OWN * SIDES + 1, state_rows, LANES), f32),
            pltpu.VMEM((12, state_rows, LANES), f32),
            pltpu.VMEM((2 * SIDES, state_rows, LANES), f32),
            dma((2,)),
            dma((pairs,)),
            dma((pairs,)),
        ],
        input_output_aliases={3: 0},
        compiler_params=limit,
    )(halo, edge_a, edge_b, base)


def solution(mesh):
    placed = (
        P(("blk", "sub"), None, None),
        P(("blk", "sub"), None, None),
        P(("blk", "sub"), None),
        P(("blk", "sub"), None),
        P(),
        P(),
        P(),
    )
    return jax.shard_map(
        per_device,
        mesh=mesh,
        in_specs=placed,
        out_specs=P(("blk", "sub"), None, None),
        check_vma=False,
    )
```

```python
import functools

import jax
import jax.numpy as jnp
from jax import lax
from jax.experimental import pallas as pl
from jax.experimental.pallas import tpu as pltpu
from jax.sharding import PartitionSpec as P

IB = 90
JB = 60
CELLS = IB * JB
COURANT = 0.2
LANES = 128
TILES = -(-CELLS // LANES)
WIDE = TILES * LANES
GAPS = JB + 1
HALF = IB // 2
PARTS = 32
X_PART = 22
SPARE = 48
PIECE = 16
SCALE = COURANT / 12.0
SIDES = 3
OWN = 8
FIRST_PAIRS = 2


def lane_of(rows):
    return lax.broadcasted_iota(jnp.int32, (rows, LANES), 1)


def rot(value, shift):
    shift = shift % LANES
    return value if shift == 0 else pltpu.roll(value, shift, 1)


def sublanes(value, shift):
    return pltpu.roll(value, shift % 8, 0)


def once(make):
    held = {}

    def get(tile):
        if tile not in held:
            held[tile] = make(tile)
        return held[tile]

    return get


def shifted(get, distance):
    offset = distance % LANES
    turned = once(lambda tile: rot(get(tile), -offset))

    def make(tile):
        low = tile + distance // LANES
        first = turned(low) if 0 <= low < TILES else jnp.zeros((8, LANES), jnp.float32)
        second = turned(low + 1) if 0 <= low + 1 < TILES else jnp.zeros((8, LANES), jnp.float32)
        return jnp.where(lane_of(8) < LANES - offset, first, second)

    return once(make)


def window(get, start, rows):
    tile, offset = start // LANES, start % LANES
    head = rot(get(tile), -offset)
    if offset == 0 or tile + 1 >= TILES:
        return head
    return jnp.where(lane_of(rows) < LANES - offset, head, rot(get(tile + 1), -offset))


def gap_groups(get, first, wide, rows):
    lane = lane_of(rows)
    held = LANES // wide
    result = []
    for at in range(0, GAPS, held):
        value = jnp.zeros((rows, LANES), jnp.float32)
        for gap in range(at, min(at + held, GAPS)):
            start = IB * gap + first
            place = (gap - at) * wide
            for tile in range(max(start, 0) // LANES, min(start + wide - 1, CELLS - 1) // LANES + 1):
                low = max(start, tile * LANES, 0)
                value = jnp.where(lane >= place + low - start, rot(get(tile), place - start + tile * LANES), value)
        result.append(value)
    return result


def lane_take(value, index):
    return jnp.take_along_axis(value, index, axis=1, mode="promise_in_bounds")


def lane_pick(pair, index):
    return jnp.where(index < LANES, lane_take(pair[0], index % LANES), lane_take(pair[1], index % LANES))


def tile_getter(ref, rows, count):
    def get(tile):
        if tile + 1 < TILES:
            return ref[rows, tile * LANES : (tile + 1) * LANES]
        rest = jnp.zeros((count, WIDE - CELLS), jnp.float32)
        return jnp.concatenate([ref[rows, tile * LANES : CELLS], rest], axis=1)

    return get


def across_pair(get):
    lane = lane_of(8)
    groups = gap_groups(get, -2, 4, 8)
    return lane_pick(groups, 4 * (lane // 2) + 1 + lane % 2), lane_pick(groups, 4 * (lane // 2) + 3 * (lane % 2))


def joined(south, north, half, rows):
    if half == 0:
        return jnp.where(lane_of(rows) < 64, south, rot(north, 64))
    return jnp.where(lane_of(rows) < 64, rot(south, -HALF), rot(north, 64 - HALF))


def pair_copies(source, target, sems, first, pairs):
    copies = []
    for pair in range(pairs):
        into = target.at[pl.ds(8 * pair, 8)].reshape(2, 4, CELLS)
        copies.append(pltpu.make_async_copy(source.at[pl.ds(2 * (first + pair), 2)], into, sems.at[pair]))
    return copies


def pack_kernel(tracer_ref, velocity_ref, depth_ref, out_ref, x_ref, v_ref, d_ref, strip_ref, x_sems, v_sems, d_sem):
    count = depth_ref.shape[0]
    pairs = count // 2
    x_copies = pair_copies(tracer_ref, x_ref, x_sems, 0, pairs)
    v_copies = pair_copies(velocity_ref, v_ref, v_sems, 0, pairs)
    d_copy = pltpu.make_async_copy(depth_ref, d_ref, d_sem)
    for pair in range(pairs):
        x_copies[pair].start()
        v_copies[pair].start()
    d_copy.start()
    for pair in range(pairs):
        rows = pl.ds(8 * pair, 8)
        x_copies[pair].wait()
        get_x = tile_getter(x_ref, rows, 8)
        near, far = across_pair(get_x)
        south = [window(get_x, 0, 8), window(get_x, IB, 8)]
        north = [window(get_x, CELLS - IB, 8), window(get_x, CELLS - 2 * IB, 8)]
        v_copies[pair].wait()
        get_v = tile_getter(v_ref, rows, 8)
        v_south, v_north = window(get_v, 0, 8), window(get_v, CELLS - IB, 8)
        strips = [joined(south[0], north[0], half, 8) for half in range(2)]
        strips += [joined(south[1], north[1], half, 8) for half in range(2)]
        strips += [joined(v_south, v_north, half, 8) for half in range(2)]
        strips += [near, far, gap_groups(get_v, -1, 2, 8)[0]]
        for index, strip in enumerate(strips):
            strip_ref[index, rows, :] = strip

    d_copy.wait()
    if out_ref.shape[0] > PARTS * count:
        rest = out_ref.shape[0] - PARTS * count
        out_ref[PARTS * count :, :] = jnp.zeros((rest, LANES), jnp.float32)
    slot_lane = lane_of(count)
    get_d = tile_getter(d_ref, slice(None), count)
    d_south, d_north = window(get_d, 0, count), window(get_d, CELLS - IB, count)
    d_gaps = gap_groups(get_d, -1, 2, count)[0]
    spare = (slot_lane >= SPARE) & (slot_lane < SPARE + PIECE)

    def put(part, value):
        out_ref[part * count : (part + 1) * count, :] = value

    for chan in range(4):
        rows = pl.ds(chan, count, stride=4)
        for half in range(2):
            for deep in range(2):
                part = 2 * (4 * deep + chan) + half
                value = strip_ref[2 * deep + half, rows, :]
                if part < 8:
                    value = jnp.where(spare, rot(d_gaps, SPARE - PIECE * part), value)
                put(part, value)
            if chan >= 2:
                put(2 * (8 + chan - 2) + half, strip_ref[4 + half, rows, :])
        put(X_PART + chan, strip_ref[6, rows, :])
        put(X_PART + 4 + chan, strip_ref[7, rows, :])
        if chan < 2:
            put(X_PART + 8 + chan, strip_ref[8, rows, :])
    for half in range(2):
        put(20 + half, joined(d_south, d_north, half, count))


def route_kernel(part_ref, code_ref, held_ref, out_ref):
    total = held_ref.shape[0]
    rows = out_ref.shape[0]
    part = part_ref[0]
    picked = [jnp.zeros((rows, 2 * LANES), jnp.float32) for _ in range(5)]
    for start in range(0, total, rows):
        held = held_ref[start : start + rows, :]
        high = held.astype(jnp.bfloat16)
        low = (held - high.astype(jnp.float32)).astype(jnp.bfloat16)
        halves = jnp.concatenate([high, low], axis=1)
        source = lax.broadcasted_iota(jnp.int32, (rows, rows), 1) + start
        for side in range(5):
            one_hot = jnp.where(code_ref[:, side : side + 1] == source, 1.0, 0.0).astype(jnp.bfloat16)
            picked[side] += jnp.dot(one_hot, halves, preferred_element_type=jnp.float32)
    west, east, south, north, fold = [value[:, :LANES] + value[:, LANES:] for value in picked]
    lane = lane_of(rows)
    along_x = (part >= X_PART) | ((part < 8) & (lane >= SPARE) & (lane < SPARE + PIECE))
    x_side = jnp.where(lane % 2 == 0, west, east)
    y_side = jnp.where(lane < 64, north + rot(fold, 64), south)
    out_ref[...] = jnp.where(along_x, x_side, y_side)


def bulk_kernel(first, my_ref, tracer_ref, velocity_ref, depth_ref, kappa_ref, code_ref,
                base_ref, edge_ref, y_ref, x_ref, v_ref, d_ref, k_ref, d8_ref, k8_ref, w_ref, z_ref, x_sems, v_sems, y_sems, d_sems):
    count = depth_ref.shape[0]
    pairs = edge_ref.shape[1] // 8
    x_copies = pair_copies(tracer_ref, x_ref, x_sems, first, pairs)
    v_copies = pair_copies(velocity_ref, v_ref, v_sems, first, pairs)
    d_copy = pltpu.make_async_copy(depth_ref, d_ref, d_sems.at[0])
    k_copy = pltpu.make_async_copy(kappa_ref, k_ref, d_sems.at[1])
    d_copy.start()
    k_copy.start()
    for pair in range(pairs):
        v_copies[pair].start()
        x_copies[pair].start()
    lane = lane_of(8)
    row = lax.broadcasted_iota(jnp.int32, (8, LANES), 0)
    x_row, even, place = row % 4 < 2, row % 2 == 0, row % 4
    level = (row % 2).astype(jnp.float32)
    zero = jnp.zeros((8, LANES), jnp.float32)

    def all_rows(value, chosen):
        result = value
        for at in range(4):
            if at != chosen:
                result = jnp.where(place == at, sublanes(value, at - chosen), result)
        return result

    def wet_of(depth):
        return jnp.clip(depth - level, 0.0, 1.0)

    for copy, source, target in ((d_copy, d_ref, d8_ref), (k_copy, k_ref, k8_ref)):
        copy.wait()
        for pair in range(pairs):
            slot = 2 * (first + pair)
            for start in range(0, CELLS, LANES):
                columns = slice(start, min(start + LANES, CELLS))
                shape = (8, columns.stop - start)
                top, low = [jnp.broadcast_to(source[slot + at : slot + at + 1, columns], shape) for at in range(2)]
                target[8 * pair : 8 * pair + 8, columns] = jnp.where(row[:, : shape[1]] < 4, top, low)

    def one_pair(pair):
        slot = 2 * (first + pair)
        rows = pl.ds(pl.multiple_of(8 * pair, 8), 8)
        for source, target, sems in ((velocity_ref, v_ref, v_sems), (tracer_ref, x_ref, x_sems)):
            pltpu.make_async_copy(
                source.at[pl.ds(0, 2)], target.at[rows].reshape(2, 4, CELLS), sems.at[pair]).wait()

        codes = [code_ref[pl.ds(my_ref[0] * count + slot + at, 1), :] for at in range(2)]

        def flag(column):
            pieces = [jnp.broadcast_to(code[:, column : column + 1], (8, LANES)) for code in codes]
            return jnp.where(row < 4, pieces[0], pieces[1]) >= 0

        live, folded = flag(5), flag(4)
        state, velocity = once(tile_getter(x_ref, rows, 8)), once(tile_getter(v_ref, rows, 8))
        depth, kappa = once(tile_getter(d8_ref, rows, 8)), once(tile_getter(k8_ref, rows, 8))
        wet = once(lambda tile: wet_of(depth(tile)))

        @once
        def ratio(tile):
            other = jnp.clip(depth(tile) - (1.0 - level), 0.0, 1.0)
            coupling = kappa(tile) * (wet(tile) * other)
            return coupling / (1.0 + 2.0 * coupling)

        next_vel = [shifted(velocity, 1), shifted(velocity, IB)]
        next_wet = [shifted(wet, 1), shifted(wet, IB)]

        @once
        def face(tile):
            rims = [at - tile * LANES for at in range(IB - 1, CELLS, IB) if at // LANES == tile]
            rim = functools.reduce(jnp.logical_or, [lane == at for at in rims]) if rims else None
            across = next_wet[0](tile) if rim is None else jnp.where(rim, 0.0, next_wet[0](tile))
            speed = velocity(tile) + jnp.where(x_row, next_vel[0](tile), next_vel[1](tile))
            value = SCALE * speed * (wet(tile) * jnp.where(x_row, across, next_wet[1](tile)))
            w_ref[:, tile * LANES : (tile + 1) * LANES] = value
            return value

        face_x = once(lambda tile: jnp.where(x_row, face(tile), sublanes(face(tile), 2)))
        face_y = once(lambda tile: jnp.where(x_row, sublanes(face(tile), -2), face(tile)))
        five = once(lambda tile: 5.0 * state(tile))
        two = once(lambda tile: 2.0 * state(tile))

        def divergence(speed, distance):
            before, after = shifted(state, -distance), shifted(state, distance)
            lower = once(lambda tile: five(tile) - before(tile) + 2.0 * after(tile))
            upper = shifted(once(lambda tile: five(tile) - after(tile)), distance)

            @once
            def flux(tile):
                value = jnp.maximum(speed(tile), 0.0) * lower(tile)
                return value + jnp.minimum(speed(tile), 0.0) * (two(tile) + upper(tile))

            back = shifted(flux, -distance)
            for stage in (after, before, lower, upper, flux, back):
                for tile in range(TILES):
                    stage(tile)
            return once(lambda tile: flux(tile) - back(tile))

        for stage in (depth, wet, ratio, *next_vel, *next_wet, face):
            for tile in range(TILES):
                stage(tile)
        change_x, change_y = divergence(face_x, 1), divergence(face_y, IB)
        for tile in range(TILES):
            explicit = state(tile) - wet(tile) * (change_x(tile) + change_y(tile))
            other = jnp.where(even, sublanes(explicit, -1), sublanes(explicit, 1))
            value = jnp.where(live, explicit + ratio(tile) * (other - explicit), zero)
            stop = min((tile + 1) * LANES, CELLS)
            y_ref[rows, tile * LANES : stop] = value[:, : stop - tile * LANES]
            mixed = jnp.where(x_row, face(tile), jnp.where(even, ratio(tile), depth(tile)))
            z_ref[:, tile * LANES : (tile + 1) * LANES] = mixed

        pltpu.make_async_copy(
            y_ref.at[rows].reshape(2, 4, CELLS), base_ref.at[pl.ds(slot, 2)], y_sems.at[pair]).start()
        get_w, get_z = [lambda tile, ref=ref: ref[:, tile * LANES : (tile + 1) * LANES] for ref in (w_ref, z_ref)]
        groups = gap_groups(get_z, -2, 4, 8)
        east = lane % 2 == 0
        near, far = across_pair(state)
        normal = gap_groups(velocity, -1, 2, 8)[0]
        normal = jnp.where(x_row, normal, sublanes(normal, 2))
        rim_speed = lane_pick(groups, 4 * (lane // 2) + 2 * (lane % 2))
        rim_speed = jnp.where(x_row, rim_speed, sublanes(rim_speed, 2))
        sides = [(
            near, far, jnp.where(east, -normal, normal), jnp.where(east, -rim_speed, rim_speed),
            lane_pick(groups, 4 * (lane // 2) + 1 + lane % 2), lane_pick(groups, 4 * (lane // 2) + 3 * (lane % 2)),
        )]
        for outer, inner, edge, sign in ((0, IB, 0, 1.0), (CELLS - IB, CELLS - 2 * IB, CELLS - 2 * IB, -1.0)):
            normal, rim_speed = window(velocity, outer, 8), window(get_w, edge, 8)
            normal = sign * jnp.where(x_row, sublanes(normal, -2), normal)
            rim_speed = sign * jnp.where(x_row, sublanes(rim_speed, -2), rim_speed)
            sides.append((window(state, outer, 8), window(state, inner, 8), normal, rim_speed,
                          window(get_z, outer, 8), window(get_z, inner, 8)))
        for side, (near, far, normal, rim_speed, outer, inner) in enumerate(sides):
            values = (near, far, normal, jnp.where(live, jnp.maximum(rim_speed, 0.0), zero), wet_of(all_rows(outer, 3)),
                      wet_of(all_rows(inner, 3)), all_rows(outer, 2), all_rows(inner, 2))
            for index, value in enumerate(values):
                edge_ref[OWN * side + index, rows, :] = value
        edge_ref[OWN * SIDES, rows, :] = jnp.where(folded, 1.0, zero)

    pl.loop(0, pairs)(one_pair)
    for pair in range(pairs):
        slots = pl.ds(2 * (first + pair), 2)
        rows = y_ref.at[pl.ds(8 * pair, 8)].reshape(2, 4, CELLS)
        pltpu.make_async_copy(rows, base_ref.at[slots], y_sems.at[pair]).wait()


def finish_kernel(halo_ref, edge_a_ref, edge_b_ref, base_ref, out_ref,
                  y_ref, own_ref, raw_ref, delta_ref, own_sems, in_sems, out_sems):
    count = out_ref.shape[0]
    pairs = count // 2
    rows = 4 * count
    split = edge_a_ref.shape[1]
    own_copies = [
        pltpu.make_async_copy(edge_a_ref, own_ref.at[:, pl.ds(0, split)], own_sems.at[0]),
        pltpu.make_async_copy(edge_b_ref, own_ref.at[:, pl.ds(split, rows - split)], own_sems.at[1]),
    ]
    in_copies = pair_copies(base_ref, y_ref, in_sems, 0, pairs)
    for copy in own_copies + in_copies:
        copy.start()
    lane = lane_of(rows)
    level = (lax.broadcasted_iota(jnp.int32, (rows, LANES), 0) % 2).astype(jnp.float32)

    def part(index):
        return halo_ref[index * count : (index + 1) * count, :]

    def assembled(index, parts):
        for chan, value in enumerate(parts):
            raw_ref[index, pl.ds(chan, count, stride=4), :] = value
        return raw_ref[index]

    mirror = jnp.where(lane < IB, IB - 1 - lane, lane)
    slot_lane = lane_of(count)
    depth_x = rot(part(0), -SPARE)
    for index in range(1, 8):
        depth_x = jnp.where(slot_lane >= PIECE * index, rot(part(index), PIECE * index - SPARE), depth_x)
    x_raw = [[part(X_PART + chan) for chan in range(4)], [part(X_PART + 4 + chan) for chan in range(4)],
             [part(X_PART + 8 + chan % 2) for chan in range(4)], [depth_x] * 4]
    y_values = [list(range(4)), list(range(4, 8)), [8, 9, 8, 9], [10] * 4]
    x_halo, south_halo, north_raw = [], [], []
    for kind in range(4):
        raw = assembled(3 * kind, x_raw[kind])
        x_halo.append(jnp.where(lane % 2 == 0, rot(raw, 1), rot(raw, -1)))
        first, second = [assembled(3 * kind + 1 + half, [part(2 * value + half) for value in y_values[kind]])
                         for half in range(2)]
        south_halo.append(jnp.where(lane < HALF, rot(first, 64), rot(second, 64 + HALF)))
        north_raw.append(jnp.where(lane < HALF, first, rot(second, HALF)))
    for copy in own_copies:
        copy.wait()
    folded = own_ref[OWN * SIDES] > 0.0
    north_halo = []
    for kind, raw in enumerate(north_raw):
        turned = lane_take(raw, mirror)
        north_halo.append(jnp.where(folded, -turned if kind == 2 else turned, raw))

    for side, (out_near, out_far, out_normal, out_depth) in enumerate((x_halo, south_halo, north_halo)):
        near, far, normal, rim_speed, wet, inner_wet, ratio, inner_ratio = [
            own_ref[OWN * side + index] for index in range(OWN)]
        if side == 0:
            out_normal = jnp.where(lane % 2 == 0, -out_normal, out_normal)
            beyond = out_near - jnp.where(lane % 2 == 0, rot(near, -1), rot(near, 1))
        else:
            out_normal = -out_normal if side == 2 else out_normal
            beyond = out_near
        speed = SCALE * (normal + out_normal) * (wet * jnp.clip(out_depth - level, 0.0, 1.0))
        flux = jnp.maximum(speed, 0.0) * (5.0 * out_near + 2.0 * near - out_far)
        flux += jnp.minimum(speed, 0.0) * (2.0 * out_near + 5.0 * near - far)
        inner_flux = rim_speed * beyond
        for place, (change, share) in enumerate(((wet * (flux + inner_flux), ratio),
                                                 (-inner_wet * inner_flux, inner_ratio))):
            other = jnp.where(level == 0.0, pltpu.roll(change, rows - 1, 0), pltpu.roll(change, 1, 0))
            delta_ref[2 * side + place] = change + share * (other - change)

    lane = lane_of(8)
    out_copies = []
    for pair in range(pairs):
        mine = pl.ds(8 * pair, 8)
        in_copies[pair].wait()
        near, deep, south, south_in, north, north_in = [delta_ref[index, mine, :] for index in range(2 * SIDES)]
        groups = []
        for at in range(2):
            index = 2 * (lane // 4) + (lane % 4) // 2 + 64 * at
            outer, inner = lane_take(near, index), lane_take(deep, index)
            groups.append(jnp.where((lane % 4 == 1) | (lane % 4 == 2), outer, inner))
        placed = [(groups[gap // 32], 4 * (gap % 32), IB * gap - 2, 4) for gap in range(GAPS)]
        placed += [(south, 0, 0, IB), (south_in, 0, IB, IB)]
        placed += [(north, 0, CELLS - IB, IB), (north_in, 0, CELLS - 2 * IB, IB)]
        for tile in range(TILES):
            at, stop = tile * LANES, min((tile + 1) * LANES, CELLS)
            change = jnp.zeros((8, LANES), jnp.float32)
            for source, origin, start, wide in placed:
                low, high = max(start, at, 0), min(start + wide, stop)
                if low < high:
                    inside = (lane >= low - at) & (lane < high - at)
                    change += jnp.where(inside, rot(source, start - at - origin), 0.0)
            y_ref[mine, at:stop] = y_ref[mine, at:stop] + change[:, : stop - at]
        copy = pltpu.make_async_copy(
            y_ref.at[mine].reshape(2, 4, CELLS), out_ref.at[pl.ds(2 * pair, 2)], out_sems.at[pair])
        copy.start()
        out_copies.append(copy)
    for copy in out_copies:
        copy.wait()


def route_codes(block_owner, neighbours, fold_partner, slot_total):
    block_count = block_owner.shape[0]
    hits = block_owner[None, :] == jnp.arange(slot_total, dtype=jnp.int32)[:, None]
    links = jnp.concatenate([neighbours, fold_partner[:, None]], axis=1)
    linked = links[:, :, None] == jnp.arange(block_count, dtype=jnp.int32)[None, None, :]
    link_slots = jnp.max(jnp.where(linked, block_owner[None, None, :], -1), axis=2)
    link_slots = jnp.concatenate([link_slots, block_owner[:, None]], axis=1)
    return jnp.max(jnp.where(hits[:, :, None], link_slots[None], -1), axis=1)


def per_device(tracers, velocity, kappa, kmt, block_owner, neighbours, fold_partner):
    slot_count, chans = tracers.shape[:2]
    sub_count = lax.axis_size("sub")
    device_count = lax.axis_size("blk") * sub_count
    if device_count % PARTS or chans != 4 or slot_count % 2 or slot_count < 2 * FIRST_PAIRS + 2:
        raise ValueError("unsupported sizes")
    my_index = (lax.axis_index("blk") * sub_count + lax.axis_index("sub")).astype(jnp.int32).reshape(1)
    axes = ("blk", "sub")
    pairs = slot_count // 2
    slot_total = device_count * slot_count
    state_rows = 4 * slot_count
    f32 = jnp.float32
    in_hbm = pl.BlockSpec(memory_space=pltpu.HBM)
    anywhere = pl.BlockSpec(memory_space=pl.ANY)
    in_vmem = pl.BlockSpec(memory_space=pltpu.VMEM)
    in_smem = pl.BlockSpec(memory_space=pltpu.SMEM)
    dma = pltpu.SemaphoreType.DMA
    limit = pltpu.CompilerParams(vmem_limit_bytes=32 * 1024 * 1024)

    def exchanged(pieces):
        pieces = pieces.reshape(device_count, slot_count, 1, LANES)
        return lax.all_to_all(pieces, axes, 0, 0, tiled=True).reshape(slot_total, LANES)

    pack = pl.pallas_call(
        pack_kernel,
        out_shape=jax.ShapeDtypeStruct((slot_total, LANES), f32),
        in_specs=[in_hbm, in_hbm, in_hbm],
        out_specs=in_vmem,
        scratch_shapes=[
            pltpu.VMEM((state_rows, CELLS), f32),
            pltpu.VMEM((state_rows, CELLS), f32),
            pltpu.VMEM((slot_count, CELLS), f32),
            pltpu.VMEM((9, state_rows, LANES), f32),
            dma((pairs,)),
            dma((pairs,)),
            dma,
        ],
        cost_estimate=pl.CostEstimate(flops=4_000_000, bytes_accessed=2_400_000, transcendentals=0),
    )(tracers, velocity, kmt)
    pack, *later = lax.optimization_barrier((pack, tracers, velocity, kmt, kappa))
    held = exchanged(pack)
    codes = route_codes(block_owner, neighbours, fold_partner, slot_total)

    def bulk(first, some, codes, base):
        kernel = functools.partial(bulk_kernel, first)
        extra = [] if base is None else [base]
        if extra:
            kernel = lambda *refs: bulk_kernel(first, *refs[:6], *refs[7:])
        return pl.pallas_call(
            kernel,
            out_shape=[
                jax.ShapeDtypeStruct(tracers.shape, f32),
                jax.ShapeDtypeStruct((OWN * SIDES + 1, 8 * some, LANES), f32),
            ],
            in_specs=[in_smem, in_hbm, in_hbm, in_hbm, in_hbm, in_vmem] + [in_hbm] * len(extra),
            out_specs=[in_hbm, in_vmem],
            scratch_shapes=[
                pltpu.VMEM((8 * some, CELLS), f32),
                pltpu.VMEM((8 * some, CELLS), f32),
                pltpu.VMEM((8 * some, CELLS), f32),
                pltpu.VMEM((slot_count, CELLS), f32),
                pltpu.VMEM((slot_count, CELLS), f32),
                pltpu.VMEM((8 * some, CELLS), f32),
                pltpu.VMEM((8 * some, CELLS), f32),
                pltpu.VMEM((8, WIDE), f32),
                pltpu.VMEM((8, WIDE), f32),
                dma((some,)),
                dma((some,)),
                dma((some,)),
                dma((2,)),
            ],
            input_output_aliases={6: 0} if extra else {},
            compiler_params=limit,
            cost_estimate=pl.CostEstimate(flops=4_000_000 * some, bytes_accessed=800_000 * some, transcendentals=0),
        )(my_index, *later, codes, *extra)

    base, edge_a = bulk(0, FIRST_PAIRS, codes, None)
    held, edge_a = lax.optimization_barrier((held, edge_a))

    routed_rows = PARTS * slot_count
    routed = pl.pallas_call(
        route_kernel,
        grid=(device_count // PARTS,),
        out_shape=jax.ShapeDtypeStruct((slot_total, LANES), f32),
        in_specs=[
            in_smem,
            pl.BlockSpec((routed_rows, 6), lambda step: (step, 0)),
            pl.BlockSpec((slot_total, LANES), lambda step: (0, 0)),
        ],
        out_specs=pl.BlockSpec((routed_rows, LANES), lambda step: (step, 0)),
        compiler_params=limit,
    )(my_index, codes, held)

    routed, base = lax.optimization_barrier((routed, base))
    base, edge_b = bulk(FIRST_PAIRS, pairs - FIRST_PAIRS, codes, base)
    halo = exchanged(routed)[: PARTS * slot_count]

    return pl.pallas_call(
        finish_kernel,
        out_shape=jax.ShapeDtypeStruct(tracers.shape, f32),
        in_specs=[in_vmem, anywhere, anywhere, in_hbm],
        out_specs=in_hbm,
        scratch_shapes=[
            pltpu.VMEM((state_rows, CELLS), f32),
            pltpu.VMEM((OWN * SIDES + 1, state_rows, LANES), f32),
            pltpu.VMEM((12, state_rows, LANES), f32),
            pltpu.VMEM((2 * SIDES, state_rows, LANES), f32),
            dma((2,)),
            dma((pairs,)),
            dma((pairs,)),
        ],
        input_output_aliases={3: 0},
        compiler_params=limit,
    )(halo, edge_a, edge_b, base)


def solution(mesh):
    placed = (
        P(("blk", "sub"), None, None),
        P(("blk", "sub"), None, None),
        P(("blk", "sub"), None),
        P(("blk", "sub"), None),
        P(),
        P(),
        P(),
    )
    return jax.shard_map(
        per_device,
        mesh=mesh,
        in_specs=placed,
        out_specs=P(("blk", "sub"), None, None),
        check_vma=False,
    )
```

```python
import functools

import jax
import jax.numpy as jnp
from jax import lax
from jax.experimental import pallas as pl
from jax.experimental.pallas import tpu as pltpu
from jax.sharding import PartitionSpec as P

IB = 90
JB = 60
CELLS = IB * JB
COURANT = 0.2
LANES = 128
TILES = -(-CELLS // LANES)
WIDE = TILES * LANES
GAPS = JB + 1
HALF = IB // 2
PARTS = 32
X_PART = 22
SPARE = 48
PIECE = 16
SCALE = COURANT / 12.0
SIDES = 3
OWN = 8
FIRST_PAIRS = 2


def lane_of(rows):
    return lax.broadcasted_iota(jnp.int32, (rows, LANES), 1)


def rot(value, shift):
    shift = shift % LANES
    return value if shift == 0 else pltpu.roll(value, shift, 1)


def sublanes(value, shift):
    return pltpu.roll(value, shift % 8, 0)


def once(make):
    held = {}

    def get(tile):
        if tile not in held:
            held[tile] = make(tile)
        return held[tile]

    return get


def shifted(get, distance):
    offset = distance % LANES
    turned = once(lambda tile: rot(get(tile), -offset))

    def make(tile):
        low = tile + distance // LANES
        first = turned(low) if 0 <= low < TILES else jnp.zeros((8, LANES), jnp.float32)
        second = turned(low + 1) if 0 <= low + 1 < TILES else jnp.zeros((8, LANES), jnp.float32)
        return jnp.where(lane_of(8) < LANES - offset, first, second)

    return once(make)


def window(get, start, rows):
    tile, offset = start // LANES, start % LANES
    head = rot(get(tile), -offset)
    if offset == 0 or tile + 1 >= TILES:
        return head
    return jnp.where(lane_of(rows) < LANES - offset, head, rot(get(tile + 1), -offset))


def gap_groups(get, first, wide, rows):
    lane = lane_of(rows)
    held = LANES // wide
    result = []
    for at in range(0, GAPS, held):
        value = jnp.zeros((rows, LANES), jnp.float32)
        for gap in range(at, min(at + held, GAPS)):
            start = IB * gap + first
            place = (gap - at) * wide
            for tile in range(max(start, 0) // LANES, min(start + wide - 1, CELLS - 1) // LANES + 1):
                low = max(start, tile * LANES, 0)
                value = jnp.where(lane >= place + low - start, rot(get(tile), place - start + tile * LANES), value)
        result.append(value)
    return result


def lane_take(value, index):
    return jnp.take_along_axis(value, index, axis=1, mode="promise_in_bounds")


def lane_pick(pair, index):
    return jnp.where(index < LANES, lane_take(pair[0], index % LANES), lane_take(pair[1], index % LANES))


def tile_getter(ref, rows, count):
    def get(tile):
        if tile + 1 < TILES:
            return ref[rows, tile * LANES : (tile + 1) * LANES]
        rest = jnp.zeros((count, WIDE - CELLS), jnp.float32)
        return jnp.concatenate([ref[rows, tile * LANES : CELLS], rest], axis=1)

    return get


def across_pair(get):
    lane = lane_of(8)
    groups = gap_groups(get, -2, 4, 8)
    return lane_pick(groups, 4 * (lane // 2) + 1 + lane % 2), lane_pick(groups, 4 * (lane // 2) + 3 * (lane % 2))


def joined(south, north, half, rows):
    if half == 0:
        return jnp.where(lane_of(rows) < 64, south, rot(north, 64))
    return jnp.where(lane_of(rows) < 64, rot(south, -HALF), rot(north, 64 - HALF))


def pair_copies(source, target, sems, first, pairs):
    copies = []
    for pair in range(pairs):
        into = target.at[pl.ds(8 * pair, 8)].reshape(2, 4, CELLS)
        copies.append(pltpu.make_async_copy(source.at[pl.ds(2 * (first + pair), 2)], into, sems.at[pair]))
    return copies


def pack_kernel(tracer_ref, velocity_ref, depth_ref, out_ref, x_ref, v_ref, d_ref, strip_ref, x_sems, v_sems, d_sem):
    count = depth_ref.shape[0]
    pairs = count // 2
    x_copies = pair_copies(tracer_ref, x_ref, x_sems, 0, pairs)
    v_copies = pair_copies(velocity_ref, v_ref, v_sems, 0, pairs)
    d_copy = pltpu.make_async_copy(depth_ref, d_ref, d_sem)
    for pair in range(pairs):
        x_copies[pair].start()
        v_copies[pair].start()
    d_copy.start()
    for pair in range(pairs):
        rows = pl.ds(8 * pair, 8)
        x_copies[pair].wait()
        get_x = tile_getter(x_ref, rows, 8)
        near, far = across_pair(get_x)
        south = [window(get_x, 0, 8), window(get_x, IB, 8)]
        north = [window(get_x, CELLS - IB, 8), window(get_x, CELLS - 2 * IB, 8)]
        v_copies[pair].wait()
        get_v = tile_getter(v_ref, rows, 8)
        v_south, v_north = window(get_v, 0, 8), window(get_v, CELLS - IB, 8)
        strips = [joined(south[0], north[0], half, 8) for half in range(2)]
        strips += [joined(south[1], north[1], half, 8) for half in range(2)]
        strips += [joined(v_south, v_north, half, 8) for half in range(2)]
        strips += [near, far, gap_groups(get_v, -1, 2, 8)[0]]
        for index, strip in enumerate(strips):
            strip_ref[index, rows, :] = strip

    d_copy.wait()
    if out_ref.shape[0] > PARTS * count:
        rest = out_ref.shape[0] - PARTS * count
        out_ref[PARTS * count :, :] = jnp.zeros((rest, LANES), jnp.float32)
    slot_lane = lane_of(count)
    get_d = tile_getter(d_ref, slice(None), count)
    d_south, d_north = window(get_d, 0, count), window(get_d, CELLS - IB, count)
    d_gaps = gap_groups(get_d, -1, 2, count)[0]
    spare = (slot_lane >= SPARE) & (slot_lane < SPARE + PIECE)

    def put(part, value):
        out_ref[part * count : (part + 1) * count, :] = value

    for chan in range(4):
        rows = pl.ds(chan, count, stride=4)
        for half in range(2):
            for deep in range(2):
                part = 2 * (4 * deep + chan) + half
                value = strip_ref[2 * deep + half, rows, :]
                if part < 8:
                    value = jnp.where(spare, rot(d_gaps, SPARE - PIECE * part), value)
                put(part, value)
            if chan >= 2:
                put(2 * (8 + chan - 2) + half, strip_ref[4 + half, rows, :])
        put(X_PART + chan, strip_ref[6, rows, :])
        put(X_PART + 4 + chan, strip_ref[7, rows, :])
        if chan < 2:
            put(X_PART + 8 + chan, strip_ref[8, rows, :])
    for half in range(2):
        put(20 + half, joined(d_south, d_north, half, count))


def route_kernel(part_ref, code_ref, held_ref, out_ref):
    total = held_ref.shape[0]
    rows = out_ref.shape[0]
    part = part_ref[0]
    picked = [jnp.zeros((rows, 2 * LANES), jnp.float32) for _ in range(5)]
    for start in range(0, total, rows):
        held = held_ref[start : start + rows, :]
        high = held.astype(jnp.bfloat16)
        low = (held - high.astype(jnp.float32)).astype(jnp.bfloat16)
        halves = jnp.concatenate([high, low], axis=1)
        source = lax.broadcasted_iota(jnp.int32, (rows, rows), 1) + start
        for side in range(5):
            one_hot = jnp.where(code_ref[:, side : side + 1] == source, 1.0, 0.0).astype(jnp.bfloat16)
            picked[side] += jnp.dot(one_hot, halves, preferred_element_type=jnp.float32)
    west, east, south, north, fold = [value[:, :LANES] + value[:, LANES:] for value in picked]
    lane = lane_of(rows)
    along_x = (part >= X_PART) | ((part < 8) & (lane >= SPARE) & (lane < SPARE + PIECE))
    x_side = jnp.where(lane % 2 == 0, west, east)
    y_side = jnp.where(lane < 64, north + rot(fold, 64), south)
    out_ref[...] = jnp.where(along_x, x_side, y_side)


def bulk_kernel(first, my_ref, tracer_ref, velocity_ref, depth_ref, kappa_ref, code_ref,
                base_ref, edge_ref, y_ref, x_ref, v_ref, d_ref, k_ref, d8_ref, k8_ref, w_ref, z_ref, x_sems, v_sems, y_sems, d_sems):
    count = depth_ref.shape[0]
    pairs = edge_ref.shape[1] // 8
    x_copies = pair_copies(tracer_ref, x_ref, x_sems, first, pairs)
    v_copies = pair_copies(velocity_ref, v_ref, v_sems, first, pairs)
    d_copy = pltpu.make_async_copy(depth_ref, d_ref, d_sems.at[0])
    k_copy = pltpu.make_async_copy(kappa_ref, k_ref, d_sems.at[1])
    d_copy.start()
    k_copy.start()
    for pair in range(pairs):
        v_copies[pair].start()
        x_copies[pair].start()
    lane = lane_of(8)
    row = lax.broadcasted_iota(jnp.int32, (8, LANES), 0)
    x_row, even, place = row % 4 < 2, row % 2 == 0, row % 4
    level = (row % 2).astype(jnp.float32)
    zero = jnp.zeros((8, LANES), jnp.float32)

    def all_rows(value, chosen):
        result = value
        for at in range(4):
            if at != chosen:
                result = jnp.where(place == at, sublanes(value, at - chosen), result)
        return result

    def wet_of(depth):
        return jnp.clip(depth - level, 0.0, 1.0)

    for copy, source, target in ((d_copy, d_ref, d8_ref), (k_copy, k_ref, k8_ref)):
        copy.wait()
        for pair in range(pairs):
            slot = 2 * (first + pair)
            for start in range(0, CELLS, LANES):
                columns = slice(start, min(start + LANES, CELLS))
                shape = (8, columns.stop - start)
                top, low = [jnp.broadcast_to(source[slot + at : slot + at + 1, columns], shape) for at in range(2)]
                target[8 * pair : 8 * pair + 8, columns] = jnp.where(row[:, : shape[1]] < 4, top, low)

    def one_pair(pair):
        slot = 2 * (first + pair)
        rows = pl.ds(pl.multiple_of(8 * pair, 8), 8)
        for source, target, sems in ((velocity_ref, v_ref, v_sems), (tracer_ref, x_ref, x_sems)):
            pltpu.make_async_copy(
                source.at[pl.ds(0, 2)], target.at[rows].reshape(2, 4, CELLS), sems.at[pair]).wait()

        codes = [code_ref[pl.ds(my_ref[0] * count + slot + at, 1), :] for at in range(2)]

        def flag(column):
            pieces = [jnp.broadcast_to(code[:, column : column + 1], (8, LANES)) for code in codes]
            return jnp.where(row < 4, pieces[0], pieces[1]) >= 0

        live, folded = flag(5), flag(4)
        state, velocity = once(tile_getter(x_ref, rows, 8)), once(tile_getter(v_ref, rows, 8))
        depth, kappa = once(tile_getter(d8_ref, rows, 8)), once(tile_getter(k8_ref, rows, 8))
        wet = once(lambda tile: wet_of(depth(tile)))

        @once
        def ratio(tile):
            other = jnp.clip(depth(tile) - (1.0 - level), 0.0, 1.0)
            coupling = kappa(tile) * (wet(tile) * other)
            return coupling / (1.0 + 2.0 * coupling)

        next_vel = [shifted(velocity, 1), shifted(velocity, IB)]
        next_wet = [shifted(wet, 1), shifted(wet, IB)]

        @once
        def face(tile):
            rims = [at - tile * LANES for at in range(IB - 1, CELLS, IB) if at // LANES == tile]
            rim = functools.reduce(jnp.logical_or, [lane == at for at in rims]) if rims else None
            across = next_wet[0](tile) if rim is None else jnp.where(rim, 0.0, next_wet[0](tile))
            speed = velocity(tile) + jnp.where(x_row, next_vel[0](tile), next_vel[1](tile))
            value = SCALE * speed * (wet(tile) * jnp.where(x_row, across, next_wet[1](tile)))
            w_ref[:, tile * LANES : (tile + 1) * LANES] = value
            return value

        face_x = once(lambda tile: jnp.where(x_row, face(tile), sublanes(face(tile), 2)))
        face_y = once(lambda tile: jnp.where(x_row, sublanes(face(tile), -2), face(tile)))
        five = once(lambda tile: 5.0 * state(tile))
        two = once(lambda tile: 2.0 * state(tile))

        def divergence(speed, distance):
            before, after = shifted(state, -distance), shifted(state, distance)
            lower = once(lambda tile: five(tile) - before(tile) + 2.0 * after(tile))
            upper = shifted(once(lambda tile: five(tile) - after(tile)), distance)

            @once
            def flux(tile):
                value = jnp.maximum(speed(tile), 0.0) * lower(tile)
                return value + jnp.minimum(speed(tile), 0.0) * (two(tile) + upper(tile))

            back = shifted(flux, -distance)
            for stage in (after, before, lower, upper, flux, back):
                for tile in range(TILES):
                    stage(tile)
            return once(lambda tile: flux(tile) - back(tile))

        for stage in (depth, wet, ratio, *next_vel, *next_wet, face):
            for tile in range(TILES):
                stage(tile)
        change_x, change_y = divergence(face_x, 1), divergence(face_y, IB)
        for tile in range(TILES):
            explicit = state(tile) - wet(tile) * (change_x(tile) + change_y(tile))
            other = jnp.where(even, sublanes(explicit, -1), sublanes(explicit, 1))
            value = jnp.where(live, explicit + ratio(tile) * (other - explicit), zero)
            stop = min((tile + 1) * LANES, CELLS)
            y_ref[rows, tile * LANES : stop] = value[:, : stop - tile * LANES]
            mixed = jnp.where(x_row, face(tile), jnp.where(even, ratio(tile), depth(tile)))
            z_ref[:, tile * LANES : (tile + 1) * LANES] = mixed

        pltpu.make_async_copy(
            y_ref.at[rows].reshape(2, 4, CELLS), base_ref.at[pl.ds(slot, 2)], y_sems.at[pair]).start()
        get_w, get_z = [lambda tile, ref=ref: ref[:, tile * LANES : (tile + 1) * LANES] for ref in (w_ref, z_ref)]
        groups = gap_groups(get_z, -2, 4, 8)
        east = lane % 2 == 0
        near, far = across_pair(state)
        normal = gap_groups(velocity, -1, 2, 8)[0]
        normal = jnp.where(x_row, normal, sublanes(normal, 2))
        rim_speed = lane_pick(groups, 4 * (lane // 2) + 2 * (lane % 2))
        rim_speed = jnp.where(x_row, rim_speed, sublanes(rim_speed, 2))
        sides = [(
            near, far, jnp.where(east, -normal, normal), jnp.where(east, -rim_speed, rim_speed),
            lane_pick(groups, 4 * (lane // 2) + 1 + lane % 2), lane_pick(groups, 4 * (lane // 2) + 3 * (lane % 2)),
        )]
        for outer, inner, edge, sign in ((0, IB, 0, 1.0), (CELLS - IB, CELLS - 2 * IB, CELLS - 2 * IB, -1.0)):
            normal, rim_speed = window(velocity, outer, 8), window(get_w, edge, 8)
            normal = sign * jnp.where(x_row, sublanes(normal, -2), normal)
            rim_speed = sign * jnp.where(x_row, sublanes(rim_speed, -2), rim_speed)
            sides.append((window(state, outer, 8), window(state, inner, 8), normal, rim_speed,
                          window(get_z, outer, 8), window(get_z, inner, 8)))
        for side, (near, far, normal, rim_speed, outer, inner) in enumerate(sides):
            values = (near, far, normal, jnp.where(live, jnp.maximum(rim_speed, 0.0), zero), wet_of(all_rows(outer, 3)),
                      wet_of(all_rows(inner, 3)), all_rows(outer, 2), all_rows(inner, 2))
            for index, value in enumerate(values):
                edge_ref[OWN * side + index, rows, :] = value
        edge_ref[OWN * SIDES, rows, :] = jnp.where(folded, 1.0, zero)

    pl.loop(0, pairs)(one_pair)
    for pair in range(pairs):
        slots = pl.ds(2 * (first + pair), 2)
        rows = y_ref.at[pl.ds(8 * pair, 8)].reshape(2, 4, CELLS)
        pltpu.make_async_copy(rows, base_ref.at[slots], y_sems.at[pair]).wait()


def finish_kernel(halo_ref, edge_a_ref, edge_b_ref, base_ref, out_ref,
                  y_ref, own_ref, raw_ref, delta_ref, own_sems, in_sems, out_sems):
    count = out_ref.shape[0]
    pairs = count // 2
    rows = 4 * count
    split = edge_a_ref.shape[1]
    own_copies = [
        pltpu.make_async_copy(edge_a_ref, own_ref.at[:, pl.ds(0, split)], own_sems.at[0]),
        pltpu.make_async_copy(edge_b_ref, own_ref.at[:, pl.ds(split, rows - split)], own_sems.at[1]),
    ]
    in_copies = pair_copies(base_ref, y_ref, in_sems, 0, pairs)
    for copy in own_copies + in_copies:
        copy.start()
    lane = lane_of(rows)
    level = (lax.broadcasted_iota(jnp.int32, (rows, LANES), 0) % 2).astype(jnp.float32)

    def part(index):
        return halo_ref[index * count : (index + 1) * count, :]

    def assembled(index, parts):
        for chan, value in enumerate(parts):
            raw_ref[index, pl.ds(chan, count, stride=4), :] = value
        return raw_ref[index]

    mirror = jnp.where(lane < IB, IB - 1 - lane, lane)
    slot_lane = lane_of(count)
    depth_x = rot(part(0), -SPARE)
    for index in range(1, 8):
        depth_x = jnp.where(slot_lane >= PIECE * index, rot(part(index), PIECE * index - SPARE), depth_x)
    x_raw = [[part(X_PART + chan) for chan in range(4)], [part(X_PART + 4 + chan) for chan in range(4)],
             [part(X_PART + 8 + chan % 2) for chan in range(4)], [depth_x] * 4]
    y_values = [list(range(4)), list(range(4, 8)), [8, 9, 8, 9], [10] * 4]
    x_halo, south_halo, north_raw = [], [], []
    for kind in range(4):
        raw = assembled(3 * kind, x_raw[kind])
        x_halo.append(jnp.where(lane % 2 == 0, rot(raw, 1), rot(raw, -1)))
        first, second = [assembled(3 * kind + 1 + half, [part(2 * value + half) for value in y_values[kind]])
                         for half in range(2)]
        south_halo.append(jnp.where(lane < HALF, rot(first, 64), rot(second, 64 + HALF)))
        north_raw.append(jnp.where(lane < HALF, first, rot(second, HALF)))
    for copy in own_copies:
        copy.wait()
    folded = own_ref[OWN * SIDES] > 0.0
    north_halo = []
    for kind, raw in enumerate(north_raw):
        turned = lane_take(raw, mirror)
        north_halo.append(jnp.where(folded, -turned if kind == 2 else turned, raw))

    for side, (out_near, out_far, out_normal, out_depth) in enumerate((x_halo, south_halo, north_halo)):
        near, far, normal, rim_speed, wet, inner_wet, ratio, inner_ratio = [
            own_ref[OWN * side + index] for index in range(OWN)]
        if side == 0:
            out_normal = jnp.where(lane % 2 == 0, -out_normal, out_normal)
            beyond = out_near - jnp.where(lane % 2 == 0, rot(near, -1), rot(near, 1))
        else:
            out_normal = -out_normal if side == 2 else out_normal
            beyond = out_near
        speed = SCALE * (normal + out_normal) * (wet * jnp.clip(out_depth - level, 0.0, 1.0))
        flux = jnp.maximum(speed, 0.0) * (5.0 * out_near + 2.0 * near - out_far)
        flux += jnp.minimum(speed, 0.0) * (2.0 * out_near + 5.0 * near - far)
        inner_flux = rim_speed * beyond
        for place, (change, share) in enumerate(((wet * (flux + inner_flux), ratio),
                                                 (-inner_wet * inner_flux, inner_ratio))):
            other = jnp.where(level == 0.0, pltpu.roll(change, rows - 1, 0), pltpu.roll(change, 1, 0))
            delta_ref[2 * side + place] = change + share * (other - change)

    lane = lane_of(8)
    out_copies = []
    for pair in range(pairs):
        mine = pl.ds(8 * pair, 8)
        in_copies[pair].wait()
        near, deep, south, south_in, north, north_in = [delta_ref[index, mine, :] for index in range(2 * SIDES)]
        groups = []
        for at in range(2):
            index = 2 * (lane // 4) + (lane % 4) // 2 + 64 * at
            outer, inner = lane_take(near, index), lane_take(deep, index)
            groups.append(jnp.where((lane % 4 == 1) | (lane % 4 == 2), outer, inner))
        placed = [(groups[gap // 32], 4 * (gap % 32), IB * gap - 2, 4) for gap in range(GAPS)]
        placed += [(south, 0, 0, IB), (south_in, 0, IB, IB)]
        placed += [(north, 0, CELLS - IB, IB), (north_in, 0, CELLS - 2 * IB, IB)]
        for tile in range(TILES):
            at, stop = tile * LANES, min((tile + 1) * LANES, CELLS)
            change = jnp.zeros((8, LANES), jnp.float32)
            for source, origin, start, wide in placed:
                low, high = max(start, at, 0), min(start + wide, stop)
                if low < high:
                    inside = (lane >= low - at) & (lane < high - at)
                    change += jnp.where(inside, rot(source, start - at - origin), 0.0)
            y_ref[mine, at:stop] = y_ref[mine, at:stop] + change[:, : stop - at]
        copy = pltpu.make_async_copy(
            y_ref.at[mine].reshape(2, 4, CELLS), out_ref.at[pl.ds(2 * pair, 2)], out_sems.at[pair])
        copy.start()
        out_copies.append(copy)
    for copy in out_copies:
        copy.wait()


def route_codes(block_owner, neighbours, fold_partner, slot_total):
    block_count = block_owner.shape[0]
    hits = block_owner[None, :] == jnp.arange(slot_total, dtype=jnp.int32)[:, None]
    links = jnp.concatenate([neighbours, fold_partner[:, None]], axis=1)
    linked = links[:, :, None] == jnp.arange(block_count, dtype=jnp.int32)[None, None, :]
    link_slots = jnp.max(jnp.where(linked, block_owner[None, None, :], -1), axis=2)
    link_slots = jnp.concatenate([link_slots, block_owner[:, None]], axis=1)
    return jnp.max(jnp.where(hits[:, :, None], link_slots[None], -1), axis=1)


def per_device(tracers, velocity, kappa, kmt, block_owner, neighbours, fold_partner):
    slot_count, chans = tracers.shape[:2]
    sub_count = lax.axis_size("sub")
    device_count = lax.axis_size("blk") * sub_count
    if device_count % PARTS or chans != 4 or slot_count % 2 or slot_count < 2 * FIRST_PAIRS + 2:
        raise ValueError("unsupported sizes")
    my_index = (lax.axis_index("blk") * sub_count + lax.axis_index("sub")).astype(jnp.int32).reshape(1)
    axes = ("blk", "sub")
    pairs = slot_count // 2
    slot_total = device_count * slot_count
    state_rows = 4 * slot_count
    f32 = jnp.float32
    in_hbm = pl.BlockSpec(memory_space=pltpu.HBM)
    anywhere = pl.BlockSpec(memory_space=pl.ANY)
    in_vmem = pl.BlockSpec(memory_space=pltpu.VMEM)
    in_smem = pl.BlockSpec(memory_space=pltpu.SMEM)
    dma = pltpu.SemaphoreType.DMA
    limit = pltpu.CompilerParams(vmem_limit_bytes=32 * 1024 * 1024)

    def exchanged(pieces):
        pieces = pieces.reshape(device_count, slot_count, 1, LANES)
        return lax.all_to_all(pieces, axes, 0, 0, tiled=True).reshape(slot_total, LANES)

    pack = pl.pallas_call(
        pack_kernel,
        out_shape=jax.ShapeDtypeStruct((slot_total, LANES), f32),
        in_specs=[in_hbm, in_hbm, in_hbm],
        out_specs=in_vmem,
        scratch_shapes=[
            pltpu.VMEM((state_rows, CELLS), f32),
            pltpu.VMEM((state_rows, CELLS), f32),
            pltpu.VMEM((slot_count, CELLS), f32),
            pltpu.VMEM((9, state_rows, LANES), f32),
            dma((pairs,)),
            dma((pairs,)),
            dma,
        ],
        compiler_params=pltpu.CompilerParams(vmem_limit_bytes=127 * 512 * 1024),
        cost_estimate=pl.CostEstimate(flops=4_000_000, bytes_accessed=2_400_000, transcendentals=0),
    )(tracers, velocity, kmt)
    held = exchanged(pack)
    codes = route_codes(block_owner, neighbours, fold_partner, slot_total)

    def bulk(first, some, codes, base):
        kernel = functools.partial(bulk_kernel, first)
        extra = [] if base is None else [base]
        if extra:
            kernel = lambda *refs: bulk_kernel(first, *refs[:6], *refs[7:])
        return pl.pallas_call(
            kernel,
            out_shape=[
                jax.ShapeDtypeStruct(tracers.shape, f32),
                jax.ShapeDtypeStruct((OWN * SIDES + 1, 8 * some, LANES), f32),
            ],
            in_specs=[in_smem, in_hbm, in_hbm, in_hbm, in_hbm, in_vmem] + [in_hbm] * len(extra),
            out_specs=[in_hbm, in_vmem],
            scratch_shapes=[
                pltpu.VMEM((8 * some, CELLS), f32),
                pltpu.VMEM((8 * some, CELLS), f32),
                pltpu.VMEM((8 * some, CELLS), f32),
                pltpu.VMEM((slot_count, CELLS), f32),
                pltpu.VMEM((slot_count, CELLS), f32),
                pltpu.VMEM((8 * some, CELLS), f32),
                pltpu.VMEM((8 * some, CELLS), f32),
                pltpu.VMEM((8, WIDE), f32),
                pltpu.VMEM((8, WIDE), f32),
                dma((some,)),
                dma((some,)),
                dma((some,)),
                dma((2,)),
            ],
            input_output_aliases={6: 0} if extra else {},
            compiler_params=limit,
            cost_estimate=pl.CostEstimate(flops=4_000_000 * some, bytes_accessed=800_000 * some, transcendentals=0),
        )(my_index, tracers, velocity, kmt, kappa, codes, *extra)

    base, edge_a = bulk(0, FIRST_PAIRS, codes, None)
    held, edge_a = lax.optimization_barrier((held, edge_a))

    routed_rows = PARTS * slot_count
    routed = pl.pallas_call(
        route_kernel,
        grid=(device_count // PARTS,),
        out_shape=jax.ShapeDtypeStruct((slot_total, LANES), f32),
        in_specs=[
            in_smem,
            pl.BlockSpec((routed_rows, 6), lambda step: (step, 0)),
            pl.BlockSpec((slot_total, LANES), lambda step: (0, 0)),
        ],
        out_specs=pl.BlockSpec((routed_rows, LANES), lambda step: (step, 0)),
        compiler_params=limit,
    )(my_index, codes, held)

    routed, base = lax.optimization_barrier((routed, base))
    base, edge_b = bulk(FIRST_PAIRS, pairs - FIRST_PAIRS, codes, base)
    halo = exchanged(routed)[: PARTS * slot_count]

    return pl.pallas_call(
        finish_kernel,
        out_shape=jax.ShapeDtypeStruct(tracers.shape, f32),
        in_specs=[in_vmem, anywhere, anywhere, in_hbm],
        out_specs=in_hbm,
        scratch_shapes=[
            pltpu.VMEM((state_rows, CELLS), f32),
            pltpu.VMEM((OWN * SIDES + 1, state_rows, LANES), f32),
            pltpu.VMEM((12, state_rows, LANES), f32),
            pltpu.VMEM((2 * SIDES, state_rows, LANES), f32),
            dma((2,)),
            dma((pairs,)),
            dma((pairs,)),
        ],
        input_output_aliases={3: 0},
        compiler_params=limit,
    )(halo, edge_a, edge_b, base)


def solution(mesh):
    placed = (
        P(("blk", "sub"), None, None),
        P(("blk", "sub"), None, None),
        P(("blk", "sub"), None),
        P(("blk", "sub"), None),
        P(),
        P(),
        P(),
    )
    return jax.shard_map(
        per_device,
        mesh=mesh,
        in_specs=placed,
        out_specs=P(("blk", "sub"), None, None),
        check_vma=False,
    )
```

```python
import functools

import jax
import jax.numpy as jnp
from jax import lax
from jax.experimental import pallas as pl
from jax.experimental.pallas import tpu as pltpu
from jax.sharding import PartitionSpec as P

IB = 90
JB = 60
CELLS = IB * JB
COURANT = 0.2
LANES = 128
TILES = -(-CELLS // LANES)
WIDE = TILES * LANES
GAPS = JB + 1
HALF = IB // 2
PARTS = 32
X_PART = 22
SPARE = 48
PIECE = 16
SCALE = COURANT / 12.0
SIDES = 3
OWN = 8
FIRST_PAIRS = 2


def lane_of(rows):
    return lax.broadcasted_iota(jnp.int32, (rows, LANES), 1)


def rot(value, shift):
    shift = shift % LANES
    return value if shift == 0 else pltpu.roll(value, shift, 1)


def sublanes(value, shift):
    return pltpu.roll(value, shift % 8, 0)


def once(make):
    held = {}

    def get(tile):
        if tile not in held:
            held[tile] = make(tile)
        return held[tile]

    return get


def shifted(get, distance):
    offset = distance % LANES
    turned = once(lambda tile: rot(get(tile), -offset))

    def make(tile):
        low = tile + distance // LANES
        first = turned(low) if 0 <= low < TILES else jnp.zeros((8, LANES), jnp.float32)
        second = turned(low + 1) if 0 <= low + 1 < TILES else jnp.zeros((8, LANES), jnp.float32)
        return jnp.where(lane_of(8) < LANES - offset, first, second)

    return once(make)


def window(get, start, rows):
    tile, offset = start // LANES, start % LANES
    head = rot(get(tile), -offset)
    if offset == 0 or tile + 1 >= TILES:
        return head
    return jnp.where(lane_of(rows) < LANES - offset, head, rot(get(tile + 1), -offset))


def gap_strip(get, offset, wide, rows):
    lane = lane_of(rows)
    place = 1 if wide == 1 and offset > 0 else 0
    value = jnp.zeros((rows, LANES), jnp.float32)
    for turn in range(16):
        cells = []
        for gap in range(turn, GAPS, 16):
            cell = IB * gap + offset
            if cell + wide > 0:
                cells.append((max(cell, 0) % LANES, max(cell, 0) // LANES))
        cells.sort()
        merged = get(cells[0][1])
        for at, tile in cells[1:]:
            merged = jnp.where(lane >= at, get(tile), merged)
        moved = rot(merged, 2 * turn + place - IB * turn - offset)
        value = jnp.where(lane % 32 >= 2 * turn + place, moved, value)
    return value


def edge_strip(get, rows):
    return jnp.where(lane_of(rows) == 0, 0.0, gap_strip(get, -1, 2, rows))


def inner_strip(get, rows):
    return jnp.where(lane_of(rows) % 2 == 0, gap_strip(get, -2, 1, rows), gap_strip(get, 1, 1, rows))


def lane_take(value, index):
    return jnp.take_along_axis(value, index, axis=1, mode="promise_in_bounds")


def tile_getter(ref, rows, count):
    def get(tile):
        if tile + 1 < TILES:
            return ref[rows, tile * LANES : (tile + 1) * LANES]
        rest = jnp.zeros((count, WIDE - CELLS), jnp.float32)
        return jnp.concatenate([ref[rows, tile * LANES : CELLS], rest], axis=1)

    return get


def joined(south, north, half, rows):
    if half == 0:
        return jnp.where(lane_of(rows) < 64, south, rot(north, 64))
    return jnp.where(lane_of(rows) < 64, rot(south, -HALF), rot(north, 64 - HALF))


def pair_copies(source, target, sems, first, pairs):
    copies = []
    for pair in range(pairs):
        into = target.at[pl.ds(8 * pair, 8)].reshape(2, 4, CELLS)
        copies.append(pltpu.make_async_copy(source.at[pl.ds(2 * (first + pair), 2)], into, sems.at[pair]))
    return copies


def pack_kernel(tracer_ref, velocity_ref, depth_ref, out_ref, x_ref, v_ref, d_ref, strip_ref, x_sems, v_sems, d_sem):
    count = depth_ref.shape[0]
    pairs = count // 2
    x_copies = pair_copies(tracer_ref, x_ref, x_sems, 0, pairs)
    v_copies = pair_copies(velocity_ref, v_ref, v_sems, 0, pairs)
    d_copy = pltpu.make_async_copy(depth_ref, d_ref, d_sem)
    for pair in range(pairs):
        x_copies[pair].start()
        v_copies[pair].start()
    d_copy.start()
    for pair in range(pairs):
        rows = pl.ds(8 * pair, 8)
        x_copies[pair].wait()
        get_x = tile_getter(x_ref, rows, 8)
        near, far = edge_strip(get_x, 8), inner_strip(get_x, 8)
        south = [window(get_x, 0, 8), window(get_x, IB, 8)]
        north = [window(get_x, CELLS - IB, 8), window(get_x, CELLS - 2 * IB, 8)]
        v_copies[pair].wait()
        get_v = tile_getter(v_ref, rows, 8)
        v_south, v_north = window(get_v, 0, 8), window(get_v, CELLS - IB, 8)
        strips = [joined(south[0], north[0], half, 8) for half in range(2)]
        strips += [joined(south[1], north[1], half, 8) for half in range(2)]
        strips += [joined(v_south, v_north, half, 8) for half in range(2)]
        strips += [near, far, edge_strip(get_v, 8)]
        for index, strip in enumerate(strips):
            strip_ref[index, rows, :] = strip

    d_copy.wait()
    if out_ref.shape[0] > PARTS * count:
        rest = out_ref.shape[0] - PARTS * count
        out_ref[PARTS * count :, :] = jnp.zeros((rest, LANES), jnp.float32)
    slot_lane = lane_of(count)
    get_d = tile_getter(d_ref, slice(None), count)
    d_south, d_north = window(get_d, 0, count), window(get_d, CELLS - IB, count)
    d_gaps = edge_strip(get_d, count)
    spare = (slot_lane >= SPARE) & (slot_lane < SPARE + PIECE)

    def put(part, value):
        out_ref[part * count : (part + 1) * count, :] = value

    for chan in range(4):
        rows = pl.ds(chan, count, stride=4)
        for half in range(2):
            for deep in range(2):
                part = 2 * (4 * deep + chan) + half
                value = strip_ref[2 * deep + half, rows, :]
                if part < 8:
                    value = jnp.where(spare, rot(d_gaps, SPARE - PIECE * part), value)
                put(part, value)
            if chan >= 2:
                put(2 * (8 + chan - 2) + half, strip_ref[4 + half, rows, :])
        put(X_PART + chan, strip_ref[6, rows, :])
        put(X_PART + 4 + chan, strip_ref[7, rows, :])
        if chan < 2:
            put(X_PART + 8 + chan, strip_ref[8, rows, :])
    for half in range(2):
        put(20 + half, joined(d_south, d_north, half, count))


def route_kernel(part_ref, code_ref, held_ref, out_ref):
    total = held_ref.shape[0]
    rows = out_ref.shape[0]
    part = part_ref[0]
    picked = [jnp.zeros((rows, 2 * LANES), jnp.float32) for _ in range(5)]
    for start in range(0, total, rows):
        held = held_ref[start : start + rows, :]
        high = held.astype(jnp.bfloat16)
        low = (held - high.astype(jnp.float32)).astype(jnp.bfloat16)
        halves = jnp.concatenate([high, low], axis=1)
        source = lax.broadcasted_iota(jnp.int32, (rows, rows), 1) + start
        for side in range(5):
            one_hot = jnp.where(code_ref[:, side : side + 1] == source, 1.0, 0.0).astype(jnp.bfloat16)
            picked[side] += jnp.dot(one_hot, halves, preferred_element_type=jnp.float32)
    west, east, south, north, fold = [value[:, :LANES] + value[:, LANES:] for value in picked]
    lane = lane_of(rows)
    along_x = (part >= X_PART) | ((part < 8) & (lane >= SPARE) & (lane < SPARE + PIECE))
    x_side = jnp.where(lane % 2 == 0, west, east)
    y_side = jnp.where(lane < 64, north + rot(fold, 64), south)
    out_ref[...] = jnp.where(along_x, x_side, y_side)


def bulk_kernel(first, my_ref, tracer_ref, velocity_ref, depth_ref, kappa_ref, code_ref,
                base_ref, edge_ref, y_ref, x_ref, v_ref, d_ref, k_ref, d8_ref, k8_ref, w_ref, z_ref, x_sems, v_sems, y_sems, d_sems):
    count = depth_ref.shape[0]
    pairs = edge_ref.shape[1] // 8
    x_copies = pair_copies(tracer_ref, x_ref, x_sems, first, pairs)
    v_copies = pair_copies(velocity_ref, v_ref, v_sems, first, pairs)
    d_copy = pltpu.make_async_copy(depth_ref, d_ref, d_sems.at[0])
    k_copy = pltpu.make_async_copy(kappa_ref, k_ref, d_sems.at[1])
    d_copy.start()
    k_copy.start()
    for pair in range(pairs):
        v_copies[pair].start()
        x_copies[pair].start()
    lane = lane_of(8)
    row = lax.broadcasted_iota(jnp.int32, (8, LANES), 0)
    x_row, even, place = row % 4 < 2, row % 2 == 0, row % 4
    level = (row % 2).astype(jnp.float32)
    zero = jnp.zeros((8, LANES), jnp.float32)

    def all_rows(value, chosen):
        result = value
        for at in range(4):
            if at != chosen:
                result = jnp.where(place == at, sublanes(value, at - chosen), result)
        return result

    def wet_of(depth):
        return jnp.clip(depth - level, 0.0, 1.0)

    for copy, source, target in ((d_copy, d_ref, d8_ref), (k_copy, k_ref, k8_ref)):
        copy.wait()
        for pair in range(pairs):
            slot = 2 * (first + pair)
            for start in range(0, CELLS, LANES):
                columns = slice(start, min(start + LANES, CELLS))
                shape = (8, columns.stop - start)
                top, low = [jnp.broadcast_to(source[slot + at : slot + at + 1, columns], shape) for at in range(2)]
                target[8 * pair : 8 * pair + 8, columns] = jnp.where(row[:, : shape[1]] < 4, top, low)

    def one_pair(pair):
        slot = 2 * (first + pair)
        rows = pl.ds(pl.multiple_of(8 * pair, 8), 8)
        for source, target, sems in ((velocity_ref, v_ref, v_sems), (tracer_ref, x_ref, x_sems)):
            pltpu.make_async_copy(
                source.at[pl.ds(0, 2)], target.at[rows].reshape(2, 4, CELLS), sems.at[pair]).wait()

        codes = [code_ref[pl.ds(my_ref[0] * count + slot + at, 1), :] for at in range(2)]

        def flag(column):
            pieces = [jnp.broadcast_to(code[:, column : column + 1], (8, LANES)) for code in codes]
            return jnp.where(row < 4, pieces[0], pieces[1]) >= 0

        live, folded = flag(5), flag(4)
        state, velocity = once(tile_getter(x_ref, rows, 8)), once(tile_getter(v_ref, rows, 8))
        depth, kappa = once(tile_getter(d8_ref, rows, 8)), once(tile_getter(k8_ref, rows, 8))
        wet = once(lambda tile: wet_of(depth(tile)))

        @once
        def ratio(tile):
            other = jnp.clip(depth(tile) - (1.0 - level), 0.0, 1.0)
            coupling = kappa(tile) * (wet(tile) * other)
            return coupling / (1.0 + 2.0 * coupling)

        next_vel = [shifted(velocity, 1), shifted(velocity, IB)]
        next_wet = [shifted(wet, 1), shifted(wet, IB)]

        @once
        def face(tile):
            rims = [at - tile * LANES for at in range(IB - 1, CELLS, IB) if at // LANES == tile]
            rim = functools.reduce(jnp.logical_or, [lane == at for at in rims]) if rims else None
            across = next_wet[0](tile) if rim is None else jnp.where(rim, 0.0, next_wet[0](tile))
            speed = velocity(tile) + jnp.where(x_row, next_vel[0](tile), next_vel[1](tile))
            value = SCALE * speed * (wet(tile) * jnp.where(x_row, across, next_wet[1](tile)))
            w_ref[:, tile * LANES : (tile + 1) * LANES] = value
            return value

        face_x = once(lambda tile: jnp.where(x_row, face(tile), sublanes(face(tile), 2)))
        face_y = once(lambda tile: jnp.where(x_row, sublanes(face(tile), -2), face(tile)))
        five = once(lambda tile: 5.0 * state(tile))
        two = once(lambda tile: 2.0 * state(tile))

        def divergence(speed, distance):
            before, after = shifted(state, -distance), shifted(state, distance)
            lower = once(lambda tile: five(tile) - before(tile) + 2.0 * after(tile))
            upper = shifted(once(lambda tile: five(tile) - after(tile)), distance)

            @once
            def flux(tile):
                value = jnp.maximum(speed(tile), 0.0) * lower(tile)
                return value + jnp.minimum(speed(tile), 0.0) * (two(tile) + upper(tile))

            back = shifted(flux, -distance)
            for stage in (after, before, lower, upper, flux, back):
                for tile in range(TILES):
                    stage(tile)
            return once(lambda tile: flux(tile) - back(tile))

        for stage in (depth, wet, ratio, *next_vel, *next_wet, face):
            for tile in range(TILES):
                stage(tile)
        change_x, change_y = divergence(face_x, 1), divergence(face_y, IB)
        for tile in range(TILES):
            explicit = state(tile) - wet(tile) * (change_x(tile) + change_y(tile))
            other = jnp.where(even, sublanes(explicit, -1), sublanes(explicit, 1))
            value = jnp.where(live, explicit + ratio(tile) * (other - explicit), zero)
            stop = min((tile + 1) * LANES, CELLS)
            y_ref[rows, tile * LANES : stop] = value[:, : stop - tile * LANES]
            mixed = jnp.where(x_row, face(tile), jnp.where(even, ratio(tile), depth(tile)))
            z_ref[:, tile * LANES : (tile + 1) * LANES] = mixed

        pltpu.make_async_copy(
            y_ref.at[rows].reshape(2, 4, CELLS), base_ref.at[pl.ds(slot, 2)], y_sems.at[pair]).start()
        get_w, get_z = [lambda tile, ref=ref: ref[:, tile * LANES : (tile + 1) * LANES] for ref in (w_ref, z_ref)]
        east = lane % 2 == 0
        near, far, normal = edge_strip(state, 8), inner_strip(state, 8), edge_strip(velocity, 8)
        outer, inner = edge_strip(get_z, 8), inner_strip(get_z, 8)
        normal = jnp.where(x_row, normal, sublanes(normal, 2))
        rim_speed = jnp.where(east, inner, outer)
        rim_speed = jnp.where(x_row, rim_speed, sublanes(rim_speed, 2))
        sides = [(
            near, far, jnp.where(east, -normal, normal), jnp.where(east, -rim_speed, rim_speed), outer, inner,
        )]
        for outer, inner, edge, sign in ((0, IB, 0, 1.0), (CELLS - IB, CELLS - 2 * IB, CELLS - 2 * IB, -1.0)):
            normal, rim_speed = window(velocity, outer, 8), window(get_w, edge, 8)
            normal = sign * jnp.where(x_row, sublanes(normal, -2), normal)
            rim_speed = sign * jnp.where(x_row, sublanes(rim_speed, -2), rim_speed)
            sides.append((window(state, outer, 8), window(state, inner, 8), normal, rim_speed,
                          window(get_z, outer, 8), window(get_z, inner, 8)))
        for side, (near, far, normal, rim_speed, outer, inner) in enumerate(sides):
            values = (near, far, normal, jnp.where(live, jnp.maximum(rim_speed, 0.0), zero), wet_of(all_rows(outer, 3)),
                      wet_of(all_rows(inner, 3)), all_rows(outer, 2), all_rows(inner, 2))
            for index, value in enumerate(values):
                edge_ref[OWN * side + index, rows, :] = value
        edge_ref[OWN * SIDES, rows, :] = jnp.where(folded, 1.0, zero)

    pl.loop(0, pairs)(one_pair)
    for pair in range(pairs):
        slots = pl.ds(2 * (first + pair), 2)
        rows = y_ref.at[pl.ds(8 * pair, 8)].reshape(2, 4, CELLS)
        pltpu.make_async_copy(rows, base_ref.at[slots], y_sems.at[pair]).wait()


def finish_kernel(halo_ref, edge_a_ref, edge_b_ref, base_ref, out_ref,
                  y_ref, own_ref, raw_ref, delta_ref, own_sems, in_sems, out_sems):
    count = out_ref.shape[0]
    pairs = count // 2
    rows = 4 * count
    split = edge_a_ref.shape[1]
    own_copies = [
        pltpu.make_async_copy(edge_a_ref, own_ref.at[:, pl.ds(0, split)], own_sems.at[0]),
        pltpu.make_async_copy(edge_b_ref, own_ref.at[:, pl.ds(split, rows - split)], own_sems.at[1]),
    ]
    in_copies = pair_copies(base_ref, y_ref, in_sems, 0, pairs)
    for copy in own_copies + in_copies:
        copy.start()
    lane = lane_of(rows)
    level = (lax.broadcasted_iota(jnp.int32, (rows, LANES), 0) % 2).astype(jnp.float32)

    def part(index):
        return halo_ref[index * count : (index + 1) * count, :]

    def assembled(index, parts):
        for chan, value in enumerate(parts):
            raw_ref[index, pl.ds(chan, count, stride=4), :] = value
        return raw_ref[index]

    mirror = jnp.where(lane < IB, IB - 1 - lane, lane)
    slot_lane = lane_of(count)
    depth_x = rot(part(0), -SPARE)
    for index in range(1, 8):
        depth_x = jnp.where(slot_lane >= PIECE * index, rot(part(index), PIECE * index - SPARE), depth_x)
    x_raw = [[part(X_PART + chan) for chan in range(4)], [part(X_PART + 4 + chan) for chan in range(4)],
             [part(X_PART + 8 + chan % 2) for chan in range(4)], [depth_x] * 4]
    y_values = [list(range(4)), list(range(4, 8)), [8, 9, 8, 9], [10] * 4]
    x_halo, south_halo, north_raw = [], [], []
    for kind in range(4):
        raw = assembled(3 * kind, x_raw[kind])
        x_halo.append(jnp.where(lane % 2 == 0, rot(raw, 1), rot(raw, -1)))
        first, second = [assembled(3 * kind + 1 + half, [part(2 * value + half) for value in y_values[kind]])
                         for half in range(2)]
        south_halo.append(jnp.where(lane < HALF, rot(first, 64), rot(second, 64 + HALF)))
        north_raw.append(jnp.where(lane < HALF, first, rot(second, HALF)))
    for copy in own_copies:
        copy.wait()
    folded = own_ref[OWN * SIDES] > 0.0
    north_halo = []
    for kind, raw in enumerate(north_raw):
        turned = lane_take(raw, mirror)
        north_halo.append(jnp.where(folded, -turned if kind == 2 else turned, raw))

    for side, (out_near, out_far, out_normal, out_depth) in enumerate((x_halo, south_halo, north_halo)):
        near, far, normal, rim_speed, wet, inner_wet, ratio, inner_ratio = [
            own_ref[OWN * side + index] for index in range(OWN)]
        if side == 0:
            out_normal = jnp.where(lane % 2 == 0, -out_normal, out_normal)
            beyond = out_near - jnp.where(lane % 2 == 0, rot(near, -1), rot(near, 1))
        else:
            out_normal = -out_normal if side == 2 else out_normal
            beyond = out_near
        speed = SCALE * (normal + out_normal) * (wet * jnp.clip(out_depth - level, 0.0, 1.0))
        flux = jnp.maximum(speed, 0.0) * (5.0 * out_near + 2.0 * near - out_far)
        flux += jnp.minimum(speed, 0.0) * (2.0 * out_near + 5.0 * near - far)
        inner_flux = rim_speed * beyond
        for place, (change, share) in enumerate(((wet * (flux + inner_flux), ratio),
                                                 (-inner_wet * inner_flux, inner_ratio))):
            other = jnp.where(level == 0.0, pltpu.roll(change, rows - 1, 0), pltpu.roll(change, 1, 0))
            delta_ref[2 * side + place] = change + share * (other - change)

    lane = lane_of(8)
    out_copies = []
    for pair in range(pairs):
        mine = pl.ds(8 * pair, 8)
        in_copies[pair].wait()
        near, deep, south, south_in, north, north_in = [delta_ref[index, mine, :] for index in range(2 * SIDES)]
        groups = []
        for at in range(2):
            index = 2 * (lane // 4) + (lane % 4) // 2 + 64 * at
            outer, inner = lane_take(near, index), lane_take(deep, index)
            groups.append(jnp.where((lane % 4 == 1) | (lane % 4 == 2), outer, inner))
        placed = [(groups[gap // 32], 4 * (gap % 32), IB * gap - 2, 4) for gap in range(GAPS)]
        placed += [(south, 0, 0, IB), (south_in, 0, IB, IB)]
        placed += [(north, 0, CELLS - IB, IB), (north_in, 0, CELLS - 2 * IB, IB)]
        for tile in range(TILES):
            at, stop = tile * LANES, min((tile + 1) * LANES, CELLS)
            change = jnp.zeros((8, LANES), jnp.float32)
            for source, origin, start, wide in placed:
                low, high = max(start, at, 0), min(start + wide, stop)
                if low < high:
                    inside = (lane >= low - at) & (lane < high - at)
                    change += jnp.where(inside, rot(source, start - at - origin), 0.0)
            y_ref[mine, at:stop] = y_ref[mine, at:stop] + change[:, : stop - at]
        copy = pltpu.make_async_copy(
            y_ref.at[mine].reshape(2, 4, CELLS), out_ref.at[pl.ds(2 * pair, 2)], out_sems.at[pair])
        copy.start()
        out_copies.append(copy)
    for copy in out_copies:
        copy.wait()


def route_codes(block_owner, neighbours, fold_partner, slot_total):
    block_count = block_owner.shape[0]
    hits = block_owner[None, :] == jnp.arange(slot_total, dtype=jnp.int32)[:, None]
    links = jnp.concatenate([neighbours, fold_partner[:, None]], axis=1)
    linked = links[:, :, None] == jnp.arange(block_count, dtype=jnp.int32)[None, None, :]
    link_slots = jnp.max(jnp.where(linked, block_owner[None, None, :], -1), axis=2)
    link_slots = jnp.concatenate([link_slots, block_owner[:, None]], axis=1)
    return jnp.max(jnp.where(hits[:, :, None], link_slots[None], -1), axis=1)


def per_device(tracers, velocity, kappa, kmt, block_owner, neighbours, fold_partner):
    slot_count, chans = tracers.shape[:2]
    sub_count = lax.axis_size("sub")
    device_count = lax.axis_size("blk") * sub_count
    if device_count % PARTS or chans != 4 or slot_count % 2 or slot_count < 2 * FIRST_PAIRS + 2:
        raise ValueError("unsupported sizes")
    my_index = (lax.axis_index("blk") * sub_count + lax.axis_index("sub")).astype(jnp.int32).reshape(1)
    axes = ("blk", "sub")
    pairs = slot_count // 2
    slot_total = device_count * slot_count
    state_rows = 4 * slot_count
    f32 = jnp.float32
    in_hbm = pl.BlockSpec(memory_space=pltpu.HBM)
    anywhere = pl.BlockSpec(memory_space=pl.ANY)
    in_vmem = pl.BlockSpec(memory_space=pltpu.VMEM)
    in_smem = pl.BlockSpec(memory_space=pltpu.SMEM)
    dma = pltpu.SemaphoreType.DMA
    limit = pltpu.CompilerParams(vmem_limit_bytes=32 * 1024 * 1024)

    def exchanged(pieces):
        pieces = pieces.reshape(device_count, slot_count, 1, LANES)
        return lax.all_to_all(pieces, axes, 0, 0, tiled=True).reshape(slot_total, LANES)

    pack = pl.pallas_call(
        pack_kernel,
        out_shape=jax.ShapeDtypeStruct((slot_total, LANES), f32),
        in_specs=[in_hbm, in_hbm, in_hbm],
        out_specs=in_vmem,
        scratch_shapes=[
            pltpu.VMEM((state_rows, CELLS), f32),
            pltpu.VMEM((state_rows, CELLS), f32),
            pltpu.VMEM((slot_count, CELLS), f32),
            pltpu.VMEM((9, state_rows, LANES), f32),
            dma((pairs,)),
            dma((pairs,)),
            dma,
        ],
        cost_estimate=pl.CostEstimate(flops=4_000_000, bytes_accessed=2_400_000, transcendentals=0),
    )(tracers, velocity, kmt)
    held = exchanged(pack)
    codes = route_codes(block_owner, neighbours, fold_partner, slot_total)

    def bulk(first, some, codes, base):
        kernel = functools.partial(bulk_kernel, first)
        extra = [] if base is None else [base]
        if extra:
            kernel = lambda *refs: bulk_kernel(first, *refs[:6], *refs[7:])
        return pl.pallas_call(
            kernel,
            out_shape=[
                jax.ShapeDtypeStruct(tracers.shape, f32),
                jax.ShapeDtypeStruct((OWN * SIDES + 1, 8 * some, LANES), f32),
            ],
            in_specs=[in_smem, in_hbm, in_hbm, in_hbm, in_hbm, in_vmem] + [in_hbm] * len(extra),
            out_specs=[in_hbm, in_vmem],
            scratch_shapes=[
                pltpu.VMEM((8 * some, CELLS), f32),
                pltpu.VMEM((8 * some, CELLS), f32),
                pltpu.VMEM((8 * some, CELLS), f32),
                pltpu.VMEM((slot_count, CELLS), f32),
                pltpu.VMEM((slot_count, CELLS), f32),
                pltpu.VMEM((8 * some, CELLS), f32),
                pltpu.VMEM((8 * some, CELLS), f32),
                pltpu.VMEM((8, WIDE), f32),
                pltpu.VMEM((8, WIDE), f32),
                dma((some,)),
                dma((some,)),
                dma((some,)),
                dma((2,)),
            ],
            input_output_aliases={6: 0} if extra else {},
            compiler_params=limit,
            cost_estimate=pl.CostEstimate(flops=4_000_000 * some, bytes_accessed=800_000 * some, transcendentals=0),
        )(my_index, tracers, velocity, kmt, kappa, codes, *extra)

    base, edge_a = bulk(0, FIRST_PAIRS, codes, None)
    held, edge_a = lax.optimization_barrier((held, edge_a))

    routed_rows = PARTS * slot_count
    routed = pl.pallas_call(
        route_kernel,
        grid=(device_count // PARTS,),
        out_shape=jax.ShapeDtypeStruct((slot_total, LANES), f32),
        in_specs=[
            in_smem,
            pl.BlockSpec((routed_rows, 6), lambda step: (step, 0)),
            pl.BlockSpec((slot_total, LANES), lambda step: (0, 0)),
        ],
        out_specs=pl.BlockSpec((routed_rows, LANES), lambda step: (step, 0)),
        compiler_params=limit,
    )(my_index, codes, held)

    routed, base = lax.optimization_barrier((routed, base))
    base, edge_b = bulk(FIRST_PAIRS, pairs - FIRST_PAIRS, codes, base)
    halo = exchanged(routed)[: PARTS * slot_count]

    return pl.pallas_call(
        finish_kernel,
        out_shape=jax.ShapeDtypeStruct(tracers.shape, f32),
        in_specs=[in_vmem, anywhere, anywhere, in_hbm],
        out_specs=in_hbm,
        scratch_shapes=[
            pltpu.VMEM((state_rows, CELLS), f32),
            pltpu.VMEM((OWN * SIDES + 1, state_rows, LANES), f32),
            pltpu.VMEM((12, state_rows, LANES), f32),
            pltpu.VMEM((2 * SIDES, state_rows, LANES), f32),
            dma((2,)),
            dma((pairs,)),
            dma((pairs,)),
        ],
        input_output_aliases={3: 0},
        compiler_params=limit,
    )(halo, edge_a, edge_b, base)


def solution(mesh):
    placed = (
        P(("blk", "sub"), None, None),
        P(("blk", "sub"), None, None),
        P(("blk", "sub"), None),
        P(("blk", "sub"), None),
        P(),
        P(),
        P(),
    )
    return jax.shard_map(
        per_device,
        mesh=mesh,
        in_specs=placed,
        out_specs=P(("blk", "sub"), None, None),
        check_vma=False,
    )
```

```python
import functools

import jax
import jax.numpy as jnp
from jax import lax
from jax.experimental import pallas as pl
from jax.experimental.pallas import tpu as pltpu
from jax.sharding import PartitionSpec as P

IB = 90
JB = 60
CELLS = IB * JB
COURANT = 0.2
LANES = 128
TILES = -(-CELLS // LANES)
WIDE = TILES * LANES
GAPS = JB + 1
HALF = IB // 2
PARTS = 32
X_PART = 22
SPARE = 48
PIECE = 16
SCALE = COURANT / 12.0
SIDES = 3
OWN = 8
FIRST_PAIRS = 2


def lane_of(rows):
    return lax.broadcasted_iota(jnp.int32, (rows, LANES), 1)


def rot(value, shift):
    shift = shift % LANES
    return value if shift == 0 else pltpu.roll(value, shift, 1)


def sublanes(value, shift):
    return pltpu.roll(value, shift % 8, 0)


def once(make):
    held = {}

    def get(tile):
        if tile not in held:
            held[tile] = make(tile)
        return held[tile]

    return get


def shifted(get, distance):
    offset = distance % LANES
    turned = once(lambda tile: rot(get(tile), -offset))

    def make(tile):
        low = tile + distance // LANES
        first = turned(low) if 0 <= low < TILES else jnp.zeros((8, LANES), jnp.float32)
        second = turned(low + 1) if 0 <= low + 1 < TILES else jnp.zeros((8, LANES), jnp.float32)
        return jnp.where(lane_of(8) < LANES - offset, first, second)

    return once(make)


def window(get, start, rows):
    tile, offset = start // LANES, start % LANES
    value = get(tile)
    if offset > 0 and tile + 1 < TILES:
        value = jnp.where(lane_of(rows) < offset, get(tile + 1), value)
    return rot(value, -offset)


def gap_strip(get, offset, wide, rows):
    lane = lane_of(rows)
    place = 1 if wide == 1 and offset > 0 else 0
    value = jnp.zeros((rows, LANES), jnp.float32)
    for turn in range(16):
        cells = []
        for gap in range(turn, GAPS, 16):
            cell = IB * gap + offset
            if cell + wide > 0:
                cells.append((max(cell, 0) % LANES, max(cell, 0) // LANES))
        cells.sort()
        merged = get(cells[0][1])
        for at, tile in cells[1:]:
            merged = jnp.where(lane >= at, get(tile), merged)
        moved = rot(merged, 2 * turn + place - IB * turn - offset)
        value = jnp.where(lane % 32 >= 2 * turn + place, moved, value)
    return value


def edge_strip(get, rows):
    return jnp.where(lane_of(rows) == 0, 0.0, gap_strip(get, -1, 2, rows))


def inner_strip(get, rows):
    return jnp.where(lane_of(rows) % 2 == 0, gap_strip(get, -2, 1, rows), gap_strip(get, 1, 1, rows))


def lane_take(value, index):
    return jnp.take_along_axis(value, index, axis=1, mode="promise_in_bounds")


def tile_getter(ref, rows, count):
    def get(tile):
        if tile + 1 < TILES:
            return ref[rows, tile * LANES : (tile + 1) * LANES]
        rest = jnp.zeros((count, WIDE - CELLS), jnp.float32)
        return jnp.concatenate([ref[rows, tile * LANES : CELLS], rest], axis=1)

    return get


def joined(south, north, half, rows):
    if half == 0:
        return jnp.where(lane_of(rows) < 64, south, rot(north, 64))
    return jnp.where(lane_of(rows) < 64, rot(south, -HALF), rot(north, 64 - HALF))


def pair_copies(source, target, sems, first, pairs):
    copies = []
    for pair in range(pairs):
        into = target.at[pl.ds(8 * pair, 8)].reshape(2, 4, CELLS)
        copies.append(pltpu.make_async_copy(source.at[pl.ds(2 * (first + pair), 2)], into, sems.at[pair]))
    return copies


def pack_kernel(tracer_ref, velocity_ref, depth_ref, out_ref, x_ref, v_ref, d_ref, strip_ref, x_sems, v_sems, d_sem):
    count = depth_ref.shape[0]
    pairs = count // 2
    x_copies = pair_copies(tracer_ref, x_ref, x_sems, 0, pairs)
    v_copies = pair_copies(velocity_ref, v_ref, v_sems, 0, pairs)
    d_copy = pltpu.make_async_copy(depth_ref, d_ref, d_sem)
    for pair in range(pairs):
        x_copies[pair].start()
        v_copies[pair].start()
    d_copy.start()
    for pair in range(pairs):
        rows = pl.ds(8 * pair, 8)
        x_copies[pair].wait()
        get_x = tile_getter(x_ref, rows, 8)
        near, far = edge_strip(get_x, 8), inner_strip(get_x, 8)
        south = [window(get_x, 0, 8), window(get_x, IB, 8)]
        north = [window(get_x, CELLS - IB, 8), window(get_x, CELLS - 2 * IB, 8)]
        v_copies[pair].wait()
        get_v = tile_getter(v_ref, rows, 8)
        v_south, v_north = window(get_v, 0, 8), window(get_v, CELLS - IB, 8)
        strips = [joined(south[0], north[0], half, 8) for half in range(2)]
        strips += [joined(south[1], north[1], half, 8) for half in range(2)]
        strips += [joined(v_south, v_north, half, 8) for half in range(2)]
        strips += [near, far, edge_strip(get_v, 8)]
        for index, strip in enumerate(strips):
            strip_ref[index, rows, :] = strip

    d_copy.wait()
    if out_ref.shape[0] > PARTS * count:
        rest = out_ref.shape[0] - PARTS * count
        out_ref[PARTS * count :, :] = jnp.zeros((rest, LANES), jnp.float32)
    slot_lane = lane_of(count)
    get_d = tile_getter(d_ref, slice(None), count)
    d_south, d_north = window(get_d, 0, count), window(get_d, CELLS - IB, count)
    d_gaps = edge_strip(get_d, count)
    spare = (slot_lane >= SPARE) & (slot_lane < SPARE + PIECE)

    def put(part, value):
        out_ref[part * count : (part + 1) * count, :] = value

    for chan in range(4):
        rows = pl.ds(chan, count, stride=4)
        for half in range(2):
            for deep in range(2):
                part = 2 * (4 * deep + chan) + half
                value = strip_ref[2 * deep + half, rows, :]
                if part < 8:
                    value = jnp.where(spare, rot(d_gaps, SPARE - PIECE * part), value)
                put(part, value)
            if chan >= 2:
                put(2 * (8 + chan - 2) + half, strip_ref[4 + half, rows, :])
        put(X_PART + chan, strip_ref[6, rows, :])
        put(X_PART + 4 + chan, strip_ref[7, rows, :])
        if chan < 2:
            put(X_PART + 8 + chan, strip_ref[8, rows, :])
    for half in range(2):
        put(20 + half, joined(d_south, d_north, half, count))


def route_kernel(part_ref, code_ref, held_ref, out_ref):
    total = held_ref.shape[0]
    rows = out_ref.shape[0]
    part = part_ref[0]
    fold = code_ref[:, 4:5]
    wanted = [code_ref[:, side : side + 1] for side in range(3)] + [jnp.maximum(code_ref[:, 3:4], fold)]
    picked = [jnp.zeros((rows, 2 * LANES), jnp.float32) for _ in wanted]
    for start in range(0, total, rows):
        held = held_ref[start : start + rows, :]
        high = held.astype(jnp.bfloat16)
        low = (held - high.astype(jnp.float32)).astype(jnp.bfloat16)
        halves = jnp.concatenate([high, low], axis=1)
        source = lax.broadcasted_iota(jnp.int32, (rows, rows), 1) + start
        for side, code in enumerate(wanted):
            one_hot = jnp.where(code == source, 1.0, 0.0).astype(jnp.bfloat16)
            picked[side] += jnp.dot(one_hot, halves, preferred_element_type=jnp.float32)
    west, east, south, north = [value[:, :LANES] + value[:, LANES:] for value in picked]
    lane = lane_of(rows)
    along_x = (part >= X_PART) | ((part < 8) & (lane >= SPARE) & (lane < SPARE + PIECE))
    x_side = jnp.where(lane % 2 == 0, west, east)
    y_side = jnp.where(lane < 64, jnp.where(fold >= 0, rot(north, 64), north), south)
    out_ref[...] = jnp.where(along_x, x_side, y_side)


def bulk_kernel(first, my_ref, tracer_ref, velocity_ref, depth_ref, kappa_ref, code_ref,
                base_ref, edge_ref, y_ref, x_ref, v_ref, d_ref, k_ref, d8_ref, k8_ref, w_ref, z_ref, x_sems, v_sems, y_sems, d_sems):
    count = depth_ref.shape[0]
    pairs = edge_ref.shape[1] // 8
    x_copies = pair_copies(tracer_ref, x_ref, x_sems, first, pairs)
    v_copies = pair_copies(velocity_ref, v_ref, v_sems, first, pairs)
    d_copy = pltpu.make_async_copy(depth_ref, d_ref, d_sems.at[0])
    k_copy = pltpu.make_async_copy(kappa_ref, k_ref, d_sems.at[1])
    d_copy.start()
    k_copy.start()
    for pair in range(pairs):
        v_copies[pair].start()
        x_copies[pair].start()
    lane = lane_of(8)
    row = lax.broadcasted_iota(jnp.int32, (8, LANES), 0)
    x_row, even, place = row % 4 < 2, row % 2 == 0, row % 4
    level = (row % 2).astype(jnp.float32)
    zero = jnp.zeros((8, LANES), jnp.float32)

    def all_rows(value, chosen):
        result = value
        for at in range(4):
            if at != chosen:
                result = jnp.where(place == at, sublanes(value, at - chosen), result)
        return result

    def wet_of(depth):
        return jnp.clip(depth - level, 0.0, 1.0)

    for copy, source, target in ((d_copy, d_ref, d8_ref), (k_copy, k_ref, k8_ref)):
        copy.wait()
        for pair in range(pairs):
            slot = 2 * (first + pair)
            for start in range(0, CELLS, LANES):
                columns = slice(start, min(start + LANES, CELLS))
                shape = (8, columns.stop - start)
                top, low = [jnp.broadcast_to(source[slot + at : slot + at + 1, columns], shape) for at in range(2)]
                target[8 * pair : 8 * pair + 8, columns] = jnp.where(row[:, : shape[1]] < 4, top, low)

    def one_pair(pair):
        slot = 2 * (first + pair)
        rows = pl.ds(pl.multiple_of(8 * pair, 8), 8)
        for source, target, sems in ((velocity_ref, v_ref, v_sems), (tracer_ref, x_ref, x_sems)):
            pltpu.make_async_copy(
                source.at[pl.ds(0, 2)], target.at[rows].reshape(2, 4, CELLS), sems.at[pair]).wait()

        codes = [code_ref[pl.ds(my_ref[0] * count + slot + at, 1), :] for at in range(2)]

        def flag(column):
            pieces = [jnp.broadcast_to(code[:, column : column + 1], (8, LANES)) for code in codes]
            return jnp.where(row < 4, pieces[0], pieces[1]) >= 0

        live, folded = flag(5), flag(4)
        state, velocity = once(tile_getter(x_ref, rows, 8)), once(tile_getter(v_ref, rows, 8))
        depth, kappa = once(tile_getter(d8_ref, rows, 8)), once(tile_getter(k8_ref, rows, 8))
        wet = once(lambda tile: wet_of(depth(tile)))

        @once
        def ratio(tile):
            other = jnp.clip(depth(tile) - (1.0 - level), 0.0, 1.0)
            coupling = kappa(tile) * (wet(tile) * other)
            return coupling / (1.0 + 2.0 * coupling)

        next_vel = [shifted(velocity, 1), shifted(velocity, IB)]
        next_wet = [shifted(wet, 1), shifted(wet, IB)]

        @once
        def face(tile):
            rims = [at - tile * LANES for at in range(IB - 1, CELLS, IB) if at // LANES == tile]
            rim = functools.reduce(jnp.logical_or, [lane == at for at in rims]) if rims else None
            across = next_wet[0](tile) if rim is None else jnp.where(rim, 0.0, next_wet[0](tile))
            speed = velocity(tile) + jnp.where(x_row, next_vel[0](tile), next_vel[1](tile))
            value = SCALE * speed * (wet(tile) * jnp.where(x_row, across, next_wet[1](tile)))
            w_ref[:, tile * LANES : (tile + 1) * LANES] = value
            return value

        face_x = once(lambda tile: jnp.where(x_row, face(tile), sublanes(face(tile), 2)))
        face_y = once(lambda tile: jnp.where(x_row, sublanes(face(tile), -2), face(tile)))
        five = once(lambda tile: 5.0 * state(tile))
        two = once(lambda tile: 2.0 * state(tile))

        def divergence(speed, distance):
            before, after = shifted(state, -distance), shifted(state, distance)
            lower = once(lambda tile: five(tile) - before(tile) + 2.0 * after(tile))
            upper = shifted(once(lambda tile: five(tile) - after(tile)), distance)

            @once
            def flux(tile):
                value = jnp.maximum(speed(tile), 0.0) * lower(tile)
                return value + jnp.minimum(speed(tile), 0.0) * (two(tile) + upper(tile))

            back = shifted(flux, -distance)
            for stage in (after, before, lower, upper, flux, back):
                for tile in range(TILES):
                    stage(tile)
            return once(lambda tile: flux(tile) - back(tile))

        for stage in (depth, wet, ratio, *next_vel, *next_wet, face):
            for tile in range(TILES):
                stage(tile)
        change_x, change_y = divergence(face_x, 1), divergence(face_y, IB)
        for tile in range(TILES):
            explicit = state(tile) - wet(tile) * (change_x(tile) + change_y(tile))
            other = jnp.where(even, sublanes(explicit, -1), sublanes(explicit, 1))
            value = jnp.where(live, explicit + ratio(tile) * (other - explicit), zero)
            stop = min((tile + 1) * LANES, CELLS)
            y_ref[rows, tile * LANES : stop] = value[:, : stop - tile * LANES]
            mixed = jnp.where(x_row, face(tile), jnp.where(even, ratio(tile), depth(tile)))
            z_ref[:, tile * LANES : (tile + 1) * LANES] = mixed

        pltpu.make_async_copy(
            y_ref.at[rows].reshape(2, 4, CELLS), base_ref.at[pl.ds(slot, 2)], y_sems.at[pair]).start()
        get_w, get_z = [lambda tile, ref=ref: ref[:, tile * LANES : (tile + 1) * LANES] for ref in (w_ref, z_ref)]
        east = lane % 2 == 0
        near, far, normal = edge_strip(state, 8), inner_strip(state, 8), edge_strip(velocity, 8)
        outer, inner = edge_strip(get_z, 8), inner_strip(get_z, 8)
        normal = jnp.where(x_row, normal, sublanes(normal, 2))
        rim_speed = jnp.where(east, inner, outer)
        rim_speed = jnp.where(x_row, rim_speed, sublanes(rim_speed, 2))
        sides = [(
            near, far, jnp.where(east, -normal, normal), jnp.where(east, -rim_speed, rim_speed), outer, inner,
        )]
        for outer, inner, edge, sign in ((0, IB, 0, 1.0), (CELLS - IB, CELLS - 2 * IB, CELLS - 2 * IB, -1.0)):
            normal, rim_speed = window(velocity, outer, 8), window(get_w, edge, 8)
            normal = sign * jnp.where(x_row, sublanes(normal, -2), normal)
            rim_speed = sign * jnp.where(x_row, sublanes(rim_speed, -2), rim_speed)
            sides.append((window(state, outer, 8), window(state, inner, 8), normal, rim_speed,
                          window(get_z, outer, 8), window(get_z, inner, 8)))
        for side, (near, far, normal, rim_speed, outer, inner) in enumerate(sides):
            values = (near, far, normal, jnp.where(live, jnp.maximum(rim_speed, 0.0), zero), wet_of(all_rows(outer, 3)),
                      wet_of(all_rows(inner, 3)), all_rows(outer, 2), all_rows(inner, 2))
            for index, value in enumerate(values):
                edge_ref[OWN * side + index, rows, :] = value
        edge_ref[OWN * SIDES, rows, :] = jnp.where(folded, 1.0, zero)

    pl.loop(0, pairs)(one_pair)
    for pair in range(pairs):
        slots = pl.ds(2 * (first + pair), 2)
        rows = y_ref.at[pl.ds(8 * pair, 8)].reshape(2, 4, CELLS)
        pltpu.make_async_copy(rows, base_ref.at[slots], y_sems.at[pair]).wait()


def finish_kernel(arrived_ref, edge_a_ref, edge_b_ref, base_ref, out_ref,
                  halo_ref, y_ref, own_ref, raw_ref, delta_ref, own_sems, in_sems, out_sems):
    count = out_ref.shape[0]
    pairs = count // 2
    rows = 4 * count
    split = edge_a_ref.shape[1]
    halo_copy = pltpu.make_async_copy(arrived_ref, halo_ref, own_sems.at[2])
    own_copies = [
        pltpu.make_async_copy(edge_a_ref, own_ref.at[:, pl.ds(0, split)], own_sems.at[0]),
        pltpu.make_async_copy(edge_b_ref, own_ref.at[:, pl.ds(split, rows - split)], own_sems.at[1]),
    ]
    in_copies = pair_copies(base_ref, y_ref, in_sems, 0, pairs)
    for copy in [halo_copy] + own_copies + in_copies:
        copy.start()
    lane = lane_of(rows)
    level = (lax.broadcasted_iota(jnp.int32, (rows, LANES), 0) % 2).astype(jnp.float32)

    def part(index):
        return halo_ref[index * count : (index + 1) * count, :]

    def assembled(index, parts):
        for chan, value in enumerate(parts):
            raw_ref[index, pl.ds(chan, count, stride=4), :] = value
        return raw_ref[index]

    mirror = jnp.where(lane < IB, IB - 1 - lane, lane)
    slot_lane = lane_of(count)
    halo_copy.wait()
    depth_x = rot(part(0), -SPARE)
    for index in range(1, 8):
        depth_x = jnp.where(slot_lane >= PIECE * index, rot(part(index), PIECE * index - SPARE), depth_x)
    x_raw = [[part(X_PART + chan) for chan in range(4)], [part(X_PART + 4 + chan) for chan in range(4)],
             [part(X_PART + 8 + chan % 2) for chan in range(4)], [depth_x] * 4]
    y_values = [list(range(4)), list(range(4, 8)), [8, 9, 8, 9], [10] * 4]
    x_halo, south_halo, north_raw = [], [], []
    for kind in range(4):
        raw = assembled(3 * kind, x_raw[kind])
        x_halo.append(jnp.where(lane % 2 == 0, rot(raw, 1), rot(raw, -1)))
        first, second = [assembled(3 * kind + 1 + half, [part(2 * value + half) for value in y_values[kind]])
                         for half in range(2)]
        south_halo.append(jnp.where(lane < HALF, rot(first, 64), rot(second, 64 + HALF)))
        north_raw.append(jnp.where(lane < HALF, first, rot(second, HALF)))
    for copy in own_copies:
        copy.wait()
    folded = own_ref[OWN * SIDES] > 0.0
    north_halo = []
    for kind, raw in enumerate(north_raw):
        turned = lane_take(raw, mirror)
        north_halo.append(jnp.where(folded, -turned if kind == 2 else turned, raw))

    for side, (out_near, out_far, out_normal, out_depth) in enumerate((x_halo, south_halo, north_halo)):
        near, far, normal, rim_speed, wet, inner_wet, ratio, inner_ratio = [
            own_ref[OWN * side + index] for index in range(OWN)]
        if side == 0:
            out_normal = jnp.where(lane % 2 == 0, -out_normal, out_normal)
            beyond = out_near - jnp.where(lane % 2 == 0, rot(near, -1), rot(near, 1))
        else:
            out_normal = -out_normal if side == 2 else out_normal
            beyond = out_near
        speed = SCALE * (normal + out_normal) * (wet * jnp.clip(out_depth - level, 0.0, 1.0))
        flux = jnp.maximum(speed, 0.0) * (5.0 * out_near + 2.0 * near - out_far)
        flux += jnp.minimum(speed, 0.0) * (2.0 * out_near + 5.0 * near - far)
        inner_flux = rim_speed * beyond
        for place, (change, share) in enumerate(((wet * (flux + inner_flux), ratio),
                                                 (-inner_wet * inner_flux, inner_ratio))):
            other = jnp.where(level == 0.0, pltpu.roll(change, rows - 1, 0), pltpu.roll(change, 1, 0))
            delta_ref[2 * side + place] = change + share * (other - change)

    lane = lane_of(8)
    out_copies = []
    for pair in range(pairs):
        mine = pl.ds(8 * pair, 8)
        in_copies[pair].wait()
        near, deep, south, south_in, north, north_in = [delta_ref[index, mine, :] for index in range(2 * SIDES)]
        groups = []
        for at in range(2):
            index = 2 * (lane // 4) + (lane % 4) // 2 + 64 * at
            outer, inner = lane_take(near, index), lane_take(deep, index)
            groups.append(jnp.where((lane % 4 == 1) | (lane % 4 == 2), outer, inner))
        placed = [(groups[gap // 32], 4 * (gap % 32), IB * gap - 2, 4) for gap in range(GAPS)]
        placed += [(south, 0, 0, IB), (south_in, 0, IB, IB)]
        placed += [(north, 0, CELLS - IB, IB), (north_in, 0, CELLS - 2 * IB, IB)]
        for tile in range(TILES):
            at, stop = tile * LANES, min((tile + 1) * LANES, CELLS)
            change = jnp.zeros((8, LANES), jnp.float32)
            for source, origin, start, wide in placed:
                low, high = max(start, at, 0), min(start + wide, stop)
                if low < high:
                    inside = (lane >= low - at) & (lane < high - at)
                    change += jnp.where(inside, rot(source, start - at - origin), 0.0)
            y_ref[mine, at:stop] = y_ref[mine, at:stop] + change[:, : stop - at]
        copy = pltpu.make_async_copy(
            y_ref.at[mine].reshape(2, 4, CELLS), out_ref.at[pl.ds(2 * pair, 2)], out_sems.at[pair])
        copy.start()
        out_copies.append(copy)
    for copy in out_copies:
        copy.wait()


def route_codes(block_owner, neighbours, fold_partner, slot_total):
    block_count = block_owner.shape[0]
    hits = block_owner[None, :] == jnp.arange(slot_total, dtype=jnp.int32)[:, None]
    links = jnp.concatenate([neighbours, fold_partner[:, None]], axis=1)
    linked = links[:, :, None] == jnp.arange(block_count, dtype=jnp.int32)[None, None, :]
    link_slots = jnp.max(jnp.where(linked, block_owner[None, None, :], -1), axis=2)
    link_slots = jnp.concatenate([link_slots, block_owner[:, None]], axis=1)
    return jnp.max(jnp.where(hits[:, :, None], link_slots[None], -1), axis=1)


def per_device(tracers, velocity, kappa, kmt, block_owner, neighbours, fold_partner):
    slot_count, chans = tracers.shape[:2]
    sub_count = lax.axis_size("sub")
    device_count = lax.axis_size("blk") * sub_count
    if device_count % PARTS or chans != 4 or slot_count % 2 or slot_count < 2 * FIRST_PAIRS + 2:
        raise ValueError("unsupported sizes")
    my_index = (lax.axis_index("blk") * sub_count + lax.axis_index("sub")).astype(jnp.int32).reshape(1)
    axes = ("blk", "sub")
    pairs = slot_count // 2
    slot_total = device_count * slot_count
    state_rows = 4 * slot_count
    f32 = jnp.float32
    in_hbm = pl.BlockSpec(memory_space=pltpu.HBM)
    anywhere = pl.BlockSpec(memory_space=pl.ANY)
    in_vmem = pl.BlockSpec(memory_space=pltpu.VMEM)
    in_smem = pl.BlockSpec(memory_space=pltpu.SMEM)
    dma = pltpu.SemaphoreType.DMA
    limit = pltpu.CompilerParams(vmem_limit_bytes=32 * 1024 * 1024)

    def exchanged(pieces):
        pieces = pieces.reshape(device_count, slot_count, 1, LANES)
        return lax.all_to_all(pieces, axes, 0, 0, tiled=True).reshape(slot_total, LANES)

    pack = pl.pallas_call(
        pack_kernel,
        out_shape=jax.ShapeDtypeStruct((slot_total, LANES), f32),
        in_specs=[in_hbm, in_hbm, in_hbm],
        out_specs=in_vmem,
        scratch_shapes=[
            pltpu.VMEM((state_rows, CELLS), f32),
            pltpu.VMEM((state_rows, CELLS), f32),
            pltpu.VMEM((slot_count, CELLS), f32),
            pltpu.VMEM((9, state_rows, LANES), f32),
            dma((pairs,)),
            dma((pairs,)),
            dma,
        ],
        cost_estimate=pl.CostEstimate(flops=4_000_000, bytes_accessed=2_400_000, transcendentals=0),
    )(tracers, velocity, kmt)
    held = exchanged(pack)
    codes = route_codes(block_owner, neighbours, fold_partner, slot_total)

    def bulk(first, some, codes, base):
        kernel = functools.partial(bulk_kernel, first)
        extra = [] if base is None else [base]
        if extra:
            kernel = lambda *refs: bulk_kernel(first, *refs[:6], *refs[7:])
        return pl.pallas_call(
            kernel,
            out_shape=[
                jax.ShapeDtypeStruct(tracers.shape, f32),
                jax.ShapeDtypeStruct((OWN * SIDES + 1, 8 * some, LANES), f32),
            ],
            in_specs=[in_smem, in_hbm, in_hbm, in_hbm, in_hbm, in_vmem] + [in_hbm] * len(extra),
            out_specs=[in_hbm, in_vmem],
            scratch_shapes=[
                pltpu.VMEM((8 * some, CELLS), f32),
                pltpu.VMEM((8 * some, CELLS), f32),
                pltpu.VMEM((8 * some, CELLS), f32),
                pltpu.VMEM((slot_count, CELLS), f32),
                pltpu.VMEM((slot_count, CELLS), f32),
                pltpu.VMEM((8 * some, CELLS), f32),
                pltpu.VMEM((8 * some, CELLS), f32),
                pltpu.VMEM((8, WIDE), f32),
                pltpu.VMEM((8, WIDE), f32),
                dma((some,)),
                dma((some,)),
                dma((some,)),
                dma((2,)),
            ],
            input_output_aliases={6: 0} if extra else {},
            compiler_params=limit,
            cost_estimate=pl.CostEstimate(flops=4_000_000 * some, bytes_accessed=800_000 * some, transcendentals=0),
        )(my_index, tracers, velocity, kmt, kappa, codes, *extra)

    base, edge_a = bulk(0, FIRST_PAIRS, codes, None)
    held, edge_a = lax.optimization_barrier((held, edge_a))

    routed_rows = PARTS * slot_count
    routed = pl.pallas_call(
        route_kernel,
        grid=(device_count // PARTS,),
        out_shape=jax.ShapeDtypeStruct((slot_total, LANES), f32),
        in_specs=[
            in_smem,
            pl.BlockSpec((routed_rows, 6), lambda step: (step, 0)),
            pl.BlockSpec((slot_total, LANES), lambda step: (0, 0)),
        ],
        out_specs=pl.BlockSpec((routed_rows, LANES), lambda step: (step, 0)),
        compiler_params=limit,
    )(my_index, codes, held)

    routed, base = lax.optimization_barrier((routed, base))
    base, edge_b = bulk(FIRST_PAIRS, pairs - FIRST_PAIRS, codes, base)
    halo = exchanged(routed)[: PARTS * slot_count]

    return pl.pallas_call(
        finish_kernel,
        out_shape=jax.ShapeDtypeStruct(tracers.shape, f32),
        in_specs=[anywhere, anywhere, anywhere, in_hbm],
        out_specs=in_hbm,
        scratch_shapes=[
            pltpu.VMEM((PARTS * slot_count, LANES), f32),
            pltpu.VMEM((state_rows, CELLS), f32),
            pltpu.VMEM((OWN * SIDES + 1, state_rows, LANES), f32),
            pltpu.VMEM((12, state_rows, LANES), f32),
            pltpu.VMEM((2 * SIDES, state_rows, LANES), f32),
            dma((3,)),
            dma((pairs,)),
            dma((pairs,)),
        ],
        input_output_aliases={3: 0},
        compiler_params=limit,
    )(halo, edge_a, edge_b, base)


def solution(mesh):
    placed = (
        P(("blk", "sub"), None, None),
        P(("blk", "sub"), None, None),
        P(("blk", "sub"), None),
        P(("blk", "sub"), None),
        P(),
        P(),
        P(),
    )
    return jax.shard_map(
        per_device,
        mesh=mesh,
        in_specs=placed,
        out_specs=P(("blk", "sub"), None, None),
        check_vma=False,
    )
```

```python
import functools

import jax
import jax.numpy as jnp
from jax import lax
from jax.experimental import pallas as pl
from jax.experimental.pallas import tpu as pltpu
from jax.sharding import PartitionSpec as P

IB = 90
JB = 60
CELLS = IB * JB
COURANT = 0.2
LANES = 128
TILES = -(-CELLS // LANES)
WIDE = TILES * LANES
GAPS = JB + 1
HALF = IB // 2
PARTS = 32
X_PART = 22
SPARE = 48
PIECE = 16
SCALE = COURANT / 12.0
SIDES = 3
OWN = 8
FIRST_PAIRS = 2


def lane_of(rows):
    return lax.broadcasted_iota(jnp.int32, (rows, LANES), 1)


def rot(value, shift):
    shift = shift % LANES
    return value if shift == 0 else pltpu.roll(value, shift, 1)


def sublanes(value, shift):
    return pltpu.roll(value, shift % 8, 0)


def once(make):
    held = {}

    def get(tile):
        if tile not in held:
            held[tile] = make(tile)
        return held[tile]

    return get


def shifted(get, distance):
    offset = distance % LANES
    turned = once(lambda tile: rot(get(tile), -offset))

    def make(tile):
        low = tile + distance // LANES
        first = turned(low) if 0 <= low < TILES else jnp.zeros((8, LANES), jnp.float32)
        second = turned(low + 1) if 0 <= low + 1 < TILES else jnp.zeros((8, LANES), jnp.float32)
        return jnp.where(lane_of(8) < LANES - offset, first, second)

    return once(make)


def window(get, start, rows):
    tile, offset = start // LANES, start % LANES
    value = get(tile)
    if offset > 0 and tile + 1 < TILES:
        value = jnp.where(lane_of(rows) < offset, get(tile + 1), value)
    return rot(value, -offset)


def gap_strip(get, offset, wide, rows):
    lane = lane_of(rows)
    place = 1 if wide == 1 and offset > 0 else 0
    value = jnp.zeros((rows, LANES), jnp.float32)
    for turn in range(16):
        cells = []
        for gap in range(turn, GAPS, 16):
            cell = IB * gap + offset
            if cell + wide > 0:
                cells.append((max(cell, 0) % LANES, max(cell, 0) // LANES))
        cells.sort()
        merged = get(cells[0][1])
        for at, tile in cells[1:]:
            merged = jnp.where(lane >= at, get(tile), merged)
        moved = rot(merged, 2 * turn + place - IB * turn - offset)
        value = jnp.where(lane % 32 >= 2 * turn + place, moved, value)
    return value


def edge_strip(get, rows):
    return jnp.where(lane_of(rows) == 0, 0.0, gap_strip(get, -1, 2, rows))


def inner_strip(get, rows):
    return jnp.where(lane_of(rows) % 2 == 0, gap_strip(get, -2, 1, rows), gap_strip(get, 1, 1, rows))


def lane_take(value, index):
    return jnp.take_along_axis(value, index, axis=1, mode="promise_in_bounds")


def tile_getter(ref, rows, count):
    def get(tile):
        if tile + 1 < TILES:
            return ref[rows, tile * LANES : (tile + 1) * LANES]
        rest = jnp.zeros((count, WIDE - CELLS), jnp.float32)
        return jnp.concatenate([ref[rows, tile * LANES : CELLS], rest], axis=1)

    return get


def joined(south, north, half, rows):
    if half == 0:
        return jnp.where(lane_of(rows) < 64, south, rot(north, 64))
    return jnp.where(lane_of(rows) < 64, rot(south, -HALF), rot(north, 64 - HALF))


def pair_copies(source, target, sems, first, pairs):
    copies = []
    for pair in range(pairs):
        into = target.at[pl.ds(8 * pair, 8)].reshape(2, 4, CELLS)
        copies.append(pltpu.make_async_copy(source.at[pl.ds(2 * (first + pair), 2)], into, sems.at[pair]))
    return copies


def pack_kernel(tracer_ref, velocity_ref, depth_ref, out_ref, x_ref, v_ref, d_ref, strip_ref, x_sems, v_sems, d_sem):
    count = depth_ref.shape[0]
    pairs = count // 2
    x_copies = pair_copies(tracer_ref, x_ref, x_sems, 0, pairs)
    v_copies = pair_copies(velocity_ref, v_ref, v_sems, 0, pairs)
    d_copy = pltpu.make_async_copy(depth_ref, d_ref, d_sem)
    for pair in range(pairs):
        x_copies[pair].start()
        v_copies[pair].start()
    d_copy.start()
    for pair in range(pairs):
        rows = pl.ds(8 * pair, 8)
        x_copies[pair].wait()
        get_x = tile_getter(x_ref, rows, 8)
        near, far = edge_strip(get_x, 8), inner_strip(get_x, 8)
        south = [window(get_x, 0, 8), window(get_x, IB, 8)]
        north = [window(get_x, CELLS - IB, 8), window(get_x, CELLS - 2 * IB, 8)]
        v_copies[pair].wait()
        get_v = tile_getter(v_ref, rows, 8)
        v_south, v_north = window(get_v, 0, 8), window(get_v, CELLS - IB, 8)
        strips = [joined(south[0], north[0], half, 8) for half in range(2)]
        strips += [joined(south[1], north[1], half, 8) for half in range(2)]
        strips += [joined(v_south, v_north, half, 8) for half in range(2)]
        strips += [near, far, edge_strip(get_v, 8)]
        for index, strip in enumerate(strips):
            strip_ref[index, rows, :] = strip

    d_copy.wait()
    if out_ref.shape[0] > PARTS * count:
        rest = out_ref.shape[0] - PARTS * count
        out_ref[PARTS * count :, :] = jnp.zeros((rest, LANES), jnp.float32)
    slot_lane = lane_of(count)
    get_d = tile_getter(d_ref, slice(None), count)
    d_south, d_north = window(get_d, 0, count), window(get_d, CELLS - IB, count)
    d_gaps = edge_strip(get_d, count)
    spare = (slot_lane >= SPARE) & (slot_lane < SPARE + PIECE)

    def put(part, value):
        out_ref[part * count : (part + 1) * count, :] = value

    for chan in range(4):
        rows = pl.ds(chan, count, stride=4)
        for half in range(2):
            for deep in range(2):
                part = 2 * (4 * deep + chan) + half
                value = strip_ref[2 * deep + half, rows, :]
                if part < 8:
                    value = jnp.where(spare, rot(d_gaps, SPARE - PIECE * part), value)
                put(part, value)
            if chan >= 2:
                put(2 * (8 + chan - 2) + half, strip_ref[4 + half, rows, :])
        put(X_PART + chan, strip_ref[6, rows, :])
        put(X_PART + 4 + chan, strip_ref[7, rows, :])
        if chan < 2:
            put(X_PART + 8 + chan, strip_ref[8, rows, :])
    for half in range(2):
        put(20 + half, joined(d_south, d_north, half, count))


def route_kernel(part_ref, code_ref, held_ref, out_ref):
    total = held_ref.shape[0]
    rows = out_ref.shape[0]
    part = part_ref[0]
    fold = code_ref[:, 4:5]
    wanted = [code_ref[:, side : side + 1] for side in range(3)] + [jnp.maximum(code_ref[:, 3:4], fold)]
    picked = [jnp.zeros((rows, 2 * LANES), jnp.float32) for _ in wanted]
    for start in range(0, total, rows):
        held = held_ref[start : start + rows, :]
        high = held.astype(jnp.bfloat16)
        low = (held - high.astype(jnp.float32)).astype(jnp.bfloat16)
        halves = jnp.concatenate([high, low], axis=1)
        source = lax.broadcasted_iota(jnp.int32, (rows, rows), 1) + start
        for side, code in enumerate(wanted):
            one_hot = jnp.where(code == source, 1.0, 0.0).astype(jnp.bfloat16)
            picked[side] += jnp.dot(one_hot, halves, preferred_element_type=jnp.float32)
    west, east, south, north = [value[:, :LANES] + value[:, LANES:] for value in picked]
    lane = lane_of(rows)
    along_x = (part >= X_PART) | ((part < 8) & (lane >= SPARE) & (lane < SPARE + PIECE))
    x_side = jnp.where(lane % 2 == 0, west, east)
    y_side = jnp.where(lane < 64, jnp.where(fold >= 0, rot(north, 64), north), south)
    out_ref[...] = jnp.where(along_x, x_side, y_side)


def bulk_kernel(first, my_ref, tracer_ref, velocity_ref, depth_ref, kappa_ref, code_ref,
                base_ref, edge_ref, y_ref, x_ref, v_ref, d_ref, k_ref, d8_ref, k8_ref, w_ref, z_ref, x_sems, v_sems, y_sems, d_sems):
    count = depth_ref.shape[0]
    pairs = edge_ref.shape[1] // 8
    x_copies = pair_copies(tracer_ref, x_ref, x_sems, first, pairs)
    v_copies = pair_copies(velocity_ref, v_ref, v_sems, first, pairs)
    d_copy = pltpu.make_async_copy(depth_ref, d_ref, d_sems.at[0])
    k_copy = pltpu.make_async_copy(kappa_ref, k_ref, d_sems.at[1])
    d_copy.start()
    k_copy.start()
    for pair in range(pairs):
        v_copies[pair].start()
        x_copies[pair].start()
    lane = lane_of(8)
    row = lax.broadcasted_iota(jnp.int32, (8, LANES), 0)
    x_row, even, place = row % 4 < 2, row % 2 == 0, row % 4
    level = (row % 2).astype(jnp.float32)
    zero = jnp.zeros((8, LANES), jnp.float32)

    def all_rows(value, chosen):
        result = value
        for at in range(4):
            if at != chosen:
                result = jnp.where(place == at, sublanes(value, at - chosen), result)
        return result

    def wet_of(depth):
        return jnp.clip(depth - level, 0.0, 1.0)

    for copy, source, target in ((d_copy, d_ref, d8_ref), (k_copy, k_ref, k8_ref)):
        copy.wait()
        for pair in range(pairs):
            slot = 2 * (first + pair)
            for start in range(0, CELLS, LANES):
                columns = slice(start, min(start + LANES, CELLS))
                shape = (8, columns.stop - start)
                top, low = [jnp.broadcast_to(source[slot + at : slot + at + 1, columns], shape) for at in range(2)]
                target[8 * pair : 8 * pair + 8, columns] = jnp.where(row[:, : shape[1]] < 4, top, low)

    def one_pair(pair):
        slot = 2 * (first + pair)
        rows = pl.ds(pl.multiple_of(8 * pair, 8), 8)
        for source, target, sems in ((velocity_ref, v_ref, v_sems), (tracer_ref, x_ref, x_sems)):
            pltpu.make_async_copy(
                source.at[pl.ds(0, 2)], target.at[rows].reshape(2, 4, CELLS), sems.at[pair]).wait()

        codes = [code_ref[pl.ds(my_ref[0] * count + slot + at, 1), :] for at in range(2)]

        def flag(column):
            pieces = [jnp.broadcast_to(code[:, column : column + 1], (8, LANES)) for code in codes]
            return jnp.where(row < 4, pieces[0], pieces[1]) >= 0

        live, folded = flag(5), flag(4)
        state, velocity = once(tile_getter(x_ref, rows, 8)), once(tile_getter(v_ref, rows, 8))
        depth, kappa = once(tile_getter(d8_ref, rows, 8)), once(tile_getter(k8_ref, rows, 8))
        wet = once(lambda tile: wet_of(depth(tile)))

        @once
        def ratio(tile):
            other = jnp.clip(depth(tile) - (1.0 - level), 0.0, 1.0)
            coupling = kappa(tile) * (wet(tile) * other)
            return coupling / (1.0 + 2.0 * coupling)

        next_vel = [shifted(velocity, 1), shifted(velocity, IB)]
        next_wet = [shifted(wet, 1), shifted(wet, IB)]

        @once
        def face(tile):
            rims = [at - tile * LANES for at in range(IB - 1, CELLS, IB) if at // LANES == tile]
            rim = functools.reduce(jnp.logical_or, [lane == at for at in rims]) if rims else None
            across = next_wet[0](tile) if rim is None else jnp.where(rim, 0.0, next_wet[0](tile))
            speed = velocity(tile) + jnp.where(x_row, next_vel[0](tile), next_vel[1](tile))
            value = SCALE * speed * (wet(tile) * jnp.where(x_row, across, next_wet[1](tile)))
            w_ref[:, tile * LANES : (tile + 1) * LANES] = value
            return value

        face_x = once(lambda tile: jnp.where(x_row, face(tile), sublanes(face(tile), 2)))
        face_y = once(lambda tile: jnp.where(x_row, sublanes(face(tile), -2), face(tile)))
        five = once(lambda tile: 5.0 * state(tile))
        two = once(lambda tile: 2.0 * state(tile))

        def divergence(speed, distance):
            before, after = shifted(state, -distance), shifted(state, distance)
            lower = once(lambda tile: five(tile) - before(tile) + 2.0 * after(tile))
            upper = shifted(once(lambda tile: five(tile) - after(tile)), distance)

            @once
            def flux(tile):
                value = jnp.maximum(speed(tile), 0.0) * lower(tile)
                return value + jnp.minimum(speed(tile), 0.0) * (two(tile) + upper(tile))

            back = shifted(flux, -distance)
            for stage in (after, before, lower, upper, flux, back):
                for tile in range(TILES):
                    stage(tile)
            return once(lambda tile: flux(tile) - back(tile))

        for stage in (depth, wet, ratio, *next_vel, *next_wet, face):
            for tile in range(TILES):
                stage(tile)
        change_x, change_y = divergence(face_x, 1), divergence(face_y, IB)
        for tile in range(TILES):
            explicit = state(tile) - wet(tile) * (change_x(tile) + change_y(tile))
            other = jnp.where(even, sublanes(explicit, -1), sublanes(explicit, 1))
            value = jnp.where(live, explicit + ratio(tile) * (other - explicit), zero)
            stop = min((tile + 1) * LANES, CELLS)
            y_ref[rows, tile * LANES : stop] = value[:, : stop - tile * LANES]
            mixed = jnp.where(x_row, face(tile), jnp.where(even, ratio(tile), depth(tile)))
            z_ref[:, tile * LANES : (tile + 1) * LANES] = mixed

        pltpu.make_async_copy(
            y_ref.at[rows].reshape(2, 4, CELLS), base_ref.at[pl.ds(slot, 2)], y_sems.at[pair]).start()
        get_w, get_z = [lambda tile, ref=ref: ref[:, tile * LANES : (tile + 1) * LANES] for ref in (w_ref, z_ref)]
        east = lane % 2 == 0
        near, far, normal = edge_strip(state, 8), inner_strip(state, 8), edge_strip(velocity, 8)
        outer, inner = edge_strip(get_z, 8), inner_strip(get_z, 8)
        normal = jnp.where(x_row, normal, sublanes(normal, 2))
        rim_speed = jnp.where(east, inner, outer)
        rim_speed = jnp.where(x_row, rim_speed, sublanes(rim_speed, 2))
        sides = [(
            near, far, jnp.where(east, -normal, normal), jnp.where(east, -rim_speed, rim_speed), outer, inner,
        )]
        for outer, inner, edge, sign in ((0, IB, 0, 1.0), (CELLS - IB, CELLS - 2 * IB, CELLS - 2 * IB, -1.0)):
            normal, rim_speed = window(velocity, outer, 8), window(get_w, edge, 8)
            normal = sign * jnp.where(x_row, sublanes(normal, -2), normal)
            rim_speed = sign * jnp.where(x_row, sublanes(rim_speed, -2), rim_speed)
            sides.append((window(state, outer, 8), window(state, inner, 8), normal, rim_speed,
                          window(get_z, outer, 8), window(get_z, inner, 8)))
        for side, (near, far, normal, rim_speed, outer, inner) in enumerate(sides):
            values = (near, far, normal, jnp.where(live, jnp.maximum(rim_speed, 0.0), zero), wet_of(all_rows(outer, 3)),
                      wet_of(all_rows(inner, 3)), all_rows(outer, 2), all_rows(inner, 2))
            for index, value in enumerate(values):
                edge_ref[OWN * side + index, rows, :] = value
        edge_ref[OWN * SIDES, rows, :] = jnp.where(folded, 1.0, zero)

    pl.loop(0, pairs)(one_pair)
    for pair in range(pairs):
        slots = pl.ds(2 * (first + pair), 2)
        rows = y_ref.at[pl.ds(8 * pair, 8)].reshape(2, 4, CELLS)
        pltpu.make_async_copy(rows, base_ref.at[slots], y_sems.at[pair]).wait()


def finish_kernel(halo_ref, edge_a_ref, edge_b_ref, base_ref, out_ref,
                  y_ref, raw_ref, delta_ref, in_sems, out_sems):
    count = out_ref.shape[0]
    pairs = count // 2
    rows = 4 * count
    in_copies = pair_copies(base_ref, y_ref, in_sems, 0, pairs)
    for copy in in_copies:
        copy.start()

    def own(index):
        return jnp.concatenate([edge_a_ref[index], edge_b_ref[index]], axis=0)

    lane = lane_of(rows)
    level = (lax.broadcasted_iota(jnp.int32, (rows, LANES), 0) % 2).astype(jnp.float32)

    def part(index):
        return halo_ref[index * count : (index + 1) * count, :]

    def assembled(index, parts):
        for chan, value in enumerate(parts):
            raw_ref[index, pl.ds(chan, count, stride=4), :] = value
        return raw_ref[index]

    mirror = jnp.where(lane < IB, IB - 1 - lane, lane)
    slot_lane = lane_of(count)
    depth_x = rot(part(0), -SPARE)
    for index in range(1, 8):
        depth_x = jnp.where(slot_lane >= PIECE * index, rot(part(index), PIECE * index - SPARE), depth_x)
    x_raw = [[part(X_PART + chan) for chan in range(4)], [part(X_PART + 4 + chan) for chan in range(4)],
             [part(X_PART + 8 + chan % 2) for chan in range(4)], [depth_x] * 4]
    y_values = [list(range(4)), list(range(4, 8)), [8, 9, 8, 9], [10] * 4]
    x_halo, south_halo, north_raw = [], [], []
    for kind in range(4):
        raw = assembled(3 * kind, x_raw[kind])
        x_halo.append(jnp.where(lane % 2 == 0, rot(raw, 1), rot(raw, -1)))
        first, second = [assembled(3 * kind + 1 + half, [part(2 * value + half) for value in y_values[kind]])
                         for half in range(2)]
        south_halo.append(jnp.where(lane < HALF, rot(first, 64), rot(second, 64 + HALF)))
        north_raw.append(jnp.where(lane < HALF, first, rot(second, HALF)))
    folded = own(OWN * SIDES) > 0.0
    north_halo = []
    for kind, raw in enumerate(north_raw):
        turned = lane_take(raw, mirror)
        north_halo.append(jnp.where(folded, -turned if kind == 2 else turned, raw))

    for side, (out_near, out_far, out_normal, out_depth) in enumerate((x_halo, south_halo, north_halo)):
        near, far, normal, rim_speed, wet, inner_wet, ratio, inner_ratio = [
            own(OWN * side + index) for index in range(OWN)]
        if side == 0:
            out_normal = jnp.where(lane % 2 == 0, -out_normal, out_normal)
            beyond = out_near - jnp.where(lane % 2 == 0, rot(near, -1), rot(near, 1))
        else:
            out_normal = -out_normal if side == 2 else out_normal
            beyond = out_near
        speed = SCALE * (normal + out_normal) * (wet * jnp.clip(out_depth - level, 0.0, 1.0))
        flux = jnp.maximum(speed, 0.0) * (5.0 * out_near + 2.0 * near - out_far)
        flux += jnp.minimum(speed, 0.0) * (2.0 * out_near + 5.0 * near - far)
        inner_flux = rim_speed * beyond
        for place, (change, share) in enumerate(((wet * (flux + inner_flux), ratio),
                                                 (-inner_wet * inner_flux, inner_ratio))):
            other = jnp.where(level == 0.0, pltpu.roll(change, rows - 1, 0), pltpu.roll(change, 1, 0))
            delta_ref[2 * side + place] = change + share * (other - change)

    lane = lane_of(8)
    out_copies = []
    for pair in range(pairs):
        mine = pl.ds(8 * pair, 8)
        in_copies[pair].wait()
        near, deep, south, south_in, north, north_in = [delta_ref[index, mine, :] for index in range(2 * SIDES)]
        groups = []
        for at in range(2):
            index = 2 * (lane // 4) + (lane % 4) // 2 + 64 * at
            outer, inner = lane_take(near, index), lane_take(deep, index)
            groups.append(jnp.where((lane % 4 == 1) | (lane % 4 == 2), outer, inner))
        placed = [(groups[gap // 32], 4 * (gap % 32), IB * gap - 2, 4) for gap in range(GAPS)]
        placed += [(south, 0, 0, IB), (south_in, 0, IB, IB)]
        placed += [(north, 0, CELLS - IB, IB), (north_in, 0, CELLS - 2 * IB, IB)]
        for tile in range(TILES):
            at, stop = tile * LANES, min((tile + 1) * LANES, CELLS)
            change = jnp.zeros((8, LANES), jnp.float32)
            for source, origin, start, wide in placed:
                low, high = max(start, at, 0), min(start + wide, stop)
                if low < high:
                    inside = (lane >= low - at) & (lane < high - at)
                    change += jnp.where(inside, rot(source, start - at - origin), 0.0)
            y_ref[mine, at:stop] = y_ref[mine, at:stop] + change[:, : stop - at]
        copy = pltpu.make_async_copy(
            y_ref.at[mine].reshape(2, 4, CELLS), out_ref.at[pl.ds(2 * pair, 2)], out_sems.at[pair])
        copy.start()
        out_copies.append(copy)
    for copy in out_copies:
        copy.wait()


def route_codes(block_owner, neighbours, fold_partner, slot_total):
    block_count = block_owner.shape[0]
    hits = block_owner[None, :] == jnp.arange(slot_total, dtype=jnp.int32)[:, None]
    links = jnp.concatenate([neighbours, fold_partner[:, None]], axis=1)
    linked = links[:, :, None] == jnp.arange(block_count, dtype=jnp.int32)[None, None, :]
    link_slots = jnp.max(jnp.where(linked, block_owner[None, None, :], -1), axis=2)
    link_slots = jnp.concatenate([link_slots, block_owner[:, None]], axis=1)
    return jnp.max(jnp.where(hits[:, :, None], link_slots[None], -1), axis=1)


def per_device(tracers, velocity, kappa, kmt, block_owner, neighbours, fold_partner):
    slot_count, chans = tracers.shape[:2]
    sub_count = lax.axis_size("sub")
    device_count = lax.axis_size("blk") * sub_count
    if device_count % PARTS or chans != 4 or slot_count % 2 or slot_count < 2 * FIRST_PAIRS + 2:
        raise ValueError("unsupported sizes")
    my_index = (lax.axis_index("blk") * sub_count + lax.axis_index("sub")).astype(jnp.int32).reshape(1)
    axes = ("blk", "sub")
    pairs = slot_count // 2
    slot_total = device_count * slot_count
    state_rows = 4 * slot_count
    f32 = jnp.float32
    in_hbm = pl.BlockSpec(memory_space=pltpu.HBM)
    in_vmem = pl.BlockSpec(memory_space=pltpu.VMEM)
    in_smem = pl.BlockSpec(memory_space=pltpu.SMEM)
    dma = pltpu.SemaphoreType.DMA
    limit = pltpu.CompilerParams(vmem_limit_bytes=32 * 1024 * 1024)

    def exchanged(pieces):
        pieces = pieces.reshape(device_count, slot_count, 1, LANES)
        return lax.all_to_all(pieces, axes, 0, 0, tiled=True).reshape(slot_total, LANES)

    pack = pl.pallas_call(
        pack_kernel,
        out_shape=jax.ShapeDtypeStruct((slot_total, LANES), f32),
        in_specs=[in_hbm, in_hbm, in_hbm],
        out_specs=in_vmem,
        scratch_shapes=[
            pltpu.VMEM((state_rows, CELLS), f32),
            pltpu.VMEM((state_rows, CELLS), f32),
            pltpu.VMEM((slot_count, CELLS), f32),
            pltpu.VMEM((9, state_rows, LANES), f32),
            dma((pairs,)),
            dma((pairs,)),
            dma,
        ],
        cost_estimate=pl.CostEstimate(flops=4_000_000, bytes_accessed=2_400_000, transcendentals=0),
    )(tracers, velocity, kmt)
    held = exchanged(pack)
    codes = route_codes(block_owner, neighbours, fold_partner, slot_total)

    def bulk(first, some, codes, base):
        kernel = functools.partial(bulk_kernel, first)
        extra = [] if base is None else [base]
        if extra:
            kernel = lambda *refs: bulk_kernel(first, *refs[:6], *refs[7:])
        return pl.pallas_call(
            kernel,
            out_shape=[
                jax.ShapeDtypeStruct(tracers.shape, f32),
                jax.ShapeDtypeStruct((OWN * SIDES + 1, 8 * some, LANES), f32),
            ],
            in_specs=[in_smem, in_hbm, in_hbm, in_hbm, in_hbm, in_vmem] + [in_hbm] * len(extra),
            out_specs=[in_hbm, in_vmem],
            scratch_shapes=[
                pltpu.VMEM((8 * some, CELLS), f32),
                pltpu.VMEM((8 * some, CELLS), f32),
                pltpu.VMEM((8 * some, CELLS), f32),
                pltpu.VMEM((slot_count, CELLS), f32),
                pltpu.VMEM((slot_count, CELLS), f32),
                pltpu.VMEM((8 * some, CELLS), f32),
                pltpu.VMEM((8 * some, CELLS), f32),
                pltpu.VMEM((8, WIDE), f32),
                pltpu.VMEM((8, WIDE), f32),
                dma((some,)),
                dma((some,)),
                dma((some,)),
                dma((2,)),
            ],
            input_output_aliases={6: 0} if extra else {},
            compiler_params=limit,
            cost_estimate=pl.CostEstimate(flops=4_000_000 * some, bytes_accessed=800_000 * some, transcendentals=0),
        )(my_index, tracers, velocity, kmt, kappa, codes, *extra)

    base, edge_a = bulk(0, FIRST_PAIRS, codes, None)
    held, edge_a = lax.optimization_barrier((held, edge_a))

    routed_rows = PARTS * slot_count
    blocks = dict(in_specs=[in_smem, in_vmem, in_vmem], out_specs=in_vmem)
    if device_count > PARTS:
        blocks = dict(
            grid=(device_count // PARTS,),
            in_specs=[
                in_smem,
                pl.BlockSpec((routed_rows, 6), lambda step: (step, 0)),
                pl.BlockSpec((slot_total, LANES), lambda step: (0, 0)),
            ],
            out_specs=pl.BlockSpec((routed_rows, LANES), lambda step: (step, 0)),
        )
    routed = pl.pallas_call(
        route_kernel,
        out_shape=jax.ShapeDtypeStruct((slot_total, LANES), f32),
        compiler_params=limit,
        **blocks,
    )(my_index, codes, held)
    routed, base = lax.optimization_barrier((routed, base))
    base, edge_b = bulk(FIRST_PAIRS, pairs - FIRST_PAIRS, codes, base)
    halo = exchanged(routed)[: PARTS * slot_count]

    return pl.pallas_call(
        finish_kernel,
        out_shape=jax.ShapeDtypeStruct(tracers.shape, f32),
        in_specs=[in_vmem, in_vmem, in_vmem, in_hbm],
        out_specs=in_hbm,
        scratch_shapes=[
            pltpu.VMEM((state_rows, CELLS), f32),
            pltpu.VMEM((12, state_rows, LANES), f32),
            pltpu.VMEM((2 * SIDES, state_rows, LANES), f32),
            dma((pairs,)),
            dma((pairs,)),
        ],
        input_output_aliases={3: 0},
        compiler_params=limit,
    )(halo, edge_a, edge_b, base)


def solution(mesh):
    placed = (
        P(("blk", "sub"), None, None),
        P(("blk", "sub"), None, None),
        P(("blk", "sub"), None),
        P(("blk", "sub"), None),
        P(),
        P(),
        P(),
    )
    return jax.shard_map(
        per_device,
        mesh=mesh,
        in_specs=placed,
        out_specs=P(("blk", "sub"), None, None),
        check_vma=False,
    )
```

```python
import functools

import jax
import jax.numpy as jnp
from jax import lax
from jax.experimental import pallas as pl
from jax.experimental.pallas import tpu as pltpu
from jax.sharding import PartitionSpec as P

IB = 90
JB = 60
CELLS = IB * JB
COURANT = 0.2
LANES = 128
TILES = -(-CELLS // LANES)
WIDE = TILES * LANES
GAPS = JB + 1
HALF = IB // 2
PARTS = 32
X_PART = 22
SPARE = 48
PIECE = 16
SCALE = COURANT / 12.0
SIDES = 3
OWN = 8
FIRST_PAIRS = 2
AHEAD = 3


def lane_of(rows):
    return lax.broadcasted_iota(jnp.int32, (rows, LANES), 1)


def rot(value, shift):
    shift = shift % LANES
    return value if shift == 0 else pltpu.roll(value, shift, 1)


def sublanes(value, shift):
    return pltpu.roll(value, shift % 8, 0)


def once(make):
    held = {}

    def get(tile):
        if tile not in held:
            held[tile] = make(tile)
        return held[tile]

    return get


def shifted(get, distance):
    offset = distance % LANES
    turned = once(lambda tile: rot(get(tile), -offset))

    def make(tile):
        low = tile + distance // LANES
        first = turned(low) if 0 <= low < TILES else jnp.zeros((8, LANES), jnp.float32)
        second = turned(low + 1) if 0 <= low + 1 < TILES else jnp.zeros((8, LANES), jnp.float32)
        return jnp.where(lane_of(8) < LANES - offset, first, second)

    return once(make)


def window(get, start, rows):
    tile, offset = start // LANES, start % LANES
    value = get(tile)
    if offset > 0 and tile + 1 < TILES:
        value = jnp.where(lane_of(rows) < offset, get(tile + 1), value)
    return rot(value, -offset)


def gap_strip(get, offset, wide, rows):
    lane = lane_of(rows)
    place = 1 if wide == 1 and offset > 0 else 0
    value = jnp.zeros((rows, LANES), jnp.float32)
    for turn in range(16):
        cells = []
        for gap in range(turn, GAPS, 16):
            cell = IB * gap + offset
            if cell + wide > 0:
                cells.append((max(cell, 0) % LANES, max(cell, 0) // LANES))
        cells.sort()
        merged = get(cells[0][1])
        for at, tile in cells[1:]:
            merged = jnp.where(lane >= at, get(tile), merged)
        moved = rot(merged, 2 * turn + place - IB * turn - offset)
        value = jnp.where(lane % 32 >= 2 * turn + place, moved, value)
    return value


def edge_strip(get, rows):
    return jnp.where(lane_of(rows) == 0, 0.0, gap_strip(get, -1, 2, rows))


def inner_strip(get, rows):
    return jnp.where(lane_of(rows) % 2 == 0, gap_strip(get, -2, 1, rows), gap_strip(get, 1, 1, rows))


def lane_take(value, index):
    return jnp.take_along_axis(value, index, axis=1, mode="promise_in_bounds")


def tile_getter(ref, rows, count):
    def get(tile):
        if tile + 1 < TILES:
            return ref[rows, tile * LANES : (tile + 1) * LANES]
        rest = jnp.zeros((count, WIDE - CELLS), jnp.float32)
        return jnp.concatenate([ref[rows, tile * LANES : CELLS], rest], axis=1)

    return get


def joined(south, north, half, rows):
    if half == 0:
        return jnp.where(lane_of(rows) < 64, south, rot(north, 64))
    return jnp.where(lane_of(rows) < 64, rot(south, -HALF), rot(north, 64 - HALF))


def pair_copies(source, target, sems, first, pairs):
    copies = []
    for pair in range(pairs):
        into = target.at[pl.ds(8 * pair, 8)].reshape(2, 4, CELLS)
        copies.append(pltpu.make_async_copy(source.at[pl.ds(2 * (first + pair), 2)], into, sems.at[pair]))
    return copies


def pack_kernel(tracer_ref, velocity_ref, depth_ref, out_ref, x_ref, v_ref, d_ref, strip_ref, x_sems, v_sems, d_sem):
    count = depth_ref.shape[0]
    pairs = count // 2
    x_copies = pair_copies(tracer_ref, x_ref, x_sems, 0, pairs)
    v_copies = pair_copies(velocity_ref, v_ref, v_sems, 0, pairs)
    d_copy = pltpu.make_async_copy(depth_ref, d_ref, d_sem)
    for pair in range(pairs):
        x_copies[pair].start()
        v_copies[pair].start()
    d_copy.start()
    for pair in range(pairs):
        rows = pl.ds(8 * pair, 8)
        x_copies[pair].wait()
        get_x = tile_getter(x_ref, rows, 8)
        near, far = edge_strip(get_x, 8), inner_strip(get_x, 8)
        south = [window(get_x, 0, 8), window(get_x, IB, 8)]
        north = [window(get_x, CELLS - IB, 8), window(get_x, CELLS - 2 * IB, 8)]
        v_copies[pair].wait()
        get_v = tile_getter(v_ref, rows, 8)
        v_south, v_north = window(get_v, 0, 8), window(get_v, CELLS - IB, 8)
        strips = [joined(south[0], north[0], half, 8) for half in range(2)]
        strips += [joined(south[1], north[1], half, 8) for half in range(2)]
        strips += [joined(v_south, v_north, half, 8) for half in range(2)]
        strips += [near, far, edge_strip(get_v, 8)]
        for index, strip in enumerate(strips):
            strip_ref[index, rows, :] = strip

    d_copy.wait()
    if out_ref.shape[0] > PARTS * count:
        rest = out_ref.shape[0] - PARTS * count
        out_ref[PARTS * count :, :] = jnp.zeros((rest, LANES), jnp.float32)
    slot_lane = lane_of(count)
    get_d = tile_getter(d_ref, slice(None), count)
    d_south, d_north = window(get_d, 0, count), window(get_d, CELLS - IB, count)
    d_gaps = edge_strip(get_d, count)
    spare = (slot_lane >= SPARE) & (slot_lane < SPARE + PIECE)

    def put(part, value):
        out_ref[part * count : (part + 1) * count, :] = value

    for chan in range(4):
        rows = pl.ds(chan, count, stride=4)
        for half in range(2):
            for deep in range(2):
                part = 2 * (4 * deep + chan) + half
                value = strip_ref[2 * deep + half, rows, :]
                if part < 8:
                    value = jnp.where(spare, rot(d_gaps, SPARE - PIECE * part), value)
                put(part, value)
            if chan >= 2:
                put(2 * (8 + chan - 2) + half, strip_ref[4 + half, rows, :])
        put(X_PART + chan, strip_ref[6, rows, :])
        put(X_PART + 4 + chan, strip_ref[7, rows, :])
        if chan < 2:
            put(X_PART + 8 + chan, strip_ref[8, rows, :])
    for half in range(2):
        put(20 + half, joined(d_south, d_north, half, count))


def route_kernel(part_ref, code_ref, held_ref, out_ref):
    total = held_ref.shape[0]
    rows = out_ref.shape[0]
    part = part_ref[0]
    fold = code_ref[:, 4:5]
    wanted = [code_ref[:, side : side + 1] for side in range(3)] + [jnp.maximum(code_ref[:, 3:4], fold)]
    picked = [jnp.zeros((rows, 2 * LANES), jnp.float32) for _ in wanted]
    for start in range(0, total, rows):
        held = held_ref[start : start + rows, :]
        high = held.astype(jnp.bfloat16)
        low = (held - high.astype(jnp.float32)).astype(jnp.bfloat16)
        halves = jnp.concatenate([high, low], axis=1)
        source = lax.broadcasted_iota(jnp.int32, (rows, rows), 1) + start
        for side, code in enumerate(wanted):
            one_hot = jnp.where(code == source, 1.0, 0.0).astype(jnp.bfloat16)
            picked[side] += jnp.dot(one_hot, halves, preferred_element_type=jnp.float32)
    west, east, south, north = [value[:, :LANES] + value[:, LANES:] for value in picked]
    lane = lane_of(rows)
    along_x = (part >= X_PART) | ((part < 8) & (lane >= SPARE) & (lane < SPARE + PIECE))
    x_side = jnp.where(lane % 2 == 0, west, east)
    y_side = jnp.where(lane < 64, jnp.where(fold >= 0, rot(north, 64), north), south)
    out_ref[...] = jnp.where(along_x, x_side, y_side)


def bulk_kernel(first, my_ref, tracer_ref, velocity_ref, depth_ref, kappa_ref, code_ref,
                base_ref, edge_ref, y_ref, x_ref, v_ref, d_ref, k_ref, d8_ref, k8_ref, w_ref, z_ref, x_sems, v_sems, y_sems, d_sems):
    count = depth_ref.shape[0]
    pairs = edge_ref.shape[1] // 8
    x_copies = pair_copies(tracer_ref, x_ref, x_sems, first, pairs)
    v_copies = pair_copies(velocity_ref, v_ref, v_sems, first, pairs)
    d_copy = pltpu.make_async_copy(depth_ref, d_ref, d_sems.at[0])
    k_copy = pltpu.make_async_copy(kappa_ref, k_ref, d_sems.at[1])
    d_copy.start()
    k_copy.start()
    for pair in range(pairs):
        v_copies[pair].start()
        x_copies[pair].start()
    lane = lane_of(8)
    row = lax.broadcasted_iota(jnp.int32, (8, LANES), 0)
    x_row, even, place = row % 4 < 2, row % 2 == 0, row % 4
    level = (row % 2).astype(jnp.float32)
    zero = jnp.zeros((8, LANES), jnp.float32)

    def all_rows(value, chosen):
        result = value
        for at in range(4):
            if at != chosen:
                result = jnp.where(place == at, sublanes(value, at - chosen), result)
        return result

    def wet_of(depth):
        return jnp.clip(depth - level, 0.0, 1.0)

    for copy, source, target in ((d_copy, d_ref, d8_ref), (k_copy, k_ref, k8_ref)):
        copy.wait()
        for pair in range(pairs):
            slot = 2 * (first + pair)
            for start in range(0, CELLS, LANES):
                columns = slice(start, min(start + LANES, CELLS))
                shape = (8, columns.stop - start)
                top, low = [jnp.broadcast_to(source[slot + at : slot + at + 1, columns], shape) for at in range(2)]
                target[8 * pair : 8 * pair + 8, columns] = jnp.where(row[:, : shape[1]] < 4, top, low)

    def one_pair(pair):
        slot = 2 * (first + pair)
        rows = pl.ds(pl.multiple_of(8 * pair, 8), 8)
        for source, target, sems in ((velocity_ref, v_ref, v_sems), (tracer_ref, x_ref, x_sems)):
            pltpu.make_async_copy(
                source.at[pl.ds(0, 2)], target.at[rows].reshape(2, 4, CELLS), sems.at[pair]).wait()

        codes = [code_ref[pl.ds(my_ref[0] * count + slot + at, 1), :] for at in range(2)]

        def flag(column):
            pieces = [jnp.broadcast_to(code[:, column : column + 1], (8, LANES)) for code in codes]
            return jnp.where(row < 4, pieces[0], pieces[1]) >= 0

        live, folded = flag(5), flag(4)
        state, velocity = once(tile_getter(x_ref, rows, 8)), once(tile_getter(v_ref, rows, 8))
        depth, kappa = once(tile_getter(d8_ref, rows, 8)), once(tile_getter(k8_ref, rows, 8))
        wet = once(lambda tile: wet_of(depth(tile)))

        @once
        def ratio(tile):
            other = jnp.clip(depth(tile) - (1.0 - level), 0.0, 1.0)
            coupling = kappa(tile) * (wet(tile) * other)
            return coupling / (1.0 + 2.0 * coupling)

        next_vel = [shifted(velocity, 1), shifted(velocity, IB)]
        next_wet = [shifted(wet, 1), shifted(wet, IB)]

        @once
        def face(tile):
            rims = [at - tile * LANES for at in range(IB - 1, CELLS, IB) if at // LANES == tile]
            rim = functools.reduce(jnp.logical_or, [lane == at for at in rims]) if rims else None
            across = next_wet[0](tile) if rim is None else jnp.where(rim, 0.0, next_wet[0](tile))
            speed = velocity(tile) + jnp.where(x_row, next_vel[0](tile), next_vel[1](tile))
            value = SCALE * speed * (wet(tile) * jnp.where(x_row, across, next_wet[1](tile)))
            w_ref[:, tile * LANES : (tile + 1) * LANES] = value
            return value

        face_x = once(lambda tile: jnp.where(x_row, face(tile), sublanes(face(tile), 2)))
        face_y = once(lambda tile: jnp.where(x_row, sublanes(face(tile), -2), face(tile)))
        five = once(lambda tile: 5.0 * state(tile))
        two = once(lambda tile: 2.0 * state(tile))

        def divergence(speed, distance):
            before, after = shifted(state, -distance), shifted(state, distance)
            lower = once(lambda tile: five(tile) - before(tile) + 2.0 * after(tile))
            upper = shifted(once(lambda tile: five(tile) - after(tile)), distance)

            @once
            def flux(tile):
                value = jnp.maximum(speed(tile), 0.0) * lower(tile)
                return value + jnp.minimum(speed(tile), 0.0) * (two(tile) + upper(tile))

            back = shifted(flux, -distance)
            for stage in (after, before, lower, upper, flux, back):
                for tile in range(TILES):
                    stage(tile)
            return once(lambda tile: flux(tile) - back(tile))

        for stage in (depth, wet, ratio, *next_vel, *next_wet, face):
            for tile in range(TILES):
                stage(tile)
        change_x, change_y = divergence(face_x, 1), divergence(face_y, IB)
        for tile in range(TILES):
            explicit = state(tile) - wet(tile) * (change_x(tile) + change_y(tile))
            other = jnp.where(even, sublanes(explicit, -1), sublanes(explicit, 1))
            value = jnp.where(live, explicit + ratio(tile) * (other - explicit), zero)
            stop = min((tile + 1) * LANES, CELLS)
            y_ref[rows, tile * LANES : stop] = value[:, : stop - tile * LANES]
            mixed = jnp.where(x_row, face(tile), jnp.where(even, ratio(tile), depth(tile)))
            z_ref[:, tile * LANES : (tile + 1) * LANES] = mixed

        pltpu.make_async_copy(
            y_ref.at[rows].reshape(2, 4, CELLS), base_ref.at[pl.ds(slot, 2)], y_sems.at[pair]).start()
        get_w, get_z = [lambda tile, ref=ref: ref[:, tile * LANES : (tile + 1) * LANES] for ref in (w_ref, z_ref)]
        east = lane % 2 == 0
        near, far, normal = edge_strip(state, 8), inner_strip(state, 8), edge_strip(velocity, 8)
        outer, inner = edge_strip(get_z, 8), inner_strip(get_z, 8)
        normal = jnp.where(x_row, normal, sublanes(normal, 2))
        rim_speed = jnp.where(east, inner, outer)
        rim_speed = jnp.where(x_row, rim_speed, sublanes(rim_speed, 2))
        sides = [(
            near, far, jnp.where(east, -normal, normal), jnp.where(east, -rim_speed, rim_speed), outer, inner,
        )]
        for outer, inner, edge, sign in ((0, IB, 0, 1.0), (CELLS - IB, CELLS - 2 * IB, CELLS - 2 * IB, -1.0)):
            normal, rim_speed = window(velocity, outer, 8), window(get_w, edge, 8)
            normal = sign * jnp.where(x_row, sublanes(normal, -2), normal)
            rim_speed = sign * jnp.where(x_row, sublanes(rim_speed, -2), rim_speed)
            sides.append((window(state, outer, 8), window(state, inner, 8), normal, rim_speed,
                          window(get_z, outer, 8), window(get_z, inner, 8)))
        for side, (near, far, normal, rim_speed, outer, inner) in enumerate(sides):
            values = (near, far, normal, jnp.where(live, jnp.maximum(rim_speed, 0.0), zero), wet_of(all_rows(outer, 3)),
                      wet_of(all_rows(inner, 3)), all_rows(outer, 2), all_rows(inner, 2))
            for index, value in enumerate(values):
                edge_ref[OWN * side + index, rows, :] = value
        edge_ref[OWN * SIDES, rows, :] = jnp.where(folded, 1.0, zero)

    pl.loop(0, pairs)(one_pair)
    for pair in range(pairs):
        slots = pl.ds(2 * (first + pair), 2)
        rows = y_ref.at[pl.ds(8 * pair, 8)].reshape(2, 4, CELLS)
        pltpu.make_async_copy(rows, base_ref.at[slots], y_sems.at[pair]).wait()


def finish_kernel(halo_ref, edge_a_ref, edge_b_ref, base_ref, out_ref,
                  y_ref, ahead_ref, raw_ref, delta_ref, in_sems, out_sems):
    count = out_ref.shape[0]
    pairs = count // 2
    rows = 4 * count
    in_copies = pair_copies(base_ref, y_ref, in_sems, 0, pairs)
    for copy in in_copies:
        copy.start()

    def own(index):
        return jnp.concatenate([edge_a_ref[index], edge_b_ref[index]], axis=0)

    lane = lane_of(rows)
    level = (lax.broadcasted_iota(jnp.int32, (rows, LANES), 0) % 2).astype(jnp.float32)

    def part(index):
        return halo_ref[index * count : (index + 1) * count, :]

    def assembled(index, parts):
        for chan, value in enumerate(parts):
            raw_ref[index, pl.ds(chan, count, stride=4), :] = value
        return raw_ref[index]

    mirror = jnp.where(lane < IB, IB - 1 - lane, lane)
    slot_lane = lane_of(count)
    depth_x = rot(part(0), -SPARE)
    for index in range(1, 8):
        depth_x = jnp.where(slot_lane >= PIECE * index, rot(part(index), PIECE * index - SPARE), depth_x)
    x_raw = [[part(X_PART + chan) for chan in range(4)], [part(X_PART + 4 + chan) for chan in range(4)],
             [part(X_PART + 8 + chan % 2) for chan in range(4)], [depth_x] * 4]
    y_values = [list(range(4)), list(range(4, 8)), [8, 9, 8, 9], [10] * 4]
    x_halo, south_halo, north_raw = [], [], []
    for kind in range(4):
        raw = assembled(3 * kind, x_raw[kind])
        x_halo.append(jnp.where(lane % 2 == 0, rot(raw, 1), rot(raw, -1)))
        first, second = [assembled(3 * kind + 1 + half, [part(2 * value + half) for value in y_values[kind]])
                         for half in range(2)]
        south_halo.append(jnp.where(lane < HALF, rot(first, 64), rot(second, 64 + HALF)))
        north_raw.append(jnp.where(lane < HALF, first, rot(second, HALF)))
    folded = own(OWN * SIDES) > 0.0
    north_halo = []
    for kind, raw in enumerate(north_raw):
        turned = lane_take(raw, mirror)
        north_halo.append(jnp.where(folded, -turned if kind == 2 else turned, raw))

    for side, (out_near, out_far, out_normal, out_depth) in enumerate((x_halo, south_halo, north_halo)):
        near, far, normal, rim_speed, wet, inner_wet, ratio, inner_ratio = [
            own(OWN * side + index) for index in range(OWN)]
        if side == 0:
            out_normal = jnp.where(lane % 2 == 0, -out_normal, out_normal)
            beyond = out_near - jnp.where(lane % 2 == 0, rot(near, -1), rot(near, 1))
        else:
            out_normal = -out_normal if side == 2 else out_normal
            beyond = out_near
        speed = SCALE * (normal + out_normal) * (wet * jnp.clip(out_depth - level, 0.0, 1.0))
        flux = jnp.maximum(speed, 0.0) * (5.0 * out_near + 2.0 * near - out_far)
        flux += jnp.minimum(speed, 0.0) * (2.0 * out_near + 5.0 * near - far)
        inner_flux = rim_speed * beyond
        for place, (change, share) in enumerate(((wet * (flux + inner_flux), ratio),
                                                 (-inner_wet * inner_flux, inner_ratio))):
            other = jnp.where(level == 0.0, pltpu.roll(change, rows - 1, 0), pltpu.roll(change, 1, 0))
            delta_ref[2 * side + place] = change + share * (other - change)

    lane = lane_of(8)
    def spread(pair):
        mine = pl.ds(8 * pair, 8)
        near, deep, south, south_in, north, north_in = [delta_ref[index, mine, :] for index in range(2 * SIDES)]
        groups = []
        for at in range(2):
            index = 2 * (lane // 4) + (lane % 4) // 2 + 64 * at
            outer, inner = lane_take(near, index), lane_take(deep, index)
            groups.append(jnp.where((lane % 4 == 1) | (lane % 4 == 2), outer, inner))
        placed = [(groups[gap // 32], 4 * (gap % 32), IB * gap - 2, 4) for gap in range(GAPS)]
        placed += [(south, 0, 0, IB), (south_in, 0, IB, IB)]
        placed += [(north, 0, CELLS - IB, IB), (north_in, 0, CELLS - 2 * IB, IB)]
        for tile in range(TILES):
            at, stop = tile * LANES, min((tile + 1) * LANES, CELLS)
            change = jnp.zeros((8, LANES), jnp.float32)
            for source, origin, start, wide in placed:
                low, high = max(start, at, 0), min(start + wide, stop)
                if low < high:
                    inside = (lane >= low - at) & (lane < high - at)
                    change += jnp.where(inside, rot(source, start - at - origin), 0.0)
            yield at, stop, change[:, : stop - at]

    for pair in range(AHEAD):
        for at, stop, change in spread(pair):
            ahead_ref[pl.ds(8 * pair, 8), at:stop] = change
    out_copies = []
    for pair in range(pairs):
        mine = pl.ds(8 * pair, 8)
        in_copies[pair].wait()
        if pair < AHEAD:
            for at in range(0, CELLS, LANES):
                stop = min(at + LANES, CELLS)
                y_ref[mine, at:stop] = y_ref[mine, at:stop] + ahead_ref[mine, at:stop]
        else:
            for at, stop, change in spread(pair):
                y_ref[mine, at:stop] = y_ref[mine, at:stop] + change
        copy = pltpu.make_async_copy(
            y_ref.at[mine].reshape(2, 4, CELLS), out_ref.at[pl.ds(2 * pair, 2)], out_sems.at[pair])
        copy.start()
        out_copies.append(copy)
    for copy in out_copies:
        copy.wait()


def route_codes(block_owner, neighbours, fold_partner, slot_total):
    block_count = block_owner.shape[0]
    hits = block_owner[None, :] == jnp.arange(slot_total, dtype=jnp.int32)[:, None]
    links = jnp.concatenate([neighbours, fold_partner[:, None]], axis=1)
    linked = links[:, :, None] == jnp.arange(block_count, dtype=jnp.int32)[None, None, :]
    link_slots = jnp.max(jnp.where(linked, block_owner[None, None, :], -1), axis=2)
    link_slots = jnp.concatenate([link_slots, block_owner[:, None]], axis=1)
    return jnp.max(jnp.where(hits[:, :, None], link_slots[None], -1), axis=1)


def per_device(tracers, velocity, kappa, kmt, block_owner, neighbours, fold_partner):
    slot_count, chans = tracers.shape[:2]
    sub_count = lax.axis_size("sub")
    device_count = lax.axis_size("blk") * sub_count
    if device_count % PARTS or chans != 4 or slot_count % 2 or slot_count < 2 * FIRST_PAIRS + 2:
        raise ValueError("unsupported sizes")
    my_index = (lax.axis_index("blk") * sub_count + lax.axis_index("sub")).astype(jnp.int32).reshape(1)
    axes = ("blk", "sub")
    pairs = slot_count // 2
    slot_total = device_count * slot_count
    state_rows = 4 * slot_count
    f32 = jnp.float32
    in_hbm = pl.BlockSpec(memory_space=pltpu.HBM)
    in_vmem = pl.BlockSpec(memory_space=pltpu.VMEM)
    in_smem = pl.BlockSpec(memory_space=pltpu.SMEM)
    dma = pltpu.SemaphoreType.DMA
    limit = pltpu.CompilerParams(vmem_limit_bytes=32 * 1024 * 1024)

    def exchanged(pieces):
        pieces = pieces.reshape(device_count, slot_count, 1, LANES)
        return lax.all_to_all(pieces, axes, 0, 0, tiled=True).reshape(slot_total, LANES)

    pack = pl.pallas_call(
        pack_kernel,
        out_shape=jax.ShapeDtypeStruct((slot_total, LANES), f32),
        in_specs=[in_hbm, in_hbm, in_hbm],
        out_specs=in_vmem,
        scratch_shapes=[
            pltpu.VMEM((state_rows, CELLS), f32),
            pltpu.VMEM((state_rows, CELLS), f32),
            pltpu.VMEM((slot_count, CELLS), f32),
            pltpu.VMEM((9, state_rows, LANES), f32),
            dma((pairs,)),
            dma((pairs,)),
            dma,
        ],
        cost_estimate=pl.CostEstimate(flops=4_000_000, bytes_accessed=2_400_000, transcendentals=0),
    )(tracers, velocity, kmt)
    held = exchanged(pack)
    codes = route_codes(block_owner, neighbours, fold_partner, slot_total)

    def bulk(first, some, codes, base):
        kernel = functools.partial(bulk_kernel, first)
        extra = [] if base is None else [base]
        if extra:
            kernel = lambda *refs: bulk_kernel(first, *refs[:6], *refs[7:])
        return pl.pallas_call(
            kernel,
            out_shape=[
                jax.ShapeDtypeStruct(tracers.shape, f32),
                jax.ShapeDtypeStruct((OWN * SIDES + 1, 8 * some, LANES), f32),
            ],
            in_specs=[in_smem, in_hbm, in_hbm, in_hbm, in_hbm, in_vmem] + [in_hbm] * len(extra),
            out_specs=[in_hbm, in_vmem],
            scratch_shapes=[
                pltpu.VMEM((8 * some, CELLS), f32),
                pltpu.VMEM((8 * some, CELLS), f32),
                pltpu.VMEM((8 * some, CELLS), f32),
                pltpu.VMEM((slot_count, CELLS), f32),
                pltpu.VMEM((slot_count, CELLS), f32),
                pltpu.VMEM((8 * some, CELLS), f32),
                pltpu.VMEM((8 * some, CELLS), f32),
                pltpu.VMEM((8, WIDE), f32),
                pltpu.VMEM((8, WIDE), f32),
                dma((some,)),
                dma((some,)),
                dma((some,)),
                dma((2,)),
            ],
            input_output_aliases={6: 0} if extra else {},
            compiler_params=limit,
            cost_estimate=pl.CostEstimate(flops=4_000_000 * some, bytes_accessed=800_000 * some, transcendentals=0),
        )(my_index, tracers, velocity, kmt, kappa, codes, *extra)

    base, edge_a = bulk(0, FIRST_PAIRS, codes, None)
    held, edge_a = lax.optimization_barrier((held, edge_a))

    routed_rows = PARTS * slot_count
    blocks = dict(in_specs=[in_smem, in_vmem, in_vmem], out_specs=in_vmem)
    if device_count > PARTS:
        blocks = dict(
            grid=(device_count // PARTS,),
            in_specs=[
                in_smem,
                pl.BlockSpec((routed_rows, 6), lambda step: (step, 0)),
                pl.BlockSpec((slot_total, LANES), lambda step: (0, 0)),
            ],
            out_specs=pl.BlockSpec((routed_rows, LANES), lambda step: (step, 0)),
        )
    routed = pl.pallas_call(
        route_kernel,
        out_shape=jax.ShapeDtypeStruct((slot_total, LANES), f32),
        compiler_params=limit,
        **blocks,
    )(my_index, codes, held)
    routed, base = lax.optimization_barrier((routed, base))
    base, edge_b = bulk(FIRST_PAIRS, pairs - FIRST_PAIRS, codes, base)
    halo = exchanged(routed)[: PARTS * slot_count]

    return pl.pallas_call(
        finish_kernel,
        out_shape=jax.ShapeDtypeStruct(tracers.shape, f32),
        in_specs=[in_vmem, in_vmem, in_vmem, in_hbm],
        out_specs=in_hbm,
        scratch_shapes=[
            pltpu.VMEM((state_rows, CELLS), f32),
            pltpu.VMEM((8 * AHEAD, CELLS), f32),
            pltpu.VMEM((12, state_rows, LANES), f32),
            pltpu.VMEM((2 * SIDES, state_rows, LANES), f32),
            dma((pairs,)),
            dma((pairs,)),
        ],
        input_output_aliases={3: 0},
        compiler_params=limit,
    )(halo, edge_a, edge_b, base)


def solution(mesh):
    placed = (
        P(("blk", "sub"), None, None),
        P(("blk", "sub"), None, None),
        P(("blk", "sub"), None),
        P(("blk", "sub"), None),
        P(),
        P(),
        P(),
    )
    return jax.shard_map(
        per_device,
        mesh=mesh,
        in_specs=placed,
        out_specs=P(("blk", "sub"), None, None),
        check_vma=False,
    )
```

```python
import functools

import jax
import jax.numpy as jnp
from jax import lax
from jax.experimental import pallas as pl
from jax.experimental.pallas import tpu as pltpu
from jax.sharding import PartitionSpec as P

IB = 90
JB = 60
CELLS = IB * JB
COURANT = 0.2
LANES = 128
TILES = -(-CELLS // LANES)
WIDE = TILES * LANES
GAPS = JB + 1
HALF = IB // 2
PARTS = 32
X_PART = 22
SPARE = 48
PIECE = 16
SCALE = COURANT / 12.0
SIDES = 3
OWN = 8
FIRST_PAIRS = 2
AHEAD = 3


def lane_of(rows):
    return lax.broadcasted_iota(jnp.int32, (rows, LANES), 1)


def rot(value, shift):
    shift = shift % LANES
    return value if shift == 0 else pltpu.roll(value, shift, 1)


def sublanes(value, shift):
    return pltpu.roll(value, shift % 8, 0)


def once(make):
    held = {}

    def get(tile):
        if tile not in held:
            held[tile] = make(tile)
        return held[tile]

    return get


def shifted(get, distance):
    offset = distance % LANES
    turned = once(lambda tile: rot(get(tile), -offset))

    def make(tile):
        low = tile + distance // LANES
        first = turned(low) if 0 <= low < TILES else jnp.zeros((8, LANES), jnp.float32)
        second = turned(low + 1) if 0 <= low + 1 < TILES else jnp.zeros((8, LANES), jnp.float32)
        return jnp.where(lane_of(8) < LANES - offset, first, second)

    return once(make)


def window(get, start, rows):
    tile, offset = start // LANES, start % LANES
    value = get(tile)
    if offset > 0 and tile + 1 < TILES:
        value = jnp.where(lane_of(rows) < offset, get(tile + 1), value)
    return rot(value, -offset)


def gap_strip(get, offset, wide, rows):
    lane = lane_of(rows)
    place = 1 if wide == 1 and offset > 0 else 0
    value = jnp.zeros((rows, LANES), jnp.float32)
    for turn in range(16):
        cells = []
        for gap in range(turn, GAPS, 16):
            cell = IB * gap + offset
            if cell + wide > 0:
                cells.append((max(cell, 0) % LANES, max(cell, 0) // LANES))
        cells.sort()
        merged = get(cells[0][1])
        for at, tile in cells[1:]:
            merged = jnp.where(lane >= at, get(tile), merged)
        moved = rot(merged, 2 * turn + place - IB * turn - offset)
        value = jnp.where(lane % 32 >= 2 * turn + place, moved, value)
    return value


def edge_strip(get, rows):
    return jnp.where(lane_of(rows) == 0, 0.0, gap_strip(get, -1, 2, rows))


def inner_strip(get, rows):
    return jnp.where(lane_of(rows) % 2 == 0, gap_strip(get, -2, 1, rows), gap_strip(get, 1, 1, rows))


def lane_take(value, index):
    return jnp.take_along_axis(value, index, axis=1, mode="promise_in_bounds")


def tile_getter(ref, rows, count):
    def get(tile):
        if tile + 1 < TILES:
            return ref[rows, tile * LANES : (tile + 1) * LANES]
        rest = jnp.zeros((count, WIDE - CELLS), jnp.float32)
        return jnp.concatenate([ref[rows, tile * LANES : CELLS], rest], axis=1)

    return get


def joined(south, north, half, rows):
    if half == 0:
        return jnp.where(lane_of(rows) < 64, south, rot(north, 64))
    return jnp.where(lane_of(rows) < 64, rot(south, -HALF), rot(north, 64 - HALF))


def pair_copies(source, target, sems, first, pairs):
    copies = []
    for pair in range(pairs):
        into = target.at[pl.ds(8 * pair, 8)].reshape(2, 4, CELLS)
        copies.append(pltpu.make_async_copy(source.at[pl.ds(2 * (first + pair), 2)], into, sems.at[pair]))
    return copies


def pack_kernel(tracer_ref, velocity_ref, depth_ref, out_ref, x_ref, v_ref, d_ref, strip_ref, x_sems, v_sems, d_sem):
    count = depth_ref.shape[0]
    pairs = count // 2
    x_copies = pair_copies(tracer_ref, x_ref, x_sems, 0, pairs)
    v_copies = pair_copies(velocity_ref, v_ref, v_sems, 0, pairs)
    d_copy = pltpu.make_async_copy(depth_ref, d_ref, d_sem)
    for pair in range(pairs):
        x_copies[pair].start()
        v_copies[pair].start()
    d_copy.start()
    for pair in range(pairs):
        rows = pl.ds(8 * pair, 8)
        if pair == 0 or pair % 2 == 1:
            for arrived in range(pair, min(pair + 1 + pair % 2, pairs)):
                x_copies[arrived].wait()
                v_copies[arrived].wait()
        get_x = tile_getter(x_ref, rows, 8)
        near, far = edge_strip(get_x, 8), inner_strip(get_x, 8)
        south = [window(get_x, 0, 8), window(get_x, IB, 8)]
        north = [window(get_x, CELLS - IB, 8), window(get_x, CELLS - 2 * IB, 8)]
        get_v = tile_getter(v_ref, rows, 8)
        v_south, v_north = window(get_v, 0, 8), window(get_v, CELLS - IB, 8)
        strips = [joined(south[0], north[0], half, 8) for half in range(2)]
        strips += [joined(south[1], north[1], half, 8) for half in range(2)]
        strips += [joined(v_south, v_north, half, 8) for half in range(2)]
        strips += [near, far, edge_strip(get_v, 8)]
        for index, strip in enumerate(strips):
            strip_ref[index, rows, :] = strip

    d_copy.wait()
    if out_ref.shape[0] > PARTS * count:
        rest = out_ref.shape[0] - PARTS * count
        out_ref[PARTS * count :, :] = jnp.zeros((rest, LANES), jnp.float32)
    slot_lane = lane_of(count)
    get_d = tile_getter(d_ref, slice(None), count)
    d_south, d_north = window(get_d, 0, count), window(get_d, CELLS - IB, count)
    d_gaps = edge_strip(get_d, count)
    spare = (slot_lane >= SPARE) & (slot_lane < SPARE + PIECE)

    def put(part, value):
        out_ref[part * count : (part + 1) * count, :] = value

    for chan in range(4):
        rows = pl.ds(chan, count, stride=4)
        for half in range(2):
            for deep in range(2):
                part = 2 * (4 * deep + chan) + half
                value = strip_ref[2 * deep + half, rows, :]
                if part < 8:
                    value = jnp.where(spare, rot(d_gaps, SPARE - PIECE * part), value)
                put(part, value)
            if chan >= 2:
                put(2 * (8 + chan - 2) + half, strip_ref[4 + half, rows, :])
        put(X_PART + chan, strip_ref[6, rows, :])
        put(X_PART + 4 + chan, strip_ref[7, rows, :])
        if chan < 2:
            put(X_PART + 8 + chan, strip_ref[8, rows, :])
    for half in range(2):
        put(20 + half, joined(d_south, d_north, half, count))


def route_kernel(part_ref, code_ref, held_ref, out_ref):
    total = held_ref.shape[0]
    rows = out_ref.shape[0]
    part = part_ref[0]
    fold = code_ref[:, 4:5]
    wanted = [code_ref[:, side : side + 1] for side in range(3)] + [jnp.maximum(code_ref[:, 3:4], fold)]
    picked = jnp.zeros((len(wanted) * rows, 2 * LANES), jnp.float32)
    for start in range(0, total, rows):
        held = held_ref[start : start + rows, :]
        high = held.astype(jnp.bfloat16)
        low = (held - high.astype(jnp.float32)).astype(jnp.bfloat16)
        halves = jnp.concatenate([high, low], axis=1)
        source = lax.broadcasted_iota(jnp.int32, (rows, rows), 1) + start
        one_hots = [jnp.where(code == source, 1.0, 0.0).astype(jnp.bfloat16) for code in wanted]
        picked += jnp.dot(jnp.concatenate(one_hots, axis=0), halves, preferred_element_type=jnp.float32)
    picked = picked[:, :LANES] + picked[:, LANES:]
    west, east, south, north = [picked[side * rows : (side + 1) * rows] for side in range(4)]
    lane = lane_of(rows)
    along_x = (part >= X_PART) | ((part < 8) & (lane >= SPARE) & (lane < SPARE + PIECE))
    x_side = jnp.where(lane % 2 == 0, west, east)
    y_side = jnp.where(lane < 64, jnp.where(fold >= 0, rot(north, 64), north), south)
    out_ref[...] = jnp.where(along_x, x_side, y_side)


def bulk_kernel(first, my_ref, tracer_ref, velocity_ref, depth_ref, kappa_ref, code_ref,
                base_ref, edge_ref, y_ref, x_ref, v_ref, d_ref, k_ref, d8_ref, k8_ref, w_ref, z_ref, x_sems, v_sems, y_sems, d_sems):
    count = depth_ref.shape[0]
    pairs = edge_ref.shape[1] // 8
    x_copies = pair_copies(tracer_ref, x_ref, x_sems, first, pairs)
    v_copies = pair_copies(velocity_ref, v_ref, v_sems, first, pairs)
    d_copy = pltpu.make_async_copy(depth_ref, d_ref, d_sems.at[0])
    k_copy = pltpu.make_async_copy(kappa_ref, k_ref, d_sems.at[1])
    d_copy.start()
    k_copy.start()
    for pair in range(pairs):
        v_copies[pair].start()
        x_copies[pair].start()
    lane = lane_of(8)
    row = lax.broadcasted_iota(jnp.int32, (8, LANES), 0)
    x_row, even, place = row % 4 < 2, row % 2 == 0, row % 4
    level = (row % 2).astype(jnp.float32)
    zero = jnp.zeros((8, LANES), jnp.float32)

    def all_rows(value, chosen):
        result = value
        for at in range(4):
            if at != chosen:
                result = jnp.where(place == at, sublanes(value, at - chosen), result)
        return result

    def wet_of(depth):
        return jnp.clip(depth - level, 0.0, 1.0)

    for copy, source, target in ((d_copy, d_ref, d8_ref), (k_copy, k_ref, k8_ref)):
        copy.wait()
        for pair in range(pairs):
            slot = 2 * (first + pair)
            for start in range(0, CELLS, LANES):
                columns = slice(start, min(start + LANES, CELLS))
                shape = (8, columns.stop - start)
                top, low = [jnp.broadcast_to(source[slot + at : slot + at + 1, columns], shape) for at in range(2)]
                target[8 * pair : 8 * pair + 8, columns] = jnp.where(row[:, : shape[1]] < 4, top, low)

    def one_pair(pair):
        slot = 2 * (first + pair)
        rows = pl.ds(pl.multiple_of(8 * pair, 8), 8)
        for source, target, sems in ((velocity_ref, v_ref, v_sems), (tracer_ref, x_ref, x_sems)):
            pltpu.make_async_copy(
                source.at[pl.ds(0, 2)], target.at[rows].reshape(2, 4, CELLS), sems.at[pair]).wait()

        codes = [code_ref[pl.ds(my_ref[0] * count + slot + at, 1), :] for at in range(2)]

        def flag(column):
            pieces = [jnp.broadcast_to(code[:, column : column + 1], (8, LANES)) for code in codes]
            return jnp.where(row < 4, pieces[0], pieces[1]) >= 0

        live, folded = flag(5), flag(4)
        state, velocity = once(tile_getter(x_ref, rows, 8)), once(tile_getter(v_ref, rows, 8))
        depth, kappa = once(tile_getter(d8_ref, rows, 8)), once(tile_getter(k8_ref, rows, 8))
        wet = once(lambda tile: wet_of(depth(tile)))

        @once
        def ratio(tile):
            other = jnp.clip(depth(tile) - (1.0 - level), 0.0, 1.0)
            coupling = kappa(tile) * (wet(tile) * other)
            return coupling / (1.0 + 2.0 * coupling)

        next_vel = [shifted(velocity, 1), shifted(velocity, IB)]
        next_wet = [shifted(wet, 1), shifted(wet, IB)]

        @once
        def face(tile):
            rims = [at - tile * LANES for at in range(IB - 1, CELLS, IB) if at // LANES == tile]
            rim = functools.reduce(jnp.logical_or, [lane == at for at in rims]) if rims else None
            across = next_wet[0](tile) if rim is None else jnp.where(rim, 0.0, next_wet[0](tile))
            speed = velocity(tile) + jnp.where(x_row, next_vel[0](tile), next_vel[1](tile))
            value = SCALE * speed * (wet(tile) * jnp.where(x_row, across, next_wet[1](tile)))
            w_ref[:, tile * LANES : (tile + 1) * LANES] = value
            return value

        face_x = once(lambda tile: jnp.where(x_row, face(tile), sublanes(face(tile), 2)))
        face_y = once(lambda tile: jnp.where(x_row, sublanes(face(tile), -2), face(tile)))
        five = once(lambda tile: 5.0 * state(tile))
        two = once(lambda tile: 2.0 * state(tile))

        def divergence(speed, distance):
            before, after = shifted(state, -distance), shifted(state, distance)
            lower = once(lambda tile: five(tile) - before(tile) + 2.0 * after(tile))
            upper = shifted(once(lambda tile: five(tile) - after(tile)), distance)

            @once
            def flux(tile):
                value = jnp.maximum(speed(tile), 0.0) * lower(tile)
                return value + jnp.minimum(speed(tile), 0.0) * (two(tile) + upper(tile))

            back = shifted(flux, -distance)
            for stage in (after, before, lower, upper, flux, back):
                for tile in range(TILES):
                    stage(tile)
            return once(lambda tile: flux(tile) - back(tile))

        for stage in (depth, wet, ratio, *next_vel, *next_wet, face):
            for tile in range(TILES):
                stage(tile)
        change_x, change_y = divergence(face_x, 1), divergence(face_y, IB)
        for tile in range(TILES):
            explicit = state(tile) - wet(tile) * (change_x(tile) + change_y(tile))
            other = jnp.where(even, sublanes(explicit, -1), sublanes(explicit, 1))
            value = jnp.where(live, explicit + ratio(tile) * (other - explicit), zero)
            stop = min((tile + 1) * LANES, CELLS)
            y_ref[rows, tile * LANES : stop] = value[:, : stop - tile * LANES]
            mixed = jnp.where(x_row, face(tile), jnp.where(even, ratio(tile), depth(tile)))
            z_ref[:, tile * LANES : (tile + 1) * LANES] = mixed

        pltpu.make_async_copy(
            y_ref.at[rows].reshape(2, 4, CELLS), base_ref.at[pl.ds(slot, 2)], y_sems.at[pair]).start()
        get_w, get_z = [lambda tile, ref=ref: ref[:, tile * LANES : (tile + 1) * LANES] for ref in (w_ref, z_ref)]
        east = lane % 2 == 0
        near, far, normal = edge_strip(state, 8), inner_strip(state, 8), edge_strip(velocity, 8)
        outer, inner = edge_strip(get_z, 8), inner_strip(get_z, 8)
        normal = jnp.where(x_row, normal, sublanes(normal, 2))
        rim_speed = jnp.where(east, inner, outer)
        rim_speed = jnp.where(x_row, rim_speed, sublanes(rim_speed, 2))
        sides = [(
            near, far, jnp.where(east, -normal, normal), jnp.where(east, -rim_speed, rim_speed), outer, inner,
        )]
        for outer, inner, edge, sign in ((0, IB, 0, 1.0), (CELLS - IB, CELLS - 2 * IB, CELLS - 2 * IB, -1.0)):
            normal, rim_speed = window(velocity, outer, 8), window(get_w, edge, 8)
            normal = sign * jnp.where(x_row, sublanes(normal, -2), normal)
            rim_speed = sign * jnp.where(x_row, sublanes(rim_speed, -2), rim_speed)
            sides.append((window(state, outer, 8), window(state, inner, 8), normal, rim_speed,
                          window(get_z, outer, 8), window(get_z, inner, 8)))
        for side, (near, far, normal, rim_speed, outer, inner) in enumerate(sides):
            values = (near, far, normal, jnp.where(live, jnp.maximum(rim_speed, 0.0), zero), wet_of(all_rows(outer, 3)),
                      wet_of(all_rows(inner, 3)), all_rows(outer, 2), all_rows(inner, 2))
            for index, value in enumerate(values):
                edge_ref[OWN * side + index, rows, :] = value
        edge_ref[OWN * SIDES, rows, :] = jnp.where(folded, 1.0, zero)

    pl.loop(0, pairs)(one_pair)
    for pair in range(pairs):
        slots = pl.ds(2 * (first + pair), 2)
        rows = y_ref.at[pl.ds(8 * pair, 8)].reshape(2, 4, CELLS)
        pltpu.make_async_copy(rows, base_ref.at[slots], y_sems.at[pair]).wait()


def finish_kernel(halo_ref, edge_a_ref, edge_b_ref, base_ref, out_ref,
                  y_ref, ahead_ref, raw_ref, delta_ref, in_sems, out_sems):
    count = out_ref.shape[0]
    pairs = count // 2
    rows = 4 * count
    in_copies = pair_copies(base_ref, y_ref, in_sems, 0, pairs)
    for copy in in_copies:
        copy.start()

    def own(index):
        return jnp.concatenate([edge_a_ref[index], edge_b_ref[index]], axis=0)

    lane = lane_of(rows)
    level = (lax.broadcasted_iota(jnp.int32, (rows, LANES), 0) % 2).astype(jnp.float32)

    def part(index):
        return halo_ref[index * count : (index + 1) * count, :]

    def assembled(index, parts):
        for chan, value in enumerate(parts):
            raw_ref[index, pl.ds(chan, count, stride=4), :] = value
        return raw_ref[index]

    mirror = jnp.where(lane < IB, IB - 1 - lane, lane)
    slot_lane = lane_of(count)
    depth_x = rot(part(0), -SPARE)
    for index in range(1, 8):
        depth_x = jnp.where(slot_lane >= PIECE * index, rot(part(index), PIECE * index - SPARE), depth_x)
    x_raw = [[part(X_PART + chan) for chan in range(4)], [part(X_PART + 4 + chan) for chan in range(4)],
             [part(X_PART + 8 + chan % 2) for chan in range(4)], [depth_x] * 4]
    y_values = [list(range(4)), list(range(4, 8)), [8, 9, 8, 9], [10] * 4]
    x_halo, south_halo, north_raw = [], [], []
    for kind in range(4):
        raw = assembled(3 * kind, x_raw[kind])
        x_halo.append(jnp.where(lane % 2 == 0, rot(raw, 1), rot(raw, -1)))
        first, second = [assembled(3 * kind + 1 + half, [part(2 * value + half) for value in y_values[kind]])
                         for half in range(2)]
        south_halo.append(jnp.where(lane < HALF, rot(first, 64), rot(second, 64 + HALF)))
        north_raw.append(jnp.where(lane < HALF, first, rot(second, HALF)))
    folded = own(OWN * SIDES) > 0.0
    north_halo = []
    for kind, raw in enumerate(north_raw):
        turned = lane_take(raw, mirror)
        north_halo.append(jnp.where(folded, -turned if kind == 2 else turned, raw))

    for side, (out_near, out_far, out_normal, out_depth) in enumerate((x_halo, south_halo, north_halo)):
        near, far, normal, rim_speed, wet, inner_wet, ratio, inner_ratio = [
            own(OWN * side + index) for index in range(OWN)]
        if side == 0:
            out_normal = jnp.where(lane % 2 == 0, -out_normal, out_normal)
            beyond = out_near - jnp.where(lane % 2 == 0, rot(near, -1), rot(near, 1))
        else:
            out_normal = -out_normal if side == 2 else out_normal
            beyond = out_near
        speed = SCALE * (normal + out_normal) * (wet * jnp.clip(out_depth - level, 0.0, 1.0))
        flux = jnp.maximum(speed, 0.0) * (5.0 * out_near + 2.0 * near - out_far)
        flux += jnp.minimum(speed, 0.0) * (2.0 * out_near + 5.0 * near - far)
        inner_flux = rim_speed * beyond
        for place, (change, share) in enumerate(((wet * (flux + inner_flux), ratio),
                                                 (-inner_wet * inner_flux, inner_ratio))):
            other = jnp.where(level == 0.0, pltpu.roll(change, rows - 1, 0), pltpu.roll(change, 1, 0))
            delta_ref[2 * side + place] = change + share * (other - change)

    lane = lane_of(8)
    def spread(pair):
        mine = pl.ds(8 * pair, 8)
        near, deep, south, south_in, north, north_in = [delta_ref[index, mine, :] for index in range(2 * SIDES)]
        groups = []
        for at in range(2):
            index = 2 * (lane // 4) + (lane % 4) // 2 + 64 * at
            outer, inner = lane_take(near, index), lane_take(deep, index)
            groups.append(jnp.where((lane % 4 == 1) | (lane % 4 == 2), outer, inner))
        placed = [(groups[gap // 32], 4 * (gap % 32), IB * gap - 2, 4) for gap in range(GAPS)]
        placed += [(south, 0, 0, IB), (south_in, 0, IB, IB)]
        placed += [(north, 0, CELLS - IB, IB), (north_in, 0, CELLS - 2 * IB, IB)]
        for tile in range(TILES):
            at, stop = tile * LANES, min((tile + 1) * LANES, CELLS)
            change = jnp.zeros((8, LANES), jnp.float32)
            for source, origin, start, wide in placed:
                low, high = max(start, at, 0), min(start + wide, stop)
                if low < high:
                    inside = (lane >= low - at) & (lane < high - at)
                    change += jnp.where(inside, rot(source, start - at - origin), 0.0)
            yield at, stop, change[:, : stop - at]

    for pair in range(AHEAD):
        for at, stop, change in spread(pair):
            ahead_ref[pl.ds(8 * pair, 8), at:stop] = change
    out_copies = []
    for pair in range(pairs):
        mine = pl.ds(8 * pair, 8)
        in_copies[pair].wait()
        if pair < AHEAD:
            for at in range(0, CELLS, LANES):
                stop = min(at + LANES, CELLS)
                y_ref[mine, at:stop] = y_ref[mine, at:stop] + ahead_ref[mine, at:stop]
        else:
            for at, stop, change in spread(pair):
                y_ref[mine, at:stop] = y_ref[mine, at:stop] + change
        copy = pltpu.make_async_copy(
            y_ref.at[mine].reshape(2, 4, CELLS), out_ref.at[pl.ds(2 * pair, 2)], out_sems.at[pair])
        copy.start()
        out_copies.append(copy)
    for copy in out_copies:
        copy.wait()


def route_codes(block_owner, neighbours, fold_partner, slot_total):
    block_count = block_owner.shape[0]
    hits = block_owner[None, :] == jnp.arange(slot_total, dtype=jnp.int32)[:, None]
    links = jnp.concatenate([neighbours, fold_partner[:, None]], axis=1)
    linked = links[:, :, None] == jnp.arange(block_count, dtype=jnp.int32)[None, None, :]
    link_slots = jnp.max(jnp.where(linked, block_owner[None, None, :], -1), axis=2)
    link_slots = jnp.concatenate([link_slots, block_owner[:, None]], axis=1)
    return jnp.max(jnp.where(hits[:, :, None], link_slots[None], -1), axis=1)


def per_device(tracers, velocity, kappa, kmt, block_owner, neighbours, fold_partner):
    slot_count, chans = tracers.shape[:2]
    sub_count = lax.axis_size("sub")
    device_count = lax.axis_size("blk") * sub_count
    if device_count % PARTS or chans != 4 or slot_count % 2 or slot_count < 2 * FIRST_PAIRS + 2:
        raise ValueError("unsupported sizes")
    my_index = (lax.axis_index("blk") * sub_count + lax.axis_index("sub")).astype(jnp.int32).reshape(1)
    axes = ("blk", "sub")
    pairs = slot_count // 2
    slot_total = device_count * slot_count
    state_rows = 4 * slot_count
    f32 = jnp.float32
    in_hbm = pl.BlockSpec(memory_space=pltpu.HBM)
    in_vmem = pl.BlockSpec(memory_space=pltpu.VMEM)
    in_smem = pl.BlockSpec(memory_space=pltpu.SMEM)
    dma = pltpu.SemaphoreType.DMA
    limit = pltpu.CompilerParams(vmem_limit_bytes=32 * 1024 * 1024)

    def exchanged(pieces):
        pieces = pieces.reshape(device_count, slot_count, 1, LANES)
        return lax.all_to_all(pieces, axes, 0, 0, tiled=True).reshape(slot_total, LANES)

    pack = pl.pallas_call(
        pack_kernel,
        out_shape=jax.ShapeDtypeStruct((slot_total, LANES), f32),
        in_specs=[in_hbm, in_hbm, in_hbm],
        out_specs=in_vmem,
        scratch_shapes=[
            pltpu.VMEM((state_rows, CELLS), f32),
            pltpu.VMEM((state_rows, CELLS), f32),
            pltpu.VMEM((slot_count, CELLS), f32),
            pltpu.VMEM((9, state_rows, LANES), f32),
            dma((pairs,)),
            dma((pairs,)),
            dma,
        ],
        cost_estimate=pl.CostEstimate(flops=4_000_000, bytes_accessed=2_400_000, transcendentals=0),
    )(tracers, velocity, kmt)
    held = exchanged(pack)
    codes = route_codes(block_owner, neighbours, fold_partner, slot_total)

    def bulk(first, some, codes, base):
        kernel = functools.partial(bulk_kernel, first)
        extra = [] if base is None else [base]
        if extra:
            kernel = lambda *refs: bulk_kernel(first, *refs[:6], *refs[7:])
        return pl.pallas_call(
            kernel,
            out_shape=[
                jax.ShapeDtypeStruct(tracers.shape, f32),
                jax.ShapeDtypeStruct((OWN * SIDES + 1, 8 * some, LANES), f32),
            ],
            in_specs=[in_smem, in_hbm, in_hbm, in_hbm, in_hbm, in_vmem] + [in_hbm] * len(extra),
            out_specs=[in_hbm, in_vmem],
            scratch_shapes=[
                pltpu.VMEM((8 * some, CELLS), f32),
                pltpu.VMEM((8 * some, CELLS), f32),
                pltpu.VMEM((8 * some, CELLS), f32),
                pltpu.VMEM((slot_count, CELLS), f32),
                pltpu.VMEM((slot_count, CELLS), f32),
                pltpu.VMEM((8 * some, CELLS), f32),
                pltpu.VMEM((8 * some, CELLS), f32),
                pltpu.VMEM((8, WIDE), f32),
                pltpu.VMEM((8, WIDE), f32),
                dma((some,)),
                dma((some,)),
                dma((some,)),
                dma((2,)),
            ],
            input_output_aliases={6: 0} if extra else {},
            compiler_params=limit,
            cost_estimate=pl.CostEstimate(flops=4_000_000 * some, bytes_accessed=800_000 * some, transcendentals=0),
        )(my_index, tracers, velocity, kmt, kappa, codes, *extra)

    base, edge_a = bulk(0, FIRST_PAIRS, codes, None)
    held, edge_a = lax.optimization_barrier((held, edge_a))

    routed_rows = PARTS * slot_count
    blocks = dict(in_specs=[in_smem, in_vmem, in_vmem], out_specs=in_vmem)
    if device_count > PARTS:
        blocks = dict(
            grid=(device_count // PARTS,),
            in_specs=[
                in_smem,
                pl.BlockSpec((routed_rows, 6), lambda step: (step, 0)),
                pl.BlockSpec((slot_total, LANES), lambda step: (0, 0)),
            ],
            out_specs=pl.BlockSpec((routed_rows, LANES), lambda step: (step, 0)),
        )
    routed = pl.pallas_call(
        route_kernel,
        out_shape=jax.ShapeDtypeStruct((slot_total, LANES), f32),
        compiler_params=limit,
        **blocks,
    )(my_index, codes, held)
    routed, base = lax.optimization_barrier((routed, base))
    base, edge_b = bulk(FIRST_PAIRS, pairs - FIRST_PAIRS, codes, base)
    halo = exchanged(routed)[: PARTS * slot_count]

    return pl.pallas_call(
        finish_kernel,
        out_shape=jax.ShapeDtypeStruct(tracers.shape, f32),
        in_specs=[in_vmem, in_vmem, in_vmem, in_hbm],
        out_specs=in_hbm,
        scratch_shapes=[
            pltpu.VMEM((state_rows, CELLS), f32),
            pltpu.VMEM((8 * AHEAD, CELLS), f32),
            pltpu.VMEM((12, state_rows, LANES), f32),
            pltpu.VMEM((2 * SIDES, state_rows, LANES), f32),
            dma((pairs,)),
            dma((pairs,)),
        ],
        input_output_aliases={3: 0},
        compiler_params=limit,
    )(halo, edge_a, edge_b, base)


def solution(mesh):
    placed = (
        P(("blk", "sub"), None, None),
        P(("blk", "sub"), None, None),
        P(("blk", "sub"), None),
        P(("blk", "sub"), None),
        P(),
        P(),
        P(),
    )
    return jax.shard_map(
        per_device,
        mesh=mesh,
        in_specs=placed,
        out_specs=P(("blk", "sub"), None, None),
        check_vma=False,
    )
```

```python
import functools

import jax
import jax.numpy as jnp
from jax import lax
from jax.experimental import pallas as pl
from jax.experimental.pallas import tpu as pltpu
from jax.sharding import PartitionSpec as P

IB = 90
JB = 60
CELLS = IB * JB
COURANT = 0.2
LANES = 128
TILES = -(-CELLS // LANES)
WIDE = TILES * LANES
GAPS = JB + 1
HALF = IB // 2
PARTS = 32
X_PART = 22
SPARE = 48
PIECE = 16
SCALE = COURANT / 12.0
SIDES = 3
OWN = 8
FIRST_PAIRS = 2
AHEAD = 3


def lane_of(rows):
    return lax.broadcasted_iota(jnp.int32, (rows, LANES), 1)


def rot(value, shift):
    shift = shift % LANES
    return value if shift == 0 else pltpu.roll(value, shift, 1)


def sublanes(value, shift):
    return pltpu.roll(value, shift % 8, 0)


def once(make):
    held = {}

    def get(tile):
        if tile not in held:
            held[tile] = make(tile)
        return held[tile]

    return get


def shifted(get, distance):
    offset = distance % LANES
    turned = once(lambda tile: rot(get(tile), -offset))

    def make(tile):
        low = tile + distance // LANES
        first = turned(low) if 0 <= low < TILES else jnp.zeros((8, LANES), jnp.float32)
        second = turned(low + 1) if 0 <= low + 1 < TILES else jnp.zeros((8, LANES), jnp.float32)
        return jnp.where(lane_of(8) < LANES - offset, first, second)

    return once(make)


def window(get, start, rows):
    tile, offset = start // LANES, start % LANES
    value = get(tile)
    if offset > 0 and tile + 1 < TILES:
        value = jnp.where(lane_of(rows) < offset, get(tile + 1), value)
    return rot(value, -offset)


def gap_strip(get, offset, wide, rows):
    lane = lane_of(rows)
    place = 1 if wide == 1 and offset > 0 else 0
    value = jnp.zeros((rows, LANES), jnp.float32)
    for turn in range(16):
        cells = []
        for gap in range(turn, GAPS, 16):
            cell = IB * gap + offset
            if cell + wide > 0:
                cells.append((max(cell, 0) % LANES, max(cell, 0) // LANES))
        cells.sort()
        merged = get(cells[0][1])
        for at, tile in cells[1:]:
            merged = jnp.where(lane >= at, get(tile), merged)
        moved = rot(merged, 2 * turn + place - IB * turn - offset)
        value = jnp.where(lane % 32 >= 2 * turn + place, moved, value)
    return value


def edge_strip(get, rows):
    return jnp.where(lane_of(rows) == 0, 0.0, gap_strip(get, -1, 2, rows))


def inner_strip(get, rows):
    return jnp.where(lane_of(rows) % 2 == 0, gap_strip(get, -2, 1, rows), gap_strip(get, 1, 1, rows))


def lane_take(value, index):
    return jnp.take_along_axis(value, index, axis=1, mode="promise_in_bounds")


def tile_getter(ref, rows, count):
    def get(tile):
        if tile + 1 < TILES:
            return ref[rows, tile * LANES : (tile + 1) * LANES]
        rest = jnp.zeros((count, WIDE - CELLS), jnp.float32)
        return jnp.concatenate([ref[rows, tile * LANES : CELLS], rest], axis=1)

    return get


def joined(south, north, half, rows):
    if half == 0:
        return jnp.where(lane_of(rows) < 64, south, rot(north, 64))
    return jnp.where(lane_of(rows) < 64, rot(south, -HALF), rot(north, 64 - HALF))


def pair_copies(source, target, sems, first, pairs):
    copies = []
    for pair in range(pairs):
        into = target.at[pl.ds(8 * pair, 8)].reshape(2, 4, CELLS)
        copies.append(pltpu.make_async_copy(source.at[pl.ds(2 * (first + pair), 2)], into, sems.at[pair]))
    return copies


def pack_kernel(tracer_ref, velocity_ref, depth_ref, out_ref, x_ref, v_ref, d_ref, strip_ref, x_sems, v_sems, d_sem):
    count = depth_ref.shape[0]
    pairs = count // 2
    x_copies = pair_copies(tracer_ref, x_ref, x_sems, 0, pairs)
    v_copies = pair_copies(velocity_ref, v_ref, v_sems, 0, pairs)
    d_copy = pltpu.make_async_copy(depth_ref, d_ref, d_sem)
    for pair in range(pairs):
        x_copies[pair].start()
        v_copies[pair].start()
    d_copy.start()
    for pair in range(pairs):
        rows = pl.ds(8 * pair, 8)
        if pair in (0, FIRST_PAIRS):
            for arrived in range(pair, FIRST_PAIRS if pair == 0 else pairs):
                x_copies[arrived].wait()
                v_copies[arrived].wait()
            if pair > 0:
                d_copy.wait()
        get_x = tile_getter(x_ref, rows, 8)
        near, far = edge_strip(get_x, 8), inner_strip(get_x, 8)
        south = [window(get_x, 0, 8), window(get_x, IB, 8)]
        north = [window(get_x, CELLS - IB, 8), window(get_x, CELLS - 2 * IB, 8)]
        get_v = tile_getter(v_ref, rows, 8)
        v_south, v_north = window(get_v, 0, 8), window(get_v, CELLS - IB, 8)
        strips = [joined(south[0], north[0], half, 8) for half in range(2)]
        strips += [joined(south[1], north[1], half, 8) for half in range(2)]
        strips += [joined(v_south, v_north, half, 8) for half in range(2)]
        strips += [near, far, edge_strip(get_v, 8)]
        for index, strip in enumerate(strips):
            strip_ref[index, rows, :] = strip

    if out_ref.shape[0] > PARTS * count:
        rest = out_ref.shape[0] - PARTS * count
        out_ref[PARTS * count :, :] = jnp.zeros((rest, LANES), jnp.float32)
    slot_lane = lane_of(count)
    get_d = tile_getter(d_ref, slice(None), count)
    d_south, d_north = window(get_d, 0, count), window(get_d, CELLS - IB, count)
    d_gaps = edge_strip(get_d, count)
    spare = (slot_lane >= SPARE) & (slot_lane < SPARE + PIECE)

    def put(part, value):
        out_ref[part * count : (part + 1) * count, :] = value

    for chan in range(4):
        rows = pl.ds(chan, count, stride=4)
        for half in range(2):
            for deep in range(2):
                part = 2 * (4 * deep + chan) + half
                value = strip_ref[2 * deep + half, rows, :]
                if part < 8:
                    value = jnp.where(spare, rot(d_gaps, SPARE - PIECE * part), value)
                put(part, value)
            if chan >= 2:
                put(2 * (8 + chan - 2) + half, strip_ref[4 + half, rows, :])
        put(X_PART + chan, strip_ref[6, rows, :])
        put(X_PART + 4 + chan, strip_ref[7, rows, :])
        if chan < 2:
            put(X_PART + 8 + chan, strip_ref[8, rows, :])
    for half in range(2):
        put(20 + half, joined(d_south, d_north, half, count))


def route_kernel(part_ref, code_ref, held_ref, out_ref):
    total = held_ref.shape[0]
    rows = out_ref.shape[0]
    part = part_ref[0]
    fold = code_ref[:, 4:5]
    wanted = [code_ref[:, side : side + 1] for side in range(3)] + [jnp.maximum(code_ref[:, 3:4], fold)]
    picked = jnp.zeros((len(wanted) * rows, 2 * LANES), jnp.float32)
    for start in range(0, total, rows):
        held = held_ref[start : start + rows, :]
        high = held.astype(jnp.bfloat16)
        low = (held - high.astype(jnp.float32)).astype(jnp.bfloat16)
        halves = jnp.concatenate([high, low], axis=1)
        source = lax.broadcasted_iota(jnp.int32, (rows, rows), 1) + start
        one_hots = [jnp.where(code == source, 1.0, 0.0).astype(jnp.bfloat16) for code in wanted]
        picked += jnp.dot(jnp.concatenate(one_hots, axis=0), halves, preferred_element_type=jnp.float32)
    picked = picked[:, :LANES] + picked[:, LANES:]
    west, east, south, north = [picked[side * rows : (side + 1) * rows] for side in range(4)]
    lane = lane_of(rows)
    along_x = (part >= X_PART) | ((part < 8) & (lane >= SPARE) & (lane < SPARE + PIECE))
    x_side = jnp.where(lane % 2 == 0, west, east)
    y_side = jnp.where(lane < 64, jnp.where(fold >= 0, rot(north, 64), north), south)
    out_ref[...] = jnp.where(along_x, x_side, y_side)


def bulk_kernel(first, my_ref, tracer_ref, velocity_ref, depth_ref, kappa_ref, code_ref,
                base_ref, edge_ref, y_ref, x_ref, v_ref, d_ref, k_ref, d8_ref, k8_ref, w_ref, z_ref, x_sems, v_sems, y_sems, d_sems):
    count = depth_ref.shape[0]
    pairs = edge_ref.shape[1] // 8
    x_copies = pair_copies(tracer_ref, x_ref, x_sems, first, pairs)
    v_copies = pair_copies(velocity_ref, v_ref, v_sems, first, pairs)
    d_copy = pltpu.make_async_copy(depth_ref, d_ref, d_sems.at[0])
    k_copy = pltpu.make_async_copy(kappa_ref, k_ref, d_sems.at[1])
    d_copy.start()
    k_copy.start()
    for pair in range(pairs):
        v_copies[pair].start()
        x_copies[pair].start()
    lane = lane_of(8)
    row = lax.broadcasted_iota(jnp.int32, (8, LANES), 0)
    x_row, even, place = row % 4 < 2, row % 2 == 0, row % 4
    level = (row % 2).astype(jnp.float32)
    zero = jnp.zeros((8, LANES), jnp.float32)

    def all_rows(value, chosen):
        result = value
        for at in range(4):
            if at != chosen:
                result = jnp.where(place == at, sublanes(value, at - chosen), result)
        return result

    def wet_of(depth):
        return jnp.clip(depth - level, 0.0, 1.0)

    for copy, source, target in ((d_copy, d_ref, d8_ref), (k_copy, k_ref, k8_ref)):
        copy.wait()
        for pair in range(pairs):
            slot = 2 * (first + pair)
            for start in range(0, CELLS, LANES):
                columns = slice(start, min(start + LANES, CELLS))
                shape = (8, columns.stop - start)
                top, low = [jnp.broadcast_to(source[slot + at : slot + at + 1, columns], shape) for at in range(2)]
                target[8 * pair : 8 * pair + 8, columns] = jnp.where(row[:, : shape[1]] < 4, top, low)

    def one_pair(pair):
        slot = 2 * (first + pair)
        rows = pl.ds(pl.multiple_of(8 * pair, 8), 8)
        for source, target, sems in ((velocity_ref, v_ref, v_sems), (tracer_ref, x_ref, x_sems)):
            pltpu.make_async_copy(
                source.at[pl.ds(0, 2)], target.at[rows].reshape(2, 4, CELLS), sems.at[pair]).wait()

        codes = [code_ref[pl.ds(my_ref[0] * count + slot + at, 1), :] for at in range(2)]

        def flag(column):
            pieces = [jnp.broadcast_to(code[:, column : column + 1], (8, LANES)) for code in codes]
            return jnp.where(row < 4, pieces[0], pieces[1]) >= 0

        live, folded = flag(5), flag(4)
        state, velocity = once(tile_getter(x_ref, rows, 8)), once(tile_getter(v_ref, rows, 8))
        depth, kappa = once(tile_getter(d8_ref, rows, 8)), once(tile_getter(k8_ref, rows, 8))
        wet = once(lambda tile: wet_of(depth(tile)))

        @once
        def ratio(tile):
            other = jnp.clip(depth(tile) - (1.0 - level), 0.0, 1.0)
            coupling = kappa(tile) * (wet(tile) * other)
            return coupling / (1.0 + 2.0 * coupling)

        next_vel = [shifted(velocity, 1), shifted(velocity, IB)]
        next_wet = [shifted(wet, 1), shifted(wet, IB)]

        @once
        def face(tile):
            rims = [at - tile * LANES for at in range(IB - 1, CELLS, IB) if at // LANES == tile]
            rim = functools.reduce(jnp.logical_or, [lane == at for at in rims]) if rims else None
            across = next_wet[0](tile) if rim is None else jnp.where(rim, 0.0, next_wet[0](tile))
            speed = velocity(tile) + jnp.where(x_row, next_vel[0](tile), next_vel[1](tile))
            value = SCALE * speed * (wet(tile) * jnp.where(x_row, across, next_wet[1](tile)))
            w_ref[:, tile * LANES : (tile + 1) * LANES] = value
            return value

        face_x = once(lambda tile: jnp.where(x_row, face(tile), sublanes(face(tile), 2)))
        face_y = once(lambda tile: jnp.where(x_row, sublanes(face(tile), -2), face(tile)))
        five = once(lambda tile: 5.0 * state(tile))
        two = once(lambda tile: 2.0 * state(tile))

        def divergence(speed, distance):
            before, after = shifted(state, -distance), shifted(state, distance)
            lower = once(lambda tile: five(tile) - before(tile) + 2.0 * after(tile))
            upper = shifted(once(lambda tile: five(tile) - after(tile)), distance)

            @once
            def flux(tile):
                value = jnp.maximum(speed(tile), 0.0) * lower(tile)
                return value + jnp.minimum(speed(tile), 0.0) * (two(tile) + upper(tile))

            back = shifted(flux, -distance)
            for stage in (after, before, lower, upper, flux, back):
                for tile in range(TILES):
                    stage(tile)
            return once(lambda tile: flux(tile) - back(tile))

        for stage in (depth, wet, ratio, *next_vel, *next_wet, face):
            for tile in range(TILES):
                stage(tile)
        change_x, change_y = divergence(face_x, 1), divergence(face_y, IB)
        for tile in range(TILES):
            explicit = state(tile) - wet(tile) * (change_x(tile) + change_y(tile))
            other = jnp.where(even, sublanes(explicit, -1), sublanes(explicit, 1))
            value = jnp.where(live, explicit + ratio(tile) * (other - explicit), zero)
            stop = min((tile + 1) * LANES, CELLS)
            y_ref[rows, tile * LANES : stop] = value[:, : stop - tile * LANES]
            mixed = jnp.where(x_row, face(tile), jnp.where(even, ratio(tile), depth(tile)))
            z_ref[:, tile * LANES : (tile + 1) * LANES] = mixed

        pltpu.make_async_copy(
            y_ref.at[rows].reshape(2, 4, CELLS), base_ref.at[pl.ds(slot, 2)], y_sems.at[pair]).start()
        get_w, get_z = [lambda tile, ref=ref: ref[:, tile * LANES : (tile + 1) * LANES] for ref in (w_ref, z_ref)]
        east = lane % 2 == 0
        near, far, normal = edge_strip(state, 8), inner_strip(state, 8), edge_strip(velocity, 8)
        outer, inner = edge_strip(get_z, 8), inner_strip(get_z, 8)
        normal = jnp.where(x_row, normal, sublanes(normal, 2))
        rim_speed = jnp.where(east, inner, outer)
        rim_speed = jnp.where(x_row, rim_speed, sublanes(rim_speed, 2))
        sides = [(
            near, far, jnp.where(east, -normal, normal), jnp.where(east, -rim_speed, rim_speed), outer, inner,
        )]
        for outer, inner, edge, sign in ((0, IB, 0, 1.0), (CELLS - IB, CELLS - 2 * IB, CELLS - 2 * IB, -1.0)):
            normal, rim_speed = window(velocity, outer, 8), window(get_w, edge, 8)
            normal = sign * jnp.where(x_row, sublanes(normal, -2), normal)
            rim_speed = sign * jnp.where(x_row, sublanes(rim_speed, -2), rim_speed)
            sides.append((window(state, outer, 8), window(state, inner, 8), normal, rim_speed,
                          window(get_z, outer, 8), window(get_z, inner, 8)))
        for side, (near, far, normal, rim_speed, outer, inner) in enumerate(sides):
            values = (near, far, normal, jnp.where(live, jnp.maximum(rim_speed, 0.0), zero), wet_of(all_rows(outer, 3)),
                      wet_of(all_rows(inner, 3)), all_rows(outer, 2), all_rows(inner, 2))
            for index, value in enumerate(values):
                edge_ref[OWN * side + index, rows, :] = value
        edge_ref[OWN * SIDES, rows, :] = jnp.where(folded, 1.0, zero)

    pl.loop(0, pairs)(one_pair)
    for pair in range(pairs):
        slots = pl.ds(2 * (first + pair), 2)
        rows = y_ref.at[pl.ds(8 * pair, 8)].reshape(2, 4, CELLS)
        pltpu.make_async_copy(rows, base_ref.at[slots], y_sems.at[pair]).wait()


def finish_kernel(halo_ref, edge_a_ref, edge_b_ref, base_ref, out_ref,
                  y_ref, ahead_ref, raw_ref, delta_ref, in_sems, out_sems):
    count = out_ref.shape[0]
    pairs = count // 2
    rows = 4 * count
    in_copies = pair_copies(base_ref, y_ref, in_sems, 0, pairs)
    for copy in in_copies:
        copy.start()

    def own(index):
        return jnp.concatenate([edge_a_ref[index], edge_b_ref[index]], axis=0)

    lane = lane_of(rows)
    level = (lax.broadcasted_iota(jnp.int32, (rows, LANES), 0) % 2).astype(jnp.float32)

    def part(index):
        return halo_ref[index * count : (index + 1) * count, :]

    def assembled(index, parts):
        for chan, value in enumerate(parts):
            raw_ref[index, pl.ds(chan, count, stride=4), :] = value
        return raw_ref[index]

    mirror = jnp.where(lane < IB, IB - 1 - lane, lane)
    slot_lane = lane_of(count)
    depth_x = rot(part(0), -SPARE)
    for index in range(1, 8):
        depth_x = jnp.where(slot_lane >= PIECE * index, rot(part(index), PIECE * index - SPARE), depth_x)
    x_raw = [[part(X_PART + chan) for chan in range(4)], [part(X_PART + 4 + chan) for chan in range(4)],
             [part(X_PART + 8 + chan % 2) for chan in range(4)], [depth_x] * 4]
    y_values = [list(range(4)), list(range(4, 8)), [8, 9, 8, 9], [10] * 4]
    x_halo, south_halo, north_raw = [], [], []
    for kind in range(4):
        raw = assembled(3 * kind, x_raw[kind])
        x_halo.append(jnp.where(lane % 2 == 0, rot(raw, 1), rot(raw, -1)))
        first, second = [assembled(3 * kind + 1 + half, [part(2 * value + half) for value in y_values[kind]])
                         for half in range(2)]
        south_halo.append(jnp.where(lane < HALF, rot(first, 64), rot(second, 64 + HALF)))
        north_raw.append(jnp.where(lane < HALF, first, rot(second, HALF)))
    folded = own(OWN * SIDES) > 0.0
    north_halo = []
    for kind, raw in enumerate(north_raw):
        turned = lane_take(raw, mirror)
        north_halo.append(jnp.where(folded, -turned if kind == 2 else turned, raw))

    for side, (out_near, out_far, out_normal, out_depth) in enumerate((x_halo, south_halo, north_halo)):
        near, far, normal, rim_speed, wet, inner_wet, ratio, inner_ratio = [
            own(OWN * side + index) for index in range(OWN)]
        if side == 0:
            out_normal = jnp.where(lane % 2 == 0, -out_normal, out_normal)
            beyond = out_near - jnp.where(lane % 2 == 0, rot(near, -1), rot(near, 1))
        else:
            out_normal = -out_normal if side == 2 else out_normal
            beyond = out_near
        speed = SCALE * (normal + out_normal) * (wet * jnp.clip(out_depth - level, 0.0, 1.0))
        flux = jnp.maximum(speed, 0.0) * (5.0 * out_near + 2.0 * near - out_far)
        flux += jnp.minimum(speed, 0.0) * (2.0 * out_near + 5.0 * near - far)
        inner_flux = rim_speed * beyond
        for place, (change, share) in enumerate(((wet * (flux + inner_flux), ratio),
                                                 (-inner_wet * inner_flux, inner_ratio))):
            other = jnp.where(level == 0.0, pltpu.roll(change, rows - 1, 0), pltpu.roll(change, 1, 0))
            delta_ref[2 * side + place] = change + share * (other - change)

    lane = lane_of(8)
    def spread(pair):
        mine = pl.ds(8 * pair, 8)
        near, deep, south, south_in, north, north_in = [delta_ref[index, mine, :] for index in range(2 * SIDES)]
        groups = []
        for at in range(2):
            index = 2 * (lane // 4) + (lane % 4) // 2 + 64 * at
            outer, inner = lane_take(near, index), lane_take(deep, index)
            groups.append(jnp.where((lane % 4 == 1) | (lane % 4 == 2), outer, inner))
        placed = [(groups[gap // 32], 4 * (gap % 32), IB * gap - 2, 4) for gap in range(GAPS)]
        placed += [(south, 0, 0, IB), (south_in, 0, IB, IB)]
        placed += [(north, 0, CELLS - IB, IB), (north_in, 0, CELLS - 2 * IB, IB)]
        for tile in range(TILES):
            at, stop = tile * LANES, min((tile + 1) * LANES, CELLS)
            change = jnp.zeros((8, LANES), jnp.float32)
            for source, origin, start, wide in placed:
                low, high = max(start, at, 0), min(start + wide, stop)
                if low < high:
                    inside = (lane >= low - at) & (lane < high - at)
                    change += jnp.where(inside, rot(source, start - at - origin), 0.0)
            yield at, stop, change[:, : stop - at]

    for pair in range(AHEAD):
        for at, stop, change in spread(pair):
            ahead_ref[pl.ds(8 * pair, 8), at:stop] = change
    out_copies = []
    for pair in range(pairs):
        mine = pl.ds(8 * pair, 8)
        if pair <= AHEAD:
            for arrived in range(pair, pair + 1 if pair < AHEAD else pairs):
                in_copies[arrived].wait()
        if pair < AHEAD:
            for at in range(0, CELLS, LANES):
                stop = min(at + LANES, CELLS)
                y_ref[mine, at:stop] = y_ref[mine, at:stop] + ahead_ref[mine, at:stop]
        else:
            for at, stop, change in spread(pair):
                y_ref[mine, at:stop] = y_ref[mine, at:stop] + change
        out_copies.append(pltpu.make_async_copy(
            y_ref.at[mine].reshape(2, 4, CELLS), out_ref.at[pl.ds(2 * pair, 2)], out_sems.at[pair]))
        if pair < AHEAD:
            out_copies[pair].start()
    for copy in out_copies[AHEAD:]:
        copy.start()
    for copy in out_copies:
        copy.wait()


def route_codes(block_owner, neighbours, fold_partner, slot_total):
    block_count = block_owner.shape[0]
    hits = block_owner[None, :] == jnp.arange(slot_total, dtype=jnp.int32)[:, None]
    links = jnp.concatenate([neighbours, fold_partner[:, None]], axis=1)
    linked = links[:, :, None] == jnp.arange(block_count, dtype=jnp.int32)[None, None, :]
    link_slots = jnp.max(jnp.where(linked, block_owner[None, None, :], -1), axis=2)
    link_slots = jnp.concatenate([link_slots, block_owner[:, None]], axis=1)
    return jnp.max(jnp.where(hits[:, :, None], link_slots[None], -1), axis=1)


def per_device(tracers, velocity, kappa, kmt, block_owner, neighbours, fold_partner):
    slot_count, chans = tracers.shape[:2]
    sub_count = lax.axis_size("sub")
    device_count = lax.axis_size("blk") * sub_count
    if device_count % PARTS or chans != 4 or slot_count % 2 or slot_count < 2 * FIRST_PAIRS + 2:
        raise ValueError("unsupported sizes")
    my_index = (lax.axis_index("blk") * sub_count + lax.axis_index("sub")).astype(jnp.int32).reshape(1)
    axes = ("blk", "sub")
    pairs = slot_count // 2
    slot_total = device_count * slot_count
    state_rows = 4 * slot_count
    f32 = jnp.float32
    in_hbm = pl.BlockSpec(memory_space=pltpu.HBM)
    in_vmem = pl.BlockSpec(memory_space=pltpu.VMEM)
    in_smem = pl.BlockSpec(memory_space=pltpu.SMEM)
    dma = pltpu.SemaphoreType.DMA
    limit = pltpu.CompilerParams(vmem_limit_bytes=32 * 1024 * 1024)

    def exchanged(pieces):
        pieces = pieces.reshape(device_count, slot_count, 1, LANES)
        return lax.all_to_all(pieces, axes, 0, 0, tiled=True).reshape(slot_total, LANES)

    pack = pl.pallas_call(
        pack_kernel,
        out_shape=jax.ShapeDtypeStruct((slot_total, LANES), f32),
        in_specs=[in_hbm, in_hbm, in_hbm],
        out_specs=in_vmem,
        scratch_shapes=[
            pltpu.VMEM((state_rows, CELLS), f32),
            pltpu.VMEM((state_rows, CELLS), f32),
            pltpu.VMEM((slot_count, CELLS), f32),
            pltpu.VMEM((9, state_rows, LANES), f32),
            dma((pairs,)),
            dma((pairs,)),
            dma,
        ],
        cost_estimate=pl.CostEstimate(flops=4_000_000, bytes_accessed=2_400_000, transcendentals=0),
    )(tracers, velocity, kmt)
    held = exchanged(pack)
    codes = route_codes(block_owner, neighbours, fold_partner, slot_total)

    def bulk(first, some, codes, base):
        kernel = functools.partial(bulk_kernel, first)
        extra = [] if base is None else [base]
        if extra:
            kernel = lambda *refs: bulk_kernel(first, *refs[:6], *refs[7:])
        return pl.pallas_call(
            kernel,
            out_shape=[
                jax.ShapeDtypeStruct(tracers.shape, f32),
                jax.ShapeDtypeStruct((OWN * SIDES + 1, 8 * some, LANES), f32),
            ],
            in_specs=[in_smem, in_hbm, in_hbm, in_hbm, in_hbm, in_vmem] + [in_hbm] * len(extra),
            out_specs=[in_hbm, in_vmem],
            scratch_shapes=[
                pltpu.VMEM((8 * some, CELLS), f32),
                pltpu.VMEM((8 * some, CELLS), f32),
                pltpu.VMEM((8 * some, CELLS), f32),
                pltpu.VMEM((slot_count, CELLS), f32),
                pltpu.VMEM((slot_count, CELLS), f32),
                pltpu.VMEM((8 * some, CELLS), f32),
                pltpu.VMEM((8 * some, CELLS), f32),
                pltpu.VMEM((8, WIDE), f32),
                pltpu.VMEM((8, WIDE), f32),
                dma((some,)),
                dma((some,)),
                dma((some,)),
                dma((2,)),
            ],
            input_output_aliases={6: 0} if extra else {},
            compiler_params=limit,
            cost_estimate=pl.CostEstimate(flops=4_000_000 * some, bytes_accessed=800_000 * some, transcendentals=0),
        )(my_index, tracers, velocity, kmt, kappa, codes, *extra)

    base, edge_a = bulk(0, FIRST_PAIRS, codes, None)
    held, edge_a = lax.optimization_barrier((held, edge_a))

    routed_rows = PARTS * slot_count
    blocks = dict(in_specs=[in_smem, in_vmem, in_vmem], out_specs=in_vmem)
    if device_count > PARTS:
        blocks = dict(
            grid=(device_count // PARTS,),
            in_specs=[
                in_smem,
                pl.BlockSpec((routed_rows, 6), lambda step: (step, 0)),
                pl.BlockSpec((slot_total, LANES), lambda step: (0, 0)),
            ],
            out_specs=pl.BlockSpec((routed_rows, LANES), lambda step: (step, 0)),
        )
    routed = pl.pallas_call(
        route_kernel,
        out_shape=jax.ShapeDtypeStruct((slot_total, LANES), f32),
        compiler_params=limit,
        **blocks,
    )(my_index, codes, held)
    routed, base = lax.optimization_barrier((routed, base))
    base, edge_b = bulk(FIRST_PAIRS, pairs - FIRST_PAIRS, codes, base)
    halo = exchanged(routed)[: PARTS * slot_count]

    return pl.pallas_call(
        finish_kernel,
        out_shape=jax.ShapeDtypeStruct(tracers.shape, f32),
        in_specs=[in_vmem, in_vmem, in_vmem, in_hbm],
        out_specs=in_hbm,
        scratch_shapes=[
            pltpu.VMEM((state_rows, CELLS), f32),
            pltpu.VMEM((8 * AHEAD, CELLS), f32),
            pltpu.VMEM((12, state_rows, LANES), f32),
            pltpu.VMEM((2 * SIDES, state_rows, LANES), f32),
            dma((pairs,)),
            dma((pairs,)),
        ],
        input_output_aliases={3: 0},
        compiler_params=limit,
    )(halo, edge_a, edge_b, base)


def solution(mesh):
    placed = (
        P(("blk", "sub"), None, None),
        P(("blk", "sub"), None, None),
        P(("blk", "sub"), None),
        P(("blk", "sub"), None),
        P(),
        P(),
        P(),
    )
    return jax.shard_map(
        per_device,
        mesh=mesh,
        in_specs=placed,
        out_specs=P(("blk", "sub"), None, None),
        check_vma=False,
    )
```
